128 devices in a mesh: grp: 8 (over y_hi, x), seq: 16 (over y_lo, z, core).
Axes of the slice: x: 4, y: 4 (y_hi: 2, y_lo: 2; y = y_hi * 2 + y_lo), z: 4, core: 2. Of those that a mesh axis runs over, the one named last changes fastest.
Arguments:
- tokens: bfloat16 [2, 8192, 2048], P(None, ('grp', 'seq')), may hold values from -6 to 6
- segment_ids: int32 [2, 8192], P(None, 'grp'), may hold values from -1 to 32, as said below
- w_qkv: bfloat16 [2048, 1920], P(('grp', 'seq')), may hold values from -0.125 to 0.125
- w_out: bfloat16 [1280, 2048], P(None, ('grp', 'seq')), may hold values from -1.5 to 1.5
- w_gate_up: bfloat16 [2048, 10240], P(('grp', 'seq')), may hold values from -0.125 to 0.125
- w_down: bfloat16 [5120, 2048], P(('grp', 'seq')), may hold values from -0.078125 to 0.078125
- attn_gain: bfloat16 [2048], P(('grp', 'seq')), may hold values from 0.5 to 1.5
- ffn_gain: bfloat16 [2048], P(('grp', 'seq')), may hold values from 0.5 to 1.5
- query_gain: bfloat16 [64], replicated, may hold values from 0.25 to 1.75
- key_gain: bfloat16 [64], replicated, may hold values from 0.25 to 1.75
- out_grad: bfloat16 [2, 8192, 2048], P(None, ('grp', 'seq')), may hold values from -6 to 6
Outputs:
- mixed: bfloat16 [2, 8192, 2048], P(None, ('grp', 'seq'))
- input_grad: float32 [2, 8192, 2048], P(None, ('grp', 'seq'))
- w_qkv_grad: float32 [2048, 1920], P(('grp', 'seq'))
- w_out_grad: float32 [1280, 2048], P(None, ('grp', 'seq'))
- w_gate_up_grad: float32 [2048, 10240], P(('grp', 'seq'))
- w_down_grad: float32 [5120, 2048], P(('grp', 'seq'))
- attn_gain_grad: float32 [2048], P(('grp', 'seq'))
- ffn_gain_grad: float32 [2048], P(('grp', 'seq'))
- query_gain_grad: float32 [64], replicated
- key_gain_grad: float32 [64], replicated
The draws below stay inside these ranges and needn't reach their ends.
Inputs may be any that keep to these rules, and one draw needn't show every extreme that they name: `segment_ids`: in each sequence the numbers never fall, start at 0 and rise by one at each new document, up to at most 32, where the remaining documents share the last number; padding (-1) fills a tail of one or more tokens. In each group one of the 2 sequences holds a document that begins within the first 64 tokens and ends within the last 64.
All inputs are finite; a program needn't handle non-finite values.
Results may differ from the reference program's by a relative error of at most 0.02.
Values may be sent and summed in bfloat16 or wider, within the bound.
A program may use at most 384 MiB of HBM per device.

```python
import jax
import jax.numpy as jnp
from jax import lax

D = 2048
Q_HEADS = 20
KV_HEADS = 5
HEAD = 64
FF = 5120
SEQ_LEN = 1024
MICRO = 2
QD = 1280
QKV = 1920
TOK_DEV = 64
TOKENS = 8192


def draw_segment_ids(key, part):
    key = jax.random.fold_in(key, 11)
    groups = TOKENS // SEQ_LEN
    count = MICRO * groups
    top_doc = SEQ_LEN // 32
    streams = jax.random.split(key, 6)
    spanning = jax.random.randint(streams[0], (groups,), 0, MICRO)
    micro_rows = jnp.arange(MICRO)[:, None]
    is_span = (micro_rows == spanning[None, :]).reshape(count, 1)
    is_full = (micro_rows == (spanning[None, :] + 1) % MICRO).reshape(count, 1)
    power = jax.random.randint(streams[1], (count, 1), 1, 8)
    rate = 2 ** power
    marks = jax.random.randint(streams[2], (count, SEQ_LEN), 0, rate) == 0
    places = jnp.arange(SEQ_LEN)[None, :]
    first = jax.random.randint(streams[3], (count, 1), 0, TOK_DEV)
    last = SEQ_LEN - 1 - jax.random.randint(streams[4], (count, 1), 0, TOK_DEV - 1)
    inside = (places > first) & (places < last)
    marks = jnp.where(is_span & inside, False, marks)
    marks = marks | is_span & ((places == first) | (places == last))
    marks = marks | is_full & (places <= top_doc)
    marks = marks | (places == 0)
    numbers = jnp.cumsum(marks.astype(jnp.int32), axis=1) - 1
    numbers = jnp.minimum(numbers, top_doc)
    room = jnp.where(is_span, SEQ_LEN - last, SEQ_LEN // 8 + 1)
    padding = 1 + jax.random.randint(streams[5], (count, 1), 0, room)
    numbers = jnp.where(places >= SEQ_LEN - padding, -1, numbers)
    return numbers.reshape(MICRO, TOKENS).astype(jnp.int32)


def level_of(key, dims, shards, least, largest):
    gain = 1.0
    for position, shards_of in shards:
        draws = jax.random.uniform(jax.random.fold_in(jax.random.fold_in(key, 6), position), (shards_of,), jnp.float32, least / len(shards), largest / len(shards))
        gain = gain * jnp.repeat(jnp.exp(draws), dims[position] // shards_of).reshape((-1,) + (1,) * (len(dims) - 1 - position))
    return gain


def scatter_about(key, shape, deviation, limit, cuts=(), held_as=jnp.bfloat16):
    gain = level_of(key, shape, cuts, -0.22, 0.18) if cuts else 1.0
    values = jax.random.normal(key, shape, jnp.float32) * deviation * gain
    return jnp.minimum(jnp.maximum(values, -limit), limit).astype(held_as)


def setup_inputs(seed: int = 0) -> dict:
    seeds = jax.random.split(jax.random.key(seed), 12)
    tokens = scatter_about(seeds[0], (MICRO, TOKENS, D), 1.0, 6.0, ((1, 128),))
    segment_ids = draw_segment_ids(jax.random.fold_in(seeds[11], 71), 0)
    w_qkv = scatter_about(seeds[2], (D, QKV), D ** -0.5, 0.125, ((0, 128),))
    w_out = scatter_about(seeds[3], (QD, D), 16 ** -0.5, 1.5, ((1, 128),))
    w_gate_up = scatter_about(seeds[4], (D, 2 * FF), D ** -0.5, 0.125, ((0, 128),))
    w_down = scatter_about(seeds[5], (FF, D), FF ** -0.5, 0.078125, ((0, 128),))
    attn_gain = jnp.clip(1.0 + 0.1 * jax.random.normal(seeds[6], (D,), jnp.float32), 0.5, 1.5).astype(jnp.bfloat16)
    ffn_gain = jnp.clip(1.0 + 0.1 * jax.random.normal(seeds[7], (D,), jnp.float32), 0.5, 1.5).astype(jnp.bfloat16)
    query_gain = jnp.clip(1.0 + 0.15 * jax.random.normal(seeds[8], (HEAD,), jnp.float32), 0.25, 1.75).astype(jnp.bfloat16)
    key_gain = jnp.clip(1.0 + 0.15 * jax.random.normal(seeds[9], (HEAD,), jnp.float32), 0.25, 1.75).astype(jnp.bfloat16)
    out_grad = scatter_about(seeds[10], (MICRO, TOKENS, D), 1.0, 6.0, ((1, 128),))
    return dict(tokens=tokens, segment_ids=segment_ids, w_qkv=w_qkv, w_out=w_out, w_gate_up=w_gate_up, w_down=w_down, attn_gain=attn_gain, ffn_gain=ffn_gain, query_gain=query_gain, key_gain=key_gain, out_grad=out_grad)


EPS = 1e-06
HIGH = lax.Precision.HIGHEST

@jax.custom_vjp
def low(v):
    return lax.optimization_barrier(v.astype(jnp.bfloat16)).astype(jnp.float32)

@jax.custom_vjp
def low_back(v):
    return v

def low_keep(v):
    return (low(v), None)

def low_pass(kept, grad):
    return (grad,)

def back_keep(v):
    return (v, None)

def back_low(kept, grad):
    return (low(grad),)
low.defvjp(low_keep, low_pass)
low_back.defvjp(back_keep, back_low)

def product(left, right):
    return jnp.dot(left, right, precision=HIGH, preferred_element_type=jnp.float32)

def rms_scale(values):
    return lax.rsqrt(lax.optimization_barrier(jnp.mean(values * values, axis=-1, keepdims=True)) + EPS)

def rotate(values):
    half = values.shape[-1] // 2
    return jnp.concatenate([-values[..., half:], values[..., :half]], axis=-1)

def rope_tables(positions):
    half = HEAD // 2
    inverse = 10000.0 ** (-jnp.arange(half, dtype=jnp.float32) / half)
    angles = positions[:, None] * inverse[None, :]
    angles = jnp.concatenate([angles, angles], axis=1)
    return (jnp.cos(angles)[:, None, :], jnp.sin(angles)[:, None, :])

def sequence_layer(hidden, seg_row, weights):
    w_qkv, w_out, w_gate_up, w_down, attn_gain, ffn_gain, query_gain, key_gain = weights
    length = hidden.shape[0]
    query_dim = Q_HEADS * HEAD
    key_dim = KV_HEADS * HEAD
    normed = low(hidden * rms_scale(hidden) * attn_gain)
    packed = low_back(product(normed, w_qkv))
    queries = packed[:, :query_dim].reshape(length, Q_HEADS, HEAD)
    keys = packed[:, query_dim:query_dim + key_dim].reshape(length, KV_HEADS, HEAD)
    values = low(packed[:, query_dim + key_dim:].reshape(length, KV_HEADS, HEAD))
    queries = queries * rms_scale(queries) * query_gain
    keys = keys * rms_scale(keys) * key_gain
    cosine, sine = rope_tables(jnp.arange(length, dtype=jnp.float32))
    queries = low(queries * cosine + rotate(queries) * sine)
    keys = low(keys * cosine + rotate(keys) * sine)
    grouped = queries.reshape(length, KV_HEADS, Q_HEADS // KV_HEADS, HEAD)
    scores = low_back(jnp.einsum('tgjd,sgd->gjts', grouped, keys, precision=HIGH) * HEAD ** (-0.5))
    places = jnp.arange(length)
    allowed = (places[None, :] <= places[:, None]) & (seg_row[None, :] == seg_row[:, None]) & (seg_row[:, None] >= 0)
    allowed = allowed | (places[None, :] == places[:, None])
    scores = jnp.where(allowed[None, None], scores, -1e+30)
    peak = lax.optimization_barrier(jnp.max(scores, axis=-1, keepdims=True))
    raised = jnp.exp(scores - peak)
    probs = low(raised / lax.optimization_barrier(jnp.sum(raised, axis=-1, keepdims=True)))
    attended = jnp.einsum('gjts,sgd->tgjd', probs, values, precision=HIGH).reshape(length, query_dim)
    attended = low(low_back(attended))
    resid = hidden + low_back(product(attended, w_out))
    normed_ffn = low(resid * rms_scale(resid) * ffn_gain)
    gate_up = low_back(product(normed_ffn, w_gate_up))
    gate = gate_up[:, :FF]
    upper = gate_up[:, FF:]
    inner = low(jax.nn.silu(gate) * upper)
    return resid + low_back(product(inner, w_down))

def reference(tokens, segment_ids, w_qkv, w_out, w_gate_up, w_down, attn_gain, ffn_gain, query_gain, key_gain, out_grad):
    hidden = tokens.astype(jnp.float32)
    weights = (w_qkv.astype(jnp.float32), w_out.astype(jnp.float32), w_gate_up.astype(jnp.float32), w_down.astype(jnp.float32), attn_gain.astype(jnp.float32), ffn_gain.astype(jnp.float32), query_gain.astype(jnp.float32), key_gain.astype(jnp.float32))
    count = tokens.shape[0] * (tokens.shape[1] // SEQ_LEN)
    seg_rows = segment_ids.reshape(count, SEQ_LEN)
    layer = jax.checkpoint(sequence_layer)

    def forward(inputs, params):
        rows = inputs.reshape(count, SEQ_LEN, inputs.shape[-1])

        def visit(carry, pair):
            return (carry, layer(pair[0], pair[1], params))
        unused, outs = lax.scan(visit, jnp.zeros((), jnp.float32), (rows, seg_rows))
        return outs.reshape(inputs.shape)
    result, pull = jax.vjp(forward, hidden, weights)
    grad_input, grad_weights = pull(out_grad.astype(jnp.float32))
    return (result.astype(jnp.bfloat16), grad_input, grad_weights[0], grad_weights[1], grad_weights[2], grad_weights[3], grad_weights[4], grad_weights[5], grad_weights[6], grad_weights[7])
```

```python
import jax
import jax.numpy as jnp
from jax import lax
from jax.experimental import pallas as pl
from jax.experimental.pallas import tpu as pltpu
from jax.sharding import PartitionSpec as P

Q_HEADS = 20
KV_HEADS = 5
GROUP = 4
HEAD = 64
D = 2048
FF = 5120
QD = 1280
KD = 320
QKV = 1920
SEQ = 1024
MICRO = 2
ROWS = 64
TOK = 128
FS = 640
EPS = 1e-06
MESH = pl.DeviceIdType.MESH
F32 = jnp.float32
BF16 = jnp.bfloat16
ANY = pl.BlockSpec(memory_space=pl.ANY)


class Place:
    def __init__(self):
        g = lax.axis_index("grp")
        s = lax.axis_index("seq")
        self.g, self.s = g, s
        self.yh, self.x = g // 4, g % 4
        self.yl, self.z, self.c = s // 8, (s // 2) % 4, s % 2
        self.y = self.yh * 2 + self.yl

    def at(self, x=None, y=None, z=None, c=None):
        x = self.x if x is None else x
        y = self.y if y is None else y
        z = self.z if z is None else z
        c = self.c if c is None else c
        return ((y // 2) * 4 + x, (y % 2) * 8 + z * 2 + c)

    def step(self, axis, k):
        if axis == "x":
            return self.at(x=(self.x + k) % 4)
        if axis == "y":
            return self.at(y=(self.y + k) % 4)
        if axis == "z":
            return self.at(z=(self.z + k) % 4)
        return self.at(c=1 - self.c)

    def pos(self, axis, k):
        return (getattr(self, axis) + k) % 4


class Links:
    def __init__(self, send_sems, recv_sems):
        self.send_sems, self.recv_sems = send_sems, recv_sems
        self.used = 0
        self.sent = []

    def send(self, src, dst, to):
        i = self.used
        self.used += 1
        copy = pltpu.make_async_remote_copy(
            src_ref=src,
            dst_ref=dst,
            send_sem=self.send_sems.at[i],
            recv_sem=self.recv_sems.at[i],
            device_id=to,
            device_id_type=MESH,
        )
        copy.start()
        self.sent.append(copy)
        return copy

    def local(self, src, dst):
        i = self.used
        self.used += 1
        copy = pltpu.make_async_copy(src, dst, self.recv_sems.at[i])
        copy.start()
        return copy

    def drain(self):
        for copy in self.sent:
            copy.wait_send()


def greet(partners):
    barrier = pltpu.get_barrier_semaphore()
    for to in partners:
        pl.semaphore_signal(barrier, inc=1, device_id=to, device_id_type=MESH)
    pl.semaphore_wait(barrier, len(partners))


def any_call(body, name, cid, n_in, outs, scratch, sems, vmem=48 << 20):
    return pl.pallas_call(
        body,
        out_shape=outs,
        in_specs=[ANY] * n_in,
        out_specs=[ANY] * len(outs),
        name=name,
        scratch_shapes=list(scratch)
        + [pltpu.SemaphoreType.DMA((sems,)), pltpu.SemaphoreType.DMA((sems,))],
        compiler_params=pltpu.CompilerParams(
            collective_id=cid, has_side_effects=True, vmem_limit_bytes=vmem
        ),
    )


def sds(shape, dtype):
    return jax.ShapeDtypeStruct(shape, dtype)


def slab_target(p):
    to = p.at(x=p.z, y=p.c * 2 + p.yl, z=p.g // 2, c=p.g % 2)
    return to


def slab_source(p):
    m = p.z * 2 + p.c
    return p.at(x=m % 4, y=(m // 4) * 2 + p.yl, z=p.x, c=p.yh)


def same(p, to):
    return (to[0] == p.g) & (to[1] == p.s)


def greet_plane(p, partners, slab_to, slab_from, own_slab):
    barrier = pltpu.get_barrier_semaphore()
    for to in partners:
        pl.semaphore_signal(barrier, inc=1, device_id=to, device_id_type=MESH)

    @pl.when(jnp.logical_not(own_slab))
    def _():
        pl.semaphore_signal(barrier, inc=1, device_id=slab_to, device_id_type=MESH)
        pl.semaphore_signal(barrier, inc=1, device_id=slab_from, device_id_type=MESH)
        pl.semaphore_wait(barrier, len(partners) + 2)

    @pl.when(own_slab)
    def _():
        pl.semaphore_wait(barrier, len(partners))


def slab_copy(src, dst, ssem, rsem, i, to):
    return pltpu.make_async_remote_copy(
        src_ref=src,
        dst_ref=dst,
        send_sem=ssem.at[i],
        recv_sem=rsem.at[i],
        device_id=to,
        device_id_type=MESH,
    )


def gather_body(wq, wo, wg, wd, og, WQ, WO, WG, WD, OG, ssem, rsem):
    p = Place()
    k = Links(ssem, rsem)
    m = p.z * 2 + p.c
    partners = [p.step(a, j) for a in "xyz" for j in (1, 2, 3)]
    partners += [p.at(z=(p.z + j) % 4, c=1 - p.c) for j in range(4)]
    slab_to, slab_from = slab_target(p), slab_source(p)
    own_slab = same(p, slab_to)
    greet_plane(p, partners, slab_to, slab_from, own_slab)

    yh, x, yl, z, c = p.yh, p.x, p.yl, p.z, p.c
    local = [
        k.local(wq, WQ.at[yh, x, yl, z, c]),
        k.local(wo, WO.at[yh, x, yl, z, c]),
        k.local(og, OG.at[z, c]),
    ]
    pieces = []
    for dz in range(4):
        for dc in range(2):
            zz, cc = (z + dz) % 4, (c + dc) % 2
            mm = zz * 2 + cc
            for half in range(2):
                src = wg.at[:, pl.ds(pl.multiple_of(half * FF + mm * FS, 128), FS)]
                dst = WG.at[yh, x, yl, m, :, pl.ds(half * FS, FS)]
                if dz == 0 and dc == 0:
                    local.append(k.local(src, dst))
                else:
                    pieces.append(k.send(src, dst, p.at(z=zz, c=cc)))
    slab_dst = WD.at[yl, z, c]
    i = k.used
    k.used += 1

    @pl.when(own_slab)
    def _():
        pltpu.make_async_copy(wd, slab_dst, rsem.at[i]).start()

    slab = slab_copy(wd, slab_dst, ssem, rsem, i, slab_to)

    @pl.when(jnp.logical_not(own_slab))
    def _():
        slab.start()

    def wq_a(*at):
        return WQ.at[(*at, slice(None), pl.ds(0, 1024))]

    def wq_b(*at):
        return WQ.at[(*at, slice(None), pl.ds(1024, 1024))]

    def wo_(*at):
        return WO.at[(*at, slice(None), slice(None))]

    every = slice(None)
    first = []
    for j in (1, 2, 3):
        first.append(k.send(wq.at[:, pl.ds(0, 1024)], wq_a(yh, x, yl, z, c), p.step("y", j)))
        first.append(k.send(wq.at[:, pl.ds(1024, 1024)], wq_b(yh, x, yl, z, c), p.step("z", j)))
        first.append(k.send(wo, wo_(yh, x, yl, z, c), p.step("x", j)))
    rows = [k.send(og, OG.at[z, c], p.step("z", j)) for j in (1, 2, 3)]
    rows_core = k.send(og, OG.at[z, c], p.step("c", 1))

    for copy in local:
        copy.wait()
    for copy in pieces:
        copy.wait_recv()

    @pl.when(own_slab)
    def _():
        pltpu.make_async_copy(wd, slab_dst, rsem.at[i]).wait()

    @pl.when(jnp.logical_not(own_slab))
    def _():
        slab.wait_recv()

    lo, hi = pl.ds(0, FS), pl.ds(FS, FS)
    dlo, dhi = pl.ds(0, 512), pl.ds(512, 512)
    mine_lo = WG.at[yh, x, yl, :, :, lo]
    mine_hi = WG.at[yh, x, yl, :, :, hi]
    slab_lo = WD.at[yl, x, yh, :, dlo]
    slab_hi = WD.at[yl, x, yh, :, dhi]
    plane = []
    for j in (1, 2, 3):
        plane.append(k.send(mine_lo, mine_lo, p.step("x", j)))
        plane.append(k.send(mine_hi, mine_hi, p.step("y", j)))
        plane.append(k.send(slab_lo, slab_lo, p.step("x", j)))
        plane.append(k.send(slab_hi, slab_hi, p.step("y", j)))

    for copy in first:
        copy.wait_recv()
    second = []
    for j in (1, 2, 3):
        src = wq_a(every, x, every, z, c)
        second.append(k.send(src, src, p.step("z", j)))
        src = wq_b(yh, x, yl, every, c)
        second.append(k.send(src, src, p.step("x", j)))
        src = wo_(yh, every, yl, z, c)
        second.append(k.send(src, src, p.step("y", j)))

    for copy in plane:
        copy.wait_recv()
    plane2 = []
    for j in (1, 2, 3):
        src = WG.at[yh, :, yl, :, :, lo]
        plane2.append(k.send(src, src, p.step("y", j)))
        src = WG.at[:, x, :, :, :, hi]
        plane2.append(k.send(src, src, p.step("x", j)))
        src = WD.at[yl, :, yh, :, dlo]
        plane2.append(k.send(src, src, p.step("y", j)))
        src = WD.at[:, x, :, :, dhi]
        plane2.append(k.send(src, src, p.step("x", j)))

    for copy in second:
        copy.wait_recv()
    third = []
    for j in (1, 2, 3):
        src = wq_a(every, x, every, every, c)
        third.append((k.send(src, src, p.step("x", j)), wq_a(every, p.pos("x", -j), every, every, c)))
        src = wq_b(yh, every, yl, every, c)
        yy = p.pos("y", -j)
        third.append(
            (k.send(src, src, p.step("y", j)), wq_b(yy // 2, every, yy % 2, every, c))
        )
        src = wo_(every, every, every, z, c)
        third.append((k.send(src, src, p.step("z", j)), wo_(every, every, every, p.pos("z", -j), c)))
    last = []
    for src in (wq_a(every, x, every, every, c), wq_b(yh, every, yl, every, c), wo_(every, every, every, z, c)):
        last.append(k.send(src, src, p.step("c", 1)))
    for j, copy in zip((1, 2, 3), rows):
        copy.wait_recv()
        src = OG.at[p.pos("z", -j), c]
        last.append(k.send(src, src, p.step("c", 1)))
    for copy, src in third:
        copy.wait_recv()
        last.append(k.send(src, src, p.step("c", 1)))
    for copy in plane2 + last + [rows_core]:
        copy.wait_recv()
    k.drain()

    @pl.when(jnp.logical_not(own_slab))
    def _():
        slab.wait_send()


def gather_weights(wq, wo, wg, wd, og):
    outs = [
        sds((2, 4, 2, 4, 2, 16, 2048), BF16),
        sds((2, 4, 2, 4, 2, 16, QD), BF16),
        sds((2, 4, 2, 8, 16, 2 * FS), BF16),
        sds((2, 4, 2, 80, 1024), BF16),
        sds((4, 2, TOK, D), BF16),
    ]
    return any_call(gather_body, "gather_weights", 0, 5, outs, [], 100)(wq, wo, wg, wd, og)


def kv_gather_body(kv, KV, ssem, rsem):
    p = Place()
    k = Links(ssem, rsem)
    yl, z, c = p.yl, p.z, p.c
    partner = p.at(y=p.yh * 2 + 1 - yl)
    greet([p.step("z", j) for j in (1, 2, 3)] + [partner, p.step("c", 1)])
    own = k.local(kv, KV.at[:, yl, z, c])
    across = k.send(kv, KV.at[:, yl, z, c], partner)
    ring = [k.send(kv, KV.at[:, yl, z, c], p.step("z", j)) for j in (1, 2, 3)]
    across.wait_recv()
    src = KV.at[:, 1 - yl, z, c]
    ring += [k.send(src, src, p.step("z", j)) for j in (1, 2, 3)]
    own.wait()
    for copy in ring:
        copy.wait_recv()
    src = KV.at[:, :, :, c]
    core = k.send(src, src, p.step("c", 1))
    core.wait_recv()
    k.drain()


def kv_gather(kv):
    outs = [sds((2, 2, 4, 2, ROWS, 2 * KD), BF16)]
    return any_call(kv_gather_body, "kv_gather", 1, 1, outs, [], 10)(kv)[0]


def kv_reduce_body(part, out, own, r0, s0, r1, s1, r2, res, ssem, rsem):
    p = Place()
    k = Links(ssem, rsem)
    yl, z, c = p.yl, p.z, p.c
    partner = p.at(y=p.yh * 2 + 1 - yl)
    greet([p.step("z", j) for j in (1, 2, 3)] + [partner, p.step("c", 1)])
    core = k.send(part.at[:, :, :, 1 - c], r0, p.step("c", 1))
    mine = k.local(part.at[:, :, :, c], own)
    mine.wait()
    core.wait_recv()

    @pl.loop(0, 4)
    def _(zz):
        for a in range(2):
            for b in range(2):
                s0[a, b, zz] = (own[a, b, zz].astype(F32) + r0[a, b, zz].astype(F32)).astype(BF16)

    ring = []
    for j in (1, 2, 3):
        zz = p.pos("z", j)
        ring.append(k.send(s0.at[:, :, zz], r1.at[j - 1], p.step("z", j)))
    for copy in ring:
        copy.wait_recv()
    for a in range(2):
        for b in range(2):
            total = s0[a, b, z].astype(F32)
            for j in range(3):
                total = total + r1[j, a, b].astype(F32)
            s1[a, b] = total.astype(BF16)
    across = k.send(s1.at[:, 1 - yl], r2, partner)
    across.wait_recv()
    for a in range(2):
        res[a] = s1[a, yl].astype(F32) + r2[a].astype(F32)
    done = k.local(res, out)
    done.wait()
    k.drain()


def kv_reduce(part):
    w = 2 * KD
    scratch = [
        pltpu.VMEM((2, 2, 4, ROWS, w), BF16),
        pltpu.VMEM((2, 2, 4, ROWS, w), BF16),
        pltpu.VMEM((2, 2, 4, ROWS, w), BF16),
        pltpu.VMEM((3, 2, 2, ROWS, w), BF16),
        pltpu.VMEM((2, 2, ROWS, w), BF16),
        pltpu.VMEM((2, ROWS, w), BF16),
        pltpu.VMEM((2, ROWS, w), F32),
    ]
    outs = [sds((2, ROWS, w), F32)]
    return any_call(kv_reduce_body, "kv_reduce", 2, 1, outs, scratch, 10)(part)[0]


def row_gather_body(rows, ALL, ssem, rsem):
    p = Place()
    k = Links(ssem, rsem)
    z, c = p.z, p.c
    greet([p.step("z", j) for j in (1, 2, 3)] + [p.step("c", 1)])
    own = k.local(rows, ALL.at[z, c])
    ring = [k.send(rows, ALL.at[z, c], p.step("z", j)) for j in (1, 2, 3)]
    core = [k.send(rows, ALL.at[z, c], p.step("c", 1))]
    for j, copy in zip((1, 2, 3), ring):
        copy.wait_recv()
        src = ALL.at[p.pos("z", -j), c]
        core.append(k.send(src, src, p.step("c", 1)))
    own.wait()
    for copy in core:
        copy.wait_recv()
    k.drain()


def row_gather(rows):
    outs = [sds((4, 2, TOK, D), BF16)]
    return any_call(row_gather_body, "row_gather", 3, 1, outs, [], 10)(rows)[0]


def row_reduce(p, k, part, own, r0, s0, r1, res):
    z, c = p.z, p.c
    core = k.send(part.at[:, 1 - c], r0, p.step("c", 1))
    mine = k.local(part.at[:, c], own)
    yield
    mine.wait()
    core.wait_recv()

    @pl.loop(0, 4)
    def _(zz):
        @pl.loop(0, TOK, step=32)
        def _(t):
            at = pl.ds(pl.multiple_of(t, 32), 32)
            s0[zz, at] = (own[zz, at].astype(F32) + r0[zz, at].astype(F32)).astype(BF16)

    ring = [k.send(s0.at[p.pos("z", j)], r1.at[j - 1], p.step("z", j)) for j in (1, 2, 3)]
    yield
    for copy in ring:
        copy.wait_recv()

    @pl.loop(0, TOK, step=32)
    def _(t):
        at = pl.ds(pl.multiple_of(t, 32), 32)
        total = s0[z, at].astype(F32)
        for j in range(3):
            total = total + r1[j, at].astype(F32)
        res[at] = total


def row_scratch():
    return [
        pltpu.VMEM((4, TOK, D), BF16),
        pltpu.VMEM((4, TOK, D), BF16),
        pltpu.VMEM((4, TOK, D), BF16),
        pltpu.VMEM((3, TOK, D), BF16),
        pltpu.VMEM((TOK, D), F32),
    ]


def row_reduce_body(part, out, own, r0, s0, r1, res, ssem, rsem):
    p = Place()
    k = Links(ssem, rsem)
    greet([p.step("z", j) for j in (1, 2, 3)] + [p.step("c", 1)])
    for _ in row_reduce(p, k, part, own, r0, s0, r1, res):
        pass
    done = k.local(res, out)
    done.wait()
    k.drain()


def row_reduce_call(part):
    outs = [sds((TOK, D), F32)]
    return any_call(row_reduce_body, "row_reduce", 4, 1, outs, row_scratch(), 10)(part)[0]


def pair_body(n, *refs):
    ins, outs = refs[:n], refs[n : 2 * n]
    ssem, rsem = refs[2 * n :]
    p = Place()
    k = Links(ssem, rsem)
    greet([p.step("c", 1)])
    copies = [k.send(i, o.at[1], p.step("c", 1)) for i, o in zip(ins, outs)]
    local = [k.local(i, o.at[0]) for i, o in zip(ins, outs)]
    for copy in local:
        copy.wait()
    for copy in copies:
        copy.wait_recv()
    k.drain()


def pair_exchange(*arrays):
    n = len(arrays)
    outs = [sds((2, *a.shape), a.dtype) for a in arrays]

    def body(*refs):
        pair_body(n, *refs)

    return any_call(body, "pair_exchange", 5, n, outs, [], 2 * n)(*arrays)


def add_blocks(dst, own, recv, chunk):
    lead, rows = dst.shape[:-2], dst.shape[-2]
    count = 1
    for n in lead:
        count *= n

    @pl.loop(0, count)
    def _(i):
        at = []
        rest = i
        for n in reversed(lead):
            at.insert(0, rest % n)
            rest = rest // n

        @pl.loop(0, rows, step=chunk)
        def _(t):
            here = (*at, pl.ds(pl.multiple_of(t, chunk), chunk))
            total = own[here].astype(F32)
            for j in range(3):
                total = total + recv[(j, *here)].astype(F32)
            dst[here] = total.astype(dst.dtype)


def staged_reduce(p, k, src, stages, scr, chunk):
    own = scr[0]
    cur = src
    for n, (axis, pick) in enumerate(stages):
        recv, total = scr[1 + 2 * n], scr[2 + 2 * n]
        if n == 0:
            mine = k.local(pick(src, p.pos(axis, 0)), own)
        ring = [k.send(pick(cur, p.pos(axis, j)), recv.at[j - 1], p.step(axis, j)) for j in (1, 2, 3)]
        yield
        if n == 0:
            mine.wait()
        for copy in ring:
            copy.wait_recv()
        add_blocks(total, own if n == 0 else pick(cur, p.pos(axis, 0)), recv, chunk)
        cur = total


def staged_scratch(shapes):
    out = [pltpu.VMEM(shapes[0], BF16)]
    for n, shape in enumerate(shapes):
        out.append(pltpu.VMEM((3, *shape), BF16))
        out.append(pltpu.VMEM(shape, F32 if n == len(shapes) - 1 else BF16))
    return out


EVERY = slice(None)


def cols_at(start, size):
    return pl.ds(start, size)


def wg_stages(half):
    cols = pl.ds(half * FS, FS)
    if half == 0:
        return [
            ("y", lambda r, i: r.at[i // 2, :, i % 2, :, cols]),
            ("x", lambda r, i: r.at[i]),
        ]
    return [
        ("x", lambda r, i: r.at[:, i, :, :, cols]),
        ("y", lambda r, i: r.at[i // 2, i % 2]),
    ]


def wd_stages(half):
    cols = pl.ds(half * 512, 512)
    if half == 0:
        return [
            ("y", lambda r, i: r.at[i % 2, :, i // 2, :, cols]),
            ("x", lambda r, i: r.at[i]),
        ]
    return [
        ("x", lambda r, i: r.at[:, i, :, :, cols]),
        ("y", lambda r, i: r.at[i % 2, i // 2]),
    ]


def q_stages(half):
    cols = pl.ds(half * 512, 512)
    if half == 0:
        return [
            ("x", lambda r, i: r.at[:, i, :, :, :, cols]),
            ("z", lambda r, i: r.at[:, :, i]),
            ("y", lambda r, i: r.at[i // 2, i % 2]),
        ]
    return [
        ("y", lambda r, i: r.at[i // 2, :, i % 2, :, :, cols]),
        ("x", lambda r, i: r.at[i]),
        ("z", lambda r, i: r.at[i]),
    ]


def o_stages():
    return [
        ("z", lambda r, i: r.at[:, :, :, i]),
        ("y", lambda r, i: r.at[i // 2, :, i % 2]),
        ("x", lambda r, i: r.at[i]),
    ]


GRAD_SHAPES = [
    [(4, 128, FS), (128, FS)],
    [(2, 2, 128, FS), (128, FS)],
    [(4, 80, 512), (80, 512)],
    [(2, 2, 80, 512), (80, 512)],
    [(2, 2, 4, 32, 512), (2, 2, 32, 512), (32, 512)],
    [(4, 4, 32, 512), (4, 32, 512), (32, 512)],
    [(2, 4, 2, 32, 640), (4, 32, 640), (32, 640)],
]


def small_reduce(p, k, part, vec, recv):
    mine = k.local(part, vec.at[0])
    mine.wait()
    for n, axis in enumerate("xyzc"):
        steps = (1,) if axis == "c" else (1, 2, 3)
        ring = [k.send(vec.at[n], recv.at[n, j - 1], p.step(axis, j)) for j in steps]
        yield
        for copy in ring:
            copy.wait_recv()
        total = vec[n]
        for j in range(len(steps)):
            total = total + recv[n, j]
        vec[n + 1] = total


def grads_body(*refs):
    dwg, dwd, dq, do, dmix, small, GWG, GWD, GQ, GO, MIX, SMALL = refs[:12]
    scr = list(refs[12:])
    parts = []
    for shapes in GRAD_SHAPES:
        n = 1 + 2 * len(shapes)
        parts.append(scr[:n])
        scr = scr[n:]
    mix, (vec, recv), (ssem, rsem) = scr[:5], scr[5:7], scr[7:9]
    p = Place()
    k = Links(ssem, rsem)
    yh, x, yl, z, c = p.yh, p.x, p.yl, p.z, p.c
    m = z * 2 + c
    partners = [p.step(a, j) for a in "xyz" for j in (1, 2, 3)]
    partners += [p.at(z=(z + j) % 4, c=1 - c) for j in range(4)]
    slab_to, slab_from = slab_target(p), slab_source(p)
    own_slab = same(p, slab_to)
    greet_plane(p, partners, slab_to, slab_from, own_slab)

    chunk = 16
    gens = [
        staged_reduce(p, k, dwg, wg_stages(0), parts[0], chunk),
        staged_reduce(p, k, dwg, wg_stages(1), parts[1], chunk),
        staged_reduce(p, k, dwd, wd_stages(0), parts[2], chunk),
        staged_reduce(p, k, dwd, wd_stages(1), parts[3], chunk),
        row_reduce(p, k, dmix, *mix),
        staged_reduce(p, k, do, o_stages(), parts[6], chunk),
        staged_reduce(p, k, dq, q_stages(0), parts[4], chunk),
        staged_reduce(p, k, dq, q_stages(1), parts[5], chunk),
        small_reduce(p, k, small, vec, recv),
    ]
    alive = list(gens)
    while alive:
        alive = [g for g in alive if next(g, alive) is not alive]

    last, local = [], []
    for half in range(2):
        total = parts[half][-1]
        cols = pl.ds(pl.multiple_of(half * FF + m * FS, 128), FS)
        for dz in range(4):
            for dc in range(2):
                zz, cc = (z + dz) % 4, (c + dc) % 2
                src = total.at[pl.ds(pl.multiple_of((zz * 2 + cc) * 16, 16), 16)]
                if dz == 0 and dc == 0:
                    local.append(k.local(src, GWG.at[:, cols]))
                else:
                    last.append(k.send(src, GWG.at[:, cols], p.at(z=zz, c=cc)))
    slabs = []
    for half in range(2):
        i = k.used
        k.used += 1
        src, dst = parts[2 + half][-1], GWD.at[:, pl.ds(half * 512, 512)]
        slabs.append((src, dst, i))

        @pl.when(own_slab)
        def _(src=src, dst=dst, i=i):
            pltpu.make_async_copy(src, dst, rsem.at[i]).start()

        @pl.when(jnp.logical_not(own_slab))
        def _(src=src, dst=dst, i=i):
            slab_copy(src, dst, ssem, rsem, i, slab_from).start()

    for total, dst in (
        (parts[4][-1], GQ.at[c, :, pl.ds(0, 512)]),
        (parts[5][-1], GQ.at[c, :, pl.ds(512, 512)]),
        (parts[6][-1], GO.at[c]),
    ):
        mine = total.at[pl.ds(pl.multiple_of(c * 16, 16), 16)]
        other = total.at[pl.ds(pl.multiple_of((1 - c) * 16, 16), 16)]
        local.append(k.local(mine, dst))
        last.append(k.send(other, dst, p.step("c", 1)))
    local.append(k.local(mix[-1], MIX))
    local.append(k.local(vec.at[4], SMALL))
    for copy in local:
        copy.wait()
    for copy in last:
        copy.wait_recv()
    for src, dst, i in slabs:

        @pl.when(own_slab)
        def _(src=src, dst=dst, i=i):
            pltpu.make_async_copy(src, dst, rsem.at[i]).wait()

        @pl.when(jnp.logical_not(own_slab))
        def _(src=src, dst=dst, i=i):
            slab_copy(src, dst, ssem, rsem, i, slab_from).wait()

    k.drain()


def reduce_grads(dwg, dwd, dq, do, dmix, small):
    outs = [
        sds((16, 2 * FF), F32),
        sds((80, 1024), F32),
        sds((2, 16, 1024), F32),
        sds((2, 16, 640), F32),
        sds((TOK, D), F32),
        sds((40, 128), F32),
    ]
    scratch = []
    for shapes in GRAD_SHAPES:
        scratch += staged_scratch(shapes)
    scratch += row_scratch()
    scratch += [pltpu.VMEM((5, 40, 128), F32), pltpu.VMEM((4, 3, 40, 128), F32)]
    return any_call(grads_body, "reduce_grads", 6, 6, outs, scratch, 110, 56 << 20)(
        dwg, dwd, dq, do, dmix, small
    )


def rms_scale(values):
    return lax.rsqrt(jnp.mean(values * values, axis=-1, keepdims=True) + EPS)


def rotate(values):
    half = values.shape[-1] // 2
    return jnp.concatenate([-values[..., half:], values[..., :half]], axis=-1)


def rotate_back(values):
    half = values.shape[-1] // 2
    return jnp.concatenate([values[..., half:], -values[..., :half]], axis=-1)


def norm_back(upstream, normed, scale, gain):
    scaled = upstream * gain
    inner = jnp.mean(scaled * normed, axis=-1, keepdims=True)
    return scale * (scaled - normed * inner)


def dot(left, right):
    return jnp.dot(left, right, preferred_element_type=F32)


def dot_last(left, right):
    return lax.dot_general(left, right, (((1,), (1,)), ((), ())), preferred_element_type=F32)


def dot_rows(left, right):
    return lax.dot_general(left, right, (((0,), (0,)), ((), ())), preferred_element_type=F32)


def rope_tables(positions):
    half = HEAD // 2
    inverse = 10000.0 ** (-jnp.arange(half, dtype=F32) / half)
    angles = positions[:, None] * inverse[None, :]
    angles = jnp.concatenate([angles, angles], axis=1)
    return (jnp.cos(angles)[:, None, :], jnp.sin(angles)[:, None, :])


def per_device(
    tokens,
    segment_ids,
    w_qkv,
    w_out,
    w_gate_up,
    w_down,
    attn_gain,
    ffn_gain,
    query_gain,
    key_gain,
    out_grad,
):
    s = lax.axis_index("seq")
    g = lax.axis_index("grp")
    c = s % 2
    start = s * ROWS
    query_gain = query_gain.astype(F32)
    key_gain = key_gain.astype(F32)
    gains = jnp.stack([attn_gain, ffn_gain], axis=1)
    wq_in = jnp.concatenate([w_qkv, jnp.pad(gains, ((0, 0), (0, 126)))], axis=1)
    og_in = out_grad.reshape(TOK, D)
    WQ, WO, WG, WD, OG = gather_weights(
        wq_in, w_out.T, w_gate_up, w_down.reshape(80, 1024), og_in
    )
    WQ = WQ.reshape(D, 2048)
    WO = WO.reshape(D, QD)
    WG = WG.reshape(D, 2 * FS)
    WD = WD.reshape(FS, D)
    OG = OG.reshape(8 * TOK, D)
    gain_one = WQ[:, QKV].astype(F32)
    gain_two = WQ[:, QKV + 1].astype(F32)

    hidden = tokens.reshape(TOK, D).astype(F32)
    scale_one = rms_scale(hidden)
    norm_one = hidden * scale_one
    normed = (norm_one * gain_one).astype(BF16)
    packed = dot(normed, WQ)
    query_raw = packed[:, :QD].reshape(TOK, Q_HEADS, HEAD)
    key_raw = packed[:, QD : QD + KD].reshape(TOK, KV_HEADS, HEAD)
    value_raw = packed[:, QD + KD : QKV]
    query_scale = rms_scale(query_raw)
    query_norm = query_raw * query_scale
    key_scale = rms_scale(key_raw)
    key_norm = key_raw * key_scale
    query_head = query_norm * query_gain
    key_head = key_norm * key_gain
    positions = (start + jnp.arange(ROWS)).astype(F32)
    positions = jnp.concatenate([positions] * MICRO)
    cosine, sine = rope_tables(positions)
    queries = (query_head * cosine + rotate(query_head) * sine).astype(BF16)
    keys_local = (key_head * cosine + rotate(key_head) * sine).astype(BF16)
    kv_local = jnp.concatenate([keys_local.reshape(TOK, KD), value_raw.astype(BF16)], axis=1)
    kv = kv_gather(kv_local.reshape(MICRO, ROWS, 2 * KD)).reshape(MICRO, SEQ, 2 * KD)
    keys = kv[:, :, :KD].reshape(MICRO, SEQ, KV_HEADS, HEAD)
    values = kv[:, :, KD:].reshape(MICRO, SEQ, KV_HEADS, HEAD)
    grouped = queries.reshape(MICRO, ROWS, KV_HEADS, GROUP, HEAD)
    query_ids = lax.dynamic_slice_in_dim(segment_ids, start, ROWS, axis=1)
    query_pos = start + jnp.arange(ROWS)
    key_pos = jnp.arange(SEQ)
    allowed = (
        (key_pos[None, None, :] <= query_pos[None, :, None])
        & (segment_ids[:, None, :] == query_ids[:, :, None])
        & (query_ids[:, :, None] >= 0)
    )
    allowed = allowed | (key_pos[None, None, :] == query_pos[None, :, None])
    factor = HEAD ** (-0.5)
    scores = (
        jnp.einsum("mtgjd,msgd->mgjts", grouped, keys, preferred_element_type=F32) * factor
    )
    scores = jnp.where(allowed[:, None, None], scores, -1e30)
    peak = jnp.max(scores, axis=-1, keepdims=True)
    raised = jnp.exp(scores - peak)
    row_total = jnp.sum(raised, axis=-1, keepdims=True)
    log_total = peak + jnp.log(row_total)
    probs = (raised / row_total).astype(BF16)
    attended = jnp.einsum("mgjts,msgd->mtgjd", probs, values, preferred_element_type=F32)
    attended = attended.reshape(TOK, QD).astype(BF16)
    resid = hidden + dot_last(attended, WO)
    scale_two = rms_scale(resid)
    norm_two = resid * scale_two
    normed_ffn = (norm_two * gain_two).astype(BF16)

    rows = row_gather(normed_ffn).reshape(8 * TOK, D)
    gate_up = dot(rows, WG)
    gate = gate_up[:, :FS]
    upper = gate_up[:, FS:]
    sigmoid_gate = jax.nn.sigmoid(gate)
    active = gate * sigmoid_gate
    inner = (active * upper).astype(BF16)
    mixed_part = dot(inner, WD).astype(BF16)
    d_inner = dot_last(OG, WD)
    d_gate = d_inner * upper * sigmoid_gate * (1.0 + gate * (1.0 - sigmoid_gate))
    d_upper = d_inner * active
    d_gate_up = jnp.concatenate([d_gate, d_upper], axis=1).astype(BF16)
    d_rows_part = dot_last(d_gate_up, WG).astype(BF16)
    grad_gate_up = dot_rows(rows, d_gate_up).astype(BF16)
    grad_down = dot_rows(inner, OG).astype(BF16)

    d_normed_ffn = row_reduce_call(d_rows_part.reshape(4, 2, TOK, D))
    upstream = og_in.astype(F32)
    ffn_term = jnp.sum(d_normed_ffn * norm_two, axis=0)
    d_resid = upstream + norm_back(d_normed_ffn, norm_two, scale_two, gain_two)
    resid_low = d_resid.astype(BF16)
    d_attended = dot(resid_low, WO).astype(BF16)
    d_attended = d_attended.reshape(MICRO, ROWS, KV_HEADS, GROUP, HEAD)
    again = jnp.exp(scores - log_total)
    again_low = again.astype(BF16)
    d_probs = jnp.einsum("mtgjd,msgd->mgjts", d_attended, values, preferred_element_type=F32)
    d_values = jnp.einsum("mgjts,mtgjd->msgd", again_low, d_attended, preferred_element_type=F32)
    row_inner = jnp.sum(again * d_probs, axis=-1, keepdims=True)
    d_scores = (again * (d_probs - row_inner)).astype(BF16)
    d_queries = (
        jnp.einsum("mgjts,msgd->mtgjd", d_scores, keys, preferred_element_type=F32) * factor
    )
    d_keys = (
        jnp.einsum("mgjts,mtgjd->msgd", d_scores, grouped, preferred_element_type=F32) * factor
    )
    kv_terms = jnp.concatenate(
        [d_keys.reshape(MICRO, SEQ, KD), d_values.reshape(MICRO, SEQ, KD)], axis=2
    ).astype(BF16)
    kv_grads = kv_reduce(kv_terms.reshape(MICRO, 2, 4, 2, ROWS, 2 * KD)).reshape(TOK, 2 * KD)
    key_grad = kv_grads[:, :KD].reshape(TOK, KV_HEADS, HEAD)
    value_grad = kv_grads[:, KD:]
    query_grad = d_queries.reshape(TOK, Q_HEADS, HEAD)
    d_query_head = query_grad * cosine + rotate_back(query_grad * sine)
    d_key_head = key_grad * cosine + rotate_back(key_grad * sine)
    query_term = jnp.sum(d_query_head * query_norm, axis=(0, 1))
    key_term = jnp.sum(d_key_head * key_norm, axis=(0, 1))
    d_query_raw = norm_back(d_query_head, query_norm, query_scale, query_gain)
    d_key_raw = norm_back(d_key_head, key_norm, key_scale, key_gain)
    d_packed = jnp.concatenate(
        [d_query_raw.reshape(TOK, QD), d_key_raw.reshape(TOK, KD), value_grad], axis=1
    ).astype(BF16)
    d_normed = dot_last(d_packed, WQ[:, :QKV])
    attn_term = jnp.sum(d_normed * norm_one, axis=0)
    input_grad = d_resid + norm_back(d_normed, norm_one, scale_one, gain_one)

    pair = pair_exchange(normed, d_packed, attended, resid_low)
    normed_2, packed_2, attended_2, low_2 = [a.reshape(2 * TOK, -1) for a in pair]
    packed_cols = lax.dynamic_slice_in_dim(packed_2, c * 896, 1024, axis=1)
    attended_cols = lax.dynamic_slice_in_dim(attended_2, c * 640, 640, axis=1)
    grad_q = dot_rows(normed_2, packed_cols).astype(BF16)
    grad_o = dot_rows(low_2, attended_cols).astype(BF16)

    small = jnp.concatenate(
        [
            attn_term.reshape(16, 128),
            ffn_term.reshape(16, 128),
            jnp.pad(jnp.concatenate([query_term, key_term]).reshape(1, 128), ((0, 7), (0, 0))),
        ],
        axis=0,
    )
    gwg, gwd, gq, go, mix, sums = reduce_grads(
        grad_gate_up.reshape(2, 4, 2, 128, 2 * FS),
        grad_down.reshape(2, 4, 2, 80, 1024),
        grad_q.reshape(2, 4, 2, 4, 32, 1024),
        grad_o.reshape(2, 4, 2, 4, 32, 640),
        mixed_part.reshape(4, 2, TOK, D),
        small,
    )
    result = (resid + mix).astype(BF16)
    w_qkv_grad = jnp.concatenate([gq[0], gq[1][:, 128:]], axis=1)
    w_out_grad = jnp.concatenate([go[0], go[1]], axis=1).T
    at = (g * 16 + s) * 16
    attn_sum = lax.dynamic_slice_in_dim(sums[:16].reshape(D), at, 16)
    ffn_sum = lax.dynamic_slice_in_dim(sums[16:32].reshape(D), at, 16)
    return (
        result.reshape(MICRO, ROWS, D),
        input_grad.reshape(MICRO, ROWS, D),
        w_qkv_grad,
        w_out_grad,
        gwg,
        gwd.reshape(40, D),
        attn_sum,
        ffn_sum,
        sums[32, :HEAD],
        sums[32, HEAD:],
    )


def solution(mesh):
    return jax.shard_map(
        per_device,
        mesh=mesh,
        in_specs=(
            P(None, ("grp", "seq"), None),
            P(None, "grp"),
            P(("grp", "seq"), None),
            P(None, ("grp", "seq")),
            P(("grp", "seq"), None),
            P(("grp", "seq"), None),
            P(("grp", "seq")),
            P(("grp", "seq")),
            P(),
            P(),
            P(None, ("grp", "seq"), None),
        ),
        out_specs=(
            P(None, ("grp", "seq"), None),
            P(None, ("grp", "seq"), None),
            P(("grp", "seq"), None),
            P(None, ("grp", "seq")),
            P(("grp", "seq"), None),
            P(("grp", "seq"), None),
            P(("grp", "seq")),
            P(("grp", "seq")),
            P(),
            P(),
        ),
        check_vma=False,
    )
```

```python
import jax
import jax.numpy as jnp
from jax import lax
from jax.experimental import pallas as pl
from jax.experimental.pallas import tpu as pltpu
from jax.sharding import PartitionSpec as P

Q_HEADS = 20
KV_HEADS = 5
GROUP = 4
HEAD = 64
D = 2048
FF = 5120
QD = 1280
KD = 320
QKV = 1920
SEQ = 1024
MICRO = 2
ROWS = 64
TOK = 128
FS = 640
EPS = 1e-06
MESH = pl.DeviceIdType.MESH
F32 = jnp.float32
BF16 = jnp.bfloat16
ANY = pl.BlockSpec(memory_space=pl.ANY)


class Place:
    def __init__(self):
        g = lax.axis_index("grp")
        s = lax.axis_index("seq")
        self.g, self.s = g, s
        self.yh, self.x = g // 4, g % 4
        self.yl, self.z, self.c = s // 8, (s // 2) % 4, s % 2
        self.y = self.yh * 2 + self.yl

    def at(self, x=None, y=None, z=None, c=None):
        x = self.x if x is None else x
        y = self.y if y is None else y
        z = self.z if z is None else z
        c = self.c if c is None else c
        return ((y // 2) * 4 + x, (y % 2) * 8 + z * 2 + c)

    def step(self, axis, k):
        if axis == "x":
            return self.at(x=(self.x + k) % 4)
        if axis == "y":
            return self.at(y=(self.y + k) % 4)
        if axis == "z":
            return self.at(z=(self.z + k) % 4)
        return self.at(c=1 - self.c)

    def pos(self, axis, k):
        return (getattr(self, axis) + k) % 4


class Links:
    def __init__(self, send_sems, recv_sems):
        self.send_sems, self.recv_sems = send_sems, recv_sems
        self.used = 0
        self.sent = []

    def send(self, src, dst, to):
        i = self.used
        self.used += 1
        copy = pltpu.make_async_remote_copy(
            src_ref=src,
            dst_ref=dst,
            send_sem=self.send_sems.at[i],
            recv_sem=self.recv_sems.at[i],
            device_id=to,
            device_id_type=MESH,
        )
        copy.start()
        self.sent.append(copy)
        return copy

    def local(self, src, dst):
        i = self.used
        self.used += 1
        copy = pltpu.make_async_copy(src, dst, self.recv_sems.at[i])
        copy.start()
        return copy

    def drain(self):
        for copy in self.sent:
            copy.wait_send()


def greet(partners):
    barrier = pltpu.get_barrier_semaphore()
    for to in partners:
        pl.semaphore_signal(barrier, inc=1, device_id=to, device_id_type=MESH)
    pl.semaphore_wait(barrier, len(partners))


def any_call(body, name, cid, n_in, outs, scratch, sems, vmem=48 << 20):
    return pl.pallas_call(
        body,
        out_shape=outs,
        in_specs=[ANY] * n_in,
        out_specs=[ANY] * len(outs),
        name=name,
        scratch_shapes=list(scratch)
        + [pltpu.SemaphoreType.DMA((sems,)), pltpu.SemaphoreType.DMA((sems,))],
        compiler_params=pltpu.CompilerParams(
            collective_id=cid, has_side_effects=True, vmem_limit_bytes=vmem
        ),
    )


def sds(shape, dtype):
    return jax.ShapeDtypeStruct(shape, dtype)


def rms_scale(values):
    return lax.rsqrt(jnp.mean(values * values, axis=-1, keepdims=True) + EPS)


def norm_back(upstream, normed, scale, gain):
    scaled = upstream * gain
    inner = jnp.mean(scaled * normed, axis=-1, keepdims=True)
    return scale * (scaled - normed * inner)


def dot(left, right):
    return jnp.dot(left, right, preferred_element_type=F32)


def dot_last(left, right):
    return lax.dot_general(left, right, (((1,), (1,)), ((), ())), preferred_element_type=F32)


def dot_rows(left, right):
    return lax.dot_general(left, right, (((0,), (0,)), ((), ())), preferred_element_type=F32)


def slab_target(p):
    to = p.at(x=p.z, y=p.c * 2 + p.yl, z=p.g // 2, c=p.g % 2)
    return to


def slab_source(p):
    m = p.z * 2 + p.c
    return p.at(x=m % 4, y=(m // 4) * 2 + p.yl, z=p.x, c=p.yh)


def same(p, to):
    return (to[0] == p.g) & (to[1] == p.s)


def greet_plane(p, partners, slab_to, slab_from, own_slab):
    barrier = pltpu.get_barrier_semaphore()
    for to in partners:
        pl.semaphore_signal(barrier, inc=1, device_id=to, device_id_type=MESH)

    @pl.when(jnp.logical_not(own_slab))
    def _():
        pl.semaphore_signal(barrier, inc=1, device_id=slab_to, device_id_type=MESH)
        pl.semaphore_signal(barrier, inc=1, device_id=slab_from, device_id_type=MESH)
        pl.semaphore_wait(barrier, len(partners) + 2)

    @pl.when(own_slab)
    def _():
        pl.semaphore_wait(barrier, len(partners))


def slab_copy(src, dst, ssem, rsem, i, to):
    return pltpu.make_async_remote_copy(
        src_ref=src,
        dst_ref=dst,
        send_sem=ssem.at[i],
        recv_sem=rsem.at[i],
        device_id=to,
        device_id_type=MESH,
    )


def row_reduce(p, k, part, own, r0, s0, r1, res):
    z, c = p.z, p.c
    core = k.send(part.at[:, 1 - c], r0, p.step("c", 1))
    mine = k.local(part.at[:, c], own)
    yield
    mine.wait()
    core.wait_recv()

    @pl.loop(0, 4)
    def _(zz):
        @pl.loop(0, TOK, step=32)
        def _(t):
            at = pl.ds(pl.multiple_of(t, 32), 32)
            s0[zz, at] = (own[zz, at].astype(F32) + r0[zz, at].astype(F32)).astype(BF16)

    ring = [k.send(s0.at[p.pos("z", j)], r1.at[j - 1], p.step("z", j)) for j in (1, 2, 3)]
    yield
    for copy in ring:
        copy.wait_recv()

    @pl.loop(0, TOK, step=32)
    def _(t):
        at = pl.ds(pl.multiple_of(t, 32), 32)
        total = s0[z, at].astype(F32)
        for j in range(3):
            total = total + r1[j, at].astype(F32)
        res[at] = total


def row_scratch():
    return [
        pltpu.VMEM((4, TOK, D), BF16),
        pltpu.VMEM((4, TOK, D), BF16),
        pltpu.VMEM((4, TOK, D), BF16),
        pltpu.VMEM((3, TOK, D), BF16),
        pltpu.VMEM((TOK, D), F32),
    ]


def pair_body(n, *refs):
    ins, outs = refs[:n], refs[n : 2 * n]
    ssem, rsem = refs[2 * n :]
    p = Place()
    k = Links(ssem, rsem)
    greet([p.step("c", 1)])
    copies = [k.send(i, o.at[1], p.step("c", 1)) for i, o in zip(ins, outs)]
    local = [k.local(i, o.at[0]) for i, o in zip(ins, outs)]
    for copy in local:
        copy.wait()
    for copy in copies:
        copy.wait_recv()
    k.drain()


def pair_exchange(*arrays):
    n = len(arrays)
    outs = [sds((2, *a.shape), a.dtype) for a in arrays]

    def body(*refs):
        pair_body(n, *refs)

    return any_call(body, "pair_exchange", 5, n, outs, [], 2 * n)(*arrays)


def add_blocks(dst, own, recv, chunk):
    lead, rows = dst.shape[:-2], dst.shape[-2]
    count = 1
    for n in lead:
        count *= n

    @pl.loop(0, count)
    def _(i):
        at = []
        rest = i
        for n in reversed(lead):
            at.insert(0, rest % n)
            rest = rest // n

        @pl.loop(0, rows, step=chunk)
        def _(t):
            here = (*at, pl.ds(pl.multiple_of(t, chunk), chunk))
            total = own[here].astype(F32)
            for j in range(3):
                total = total + recv[(j, *here)].astype(F32)
            dst[here] = total.astype(dst.dtype)


def staged_reduce(p, k, src, stages, scr, chunk):
    own = scr[0]
    cur = src
    for n, (axis, pick) in enumerate(stages):
        recv, total = scr[1 + 2 * n], scr[2 + 2 * n]
        if n == 0:
            mine = k.local(pick(src, p.pos(axis, 0)), own)
        ring = [k.send(pick(cur, p.pos(axis, j)), recv.at[j - 1], p.step(axis, j)) for j in (1, 2, 3)]
        yield
        if n == 0:
            mine.wait()
        for copy in ring:
            copy.wait_recv()
        add_blocks(total, own if n == 0 else pick(cur, p.pos(axis, 0)), recv, chunk)
        cur = total


def staged_scratch(shapes):
    out = [pltpu.VMEM(shapes[0], BF16)]
    for n, shape in enumerate(shapes):
        out.append(pltpu.VMEM((3, *shape), BF16))
        out.append(pltpu.VMEM(shape, F32 if n == len(shapes) - 1 else BF16))
    return out


EVERY = slice(None)


def wg_stages(half):
    cols = pl.ds(half * FS, FS)
    if half == 0:
        return [
            ("y", lambda r, i: r.at[i // 2, :, i % 2, :, cols]),
            ("x", lambda r, i: r.at[i]),
        ]
    return [
        ("x", lambda r, i: r.at[:, i, :, :, cols]),
        ("y", lambda r, i: r.at[i // 2, i % 2]),
    ]


def wd_stages(half):
    cols = pl.ds(half * 512, 512)
    if half == 0:
        return [
            ("y", lambda r, i: r.at[i % 2, :, i // 2, :, cols]),
            ("x", lambda r, i: r.at[i]),
        ]
    return [
        ("x", lambda r, i: r.at[:, i, :, :, cols]),
        ("y", lambda r, i: r.at[i % 2, i // 2]),
    ]


def q_stages(half):
    cols = pl.ds(half * 512, 512)
    if half == 0:
        return [
            ("x", lambda r, i: r.at[:, i, :, :, :, cols]),
            ("z", lambda r, i: r.at[:, :, i]),
            ("y", lambda r, i: r.at[i // 2, i % 2]),
        ]
    return [
        ("y", lambda r, i: r.at[i // 2, :, i % 2, :, :, cols]),
        ("x", lambda r, i: r.at[i]),
        ("z", lambda r, i: r.at[i]),
    ]


def o_stages():
    return [
        ("z", lambda r, i: r.at[:, :, :, i]),
        ("y", lambda r, i: r.at[i // 2, :, i % 2]),
        ("x", lambda r, i: r.at[i]),
    ]


GRAD_SHAPES = [
    [(4, 128, FS), (128, FS)],
    [(2, 2, 128, FS), (128, FS)],
    [(4, 80, 512), (80, 512)],
    [(2, 2, 80, 512), (80, 512)],
    [(2, 2, 4, 32, 512), (2, 2, 32, 512), (32, 512)],
    [(4, 4, 32, 512), (4, 32, 512), (32, 512)],
    [(2, 4, 2, 32, 640), (4, 32, 640), (32, 640)],
]


def small_reduce(p, k, part, vec, recv):
    mine = k.local(part, vec.at[0])
    mine.wait()
    for n, axis in enumerate("xyzc"):
        steps = (1,) if axis == "c" else (1, 2, 3)
        ring = [k.send(vec.at[n], recv.at[n, j - 1], p.step(axis, j)) for j in steps]
        yield
        for copy in ring:
            copy.wait_recv()
        total = vec[n]
        for j in range(len(steps)):
            total = total + recv[n, j]
        vec[n + 1] = total


def grads_body(*refs):
    dwg, dwd, dq, do, dmix, small, GWG, GWD, GQ, GO, MIX, SMALL = refs[:12]
    scr = list(refs[12:])
    parts = []
    for shapes in GRAD_SHAPES:
        n = 1 + 2 * len(shapes)
        parts.append(scr[:n])
        scr = scr[n:]
    mix, (vec, recv), (ssem, rsem) = scr[:5], scr[5:7], scr[7:9]
    p = Place()
    k = Links(ssem, rsem)
    yh, x, yl, z, c = p.yh, p.x, p.yl, p.z, p.c
    m = z * 2 + c
    partners = [p.step(a, j) for a in "xyz" for j in (1, 2, 3)]
    partners += [p.at(z=(z + j) % 4, c=1 - c) for j in range(4)]
    slab_to, slab_from = slab_target(p), slab_source(p)
    own_slab = same(p, slab_to)
    greet_plane(p, partners, slab_to, slab_from, own_slab)

    chunk = 16
    gens = [
        staged_reduce(p, k, dwg, wg_stages(0), parts[0], chunk),
        staged_reduce(p, k, dwg, wg_stages(1), parts[1], chunk),
        staged_reduce(p, k, dwd, wd_stages(0), parts[2], chunk),
        staged_reduce(p, k, dwd, wd_stages(1), parts[3], chunk),
        row_reduce(p, k, dmix, *mix),
        staged_reduce(p, k, do, o_stages(), parts[6], chunk),
        staged_reduce(p, k, dq, q_stages(0), parts[4], chunk),
        staged_reduce(p, k, dq, q_stages(1), parts[5], chunk),
        small_reduce(p, k, small, vec, recv),
    ]
    alive = list(gens)
    while alive:
        alive = [g for g in alive if next(g, alive) is not alive]

    last, local = [], []
    for half in range(2):
        total = parts[half][-1]
        cols = pl.ds(pl.multiple_of(half * FF + m * FS, 128), FS)
        for dz in range(4):
            for dc in range(2):
                zz, cc = (z + dz) % 4, (c + dc) % 2
                src = total.at[pl.ds(pl.multiple_of((zz * 2 + cc) * 16, 16), 16)]
                if dz == 0 and dc == 0:
                    local.append(k.local(src, GWG.at[:, cols]))
                else:
                    last.append(k.send(src, GWG.at[:, cols], p.at(z=zz, c=cc)))
    slabs = []
    for half in range(2):
        i = k.used
        k.used += 1
        src, dst = parts[2 + half][-1], GWD.at[:, pl.ds(half * 512, 512)]
        slabs.append((src, dst, i))

        @pl.when(own_slab)
        def _(src=src, dst=dst, i=i):
            pltpu.make_async_copy(src, dst, rsem.at[i]).start()

        @pl.when(jnp.logical_not(own_slab))
        def _(src=src, dst=dst, i=i):
            slab_copy(src, dst, ssem, rsem, i, slab_from).start()

    for total, dst in (
        (parts[4][-1], GQ.at[c, :, pl.ds(0, 512)]),
        (parts[5][-1], GQ.at[c, :, pl.ds(512, 512)]),
        (parts[6][-1], GO.at[c]),
    ):
        mine = total.at[pl.ds(pl.multiple_of(c * 16, 16), 16)]
        other = total.at[pl.ds(pl.multiple_of((1 - c) * 16, 16), 16)]
        local.append(k.local(mine, dst))
        last.append(k.send(other, dst, p.step("c", 1)))
    local.append(k.local(mix[-1], MIX))
    local.append(k.local(vec.at[4], SMALL))
    for copy in local:
        copy.wait()
    for copy in last:
        copy.wait_recv()
    for src, dst, i in slabs:

        @pl.when(own_slab)
        def _(src=src, dst=dst, i=i):
            pltpu.make_async_copy(src, dst, rsem.at[i]).wait()

        @pl.when(jnp.logical_not(own_slab))
        def _(src=src, dst=dst, i=i):
            slab_copy(src, dst, ssem, rsem, i, slab_from).wait()

    k.drain()


def reduce_grads(dwg, dwd, dq, do, dmix, small):
    outs = [
        sds((16, 2 * FF), F32),
        sds((80, 1024), F32),
        sds((2, 16, 1024), F32),
        sds((2, 16, 640), F32),
        sds((TOK, D), F32),
        sds((40, 128), F32),
    ]
    scratch = []
    for shapes in GRAD_SHAPES:
        scratch += staged_scratch(shapes)
    scratch += row_scratch()
    scratch += [pltpu.VMEM((5, 40, 128), F32), pltpu.VMEM((4, 3, 40, 128), F32)]
    return any_call(grads_body, "reduce_grads", 6, 6, outs, scratch, 110, 56 << 20)(
        dwg, dwd, dq, do, dmix, small
    )


def swap(a, b):
    left = lax.broadcasted_iota(jnp.int32, a.shape, 1) < ROWS
    return jnp.where(left, a, pltpu.roll(b, ROWS, 1)), jnp.where(left, pltpu.roll(a, ROWS, 1), b)


def head_scale(v):
    return lax.rsqrt(jnp.mean(v * v, axis=-2, keepdims=True) + EPS)


def half_turn(v):
    half = HEAD // 2
    return jnp.concatenate([-v[..., half:, :], v[..., :half, :]], axis=-2)


def half_back(v):
    half = HEAD // 2
    return jnp.concatenate([v[..., half:, :], -v[..., :half, :]], axis=-2)


def low(v):
    return v.astype(BF16).astype(F32)


def query_units(packed_t, g, cos, sin, gain):
    raw = packed_t[pl.ds(pl.multiple_of(g * 256, 256), 256)].reshape(GROUP, HEAD, TOK)
    head = raw * head_scale(raw) * gain
    turned = low(head * cos + half_turn(head) * sin) * (HEAD ** -0.5)
    a0, a1 = swap(turned[0], turned[1])
    b0, b1 = swap(turned[2], turned[3])
    none = jnp.zeros((HEAD, 256), F32)
    return [
        jnp.concatenate([jnp.concatenate([a, b], axis=1), none], axis=0) for a, b in ((a0, b0), (a1, b1))
    ]


def fill_bias(bias, segc, segq, start):
    @pl.loop(0, SEQ, step=128)
    def _(t):
        at = pl.ds(pl.multiple_of(t, 128), 128)
        key = lax.broadcasted_iota(jnp.int32, (128, 256), 0) + t
        query = lax.broadcasted_iota(jnp.int32, (128, 256), 1) % ROWS + start
        for m in range(MICRO):
            ok = (key <= query) & (segc[at, m : m + 1] == segq[m : m + 1, :])
            ok = ok | (key == query)
            bias[m, at] = jnp.where(ok, 3e38, -1e30)


def unit_kv(KV, m, g):
    cols = pl.ds(pl.multiple_of(g * 128, 128), 128)
    return KV[m, :, :, :, :, cols].reshape(SEQ, 128)


def front_body(*refs):
    (x_ref, wq, wo, wg, wd, og, segc, segq, cos_ref, sin_ref, qgain, kgain) = refs[:12]
    (WQ, WO, WG, WD, OG, RG, KV, pt_out, lse_out, att_out, resid_out, normed_out, gains_out) = refs[12:25]
    (wqs, wos, kvl, kvs, bias, qts, ots, n2, ssem, rsem) = refs[25:]
    p = Place()
    k = Links(ssem, rsem)
    yh, x, yl, z, c = p.yh, p.x, p.yl, p.z, p.c
    m = z * 2 + c
    yl_partner = p.at(y=p.yh * 2 + 1 - yl)
    partners = [p.step(a, j) for a in "xyz" for j in (1, 2, 3)]
    partners += [p.at(z=(z + j) % 4, c=1 - c) for j in range(4)]
    slab_to, slab_from = slab_target(p), slab_source(p)
    own_slab = same(p, slab_to)
    greet_plane(p, partners, slab_to, slab_from, own_slab)

    def wq_a(*at):
        return wqs.at[(*at, EVERY, pl.ds(0, 1024))]

    def wq_b(*at):
        return wqs.at[(*at, EVERY, pl.ds(1024, 1024))]

    def wo_(*at):
        return wos.at[(*at, EVERY, EVERY)]

    own_wq = k.local(wq, wqs.at[yh, x, yl, z, c])
    own_wo = k.local(wo, wos.at[yh, x, yl, z, c])
    q1, o1 = [], []
    for j in (1, 2, 3):
        q1.append(k.send(wq.at[:, pl.ds(0, 1024)], wq_a(yh, x, yl, z, c), p.step("y", j)))
        q1.append(k.send(wq.at[:, pl.ds(1024, 1024)], wq_b(yh, x, yl, z, c), p.step("z", j)))
    for j in (1, 2, 3):
        o1.append(k.send(wo, wo_(yh, x, yl, z, c), p.step("x", j)))
    pieces, own_pieces = [], []
    for dz in range(4):
        for dc in range(2):
            zz, cc = (z + dz) % 4, (c + dc) % 2
            mm = zz * 2 + cc
            for half in range(2):
                src = wg.at[:, pl.ds(pl.multiple_of(half * FF + mm * FS, 128), FS)]
                dst = WG.at[yh, x, yl, m, :, pl.ds(half * FS, FS)]
                if dz == 0 and dc == 0:
                    own_pieces.append(k.local(src, dst))
                else:
                    pieces.append(k.send(src, dst, p.at(z=zz, c=cc)))
    slab_dst = WD.at[yl, z, c]
    i = k.used
    k.used += 1
    slab = slab_copy(wd, slab_dst, ssem, rsem, i, slab_to)

    @pl.when(own_slab)
    def _():
        pltpu.make_async_copy(wd, slab_dst, rsem.at[i]).start()

    @pl.when(jnp.logical_not(own_slab))
    def _():
        slab.start()

    fill_bias(bias, segc, segq, p.s * ROWS)

    own_wq.wait()
    own_wo.wait()
    for copy in q1:
        copy.wait_recv()
    q2 = []
    for j in (1, 2, 3):
        src = wq_a(EVERY, x, EVERY, z, c)
        q2.append(k.send(src, src, p.step("z", j)))
        src = wq_b(yh, x, yl, EVERY, c)
        q2.append(k.send(src, src, p.step("x", j)))
    for copy in o1:
        copy.wait_recv()
    o2 = []
    for j in (1, 2, 3):
        src = wo_(yh, EVERY, yl, z, c)
        o2.append(k.send(src, src, p.step("y", j)))
    for copy in q2:
        copy.wait_recv()
    q3 = []
    for j in (1, 2, 3):
        src = wq_a(EVERY, x, EVERY, EVERY, c)
        q3.append((k.send(src, src, p.step("x", j)), wq_a(EVERY, p.pos("x", -j), EVERY, EVERY, c)))
        src = wq_b(yh, EVERY, yl, EVERY, c)
        yy = p.pos("y", -j)
        q3.append((k.send(src, src, p.step("y", j)), wq_b(yy // 2, EVERY, yy % 2, EVERY, c)))
    qc = []
    for src in (wq_a(EVERY, x, EVERY, EVERY, c), wq_b(yh, EVERY, yl, EVERY, c)):
        qc.append(k.send(src, src, p.step("c", 1)))
    for copy in o2:
        copy.wait_recv()
    o3 = []
    for j in (1, 2, 3):
        src = wo_(EVERY, EVERY, EVERY, z, c)
        o3.append((k.send(src, src, p.step("z", j)), wo_(EVERY, EVERY, EVERY, p.pos("z", -j), c)))
    oc = [k.send(wo_(EVERY, EVERY, EVERY, z, c), wo_(EVERY, EVERY, EVERY, z, c), p.step("c", 1))]

    for copy in own_pieces:
        copy.wait()
    for copy in pieces:
        copy.wait_recv()

    @pl.when(own_slab)
    def _():
        pltpu.make_async_copy(wd, slab_dst, rsem.at[i]).wait()

    @pl.when(jnp.logical_not(own_slab))
    def _():
        slab.wait_recv()

    for copy, src in q3:
        copy.wait_recv()
        qc.append(k.send(src, src, p.step("c", 1)))
    lo, hi = pl.ds(0, FS), pl.ds(FS, FS)
    dlo, dhi = pl.ds(0, 512), pl.ds(512, 512)
    plane = []
    for j in (1, 2, 3):
        for src, axis in (
            (WG.at[yh, x, yl, :, :, lo], "x"),
            (WG.at[yh, x, yl, :, :, hi], "y"),
            (WD.at[yl, x, yh, :, dlo], "x"),
            (WD.at[yl, x, yh, :, dhi], "y"),
        ):
            plane.append(k.send(src, src, p.step(axis, j)))
    for copy in qc:
        copy.wait_recv()
    keep_wq = k.local(wqs, WQ)

    pick = jnp.where(
        lax.broadcasted_iota(jnp.int32, (8, 128), 0) == lax.broadcasted_iota(jnp.int32, (8, 128), 1), 1.0, 0.0
    ).astype(BF16)
    gain_cols = wqs[:, :, :, :, :, :, pl.ds(QKV, 128)].reshape(D, 128)
    gains_out[...] = dot_last(pick, gain_cols)
    hidden = x_ref[...].astype(F32)
    normed = (hidden * rms_scale(hidden) * gains_out[0:1, :]).astype(BF16)
    normed_out[...] = normed

    @pl.loop(0, 8)
    def _(t):
        cols = pl.ds(pl.multiple_of(t * 256, 256), 256)
        w = wqs[:, :, :, :, :, :, cols].reshape(D, 256)
        pt_out[cols] = dot(normed_out[...], w).T

    cos, sin = cos_ref[...], sin_ref[...]

    @pl.loop(0, KV_HEADS)
    def _(g):
        raw = pt_out[pl.ds(pl.multiple_of(QD + g * HEAD, HEAD), HEAD)]
        head = raw * head_scale(raw) * kgain[...]
        key = head * cos + half_turn(head) * sin
        value = pt_out[pl.ds(pl.multiple_of(QD + KD + g * HEAD, HEAD), HEAD)]
        both = jnp.concatenate([key, value], axis=0).T.astype(BF16)
        cols = pl.ds(pl.multiple_of(g * 128, 128), 128)
        for mm in range(MICRO):
            kvl[mm, :, cols] = both[mm * ROWS : (mm + 1) * ROWS]

    own_kv = k.local(kvl, kvs.at[:, yl, z, c])
    across = k.send(kvl, kvs.at[:, yl, z, c], yl_partner)
    ring = [k.send(kvl, kvs.at[:, yl, z, c], p.step("z", j)) for j in (1, 2, 3)]

    @pl.loop(0, KV_HEADS)
    def _(g):
        for mm, unit in enumerate(query_units(pt_out, g, cos, sin, qgain[...])):
            qts[g, mm] = unit.astype(BF16)

    for copy in plane:
        copy.wait_recv()
    across.wait_recv()
    src = kvs.at[:, 1 - yl, z, c]
    ring += [k.send(src, src, p.step("z", j)) for j in (1, 2, 3)]
    plane2 = []
    for j in (1, 2, 3):
        for src, axis in (
            (WG.at[yh, :, yl, :, :, lo], "y"),
            (WG.at[:, x, :, :, :, hi], "x"),
            (WD.at[yl, :, yh, :, dlo], "y"),
            (WD.at[:, x, :, :, dhi], "x"),
        ):
            plane2.append(k.send(src, src, p.step(axis, j)))
    own_kv.wait()
    for copy in ring:
        copy.wait_recv()
    src = kvs.at[:, :, :, c]
    kvc = k.send(src, src, p.step("c", 1))
    for copy, src in o3:
        copy.wait_recv()
        oc.append(k.send(src, src, p.step("c", 1)))
    own_og = k.local(og, OG.at[z, c])
    rows = [k.send(og, OG.at[z, c], p.step("z", j)) for j in (1, 2, 3)]
    last = [k.send(og, OG.at[z, c], p.step("c", 1))]
    kvc.wait_recv()
    keep_kv = k.local(kvs, KV)

    @pl.loop(0, 2 * KV_HEADS)
    def _(u):
        g, mm = u // 2, u % 2
        kv = unit_kv(kvs, mm, g)
        score = jnp.minimum(dot(kv, qts[g, mm]), bias[mm])
        peak = jnp.max(score, axis=0, keepdims=True)
        raised = jnp.exp(score - peak)
        total = jnp.sum(raised, axis=0, keepdims=True)
        probs = (raised * (1.0 / total)).astype(BF16)
        ots[g, mm] = dot_rows(kv, probs)[HEAD:]
        lse_out[u] = jnp.broadcast_to(peak + jnp.log(total), (8, 256))

    for g in range(KV_HEADS):
        for t in range(2):
            cols = slice(t * 128, (t + 1) * 128)
            a, b = swap(ots[g, 0, :, cols], ots[g, 1, :, cols])
            at = (g * GROUP + 2 * t) * HEAD
            att_out[:, at : at + 128] = jnp.concatenate([a, b], axis=0).T.astype(BF16)

    for copy in oc:
        copy.wait_recv()
    keep_wo = k.local(wos, WO)

    @pl.loop(0, 8)
    def _(t):
        w = wos[t // 4, t % 4].reshape(256, QD)
        cols = pl.ds(pl.multiple_of(t * 256, 256), 256)
        resid_out[:, cols] = x_ref[:, cols].astype(F32) + dot_last(att_out[...], w)

    resid = resid_out[...]
    n2[...] = (resid * rms_scale(resid) * gains_out[1:2, :]).astype(BF16)
    own_n2 = k.local(n2, RG.at[z, c])
    ring2 = [k.send(n2, RG.at[z, c], p.step("z", j)) for j in (1, 2, 3)]
    last.append(k.send(n2, RG.at[z, c], p.step("c", 1)))
    for j, copy in zip((1, 2, 3), rows):
        copy.wait_recv()
        src = OG.at[p.pos("z", -j), c]
        last.append(k.send(src, src, p.step("c", 1)))
    for j, copy in zip((1, 2, 3), ring2):
        copy.wait_recv()
        src = RG.at[p.pos("z", -j), c]
        last.append(k.send(src, src, p.step("c", 1)))
    for copy in plane2 + last:
        copy.wait_recv()
    for copy in (keep_wq, keep_kv, keep_wo, own_og, own_n2):
        copy.wait()
    k.drain()

    @pl.when(jnp.logical_not(own_slab))
    def _():
        slab.wait_send()


VMEM = pl.BlockSpec(memory_space=pltpu.VMEM)


def front(x, wq, wo, wg, wd, og, segc, segq, cos, sin, qgain, kgain):
    hbm = [
        sds((2, 4, 2, 4, 2, 16, 2048), BF16),
        sds((2, 4, 2, 4, 2, 16, QD), BF16),
        sds((2, 4, 2, 8, 16, 2 * FS), BF16),
        sds((2, 4, 2, 80, 1024), BF16),
        sds((4, 2, TOK, D), BF16),
        sds((4, 2, TOK, D), BF16),
        sds((2, 2, 4, 2, ROWS, 2 * KD), BF16),
    ]
    vmem = [
        sds((2048, TOK), F32),
        sds((2 * KV_HEADS, 8, 256), F32),
        sds((TOK, QD), BF16),
        sds((TOK, D), F32),
        sds((TOK, D), BF16),
        sds((8, D), F32),
    ]
    scratch = [
        pltpu.VMEM((2, 4, 2, 4, 2, 16, 2048), BF16),
        pltpu.VMEM((2, 4, 2, 4, 2, 16, QD), BF16),
        pltpu.VMEM((2, ROWS, 2 * KD), BF16),
        pltpu.VMEM((2, 2, 4, 2, ROWS, 2 * KD), BF16),
        pltpu.VMEM((2, SEQ, 256), F32),
        pltpu.VMEM((KV_HEADS, 2, 128, 256), BF16),
        pltpu.VMEM((KV_HEADS, 2, HEAD, 256), F32),
        pltpu.VMEM((TOK, D), BF16),
        pltpu.SemaphoreType.DMA((120,)),
        pltpu.SemaphoreType.DMA((120,)),
    ]
    return pl.pallas_call(
        front_body,
        out_shape=hbm + vmem,
        in_specs=[VMEM] + [ANY] * 5 + [VMEM] * 6,
        out_specs=[ANY] * len(hbm) + [VMEM] * len(vmem),
        scratch_shapes=scratch,
        name="front",
        compiler_params=pltpu.CompilerParams(
            collective_id=0, has_side_effects=True, vmem_limit_bytes=56 << 20
        ),
    )(x, wq, wo, wg, wd, og, segc, segq, cos, sin, qgain, kgain)


def back_body(*refs):
    (part, x_ref, og_ref, resid_ref, gains, WQ, WO, KV, pt, lse, segc, segq, cos_ref, sin_ref, qgain, kgain) = refs[:16]
    (in_grad, dp_out, low_out, rows_out, heads_out) = refs[16:21]
    (rown, rr0, rs0, rr1, rres) = refs[21:26]
    (wqs, wos, kvs, bias, qts, qns, dts, dns, dqt, dpt, datt, dres, kpart) = refs[26:39]
    (k0, ks0, k1, ks1, k2, kres, ssem, rsem) = refs[39:]
    p = Place()
    k = Links(ssem, rsem)
    yl, z, c = p.yl, p.z, p.c
    yl_partner = p.at(y=p.yh * 2 + 1 - yl)
    greet([p.step("z", j) for j in (1, 2, 3)] + [yl_partner, p.step("c", 1)])
    get_wo = k.local(WO, wos)
    get_kv = k.local(KV, kvs)
    get_wq = k.local(WQ, wqs)
    steps = row_reduce(p, k, part, rown, rr0, rs0, rr1, rres)
    next(steps)
    fill_bias(bias, segc, segq, p.s * ROWS)
    next(steps)
    cos, sin = cos_ref[...], sin_ref[...]

    @pl.loop(0, KV_HEADS)
    def _(g):
        for mm, unit in enumerate(query_units(pt, g, cos, sin, qgain[...])):
            qts[g, mm] = unit.astype(BF16)
            qns[g, mm] = unit.T.astype(BF16)

    next(steps, None)
    resid = resid_ref[...]
    scale_two = rms_scale(resid)
    norm_two = resid * scale_two
    d_normed = rres[...]
    rows_out[1:2, :] = jnp.sum(d_normed * norm_two, axis=0, keepdims=True)
    d_resid = og_ref[...].astype(F32) + norm_back(d_normed, norm_two, scale_two, gains[1:2, :])
    dres[...] = d_resid
    low_out[...] = d_resid.astype(BF16)
    get_wo.wait()

    @pl.loop(0, 5)
    def _(t):
        cols = pl.ds(pl.multiple_of(t * 256, 256), 256)
        w = wos[:, :, :, :, :, :, cols].reshape(D, 256)
        datt[:, cols] = low(dot(low_out[...], w))

    for g in range(KV_HEADS):
        tiles = []
        for t in range(2):
            at = (g * GROUP + 2 * t) * HEAD
            both = datt[:, at : at + 128].T
            tiles.append(swap(both[:HEAD], both[HEAD:]))
        for mm in range(MICRO):
            none = jnp.zeros((HEAD, 256), F32)
            unit = jnp.concatenate([none, jnp.concatenate([tiles[0][mm], tiles[1][mm]], axis=1)], axis=0)
            dts[g, mm] = unit.astype(BF16)
            dns[g, mm] = unit.T.astype(BF16)
    get_kv.wait()

    @pl.loop(0, 2 * KV_HEADS)
    def _(u):
        g, mm = u // 2, u % 2
        kv = unit_kv(kvs, mm, g)
        score = jnp.minimum(dot(kv, qts[g, mm]), bias[mm])
        again = jnp.exp(score - lse[u, 0:1, :])
        d_probs = dot(kv, dts[g, mm])
        inner = jnp.sum(again * d_probs, axis=0, keepdims=True)
        d_scores = (again * (d_probs - inner)).astype(BF16)
        d_kv = dot(d_scores, qns[g, mm]) + dot(again.astype(BF16), dns[g, mm])
        cols = pl.ds(pl.multiple_of(g * 128, 128), 128)
        kpart[mm, :, :, :, :, cols] = d_kv.astype(BF16).reshape(2, 4, 2, ROWS, 128)
        dqt[g, mm] = dot_rows(kv, d_scores)[:HEAD] * (HEAD ** -0.5)

    core = k.send(kpart.at[:, :, :, 1 - c], k0, p.step("c", 1))
    core.wait_recv()

    @pl.loop(0, 4)
    def _(zz):
        for a in range(2):
            for b in range(2):
                ks0[a, b, zz] = (kpart[a, b, zz, c].astype(F32) + k0[a, b, zz].astype(F32)).astype(BF16)

    ring = [k.send(ks0.at[:, :, p.pos("z", j)], k1.at[j - 1], p.step("z", j)) for j in (1, 2, 3)]

    query_sum = jnp.zeros((HEAD, TOK), F32)
    for g in range(KV_HEADS):
        heads = []
        for t in range(2):
            cols = slice(t * 128, (t + 1) * 128)
            heads += list(swap(dqt[g, 0, :, cols], dqt[g, 1, :, cols]))
        for h in range(GROUP):
            at = (g * GROUP + h) * HEAD
            d_raw, term = head_back(pt[at : at + HEAD], heads[h], cos, sin, qgain[...])
            query_sum = query_sum + term
            dpt[at : at + HEAD] = d_raw
    heads_out[0] = query_sum

    for copy in ring:
        copy.wait_recv()
    for a in range(2):
        for b in range(2):
            total = ks0[a, b, z].astype(F32)
            for j in range(3):
                total = total + k1[j, a, b].astype(F32)
            ks1[a, b] = total.astype(BF16)
    across = k.send(ks1.at[:, 1 - yl], k2, yl_partner)
    across.wait_recv()
    for a in range(2):
        kres[pl.ds(a * ROWS, ROWS)] = ks1[a, yl].astype(F32) + k2[a].astype(F32)
    key_sum = jnp.zeros((HEAD, TOK), F32)
    for g in range(KV_HEADS):
        both = kres[:, g * 128 : (g + 1) * 128].T
        at = QD + g * HEAD
        d_raw, term = head_back(pt[at : at + HEAD], both[:HEAD], cos, sin, kgain[...])
        key_sum = key_sum + term
        dpt[at : at + HEAD] = d_raw
        dpt[at + KD : at + KD + HEAD] = both[HEAD:]
    heads_out[1] = key_sum
    for t in range(15):
        dp_out[:, t * 128 : (t + 1) * 128] = dpt[t * 128 : (t + 1) * 128].T.astype(BF16)
    get_wq.wait()

    @pl.loop(0, 8)
    def _(t):
        w = wqs[t // 4, t % 4].reshape(256, 2048)[:, :QKV]
        cols = pl.ds(pl.multiple_of(t * 256, 256), 256)
        in_grad[:, cols] = dot_last(dp_out[...], w)

    hidden = x_ref[...].astype(F32)
    scale_one = rms_scale(hidden)
    norm_one = hidden * scale_one
    d_normed = in_grad[...]
    rows_out[0:1, :] = jnp.sum(d_normed * norm_one, axis=0, keepdims=True)
    in_grad[...] = dres[...] + norm_back(d_normed, norm_one, scale_one, gains[0:1, :])
    k.drain()


def head_back(raw, grad, cos, sin, gain):
    scale = head_scale(raw)
    normed = raw * scale
    d_head = grad * cos + half_back(grad * sin)
    scaled = d_head * gain
    inner = jnp.mean(scaled * normed, axis=0, keepdims=True)
    return scale * (scaled - normed * inner), d_head * normed


def back(part, x, og, resid, gains, WQ, WO, KV, pt, lse, segc, segq, cos, sin, qgain, kgain):
    outs = [
        sds((TOK, D), F32),
        sds((TOK, QKV), BF16),
        sds((TOK, D), BF16),
        sds((8, D), F32),
        sds((2, HEAD, TOK), F32),
    ]
    w = 2 * KD
    scratch = row_scratch() + [
        pltpu.VMEM((2, 4, 2, 4, 2, 16, 2048), BF16),
        pltpu.VMEM((2, 4, 2, 4, 2, 16, QD), BF16),
        pltpu.VMEM((2, 2, 4, 2, ROWS, w), BF16),
        pltpu.VMEM((2, SEQ, 256), F32),
        pltpu.VMEM((KV_HEADS, 2, 128, 256), BF16),
        pltpu.VMEM((KV_HEADS, 2, 256, 128), BF16),
        pltpu.VMEM((KV_HEADS, 2, 128, 256), BF16),
        pltpu.VMEM((KV_HEADS, 2, 256, 128), BF16),
        pltpu.VMEM((KV_HEADS, 2, HEAD, 256), F32),
        pltpu.VMEM((QKV, TOK), F32),
        pltpu.VMEM((TOK, QD), F32),
        pltpu.VMEM((TOK, D), F32),
        pltpu.VMEM((2, 2, 4, 2, ROWS, w), BF16),
        pltpu.VMEM((2, 2, 4, ROWS, w), BF16),
        pltpu.VMEM((2, 2, 4, ROWS, w), BF16),
        pltpu.VMEM((3, 2, 2, ROWS, w), BF16),
        pltpu.VMEM((2, 2, ROWS, w), BF16),
        pltpu.VMEM((2, ROWS, w), BF16),
        pltpu.VMEM((TOK, w), F32),
        pltpu.SemaphoreType.DMA((20,)),
        pltpu.SemaphoreType.DMA((20,)),
    ]
    return pl.pallas_call(
        back_body,
        out_shape=outs,
        in_specs=[ANY] + [VMEM] * 4 + [ANY] * 3 + [VMEM] * 8,
        out_specs=[VMEM] * len(outs),
        scratch_shapes=scratch,
        name="back",
        compiler_params=pltpu.CompilerParams(
            collective_id=4, has_side_effects=True, vmem_limit_bytes=56 << 20
        ),
    )(part, x, og, resid, gains, WQ, WO, KV, pt, lse, segc, segq, cos, sin, qgain, kgain)


def rope_tables(start):
    half = HEAD // 2
    inverse = 10000.0 ** (-jnp.arange(half, dtype=F32) / half)
    positions = (start + jnp.arange(TOK) % ROWS).astype(F32)
    angles = inverse[:, None] * positions[None, :]
    angles = jnp.concatenate([angles, angles], axis=0)
    return jnp.cos(angles), jnp.sin(angles)


def per_device(
    tokens,
    segment_ids,
    w_qkv,
    w_out,
    w_gate_up,
    w_down,
    attn_gain,
    ffn_gain,
    query_gain,
    key_gain,
    out_grad,
):
    s = lax.axis_index("seq")
    g = lax.axis_index("grp")
    c = s % 2
    start = s * ROWS
    qgain = query_gain.astype(F32)[:, None]
    kgain = key_gain.astype(F32)[:, None]
    gains = jnp.stack([attn_gain, ffn_gain], axis=1)
    wq_in = jnp.concatenate([w_qkv, jnp.pad(gains, ((0, 0), (0, 126)))], axis=1)
    og_in = out_grad.reshape(TOK, D)
    x_in = tokens.reshape(TOK, D)
    segc = segment_ids.T
    query_ids = lax.dynamic_slice_in_dim(segment_ids, start, ROWS, axis=1)
    segq = jnp.tile(jnp.where(query_ids >= 0, query_ids, -2), (1, GROUP))
    cos, sin = rope_tables(start)
    (WQ, WO, WG, WD, OG, RG, KV, pt, lse, attended, resid, normed, gain_rows) = front(
        x_in, wq_in, w_out.T, w_gate_up, w_down.reshape(80, 1024), og_in,
        segc, segq, cos, sin, qgain, kgain,
    )
    WG = WG.reshape(D, 2 * FS)
    WD = WD.reshape(FS, D)
    OG = OG.reshape(8 * TOK, D)
    rows = RG.reshape(8 * TOK, D)

    gate_up = dot(rows, WG)
    gate = gate_up[:, :FS]
    upper = gate_up[:, FS:]
    sigmoid_gate = jax.nn.sigmoid(gate)
    active = gate * sigmoid_gate
    inner = (active * upper).astype(BF16)
    mixed_part = dot(inner, WD).astype(BF16)
    d_inner = dot_last(OG, WD)
    d_gate = d_inner * upper * sigmoid_gate * (1.0 + gate * (1.0 - sigmoid_gate))
    d_upper = d_inner * active
    d_gate_up = jnp.concatenate([d_gate, d_upper], axis=1).astype(BF16)
    d_rows_part = dot_last(d_gate_up, WG).astype(BF16)
    grad_gate_up = dot_rows(rows, d_gate_up).astype(BF16)
    grad_down = dot_rows(inner, OG).astype(BF16)

    input_grad, d_packed, resid_low, terms, head_terms = back(
        d_rows_part.reshape(4, 2, TOK, D), x_in, og_in, resid, gain_rows, WQ, WO, KV, pt, lse,
        segc, segq, cos, sin, qgain, kgain,
    )

    pair = pair_exchange(normed, d_packed, attended, resid_low)
    normed_2, packed_2, attended_2, low_2 = [a.reshape(2 * TOK, -1) for a in pair]
    packed_cols = lax.dynamic_slice_in_dim(packed_2, c * 896, 1024, axis=1)
    attended_cols = lax.dynamic_slice_in_dim(attended_2, c * 640, 640, axis=1)
    grad_q = dot_rows(normed_2, packed_cols).astype(BF16)
    grad_o = dot_rows(low_2, attended_cols).astype(BF16)

    head_sums = jnp.sum(head_terms, axis=2).reshape(1, 128)
    small = jnp.concatenate(
        [terms[:2].reshape(32, 128), jnp.pad(head_sums, ((0, 7), (0, 0)))], axis=0
    )
    gwg, gwd, gq, go, mix, sums = reduce_grads(
        grad_gate_up.reshape(2, 4, 2, 128, 2 * FS),
        grad_down.reshape(2, 4, 2, 80, 1024),
        grad_q.reshape(2, 4, 2, 4, 32, 1024),
        grad_o.reshape(2, 4, 2, 4, 32, 640),
        mixed_part.reshape(4, 2, TOK, D),
        small,
    )
    result = (resid + mix).astype(BF16)
    w_qkv_grad = jnp.concatenate([gq[0], gq[1][:, 128:]], axis=1)
    w_out_grad = jnp.concatenate([go[0], go[1]], axis=1).T
    at = (g * 16 + s) * 16
    attn_sum = lax.dynamic_slice_in_dim(sums[:16].reshape(D), at, 16)
    ffn_sum = lax.dynamic_slice_in_dim(sums[16:32].reshape(D), at, 16)
    return (
        result.reshape(MICRO, ROWS, D),
        input_grad.reshape(MICRO, ROWS, D),
        w_qkv_grad,
        w_out_grad,
        gwg,
        gwd.reshape(40, D),
        attn_sum,
        ffn_sum,
        sums[32, :HEAD],
        sums[32, HEAD:],
    )


def solution(mesh):
    return jax.shard_map(
        per_device,
        mesh=mesh,
        in_specs=(
            P(None, ("grp", "seq"), None),
            P(None, "grp"),
            P(("grp", "seq"), None),
            P(None, ("grp", "seq")),
            P(("grp", "seq"), None),
            P(("grp", "seq"), None),
            P(("grp", "seq")),
            P(("grp", "seq")),
            P(),
            P(),
            P(None, ("grp", "seq"), None),
        ),
        out_specs=(
            P(None, ("grp", "seq"), None),
            P(None, ("grp", "seq"), None),
            P(("grp", "seq"), None),
            P(None, ("grp", "seq")),
            P(("grp", "seq"), None),
            P(("grp", "seq"), None),
            P(("grp", "seq")),
            P(("grp", "seq")),
            P(),
            P(),
        ),
        check_vma=False,
    )
```

```python
import jax
import jax.numpy as jnp
from jax import lax
from jax.experimental import pallas as pl
from jax.experimental.pallas import tpu as pltpu
from jax.sharding import PartitionSpec as P

Q_HEADS = 20
KV_HEADS = 5
GROUP = 4
HEAD = 64
D = 2048
FF = 5120
QD = 1280
KD = 320
QKV = 1920
SEQ = 1024
MICRO = 2
ROWS = 64
TOK = 128
FS = 640
EPS = 1e-06
MESH = pl.DeviceIdType.MESH
F32 = jnp.float32
BF16 = jnp.bfloat16
ANY = pl.BlockSpec(memory_space=pl.ANY)


class Place:
    def __init__(self):
        g = lax.axis_index("grp")
        s = lax.axis_index("seq")
        self.g, self.s = g, s
        self.yh, self.x = g // 4, g % 4
        self.yl, self.z, self.c = s // 8, (s // 2) % 4, s % 2
        self.y = self.yh * 2 + self.yl

    def at(self, x=None, y=None, z=None, c=None):
        x = self.x if x is None else x
        y = self.y if y is None else y
        z = self.z if z is None else z
        c = self.c if c is None else c
        return ((y // 2) * 4 + x, (y % 2) * 8 + z * 2 + c)

    def step(self, axis, k):
        if axis == "x":
            return self.at(x=(self.x + k) % 4)
        if axis == "y":
            return self.at(y=(self.y + k) % 4)
        if axis == "z":
            return self.at(z=(self.z + k) % 4)
        return self.at(c=1 - self.c)

    def pos(self, axis, k):
        return (getattr(self, axis) + k) % 4


class Links:
    def __init__(self, send_sems, recv_sems):
        self.send_sems, self.recv_sems = send_sems, recv_sems
        self.used = 0
        self.sent = []

    def send(self, src, dst, to):
        i = self.used
        self.used += 1
        copy = pltpu.make_async_remote_copy(
            src_ref=src,
            dst_ref=dst,
            send_sem=self.send_sems.at[i],
            recv_sem=self.recv_sems.at[i],
            device_id=to,
            device_id_type=MESH,
        )
        copy.start()
        self.sent.append(copy)
        return copy

    def local(self, src, dst):
        i = self.used
        self.used += 1
        copy = pltpu.make_async_copy(src, dst, self.recv_sems.at[i])
        copy.start()
        return copy

    def drain(self):
        for copy in self.sent:
            copy.wait_send()


def greet(partners):
    barrier = pltpu.get_barrier_semaphore()
    for to in partners:
        pl.semaphore_signal(barrier, inc=1, device_id=to, device_id_type=MESH)
    pl.semaphore_wait(barrier, len(partners))


def sds(shape, dtype):
    return jax.ShapeDtypeStruct(shape, dtype)


def rms_scale(values):
    return lax.rsqrt(jnp.mean(values * values, axis=-1, keepdims=True) + EPS)


def norm_back(upstream, normed, scale, gain):
    scaled = upstream * gain
    inner = jnp.mean(scaled * normed, axis=-1, keepdims=True)
    return scale * (scaled - normed * inner)


def dot(left, right):
    return jnp.dot(left, right, preferred_element_type=F32)


def dot_last(left, right):
    return lax.dot_general(left, right, (((1,), (1,)), ((), ())), preferred_element_type=F32)


def dot_rows(left, right):
    return lax.dot_general(left, right, (((0,), (0,)), ((), ())), preferred_element_type=F32)


def slab_target(p):
    to = p.at(x=p.z, y=p.c * 2 + p.yl, z=p.g // 2, c=p.g % 2)
    return to


def slab_source(p):
    m = p.z * 2 + p.c
    return p.at(x=m % 4, y=(m // 4) * 2 + p.yl, z=p.x, c=p.yh)


def same(p, to):
    return (to[0] == p.g) & (to[1] == p.s)


def greet_plane(p, partners, slab_to, slab_from, own_slab):
    barrier = pltpu.get_barrier_semaphore()
    for to in partners:
        pl.semaphore_signal(barrier, inc=1, device_id=to, device_id_type=MESH)

    @pl.when(jnp.logical_not(own_slab))
    def _():
        pl.semaphore_signal(barrier, inc=1, device_id=slab_to, device_id_type=MESH)
        pl.semaphore_signal(barrier, inc=1, device_id=slab_from, device_id_type=MESH)
        pl.semaphore_wait(barrier, len(partners) + 2)

    @pl.when(own_slab)
    def _():
        pl.semaphore_wait(barrier, len(partners))


def slab_copy(src, dst, ssem, rsem, i, to):
    return pltpu.make_async_remote_copy(
        src_ref=src,
        dst_ref=dst,
        send_sem=ssem.at[i],
        recv_sem=rsem.at[i],
        device_id=to,
        device_id_type=MESH,
    )


def add_blocks(dst, own, recv, chunk):
    lead, rows = dst.shape[:-2], dst.shape[-2]
    count = 1
    for n in lead:
        count *= n

    @pl.loop(0, count)
    def _(i):
        at = []
        rest = i
        for n in reversed(lead):
            at.insert(0, rest % n)
            rest = rest // n

        @pl.loop(0, rows, step=chunk)
        def _(t):
            here = (*at, pl.ds(pl.multiple_of(t, chunk), chunk))
            total = own[here].astype(F32)
            for j in range(3):
                total = total + recv[(j, *here)].astype(F32)
            dst[here] = total.astype(dst.dtype)


def staged_reduce(p, k, src, stages, scr, chunk):
    own = scr[0]
    cur = src
    for n, (axis, pick) in enumerate(stages):
        recv = scr[1] if n == 0 else scr[2 * n]
        if n == 0:
            mine = k.local(pick(src, p.pos(axis, 0)), own)
        ring = [k.send(pick(cur, p.pos(axis, j)), recv.at[j - 1], p.step(axis, j)) for j in (1, 2, 3)]
        yield
        if n == 0:
            mine.wait()
        for copy in ring:
            copy.wait_recv()
        total = own if n == 0 else scr[2 * n + 1]
        add_blocks(total, own if n == 0 else pick(cur, p.pos(axis, 0)), recv, chunk)
        cur = total


def staged_scratch(shapes):
    out = [pltpu.VMEM(shapes[0], BF16), pltpu.VMEM((3, *shapes[0]), BF16)]
    for n, shape in enumerate(shapes[1:]):
        out.append(pltpu.VMEM((3, *shape), BF16))
        out.append(pltpu.VMEM(shape, F32 if n == len(shapes) - 2 else BF16))
    return out


EVERY = slice(None)


def wg_stages(half):
    cols = pl.ds(half * FS, FS)
    if half == 0:
        return [
            ("y", lambda r, i: r.at[i // 2, :, i % 2, :, cols]),
            ("x", lambda r, i: r.at[i]),
        ]
    return [
        ("x", lambda r, i: r.at[:, i, :, :, cols]),
        ("y", lambda r, i: r.at[i // 2, i % 2]),
    ]


def wd_stages(half):
    cols = pl.ds(half * 512, 512)
    if half == 0:
        return [
            ("y", lambda r, i: r.at[i % 2, :, i // 2, :, cols]),
            ("x", lambda r, i: r.at[i]),
        ]
    return [
        ("x", lambda r, i: r.at[:, i, :, :, cols]),
        ("y", lambda r, i: r.at[i % 2, i // 2]),
    ]


def q_stages(part):
    cols = pl.ds((0, 384, 768)[part], (384, 384, 256)[part])
    if part == 0:
        return [
            ("x", lambda r, i: r.at[:, i, :, :, :, cols]),
            ("z", lambda r, i: r.at[:, :, i]),
            ("y", lambda r, i: r.at[i // 2, i % 2]),
        ]
    if part == 1:
        return [
            ("y", lambda r, i: r.at[i // 2, :, i % 2, :, :, cols]),
            ("x", lambda r, i: r.at[i]),
            ("z", lambda r, i: r.at[i]),
        ]
    return [
        ("z", lambda r, i: r.at[:, :, :, i, :, cols]),
        ("y", lambda r, i: r.at[i // 2, :, i % 2]),
        ("x", lambda r, i: r.at[i]),
    ]


def o_stages():
    return [
        ("z", lambda r, i: r.at[:, :, :, i]),
        ("y", lambda r, i: r.at[i // 2, :, i % 2]),
        ("x", lambda r, i: r.at[i]),
    ]


PLANE_SHAPES = [
    [(4, 128, FS), (128, FS)],
    [(2, 2, 128, FS), (128, FS)],
    [(4, 80, 512), (80, 512)],
    [(2, 2, 80, 512), (80, 512)],
]
O_SHAPES = [(2, 4, 2, 32, 640), (4, 32, 640), (32, 640)]
Q_SHAPES = [
    [(2, 2, 4, 32, 384), (2, 2, 32, 384), (32, 384)],
    [(4, 4, 32, 384), (4, 32, 384), (32, 384)],
    [(2, 4, 2, 32, 256), (4, 32, 256), (32, 256)],
]


def small_reduce(p, k, part, vec, recv):
    mine = k.local(part, vec.at[0])
    mine.wait()
    for n, axis in enumerate("xyzc"):
        steps = (1,) if axis == "c" else (1, 2, 3)
        ring = [k.send(vec.at[n], recv.at[n, j - 1], p.step(axis, j)) for j in steps]
        yield
        for copy in ring:
            copy.wait_recv()
        total = vec[n]
        for j in range(len(steps)):
            total = total + recv[n, j]
        vec[n + 1] = total


def swap(a, b):
    left = lax.broadcasted_iota(jnp.int32, a.shape, 1) < ROWS
    return jnp.where(left, a, pltpu.roll(b, ROWS, 1)), jnp.where(left, pltpu.roll(a, ROWS, 1), b)


def head_scale(v):
    return lax.rsqrt(jnp.mean(v * v, axis=-2, keepdims=True) + EPS)


def half_turn(v):
    half = HEAD // 2
    return jnp.concatenate([-v[..., half:, :], v[..., :half, :]], axis=-2)


def half_back(v):
    half = HEAD // 2
    return jnp.concatenate([v[..., half:, :], -v[..., :half, :]], axis=-2)


def low(v):
    return v.astype(BF16).astype(F32)


def query_units(packed_t, g, cos, sin, gain):
    raw = packed_t[pl.ds(pl.multiple_of(g * 256, 256), 256)].reshape(GROUP, HEAD, TOK)
    head = raw * head_scale(raw) * gain
    turned = low(head * cos + half_turn(head) * sin) * (HEAD ** -0.5)
    a0, a1 = swap(turned[0], turned[1])
    b0, b1 = swap(turned[2], turned[3])
    none = jnp.zeros((HEAD, 256), F32)
    return [
        jnp.concatenate([jnp.concatenate([a, b], axis=1), none], axis=0) for a, b in ((a0, b0), (a1, b1))
    ]


def fill_bias(bias, segc, segq, start):
    @pl.loop(0, SEQ, step=128)
    def _(t):
        at = pl.ds(pl.multiple_of(t, 128), 128)
        key = lax.broadcasted_iota(jnp.int32, (128, 256), 0) + t
        query = lax.broadcasted_iota(jnp.int32, (128, 256), 1) % ROWS + start
        for m in range(MICRO):
            ok = (key <= query) & (segc[at, m : m + 1] == segq[m : m + 1, :])
            ok = ok | (key == query)
            bias[m, at] = jnp.where(ok, 3e38, -1e30)


def unit_kv(KV, m, g):
    cols = pl.ds(pl.multiple_of(g * 128, 128), 128)
    return KV[m, :, :, :, :, cols].reshape(SEQ, 128)


def front_body(*refs):
    (x_ref, wq, wo, wg, wd, og, segc, segq, cos_ref, sin_ref, qgain, kgain) = refs[:12]
    (WQ, WO, WG, WD, OG, KV, pt_out, lse_out, att_out, resid_out, normed_out, gains_out, n2_out) = refs[12:25]
    (wqs, wos, kvl, kvs, bias, qts, ots, ssem, rsem) = refs[25:]
    p = Place()
    k = Links(ssem, rsem)
    yh, x, yl, z, c = p.yh, p.x, p.yl, p.z, p.c
    m = z * 2 + c
    yl_partner = p.at(y=p.yh * 2 + 1 - yl)
    partners = [p.step(a, j) for a in "xyz" for j in (1, 2, 3)]
    partners += [p.at(z=(z + j) % 4, c=1 - c) for j in range(4)]
    slab_to, slab_from = slab_target(p), slab_source(p)
    own_slab = same(p, slab_to)
    greet_plane(p, partners, slab_to, slab_from, own_slab)

    def wq_a(*at):
        return wqs.at[(*at, EVERY, pl.ds(0, 1024))]

    def wq_b(*at):
        return wqs.at[(*at, EVERY, pl.ds(1024, 1024))]

    def wo_(*at):
        return wos.at[(*at, EVERY, EVERY)]

    own_wq = k.local(wq, wqs.at[yh, x, yl, z, c])
    own_wo = k.local(wo, wos.at[yh, x, yl, z, c])
    q1, o1 = [], []
    for j in (1, 2, 3):
        q1.append(k.send(wq.at[:, pl.ds(0, 1024)], wq_a(yh, x, yl, z, c), p.step("y", j)))
        q1.append(k.send(wq.at[:, pl.ds(1024, 1024)], wq_b(yh, x, yl, z, c), p.step("z", j)))
    for j in (1, 2, 3):
        o1.append(k.send(wo, wo_(yh, x, yl, z, c), p.step("x", j)))
    pieces, own_pieces = [], []
    for dz in range(4):
        for dc in range(2):
            zz, cc = (z + dz) % 4, (c + dc) % 2
            mm = zz * 2 + cc
            for half in range(2):
                src = wg.at[:, pl.ds(pl.multiple_of(half * FF + mm * FS, 128), FS)]
                dst = WG.at[yh, x, yl, m, :, pl.ds(half * FS, FS)]
                if dz == 0 and dc == 0:
                    own_pieces.append(k.local(src, dst))
                else:
                    pieces.append(k.send(src, dst, p.at(z=zz, c=cc)))
    slab_dst = WD.at[yl, z, c]
    i = k.used
    k.used += 1
    slab = slab_copy(wd, slab_dst, ssem, rsem, i, slab_to)

    @pl.when(own_slab)
    def _():
        pltpu.make_async_copy(wd, slab_dst, rsem.at[i]).start()

    @pl.when(jnp.logical_not(own_slab))
    def _():
        slab.start()

    fill_bias(bias, segc, segq, p.s * ROWS)

    own_wq.wait()
    own_wo.wait()
    for copy in q1:
        copy.wait_recv()
    q2 = []
    for j in (1, 2, 3):
        src = wq_a(EVERY, x, EVERY, z, c)
        q2.append(k.send(src, src, p.step("z", j)))
        src = wq_b(yh, x, yl, EVERY, c)
        q2.append(k.send(src, src, p.step("x", j)))
    for copy in o1:
        copy.wait_recv()
    o2 = []
    for j in (1, 2, 3):
        src = wo_(yh, EVERY, yl, z, c)
        o2.append(k.send(src, src, p.step("y", j)))
    for copy in q2:
        copy.wait_recv()
    q3 = []
    for j in (1, 2, 3):
        src = wq_a(EVERY, x, EVERY, EVERY, c)
        q3.append((k.send(src, src, p.step("x", j)), wq_a(EVERY, p.pos("x", -j), EVERY, EVERY, c)))
        src = wq_b(yh, EVERY, yl, EVERY, c)
        yy = p.pos("y", -j)
        q3.append((k.send(src, src, p.step("y", j)), wq_b(yy // 2, EVERY, yy % 2, EVERY, c)))
    qc = []
    for src in (wq_a(EVERY, x, EVERY, EVERY, c), wq_b(yh, EVERY, yl, EVERY, c)):
        qc.append(k.send(src, src, p.step("c", 1)))
    for copy in o2:
        copy.wait_recv()
    o3 = []
    for j in (1, 2, 3):
        src = wo_(EVERY, EVERY, EVERY, z, c)
        o3.append((k.send(src, src, p.step("z", j)), wo_(EVERY, EVERY, EVERY, p.pos("z", -j), c)))
    oc = [k.send(wo_(EVERY, EVERY, EVERY, z, c), wo_(EVERY, EVERY, EVERY, z, c), p.step("c", 1))]

    for copy in own_pieces:
        copy.wait()
    for copy in pieces:
        copy.wait_recv()

    @pl.when(own_slab)
    def _():
        pltpu.make_async_copy(wd, slab_dst, rsem.at[i]).wait()

    @pl.when(jnp.logical_not(own_slab))
    def _():
        slab.wait_recv()

    for copy, src in q3:
        copy.wait_recv()
        qc.append(k.send(src, src, p.step("c", 1)))
    lo, hi = pl.ds(0, FS), pl.ds(FS, FS)
    dlo, dhi = pl.ds(0, 512), pl.ds(512, 512)
    plane = []
    for j in (1, 2, 3):
        for src, axis in (
            (WG.at[yh, x, yl, :, :, lo], "x"),
            (WG.at[yh, x, yl, :, :, hi], "y"),
            (WD.at[yl, x, yh, :, dlo], "x"),
            (WD.at[yl, x, yh, :, dhi], "y"),
        ):
            plane.append(k.send(src, src, p.step(axis, j)))
    for copy in qc:
        copy.wait_recv()
    keep_wq = k.local(wqs, WQ)

    pick = jnp.where(
        lax.broadcasted_iota(jnp.int32, (8, 128), 0) == lax.broadcasted_iota(jnp.int32, (8, 128), 1), 1.0, 0.0
    ).astype(BF16)
    gain_cols = wqs[:, :, :, :, :, :, pl.ds(QKV, 128)].reshape(D, 128)
    gains_out[...] = dot_last(pick, gain_cols)
    hidden = x_ref[...].astype(F32)
    normed = (hidden * rms_scale(hidden) * gains_out[0:1, :]).astype(BF16)
    normed_out[...] = normed

    @pl.loop(0, 8)
    def _(t):
        cols = pl.ds(pl.multiple_of(t * 256, 256), 256)
        w = wqs[:, :, :, :, :, :, cols].reshape(D, 256)
        pt_out[cols] = dot(normed_out[...], w).T

    cos, sin = cos_ref[...], sin_ref[...]

    @pl.loop(0, KV_HEADS)
    def _(g):
        raw = pt_out[pl.ds(pl.multiple_of(QD + g * HEAD, HEAD), HEAD)]
        head = raw * head_scale(raw) * kgain[...]
        key = head * cos + half_turn(head) * sin
        value = pt_out[pl.ds(pl.multiple_of(QD + KD + g * HEAD, HEAD), HEAD)]
        both = jnp.concatenate([key, value], axis=0).T.astype(BF16)
        cols = pl.ds(pl.multiple_of(g * 128, 128), 128)
        for mm in range(MICRO):
            kvl[mm, :, cols] = both[mm * ROWS : (mm + 1) * ROWS]

    own_kv = k.local(kvl, kvs.at[:, yl, z, c])
    across = k.send(kvl, kvs.at[:, yl, z, c], yl_partner)
    ring = [k.send(kvl, kvs.at[:, yl, z, c], p.step("z", j)) for j in (1, 2, 3)]

    @pl.loop(0, KV_HEADS)
    def _(g):
        for mm, unit in enumerate(query_units(pt_out, g, cos, sin, qgain[...])):
            qts[g, mm] = unit.astype(BF16)

    for copy in plane:
        copy.wait_recv()
    across.wait_recv()
    src = kvs.at[:, 1 - yl, z, c]
    ring += [k.send(src, src, p.step("z", j)) for j in (1, 2, 3)]
    plane2 = []
    for j in (1, 2, 3):
        for src, axis in (
            (WG.at[yh, :, yl, :, :, lo], "y"),
            (WG.at[:, x, :, :, :, hi], "x"),
            (WD.at[yl, :, yh, :, dlo], "y"),
            (WD.at[:, x, :, :, dhi], "x"),
        ):
            plane2.append(k.send(src, src, p.step(axis, j)))
    own_kv.wait()
    for copy in ring:
        copy.wait_recv()
    src = kvs.at[:, :, :, c]
    kvc = k.send(src, src, p.step("c", 1))
    for copy, src in o3:
        copy.wait_recv()
        oc.append(k.send(src, src, p.step("c", 1)))
    own_og = k.local(og, OG.at[z, c])
    rows = [k.send(og, OG.at[z, c], p.step("z", j)) for j in (1, 2, 3)]
    last = [k.send(og, OG.at[z, c], p.step("c", 1))]
    kvc.wait_recv()
    keep_kv = k.local(kvs, KV)

    @pl.loop(0, 2 * KV_HEADS)
    def _(u):
        g, mm = u // 2, u % 2
        kv = unit_kv(kvs, mm, g)
        score = jnp.minimum(dot(kv, qts[g, mm]), bias[mm])
        peak = jnp.max(score, axis=0, keepdims=True)
        raised = jnp.exp(score - peak)
        total = jnp.sum(raised, axis=0, keepdims=True)
        probs = (raised * (1.0 / total)).astype(BF16)
        ots[g, mm] = dot_rows(kv, probs)[HEAD:]
        lse_out[u] = jnp.broadcast_to(peak + jnp.log(total), (8, 256))

    for g in range(KV_HEADS):
        for t in range(2):
            cols = slice(t * 128, (t + 1) * 128)
            a, b = swap(ots[g, 0, :, cols], ots[g, 1, :, cols])
            at = (g * GROUP + 2 * t) * HEAD
            att_out[:, at : at + 128] = jnp.concatenate([a, b], axis=0).T.astype(BF16)

    for copy in oc:
        copy.wait_recv()
    keep_wo = k.local(wos, WO)

    @pl.loop(0, 8)
    def _(t):
        w = wos[t // 4, t % 4].reshape(256, QD)
        cols = pl.ds(pl.multiple_of(t * 256, 256), 256)
        resid_out[:, cols] = x_ref[:, cols].astype(F32) + dot_last(att_out[...], w)

    resid = resid_out[...]
    n2_out[...] = (resid * rms_scale(resid) * gains_out[1:2, :]).astype(BF16)
    for j, copy in zip((1, 2, 3), rows):
        copy.wait_recv()
        src = OG.at[p.pos("z", -j), c]
        last.append(k.send(src, src, p.step("c", 1)))
    for copy in plane2 + last:
        copy.wait_recv()
    for copy in (keep_wq, keep_kv, keep_wo, own_og):
        copy.wait()
    k.drain()

    @pl.when(jnp.logical_not(own_slab))
    def _():
        slab.wait_send()


VMEM = pl.BlockSpec(memory_space=pltpu.VMEM)


def front(x, wq, wo, wg, wd, og, segc, segq, cos, sin, qgain, kgain):
    hbm = [
        sds((2, 4, 2, 4, 2, 16, 2048), BF16),
        sds((2, 4, 2, 4, 2, 16, QD), BF16),
        sds((2, 4, 2, 8, 16, 2 * FS), BF16),
        sds((2, 4, 2, 80, 1024), BF16),
        sds((4, 2, TOK, D), BF16),
        sds((2, 2, 4, 2, ROWS, 2 * KD), BF16),
    ]
    vmem = [
        sds((2048, TOK), F32),
        sds((2 * KV_HEADS, 8, 256), F32),
        sds((TOK, QD), BF16),
        sds((TOK, D), F32),
        sds((TOK, D), BF16),
        sds((8, D), F32),
        sds((TOK, D), BF16),
    ]
    scratch = [
        pltpu.VMEM((2, 4, 2, 4, 2, 16, 2048), BF16),
        pltpu.VMEM((2, 4, 2, 4, 2, 16, QD), BF16),
        pltpu.VMEM((2, ROWS, 2 * KD), BF16),
        pltpu.VMEM((2, 2, 4, 2, ROWS, 2 * KD), BF16),
        pltpu.VMEM((2, SEQ, 256), F32),
        pltpu.VMEM((KV_HEADS, 2, 128, 256), BF16),
        pltpu.VMEM((KV_HEADS, 2, HEAD, 256), F32),
        pltpu.SemaphoreType.DMA((120,)),
        pltpu.SemaphoreType.DMA((120,)),
    ]
    return pl.pallas_call(
        front_body,
        out_shape=hbm + vmem,
        in_specs=[VMEM] + [ANY] * 5 + [VMEM] * 6,
        out_specs=[ANY] * len(hbm) + [VMEM] * len(vmem),
        scratch_shapes=scratch,
        name="front",
        compiler_params=pltpu.CompilerParams(
            collective_id=0, has_side_effects=True, vmem_limit_bytes=56 << 20
        ),
    )(x, wq, wo, wg, wd, og, segc, segq, cos, sin, qgain, kgain)


def ffn_body(n2, OG, WG, WD, d_out, mix_out, dwg_out, dwd_out, *scr):
    (rows, ogs, wgs, wd80, wds, dgu, inn, din, part, mixs, r0, s0, r1, dwg, dwd32, dwd, ssem, rsem, lsem) = scr
    p = Place()
    z, c = p.z, p.c
    sib = p.step("c", 1)
    greet([p.step("z", j) for j in (1, 2, 3)] + [sib])

    def remote(src, dst, i, to):
        return pltpu.make_async_remote_copy(
            src_ref=src,
            dst_ref=dst,
            send_sem=ssem.at[i],
            recv_sem=rsem.at[i],
            device_id=to,
            device_id_type=MESH,
        )

    def local(src, dst, i):
        copy = pltpu.make_async_copy(src, dst, lsem.at[i])
        copy.start()
        return copy

    sent = []
    for j in (1, 2, 3):
        copy = remote(n2, rows.at[z, c], j, p.step("z", j))
        copy.start()
        sent.append(copy)
    remote(n2, rows.at[z, c], 4, sib).start()
    own = local(n2, rows.at[z, c], 0)
    get_wd = local(WD, wd80, 1)
    get_wg = local(WG, wgs, 2)
    get_og = local(OG, ogs, 3)
    get_wd.wait()

    @pl.loop(0, 8)
    def _(i):
        yl, x = i // 4, i % 4
        a, b = wd80[yl, x, 0].astype(F32), wd80[yl, x, 1].astype(F32)
        at = pl.ds(pl.multiple_of(i * 80, 80), 80)
        wds[at, :1024] = jnp.concatenate([a[:40], b[:40]], axis=0).astype(BF16)
        wds[at, 1024:] = jnp.concatenate([a[40:], b[40:]], axis=0).astype(BF16)

    own.wait()
    get_wg.wait()
    get_og.wait()

    @pl.loop(0, 4)
    def _(j):
        o = jnp.where(j == 2, 3, jnp.where(j == 3, 2, j))
        zz = (z + o) % 4
        at = pl.ds(pl.multiple_of(zz * 256, 256), 256)

        @pl.when(o > 0)
        def _():
            remote(n2, rows.at[zz, c], (4 - o) % 4, sib).wait_recv()
            remote(rows.at[zz, c], rows.at[zz, c], 4 + o, sib).start()

        remote(rows.at[zz, c], rows.at[zz, 1 - c], 4 + o, sib).wait_recv()
        r = rows[zz].reshape(256, D)
        din[...] = dot_last(ogs[zz].reshape(256, D), wds[...])
        for t in range(5):
            lo, hi = slice(t * 128, (t + 1) * 128), slice(FS + t * 128, FS + (t + 1) * 128)
            w = jnp.concatenate(
                [wgs[:, :, :, :, :, lo].reshape(D, 128), wgs[:, :, :, :, :, hi].reshape(D, 128)], axis=1
            )
            both = dot(r, w)
            gate, upper = both[:, :128], both[:, 128:]
            sig = jax.nn.sigmoid(gate)
            active = gate * sig
            d_inner = din[:, lo]
            inn[at, lo] = (active * upper).astype(BF16)
            dgu[at, lo] = (d_inner * upper * sig * (1.0 + gate * (1.0 - sig))).astype(BF16)
            dgu[at, hi] = (d_inner * active).astype(BF16)

        @pl.loop(0, 8)
        def _(t):
            w = wgs[t // 4, t % 4].reshape(256, 2 * FS)
            cols = pl.ds(pl.multiple_of(t * 256, 256), 256)
            part[zz, :, :, cols] = dot_last(dgu[at], w).astype(BF16).reshape(2, TOK, 256)

        remote(part.at[zz, 1 - c], r0.at[zz], 8 + o, sib).start()

        @pl.loop(0, 4)
        def _(t):
            cols = pl.ds(pl.multiple_of(t * 512, 512), 512)
            mixs[zz, :, :, cols] = dot(inn[at], wds[:, cols]).astype(BF16).reshape(2, TOK, 512)

        remote(part.at[zz, 1 - c], r0.at[zz], 8 + o, sib).wait_recv()

        @pl.loop(0, TOK, step=16)
        def _(t):
            here = pl.ds(pl.multiple_of(t, 16), 16)
            s0[zz, here] = (part[zz, c, here].astype(F32) + r0[zz, here].astype(F32)).astype(BF16)

        @pl.when(o > 0)
        def _():
            remote(s0.at[zz], r1.at[o - 1], 12 + o, p.at(z=zz)).start()

    out_mix = local(mixs, mix_out, 4)

    @pl.loop(0, 8)
    def _(t):
        cols = pl.ds(pl.multiple_of(t * 256, 256), 256)
        left = rows[:, :, :, cols].reshape(8 * TOK, 256)
        dwg[t // 4, t % 4] = dot_rows(left, dgu[...]).astype(BF16).reshape(2, TOK, 2 * FS)

    out_wg = local(dwg, dwg_out, 5)

    @pl.loop(0, 5)
    def _(t):
        units = pl.ds(pl.multiple_of(t * 128, 128), 128)
        dwd32[units] = dot_rows(inn[:, units], ogs[...].reshape(8 * TOK, D))

    @pl.loop(0, 8)
    def _(i):
        yl, x = i // 4, i % 4
        at = pl.ds(pl.multiple_of(i * 80, 80), 80)
        lo, hi = dwd32[at, :1024], dwd32[at, 1024:]
        dwd[yl, x, 0] = jnp.concatenate([lo[:40], hi[:40]], axis=0).astype(BF16)
        dwd[yl, x, 1] = jnp.concatenate([lo[40:], hi[40:]], axis=0).astype(BF16)

    out_wd = local(dwd, dwd_out, 6)
    for o in (1, 2, 3):
        remote(s0.at[0], r1.at[o - 1], 12 + o, sib).wait_recv()

    @pl.loop(0, TOK, step=16)
    def _(t):
        here = pl.ds(pl.multiple_of(t, 16), 16)
        total = s0[z, here].astype(F32)
        for j in range(3):
            total = total + r1[j, here].astype(F32)
        d_out[here] = total

    for copy in sent:
        copy.wait_send()
    for o in range(4):
        remote(rows.at[0, 0], rows.at[0, 0], 4 + o, sib).wait_send()
        remote(part.at[0, 0], r0.at[0], 8 + o, sib).wait_send()
    for o in (1, 2, 3):
        remote(s0.at[0], r1.at[o - 1], 12 + o, sib).wait_send()
    for copy in (out_mix, out_wg, out_wd):
        copy.wait()


def ffn(n2, OG, WG, WD):
    outs = [
        sds((TOK, D), F32),
        sds((4, 2, TOK, D), BF16),
        sds((2, 4, 2, TOK, 2 * FS), BF16),
        sds((2, 4, 2, 80, 1024), BF16),
    ]
    scratch = [
        pltpu.VMEM((4, 2, TOK, D), BF16),
        pltpu.VMEM((4, 2, TOK, D), BF16),
        pltpu.VMEM((2, 4, 2, 8, 16, 2 * FS), BF16),
        pltpu.VMEM((2, 4, 2, 80, 1024), BF16),
        pltpu.VMEM((FS, D), BF16),
        pltpu.VMEM((8 * TOK, 2 * FS), BF16),
        pltpu.VMEM((8 * TOK, FS), BF16),
        pltpu.VMEM((256, FS), F32),
        pltpu.VMEM((4, 2, TOK, D), BF16),
        pltpu.VMEM((4, 2, TOK, D), BF16),
        pltpu.VMEM((4, TOK, D), BF16),
        pltpu.VMEM((4, TOK, D), BF16),
        pltpu.VMEM((3, TOK, D), BF16),
        pltpu.VMEM((2, 4, 2, TOK, 2 * FS), BF16),
        pltpu.VMEM((FS, D), F32),
        pltpu.VMEM((2, 4, 2, 80, 1024), BF16),
        pltpu.SemaphoreType.DMA((16,)),
        pltpu.SemaphoreType.DMA((16,)),
        pltpu.SemaphoreType.DMA((7,)),
    ]
    return pl.pallas_call(
        ffn_body,
        out_shape=outs,
        in_specs=[VMEM] + [ANY] * 3,
        out_specs=[VMEM] + [ANY] * 3,
        scratch_shapes=scratch,
        name="ffn",
        compiler_params=pltpu.CompilerParams(
            collective_id=1, has_side_effects=True, vmem_limit_bytes=60 << 20
        ),
    )(n2, OG, WG, WD)


def back_body(*refs):
    (dn_ref, x_ref, og_ref, resid_ref, gains, att_ref, pt, lse, segc, segq, cos_ref, sin_ref, qgain, kgain) = refs[:14]
    (WQ, WO, KV, mix_part, dwg, dwd) = refs[14:20]
    (in_grad, dp_out, rows_out, heads_out, mixed_out, GWG, GWD, GO) = refs[20:28]
    (wos, kvs, bias, qts, qns, dts, dns, dqt, dpt, datt, dres, kpart) = refs[28:40]
    (k0, k1, ks1, k2, kres, wq2, low2, att2, do) = refs[40:49]
    scr = list(refs[49:])
    parts = []
    for shapes in PLANE_SHAPES + [O_SHAPES]:
        n = 2 * len(shapes)
        parts.append(scr[:n])
        scr = scr[n:]
    mix, (ssem, rsem) = scr[:3], scr[3:]
    p = Place()
    k = Links(ssem, rsem)
    yl, z, c = p.yl, p.z, p.c
    m = z * 2 + c
    sib = p.step("c", 1)
    yl_partner = p.at(y=p.yh * 2 + 1 - yl)
    partners = [p.step(a, j) for a in "xyz" for j in (1, 2, 3)]
    partners += [p.at(z=(z + j) % 4, c=1 - c) for j in range(4)]
    slab_to, slab_from = slab_target(p), slab_source(p)
    own_slab = same(p, slab_to)
    greet_plane(p, partners, slab_to, slab_from, own_slab)
    get_wo = k.local(WO, wos)
    get_kv = k.local(KV, kvs)
    plane = [
        staged_reduce(p, k, dwg, wg_stages(0), parts[0], 16),
        staged_reduce(p, k, dwg, wg_stages(1), parts[1], 16),
        staged_reduce(p, k, dwd, wd_stages(0), parts[2], 16),
        staged_reduce(p, k, dwd, wd_stages(1), parts[3], 16),
    ]
    for step in plane:
        next(step)
    mixing = mix_reduce(p, k, mix_part, mix, resid_ref, mixed_out)
    next(mixing)
    own_att = k.local(att_ref, att2.at[0])
    pair_att = k.send(att_ref, att2.at[1], sib)
    fill_bias(bias, segc, segq, p.s * ROWS)
    next(mixing)
    cos, sin = cos_ref[...], sin_ref[...]

    @pl.loop(0, KV_HEADS)
    def _(g):
        for mm, unit in enumerate(query_units(pt, g, cos, sin, qgain[...])):
            qts[g, mm] = unit.astype(BF16)
            qns[g, mm] = unit.T.astype(BF16)

    resid = resid_ref[...]
    scale_two = rms_scale(resid)
    norm_two = resid * scale_two
    d_normed = dn_ref[...]
    rows_out[1:2, :] = jnp.sum(d_normed * norm_two, axis=0, keepdims=True)
    d_resid = og_ref[...].astype(F32) + norm_back(d_normed, norm_two, scale_two, gains[1:2, :])
    dres[...] = d_resid
    low2[0] = d_resid.astype(BF16)
    pair_low = k.send(low2.at[0], low2.at[1], sib)
    get_wo.wait()

    @pl.loop(0, 5)
    def _(t):
        cols = pl.ds(pl.multiple_of(t * 256, 256), 256)
        w = wos[:, :, :, :, :, :, cols].reshape(D, 256)
        datt[:, cols] = low(dot(low2[0], w))

    for g in range(KV_HEADS):
        tiles = []
        for t in range(2):
            at = (g * GROUP + 2 * t) * HEAD
            both = datt[:, at : at + 128].T
            tiles.append(swap(both[:HEAD], both[HEAD:]))
        for mm in range(MICRO):
            none = jnp.zeros((HEAD, 256), F32)
            unit = jnp.concatenate([none, jnp.concatenate([tiles[0][mm], tiles[1][mm]], axis=1)], axis=0)
            dts[g, mm] = unit.astype(BF16)
            dns[g, mm] = unit.T.astype(BF16)
    get_kv.wait()

    @pl.loop(0, 2 * KV_HEADS)
    def _(u):
        g, mm = u // 2, u % 2
        kv = unit_kv(kvs, mm, g)
        score = jnp.minimum(dot(kv, qts[g, mm]), bias[mm])
        again = jnp.exp(score - lse[u, 0:1, :])
        d_probs = dot(kv, dts[g, mm])
        inner = jnp.sum(again * d_probs, axis=0, keepdims=True)
        d_scores = (again * (d_probs - inner)).astype(BF16)
        d_kv = dot(d_scores, qns[g, mm]) + dot(again.astype(BF16), dns[g, mm])
        cols = pl.ds(pl.multiple_of(g * 128, 128), 128)
        kpart[mm, :, :, :, :, cols] = d_kv.astype(BF16).reshape(2, 4, 2, ROWS, 128)
        dqt[g, mm] = dot_rows(kv, d_scores)[:HEAD] * (HEAD ** -0.5)

    core = k.send(kpart.at[:, :, :, 1 - c], k0, p.step("c", 1))
    core.wait_recv()

    @pl.loop(0, 4)
    def _(zz):
        for a in range(2):
            for b in range(2):
                k0[a, b, zz] = (kpart[a, b, zz, c].astype(F32) + k0[a, b, zz].astype(F32)).astype(BF16)

    ring = [k.send(k0.at[:, :, p.pos("z", j)], k1.at[j - 1], p.step("z", j)) for j in (1, 2, 3)]

    own_att.wait()
    pair_att.wait_recv()
    pair_low.wait_recv()
    att_cols = pl.ds(pl.multiple_of(c * 640, 128), 640)

    @pl.loop(0, 8)
    def _(t):
        cols = pl.ds(pl.multiple_of(t * 256, 256), 256)
        left = low2[:, :, cols].reshape(2 * TOK, 256)
        right = att2[:, :, att_cols].reshape(2 * TOK, 640)
        do[t // 4, t % 4] = dot_rows(left, right).astype(BF16).reshape(2, 4, 32, 640)

    outward = staged_reduce(p, k, do, o_stages(), parts[4], 16)
    next(outward)

    query_sum = jnp.zeros((HEAD, TOK), F32)
    for g in range(KV_HEADS):
        heads = []
        for t in range(2):
            cols = slice(t * 128, (t + 1) * 128)
            heads += list(swap(dqt[g, 0, :, cols], dqt[g, 1, :, cols]))
        for h in range(GROUP):
            at = (g * GROUP + h) * HEAD
            d_raw, term = head_back(pt[at : at + HEAD], heads[h], cos, sin, qgain[...])
            query_sum = query_sum + term
            dpt[at : at + HEAD] = d_raw
    heads_out[0] = query_sum

    for copy in ring:
        copy.wait_recv()
    for a in range(2):
        for b in range(2):
            total = k0[a, b, z].astype(F32)
            for j in range(3):
                total = total + k1[j, a, b].astype(F32)
            ks1[a, b] = total.astype(BF16)
    across = k.send(ks1.at[:, 1 - yl], k2, yl_partner)
    across.wait_recv()
    for a in range(2):
        kres[pl.ds(a * ROWS, ROWS)] = ks1[a, yl].astype(F32) + k2[a].astype(F32)
    key_sum = jnp.zeros((HEAD, TOK), F32)
    for g in range(KV_HEADS):
        both = kres[:, g * 128 : (g + 1) * 128].T
        at = QD + g * HEAD
        d_raw, term = head_back(pt[at : at + HEAD], both[:HEAD], cos, sin, kgain[...])
        key_sum = key_sum + term
        dpt[at : at + HEAD] = d_raw
        dpt[at + KD : at + KD + HEAD] = both[HEAD:]
    heads_out[1] = key_sum
    get_wq = [k.local(WQ.at[0, 0], wq2.at[0])]
    for t in range(15):
        dp_out[:, t * 128 : (t + 1) * 128] = dpt[t * 128 : (t + 1) * 128].T.astype(BF16)
    for step in plane:
        next(step)
    for t in range(8):
        if t < 7:
            get_wq.append(k.local(WQ.at[(t + 1) // 4, (t + 1) % 4], wq2.at[(t + 1) % 2]))
        get_wq[t].wait()
        w = wq2[t % 2].reshape(256, 2048)[:, :QKV]
        in_grad[:, t * 256 : (t + 1) * 256] = dot_last(dp_out[...], w)
    next(outward)
    hidden = x_ref[...].astype(F32)
    scale_one = rms_scale(hidden)
    norm_one = hidden * scale_one
    d_normed = in_grad[...]
    rows_out[0:1, :] = jnp.sum(d_normed * norm_one, axis=0, keepdims=True)
    in_grad[...] = dres[...] + norm_back(d_normed, norm_one, scale_one, gains[0:1, :])
    next(mixing, None)
    next(outward)
    for step in plane:
        next(step, None)

    last, local = [], []
    for half in range(2):
        total = parts[half][-1]
        cols = pl.ds(pl.multiple_of(half * FF + m * FS, 128), FS)
        for dz in range(4):
            for dc in range(2):
                zz, cc = (z + dz) % 4, (c + dc) % 2
                src = total.at[pl.ds(pl.multiple_of((zz * 2 + cc) * 16, 16), 16)]
                if dz == 0 and dc == 0:
                    local.append(k.local(src, GWG.at[:, cols]))
                else:
                    last.append(k.send(src, GWG.at[:, cols], p.at(z=zz, c=cc)))
    slabs = []
    for half in range(2):
        i = k.used
        k.used += 1
        src, dst = parts[2 + half][-1], GWD.at[:, pl.ds(half * 512, 512)]
        slabs.append((src, dst, i))

        @pl.when(own_slab)
        def _(src=src, dst=dst, i=i):
            pltpu.make_async_copy(src, dst, rsem.at[i]).start()

        @pl.when(jnp.logical_not(own_slab))
        def _(src=src, dst=dst, i=i):
            slab_copy(src, dst, ssem, rsem, i, slab_from).start()

    next(outward, None)
    total = parts[4][-1]
    mine = total.at[pl.ds(pl.multiple_of(c * 16, 16), 16)]
    other = total.at[pl.ds(pl.multiple_of((1 - c) * 16, 16), 16)]
    local.append(k.local(mine, GO.at[c]))
    last.append(k.send(other, GO.at[c], sib))
    for copy in local:
        copy.wait()
    for copy in last:
        copy.wait_recv()
    for src, dst, i in slabs:

        @pl.when(own_slab)
        def _(src=src, dst=dst, i=i):
            pltpu.make_async_copy(src, dst, rsem.at[i]).wait()

        @pl.when(jnp.logical_not(own_slab))
        def _(src=src, dst=dst, i=i):
            slab_copy(src, dst, ssem, rsem, i, slab_from).wait()

    k.drain()


def mix_reduce(p, k, part, scr, resid, out):
    own, r0, r1 = scr
    z, c = p.z, p.c
    core = k.send(part.at[:, 1 - c], r0, p.step("c", 1))
    mine = k.local(part.at[:, c], own)
    yield
    mine.wait()
    core.wait_recv()

    @pl.loop(0, 4)
    def _(zz):
        @pl.loop(0, TOK, step=16)
        def _(t):
            at = pl.ds(pl.multiple_of(t, 16), 16)
            own[zz, at] = (own[zz, at].astype(F32) + r0[zz, at].astype(F32)).astype(BF16)

    ring = [k.send(own.at[p.pos("z", j)], r1.at[j - 1], p.step("z", j)) for j in (1, 2, 3)]
    yield
    for copy in ring:
        copy.wait_recv()

    @pl.loop(0, TOK, step=16)
    def _(t):
        at = pl.ds(pl.multiple_of(t, 16), 16)
        total = own[z, at].astype(F32)
        for j in range(3):
            total = total + r1[j, at].astype(F32)
        out[at] = (resid[at] + total).astype(BF16)


def head_back(raw, grad, cos, sin, gain):
    scale = head_scale(raw)
    normed = raw * scale
    d_head = grad * cos + half_back(grad * sin)
    scaled = d_head * gain
    inner = jnp.mean(scaled * normed, axis=0, keepdims=True)
    return scale * (scaled - normed * inner), d_head * normed


def back(dn, x, og, resid, gains, att, pt, lse, segc, segq, cos, sin, qgain, kgain, WQ, WO, KV, mix, dwg, dwd):
    w = 2 * KD
    vmem = [
        sds((TOK, D), F32),
        sds((TOK, QKV), BF16),
        sds((8, D), F32),
        sds((2, HEAD, TOK), F32),
        sds((TOK, D), BF16),
    ]
    hbm = [sds((16, 2 * FF), F32), sds((80, 1024), F32), sds((2, 16, 640), F32)]
    scratch = [
        pltpu.VMEM((2, 4, 2, 4, 2, 16, QD), BF16),
        pltpu.VMEM((2, 2, 4, 2, ROWS, w), BF16),
        pltpu.VMEM((2, SEQ, 256), F32),
        pltpu.VMEM((KV_HEADS, 2, 128, 256), BF16),
        pltpu.VMEM((KV_HEADS, 2, 256, 128), BF16),
        pltpu.VMEM((KV_HEADS, 2, 128, 256), BF16),
        pltpu.VMEM((KV_HEADS, 2, 256, 128), BF16),
        pltpu.VMEM((KV_HEADS, 2, HEAD, 256), F32),
        pltpu.VMEM((QKV, TOK), F32),
        pltpu.VMEM((TOK, QD), F32),
        pltpu.VMEM((TOK, D), F32),
        pltpu.VMEM((2, 2, 4, 2, ROWS, w), BF16),
        pltpu.VMEM((2, 2, 4, ROWS, w), BF16),
        pltpu.VMEM((3, 2, 2, ROWS, w), BF16),
        pltpu.VMEM((2, 2, ROWS, w), BF16),
        pltpu.VMEM((2, ROWS, w), BF16),
        pltpu.VMEM((TOK, w), F32),
        pltpu.VMEM((2, 2, 4, 2, 16, 2048), BF16),
        pltpu.VMEM((2, TOK, D), BF16),
        pltpu.VMEM((2, TOK, QD), BF16),
        pltpu.VMEM((2, 4, 2, 4, 32, 640), BF16),
    ]
    for shapes in PLANE_SHAPES + [O_SHAPES]:
        scratch += staged_scratch(shapes)
    scratch += [
        pltpu.VMEM((4, TOK, D), BF16),
        pltpu.VMEM((4, TOK, D), BF16),
        pltpu.VMEM((3, TOK, D), BF16),
        pltpu.SemaphoreType.DMA((100,)),
        pltpu.SemaphoreType.DMA((100,)),
    ]
    return pl.pallas_call(
        back_body,
        out_shape=vmem + hbm,
        in_specs=[VMEM] * 14 + [ANY] * 6,
        out_specs=[VMEM] * len(vmem) + [ANY] * len(hbm),
        scratch_shapes=scratch,
        name="back",
        compiler_params=pltpu.CompilerParams(
            collective_id=2, has_side_effects=True, vmem_limit_bytes=60 << 20
        ),
    )(dn, x, og, resid, gains, att, pt, lse, segc, segq, cos, sin, qgain, kgain, WQ, WO, KV, mix, dwg, dwd)


def tail_body(normed, packed, small, GQ, SMALL, *scr):
    normed2, packed2, dq = scr[:3]
    scr = list(scr[3:])
    parts = []
    for shapes in Q_SHAPES:
        n = 2 * len(shapes)
        parts.append(scr[:n])
        scr = scr[n:]
    vec, recv, ssem, rsem = scr
    p = Place()
    k = Links(ssem, rsem)
    c = p.c
    sib = p.step("c", 1)
    greet([p.step(a, j) for a in "xyz" for j in (1, 2, 3)] + [sib])
    pair = [k.send(packed, packed2.at[1], sib), k.send(normed, normed2.at[1], sib)]
    own = [k.local(packed, packed2.at[0]), k.local(normed, normed2.at[0])]
    sums = small_reduce(p, k, small, vec, recv)
    next(sums)
    for copy in own:
        copy.wait()
    for copy in pair:
        copy.wait_recv()
    flows = []
    for part, (start, width) in enumerate(((0, 384), (384, 384), (768, 256))):
        cols = pl.ds(pl.multiple_of(c * 896 + start, 128), width)

        @pl.loop(0, 8)
        def _(t):
            rows = pl.ds(pl.multiple_of(t * 256, 256), 256)
            left = normed2[:, :, rows].reshape(2 * TOK, 256)
            right = packed2[:, :, cols].reshape(2 * TOK, width)
            total = dot_rows(left, right).astype(BF16).reshape(2, 4, 32, width)
            dq[t // 4, t % 4, :, :, :, pl.ds(start, width)] = total

        flow = staged_reduce(p, k, dq, q_stages(part), parts[part], 16)
        next(flow)
        flows.append(flow)
        next(sums, None)
    alive = list(flows)
    while alive:
        alive = [f for f in alive if next(f, alive) is not alive]
        next(sums, None)
    next(sums, None)
    last, local = [], []
    for part, (start, width) in enumerate(((0, 384), (384, 384), (768, 256))):
        total = parts[part][-1]
        dst = GQ.at[c, :, pl.ds(start, width)]
        local.append(k.local(total.at[pl.ds(pl.multiple_of(c * 16, 16), 16)], dst))
        last.append(k.send(total.at[pl.ds(pl.multiple_of((1 - c) * 16, 16), 16)], dst, sib))
    SMALL[...] = vec[4]
    for copy in local:
        copy.wait()
    for copy in last:
        copy.wait_recv()
    k.drain()


def tail(normed, packed, small):
    scratch = [
        pltpu.VMEM((2, TOK, D), BF16),
        pltpu.VMEM((2, TOK, QKV), BF16),
        pltpu.VMEM((2, 4, 2, 4, 32, 1024), BF16),
    ]
    for shapes in Q_SHAPES:
        scratch += staged_scratch(shapes)
    scratch += [
        pltpu.VMEM((5, 40, 128), F32),
        pltpu.VMEM((4, 3, 40, 128), F32),
        pltpu.SemaphoreType.DMA((60,)),
        pltpu.SemaphoreType.DMA((60,)),
    ]
    return pl.pallas_call(
        tail_body,
        out_shape=[sds((2, 16, 1024), F32), sds((40, 128), F32)],
        in_specs=[VMEM] * 3,
        out_specs=[ANY, VMEM],
        scratch_shapes=scratch,
        name="tail",
        compiler_params=pltpu.CompilerParams(
            collective_id=3, has_side_effects=True, vmem_limit_bytes=40 << 20
        ),
    )(normed, packed, small)


def rope_tables(start):
    half = HEAD // 2
    inverse = 10000.0 ** (-jnp.arange(half, dtype=F32) / half)
    positions = (start + jnp.arange(TOK) % ROWS).astype(F32)
    angles = inverse[:, None] * positions[None, :]
    angles = jnp.concatenate([angles, angles], axis=0)
    return jnp.cos(angles), jnp.sin(angles)


def per_device(
    tokens,
    segment_ids,
    w_qkv,
    w_out,
    w_gate_up,
    w_down,
    attn_gain,
    ffn_gain,
    query_gain,
    key_gain,
    out_grad,
):
    s = lax.axis_index("seq")
    g = lax.axis_index("grp")
    c = s % 2
    start = s * ROWS
    qgain = query_gain.astype(F32)[:, None]
    kgain = key_gain.astype(F32)[:, None]
    gains = jnp.stack([attn_gain, ffn_gain], axis=1)
    wq_in = jnp.concatenate([w_qkv, jnp.pad(gains, ((0, 0), (0, 126)))], axis=1)
    og_in = out_grad.reshape(TOK, D)
    x_in = tokens.reshape(TOK, D)
    segc = segment_ids.T
    query_ids = lax.dynamic_slice_in_dim(segment_ids, start, ROWS, axis=1)
    segq = jnp.tile(jnp.where(query_ids >= 0, query_ids, -2), (1, GROUP))
    cos, sin = rope_tables(start)
    wd_in = jnp.concatenate([w_down[:, :1024], w_down[:, 1024:]], axis=0)
    (WQ, WO, WG, WD, OG, KV, pt, lse, attended, resid, normed, gain_rows, n2) = front(
        x_in, wq_in, w_out.T, w_gate_up, wd_in, og_in, segc, segq, cos, sin, qgain, kgain
    )
    d_normed, mix_part, dwg, dwd = ffn(n2, OG, WG, WD)
    input_grad, d_packed, terms, head_terms, result, gwg, gwd, go = back(
        d_normed, x_in, og_in, resid, gain_rows, attended, pt, lse, segc, segq, cos, sin, qgain, kgain,
        WQ, WO, KV, mix_part, dwg, dwd,
    )
    head_sums = jnp.sum(head_terms, axis=2).reshape(1, 128)
    small = jnp.concatenate(
        [terms[:2].reshape(32, 128), jnp.pad(head_sums, ((0, 7), (0, 0)))], axis=0
    )
    gq, sums = tail(normed, d_packed, small)
    w_qkv_grad = jnp.concatenate([gq[0], gq[1][:, 128:]], axis=1)
    w_out_grad = jnp.concatenate([go[0], go[1]], axis=1).T
    at = (g * 16 + s) * 16
    attn_sum = lax.dynamic_slice_in_dim(sums[:16].reshape(D), at, 16)
    ffn_sum = lax.dynamic_slice_in_dim(sums[16:32].reshape(D), at, 16)
    return (
        result.reshape(MICRO, ROWS, D),
        input_grad.reshape(MICRO, ROWS, D),
        w_qkv_grad,
        w_out_grad,
        gwg,
        jnp.concatenate([gwd[:40], gwd[40:]], axis=1),
        attn_sum,
        ffn_sum,
        sums[32, :HEAD],
        sums[32, HEAD:],
    )


def solution(mesh):
    return jax.shard_map(
        per_device,
        mesh=mesh,
        in_specs=(
            P(None, ("grp", "seq"), None),
            P(None, "grp"),
            P(("grp", "seq"), None),
            P(None, ("grp", "seq")),
            P(("grp", "seq"), None),
            P(("grp", "seq"), None),
            P(("grp", "seq")),
            P(("grp", "seq")),
            P(),
            P(),
            P(None, ("grp", "seq"), None),
        ),
        out_specs=(
            P(None, ("grp", "seq"), None),
            P(None, ("grp", "seq"), None),
            P(("grp", "seq"), None),
            P(None, ("grp", "seq")),
            P(("grp", "seq"), None),
            P(("grp", "seq"), None),
            P(("grp", "seq")),
            P(("grp", "seq")),
            P(),
            P(),
        ),
        check_vma=False,
    )
```

```python
import jax
import jax.numpy as jnp
from jax import lax
from jax.experimental import pallas as pl
from jax.experimental.pallas import tpu as pltpu
from jax.sharding import PartitionSpec as P

Q_HEADS = 20
KV_HEADS = 5
GROUP = 4
HEAD = 64
D = 2048
FF = 5120
QD = 1280
KD = 320
QKV = 1920
SEQ = 1024
MICRO = 2
ROWS = 64
TOK = 128
FS = 640
EPS = 1e-06
MESH = pl.DeviceIdType.MESH
F32 = jnp.float32
BF16 = jnp.bfloat16
ANY = pl.BlockSpec(memory_space=pl.ANY)


class Place:
    def __init__(self):
        g = lax.axis_index("grp")
        s = lax.axis_index("seq")
        self.g, self.s = g, s
        self.yh, self.x = g // 4, g % 4
        self.yl, self.z, self.c = s // 8, (s // 2) % 4, s % 2
        self.y = self.yh * 2 + self.yl

    def at(self, x=None, y=None, z=None, c=None):
        x = self.x if x is None else x
        y = self.y if y is None else y
        z = self.z if z is None else z
        c = self.c if c is None else c
        return ((y // 2) * 4 + x, (y % 2) * 8 + z * 2 + c)

    def step(self, axis, k):
        if axis == "x":
            return self.at(x=(self.x + k) % 4)
        if axis == "y":
            return self.at(y=(self.y + k) % 4)
        if axis == "z":
            return self.at(z=(self.z + k) % 4)
        return self.at(c=1 - self.c)

    def pos(self, axis, k):
        return (getattr(self, axis) + k) % 4


class Links:
    def __init__(self, send_sems, recv_sems):
        self.send_sems, self.recv_sems = send_sems, recv_sems
        self.used = 0
        self.sent = []

    def plan(self, src, dst, to):
        i = self.used
        self.used += 1
        copy = pltpu.make_async_remote_copy(
            src_ref=src,
            dst_ref=dst,
            send_sem=self.send_sems.at[i],
            recv_sem=self.recv_sems.at[i],
            device_id=to,
            device_id_type=MESH,
        )
        self.sent.append(copy)
        return copy

    def send(self, src, dst, to):
        copy = self.plan(src, dst, to)
        copy.start()
        return copy

    def local(self, src, dst):
        i = self.used
        self.used += 1
        copy = pltpu.make_async_copy(src, dst, self.recv_sems.at[i])
        copy.start()
        return copy

    def drain(self):
        for copy in self.sent:
            copy.wait_send()


def greet(partners):
    barrier = pltpu.get_barrier_semaphore()
    for to in partners:
        pl.semaphore_signal(barrier, inc=1, device_id=to, device_id_type=MESH)
    pl.semaphore_wait(barrier, len(partners))


def sds(shape, dtype):
    return jax.ShapeDtypeStruct(shape, dtype)


def rms_scale(values):
    return lax.rsqrt(jnp.mean(values * values, axis=-1, keepdims=True) + EPS)


def norm_back(upstream, normed, scale, gain):
    scaled = upstream * gain
    inner = jnp.mean(scaled * normed, axis=-1, keepdims=True)
    return scale * (scaled - normed * inner)


def dot(left, right):
    return jnp.dot(left, right, preferred_element_type=F32)


def dot_last(left, right):
    return lax.dot_general(left, right, (((1,), (1,)), ((), ())), preferred_element_type=F32)


def dot_rows(left, right):
    return lax.dot_general(left, right, (((0,), (0,)), ((), ())), preferred_element_type=F32)


def slab_target(p):
    to = p.at(x=p.z, y=p.c * 2 + p.yl, z=p.g // 2, c=p.g % 2)
    return to


def slab_source(p):
    m = p.z * 2 + p.c
    return p.at(x=m % 4, y=(m // 4) * 2 + p.yl, z=p.x, c=p.yh)


def same(p, to):
    return (to[0] == p.g) & (to[1] == p.s)


def greet_plane(p, partners, slab_to, slab_from, own_slab):
    barrier = pltpu.get_barrier_semaphore()
    for to in partners:
        pl.semaphore_signal(barrier, inc=1, device_id=to, device_id_type=MESH)

    @pl.when(jnp.logical_not(own_slab))
    def _():
        pl.semaphore_signal(barrier, inc=1, device_id=slab_to, device_id_type=MESH)
        pl.semaphore_signal(barrier, inc=1, device_id=slab_from, device_id_type=MESH)
        pl.semaphore_wait(barrier, len(partners) + 2)

    @pl.when(own_slab)
    def _():
        pl.semaphore_wait(barrier, len(partners))


def slab_copy(src, dst, ssem, rsem, i, to):
    return pltpu.make_async_remote_copy(
        src_ref=src,
        dst_ref=dst,
        send_sem=ssem.at[i],
        recv_sem=rsem.at[i],
        device_id=to,
        device_id_type=MESH,
    )


def add_blocks(dst, own, recv, chunk):
    lead, rows = dst.shape[:-2], dst.shape[-2]
    count = 1
    for n in lead:
        count *= n

    @pl.loop(0, count)
    def _(i):
        at = []
        rest = i
        for n in reversed(lead):
            at.insert(0, rest % n)
            rest = rest // n

        @pl.loop(0, rows, step=chunk)
        def _(t):
            here = (*at, pl.ds(pl.multiple_of(t, chunk), chunk))
            total = own[here].astype(F32)
            for j in range(3):
                total = total + recv[(j, *here)].astype(F32)
            dst[here] = total.astype(dst.dtype)


def staged_reduce(p, k, src, stages, scr, chunk):
    own = scr[0]
    cur = src
    for n, (axis, pick) in enumerate(stages):
        recv = scr[1] if n == 0 else scr[2 * n]
        if n == 0:
            mine = k.local(pick(src, p.pos(axis, 0)), own)
        ring = [k.send(pick(cur, p.pos(axis, j)), recv.at[j - 1], p.step(axis, j)) for j in (1, 2, 3)]
        yield
        if n == 0:
            mine.wait()
        for copy in ring:
            copy.wait_recv()
        total = own if n == 0 else scr[2 * n + 1]
        add_blocks(total, own if n == 0 else pick(cur, p.pos(axis, 0)), recv, chunk)
        cur = total


def staged_scratch(shapes):
    out = [pltpu.VMEM(shapes[0], BF16), pltpu.VMEM((3, *shapes[0]), BF16)]
    for n, shape in enumerate(shapes[1:]):
        out.append(pltpu.VMEM((3, *shape), BF16))
        out.append(pltpu.VMEM(shape, BF16))
    return out


EVERY = slice(None)


def wg_stages(half):
    cols = pl.ds(half * FS, FS)
    if half == 0:
        return [
            ("y", lambda r, i: r.at[i // 2, :, i % 2, :, cols]),
            ("x", lambda r, i: r.at[i]),
        ]
    return [
        ("x", lambda r, i: r.at[:, i, :, :, cols]),
        ("y", lambda r, i: r.at[i // 2, i % 2]),
    ]


def wd_stages(half):
    cols = pl.ds(half * 512, 512)
    if half == 0:
        return [
            ("y", lambda r, i: r.at[i % 2, :, i // 2, :, cols]),
            ("x", lambda r, i: r.at[i]),
        ]
    return [
        ("x", lambda r, i: r.at[:, i, :, :, cols]),
        ("y", lambda r, i: r.at[i % 2, i // 2]),
    ]


def q_stages(half):
    cols = pl.ds(half * 128, 128)
    if half == 0:
        return [
            ("y", lambda r, i: r.at[i // 2, :, i % 2, :, cols]),
            ("x", lambda r, i: r.at[i]),
        ]
    return [
        ("x", lambda r, i: r.at[:, i, :, :, cols]),
        ("y", lambda r, i: r.at[i // 2, i % 2]),
    ]


def o_stages(part):
    cols = pl.ds((0, 256, 512)[part], (256, 256, 128)[part])
    if part == 0:
        return [
            ("x", lambda r, i: r.at[:, i, :, :, :, cols]),
            ("z", lambda r, i: r.at[:, :, i]),
            ("y", lambda r, i: r.at[i // 2, i % 2]),
        ]
    if part == 1:
        return [
            ("y", lambda r, i: r.at[i // 2, :, i % 2, :, :, cols]),
            ("x", lambda r, i: r.at[i]),
            ("z", lambda r, i: r.at[i]),
        ]
    return [
        ("z", lambda r, i: r.at[:, :, :, i, :, cols]),
        ("y", lambda r, i: r.at[i // 2, :, i % 2]),
        ("x", lambda r, i: r.at[i]),
    ]


O_PARTS = ((0, 256), (256, 256), (512, 128))
PLANE_SHAPES = [
    [(4, 128, FS), (128, FS)],
    [(2, 2, 128, FS), (128, FS)],
    [(4, 80, 512), (80, 512)],
    [(2, 2, 80, 512), (80, 512)],
    [(4, 128, 128), (128, 128)],
    [(2, 2, 128, 128), (128, 128)],
]
O_SHAPES = [
    [(2, 2, 4, 32, 256), (2, 2, 32, 256), (32, 256)],
    [(4, 4, 32, 256), (4, 32, 256), (32, 256)],
    [(2, 4, 2, 32, 128), (4, 32, 128), (32, 128)],
]


def small_reduce(p, k, vec, recv):
    for n, axis in enumerate("xyzc"):
        steps = (1,) if axis == "c" else (1, 2, 3)
        ring = [k.send(vec.at[n], recv.at[n, j - 1], p.step(axis, j)) for j in steps]
        yield
        for copy in ring:
            copy.wait_recv()
        total = vec[n]
        for j in range(len(steps)):
            total = total + recv[n, j]
        vec[n + 1] = total


def swap(a, b):
    left = lax.broadcasted_iota(jnp.int32, a.shape, 1) < ROWS
    return jnp.where(left, a, pltpu.roll(b, ROWS, 1)), jnp.where(left, pltpu.roll(a, ROWS, 1), b)


def head_scale(v):
    return lax.rsqrt(jnp.mean(v * v, axis=-2, keepdims=True) + EPS)


def half_turn(v):
    half = HEAD // 2
    return jnp.concatenate([-v[..., half:, :], v[..., :half, :]], axis=-2)


def half_back(v):
    half = HEAD // 2
    return jnp.concatenate([v[..., half:, :], -v[..., :half, :]], axis=-2)


def low(v):
    return v.astype(BF16).astype(F32)


def query_units(packed_t, g, cos, sin, gain):
    raw = packed_t[pl.ds(pl.multiple_of(g * 256, 256), 256)].reshape(GROUP, HEAD, TOK)
    head = raw * head_scale(raw) * gain
    turned = low(head * cos + half_turn(head) * sin) * (HEAD ** -0.5)
    a0, a1 = swap(turned[0], turned[1])
    b0, b1 = swap(turned[2], turned[3])
    none = jnp.zeros((HEAD, 256), F32)
    return [
        jnp.concatenate([jnp.concatenate([a, b], axis=1), none], axis=0) for a, b in ((a0, b0), (a1, b1))
    ]


def fill_bias(bias, segc, segq, start):
    @pl.loop(0, SEQ, step=128)
    def _(t):
        at = pl.ds(pl.multiple_of(t, 128), 128)
        key = lax.broadcasted_iota(jnp.int32, (128, 128), 0) + t
        query = lax.broadcasted_iota(jnp.int32, (128, 128), 1) % ROWS + start
        for m in range(MICRO):
            ok = (key <= query) & (segc[at, m : m + 1] == segq[m : m + 1, :])
            ok = ok | (key == query)
            bias[m, at] = jnp.where(ok, 3e38, -1e30)


def unit_bias(bias, m):
    half = bias[m]
    return jnp.concatenate([half, half], axis=1)


def unit_kv(KV, m, g):
    cols = pl.ds(pl.multiple_of(g * 128, 128), 128)
    return KV[m, :, :, :, :, cols].reshape(SEQ, 128)


def front_body(*refs):
    (x_in, wq, wo, wg, wd, og, segc, segq, cos_ref, sin_ref, qgain, kgain) = refs[:12]
    (WO, WG, WD, OG, NA, KV, PT, LSE, ATT, RESID, N2, gains_out) = refs[12:24]
    (xs, na, wqm, wos, pks, pk, pt, lse, att, resid, n2, kvl, kvs, bias, qts, ots, ssem, rsem) = refs[24:]
    p = Place()
    k = Links(ssem, rsem)
    yh, x, yl, z, c = p.yh, p.x, p.yl, p.z, p.c
    m = z * 2 + c
    sib = p.step("c", 1)
    yl_partner = p.at(y=p.yh * 2 + 1 - yl)
    partners = [p.step(a, j) for a in "xyz" for j in (1, 2, 3)]
    partners += [p.at(z=(z + j) % 4, c=1 - c) for j in range(4)]
    slab_to, slab_from = slab_target(p), slab_source(p)
    own_slab = same(p, slab_to)
    greet_plane(p, partners, slab_to, slab_from, own_slab)

    def spread(src_of, dst_of):
        far, near = [], None
        for dz in range(4):
            for dc in range(2):
                zz, cc = (z + dz) % 4, (c + dc) % 2
                src, dst = src_of(zz * 2 + cc), dst_of(m)
                if dz == 0 and dc == 0:
                    near = k.local(src, dst)
                else:
                    far.append(k.send(src, dst, p.at(z=zz, c=cc)))
        return near, far

    q0 = spread(
        lambda i: wq.at[:, pl.ds(pl.multiple_of(i * 256, 256), 256)], lambda i: wqm.at[yh, x, yl, i]
    )
    own_x = k.local(x_in, xs.at[z, c])
    xcore = {0: k.send(x_in, xs.at[z, c], sib)}
    own_wo = k.local(wo, wos.at[yh, x, yl, z, c])

    def wo_at(part, *at):
        return wos.at[(*at, EVERY, pl.ds((0, 512, 1024)[part], (512, 512, 256)[part]))]

    def wo_own(part):
        return wo.at[:, pl.ds((0, 512, 1024)[part], (512, 512, 256)[part])]

    o1 = []
    for j in (1, 2, 3):
        for part, axis in ((0, "z"), (1, "z"), (2, "x")):
            o1.append(k.send(wo_own(part), wo_at(part, yh, x, yl, z, c), p.step(axis, j)))
    g0 = [
        spread(
            lambda i: wg.at[:, pl.ds(pl.multiple_of(half * FF + i * FS, 128), FS)],
            lambda i: WG.at[yh, x, yl, i, :, pl.ds(half * FS, FS)],
        )
        for half in range(2)
    ]
    slab_dst = WD.at[yl, z, c]
    i = k.used
    k.used += 1
    slab = slab_copy(wd, slab_dst, ssem, rsem, i, slab_to)

    @pl.when(own_slab)
    def _():
        pltpu.make_async_copy(wd, slab_dst, rsem.at[i]).start()

    @pl.when(jnp.logical_not(own_slab))
    def _():
        slab.start()

    xring = {j: k.send(x_in, xs.at[z, c], p.step("z", j)) for j in (1, 3, 2)}

    def to_plane(blocks):
        return [k.send(b, b, p.step(axis, j)) for j in (1, 2, 3) for b, axis in blocks]

    ql, qh = pl.ds(0, 128), pl.ds(128, 128)
    lo, hi = pl.ds(0, FS), pl.ds(FS, FS)
    dlo, dhi = pl.ds(0, 512), pl.ds(512, 512)
    q0[0].wait()
    for copy in q0[1]:
        copy.wait_recv()
    q1 = to_plane(((wqm.at[yh, x, yl, :, :, ql], "x"), (wqm.at[yh, x, yl, :, :, qh], "y")))
    fill_bias(bias, segc, segq, p.s * ROWS)
    for copy in q1:
        copy.wait_recv()
    q2 = to_plane(((wqm.at[yh, :, yl, :, :, ql], "y"), (wqm.at[:, x, :, :, :, qh], "x")))
    for near, far in g0:
        near.wait()
        for copy in far:
            copy.wait_recv()

    @pl.when(own_slab)
    def _():
        pltpu.make_async_copy(wd, slab_dst, rsem.at[i]).wait()

    @pl.when(jnp.logical_not(own_slab))
    def _():
        slab.wait_recv()

    plane = to_plane(
        (
            (WG.at[yh, x, yl, :, :, lo], "x"),
            (WG.at[yh, x, yl, :, :, hi], "y"),
            (WD.at[yl, x, yh, :, dlo], "x"),
            (WD.at[yl, x, yh, :, dhi], "y"),
        ),
    )
    for copy in q2:
        copy.wait_recv()
    own_x.wait()
    own_wo.wait()
    pick = jnp.where(
        lax.broadcasted_iota(jnp.int32, (8, 128), 0) + 112 == lax.broadcasted_iota(jnp.int32, (8, 128), 1), 1.0, 0.0
    ).astype(BF16)
    gains_out[...] = dot_last(pick, wqm[:, :, :, :, :, pl.ds(128, 128)].reshape(D, 128))
    packs = []
    plane2 = []
    for o in (0, 1, 3, 2):
        zz = (z + o) % 4
        if o:
            xring[(4 - o) % 4].wait_recv()
            xcore[o] = k.send(xs.at[zz, c], xs.at[zz, c], sib)
        xcore[o].wait_recv()
        rows = xs[zz].reshape(256, D).astype(F32)
        normed = (rows * rms_scale(rows) * gains_out[0:1, :]).astype(BF16)
        na[zz] = normed.reshape(2, TOK, D)
        pks[zz] = dot(normed, wqm[...].reshape(D, 256)).astype(BF16).reshape(2, TOK, 256)
        if o:
            packs.append(k.send(pks.at[zz, c], pk.at[m], p.at(z=zz)))
        else:
            own_pk = k.local(pks.at[z, c], pk.at[m])
        packs.append(k.send(pks.at[zz, 1 - c], pk.at[m], p.at(z=zz, c=1 - c)))
        if o == 1:
            for copy in o1:
                copy.wait_recv()
            o2 = to_plane(
                (
                    (wo_at(0, yh, x, yl, EVERY, c), "y"),
                    (wo_at(1, yh, x, yl, EVERY, c), "x"),
                    (wo_at(2, yh, EVERY, yl, z, c), "y"),
                ),
            )
        if o == 3:
            for copy in plane:
                copy.wait_recv()
            plane2 = to_plane(
                (
                    (WG.at[:, x, :, :, :, hi], "x"),
                    (WD.at[yl, :, yh, :, dlo], "y"),
                    (WD.at[:, x, :, :, dhi], "x"),
                ),
            )
    keep = [k.local(na, NA)]
    own_pk.wait()
    for copy in packs:
        copy.wait_recv()
    for i8 in range(8):
        pt[i8 * 240 : (i8 + 1) * 240] = pk[i8].astype(F32).T[:240]
    cos, sin = cos_ref[...], sin_ref[...]

    @pl.loop(0, KV_HEADS)
    def _(g):
        raw = pt[pl.ds(pl.multiple_of(QD + g * HEAD, HEAD), HEAD)]
        head = raw * head_scale(raw) * kgain[...]
        key = head * cos + half_turn(head) * sin
        value = pt[pl.ds(pl.multiple_of(QD + KD + g * HEAD, HEAD), HEAD)]
        both = jnp.concatenate([key, value], axis=0).T.astype(BF16)
        cols = pl.ds(pl.multiple_of(g * 128, 128), 128)
        for mm in range(MICRO):
            kvl[mm, :, cols] = both[mm * ROWS : (mm + 1) * ROWS]

    own_kv = k.local(kvl, kvs.at[:, yl, z, c])
    across = k.send(kvl, kvs.at[:, yl, z, c], yl_partner)
    ring = [k.send(kvl, kvs.at[:, yl, z, c], p.step("z", j)) for j in (1, 2, 3)]
    keep.append(k.local(pt, PT))

    @pl.loop(0, KV_HEADS)
    def _(g):
        for mm, unit in enumerate(query_units(pt, g, cos, sin, qgain[...])):
            qts[g, mm] = unit.astype(BF16)

    across.wait_recv()
    src = kvs.at[:, 1 - yl, z, c]
    ring += [k.send(src, src, p.step("z", j)) for j in (1, 2, 3)]
    plane2 += to_plane(((WG.at[yh, :, yl, :, :, lo], "y"),))
    own_kv.wait()
    for copy in o2:
        copy.wait_recv()
    o3 = []
    for j in (1, 2, 3):
        xx, yy, zz = p.pos("x", -j), p.pos("y", -j), p.pos("z", -j)
        src = wo_at(0, EVERY, x, EVERY, EVERY, c)
        o3.append((k.send(src, src, p.step("x", j)), wo_at(0, EVERY, xx, EVERY, EVERY, c)))
        src = wo_at(1, yh, EVERY, yl, EVERY, c)
        o3.append((k.send(src, src, p.step("y", j)), wo_at(1, yy // 2, EVERY, yy % 2, EVERY, c)))
        src = wo_at(2, EVERY, EVERY, EVERY, z, c)
        o3.append((k.send(src, src, p.step("z", j)), wo_at(2, EVERY, EVERY, EVERY, zz, c)))
    oc = []
    for src in (
        wo_at(0, EVERY, x, EVERY, EVERY, c),
        wo_at(1, yh, EVERY, yl, EVERY, c),
        wo_at(2, EVERY, EVERY, EVERY, z, c),
    ):
        oc.append(k.send(src, src, sib))
    keep.append(k.local(og, OG.at[z, c]))
    rows = [k.send(og, OG.at[z, c], p.step("z", j)) for j in (1, 2, 3)]
    last = [k.send(og, OG.at[z, c], sib)]
    for copy in ring:
        copy.wait_recv()
    src = kvs.at[:, :, :, c]
    kvc = k.send(src, src, sib)
    kvc.wait_recv()
    keep.append(k.local(kvs, KV))

    @pl.loop(0, 2 * KV_HEADS)
    def _(u):
        g, mm = u // 2, u % 2
        kv = unit_kv(kvs, mm, g)
        score = jnp.minimum(dot(kv, qts[g, mm]), unit_bias(bias, mm))
        peak = jnp.max(score, axis=0, keepdims=True)
        raised = jnp.exp(score - peak)
        total = jnp.sum(raised, axis=0, keepdims=True)
        probs = (raised * (1.0 / total)).astype(BF16)
        ots[g, mm] = dot_rows(kv, probs)[HEAD:]
        lse[u] = jnp.broadcast_to(peak + jnp.log(total), (8, 256))

    for g in range(KV_HEADS):
        for t in range(2):
            cols = slice(t * 128, (t + 1) * 128)
            a, b = swap(ots[g, 0, :, cols], ots[g, 1, :, cols])
            at = (g * GROUP + 2 * t) * HEAD
            att[:, at : at + 128] = jnp.concatenate([a, b], axis=0).T.astype(BF16)
    keep += [k.local(lse, LSE), k.local(att, ATT)]
    for copy, src in o3:
        copy.wait_recv()
        oc.append(k.send(src, src, sib))
    for copy in oc:
        copy.wait_recv()
    keep.append(k.local(wos, WO))

    @pl.loop(0, 8)
    def _(t):
        w = wos[t // 4, t % 4].reshape(256, QD)
        cols = pl.ds(pl.multiple_of(t * 256, 256), 256)
        resid[:, cols] = xs[z, c, :, cols].astype(F32) + dot_last(att[...], w)

    value = resid[...]
    n2[...] = (value * rms_scale(value) * gains_out[1:2, :]).astype(BF16)
    keep += [k.local(resid, RESID), k.local(n2, N2)]
    for j, copy in zip((1, 2, 3), rows):
        copy.wait_recv()
        src = OG.at[p.pos("z", -j), c]
        last.append(k.send(src, src, sib))
    for copy in plane2 + last:
        copy.wait_recv()
    for copy in keep:
        copy.wait()
    k.drain()

    @pl.when(jnp.logical_not(own_slab))
    def _():
        slab.wait_send()


VMEM = pl.BlockSpec(memory_space=pltpu.VMEM)


def front(x, wq, wo, wg, wd, og, segc, segq, cos, sin, qgain, kgain):
    hbm = [
        sds((2, 4, 2, 4, 2, 16, QD), BF16),
        sds((2, 4, 2, 8, 16, 2 * FS), BF16),
        sds((2, 4, 2, 80, 1024), BF16),
        sds((4, 2, TOK, D), BF16),
        sds((4, 2, TOK, D), BF16),
        sds((2, 2, 4, 2, ROWS, 2 * KD), BF16),
        sds((QKV, TOK), F32),
        sds((2 * KV_HEADS, 8, 256), F32),
        sds((TOK, QD), BF16),
        sds((TOK, D), F32),
        sds((TOK, D), BF16),
    ]
    vmem = [sds((8, D), F32)]
    scratch = [
        pltpu.VMEM((4, 2, TOK, D), BF16),
        pltpu.VMEM((4, 2, TOK, D), BF16),
        pltpu.VMEM((2, 4, 2, 8, 16, 256), BF16),
        pltpu.VMEM((2, 4, 2, 4, 2, 16, QD), BF16),
        pltpu.VMEM((4, 2, TOK, 256), BF16),
        pltpu.VMEM((8, TOK, 256), BF16),
        pltpu.VMEM((QKV, TOK), F32),
        pltpu.VMEM((2 * KV_HEADS, 8, 256), F32),
        pltpu.VMEM((TOK, QD), BF16),
        pltpu.VMEM((TOK, D), F32),
        pltpu.VMEM((TOK, D), BF16),
        pltpu.VMEM((2, ROWS, 2 * KD), BF16),
        pltpu.VMEM((2, 2, 4, 2, ROWS, 2 * KD), BF16),
        pltpu.VMEM((2, SEQ, 128), F32),
        pltpu.VMEM((KV_HEADS, 2, 128, 256), BF16),
        pltpu.VMEM((KV_HEADS, 2, HEAD, 256), F32),
        pltpu.SemaphoreType.DMA((170,)),
        pltpu.SemaphoreType.DMA((170,)),
    ]
    return pl.pallas_call(
        front_body,
        out_shape=hbm + vmem,
        in_specs=[ANY] * 6 + [VMEM] * 6,
        out_specs=[ANY] * len(hbm) + [VMEM] * len(vmem),
        scratch_shapes=scratch,
        name="front",
        compiler_params=pltpu.CompilerParams(
            collective_id=0, has_side_effects=True, vmem_limit_bytes=56 << 20
        ),
    )(x, wq, wo, wg, wd, og, segc, segq, cos, sin, qgain, kgain)


def ffn_body(n2, OG, WG, WD, wq, d_out, mix_out, dwg_out, dwd_out, WQ, *scr):
    (rows, ogs, wgs, wd80, wds, dgu, inn, din, part, mixs, r0, s0, r1, m0, dwg, dwd32, dwd) = scr[:17]
    (dn, ssem, rsem, lsem, wsem, vsem) = scr[17:]
    p = Place()
    k = Links(wsem, vsem)
    yh, x, yl, z, c = p.yh, p.x, p.yl, p.z, p.c
    sib = p.step("c", 1)
    greet([p.step(a, j) for a in "xyz" for j in (1, 2, 3)] + [sib])

    def remote(src, dst, i, to):
        return pltpu.make_async_remote_copy(
            src_ref=src,
            dst_ref=dst,
            send_sem=ssem.at[i],
            recv_sem=rsem.at[i],
            device_id=to,
            device_id_type=MESH,
        )

    def local(src, dst, i):
        copy = pltpu.make_async_copy(src, dst, lsem.at[i])
        copy.start()
        return copy

    def half_of(half, *at):
        return WQ.at[(*at, EVERY, pl.ds(half * 1024, 1024))]

    whole = (EVERY, EVERY, EVERY, EVERY, c)
    own_wq = k.local(wq, WQ.at[yh, x, yl, z, c])
    q1 = [k.plan(wq, WQ.at[yh, x, yl, z, c], p.step("z", j)) for j in (1, 2, 3)]
    q2, q3 = [], []
    for j in (1, 2, 3):
        for half, axis in ((0, "y"), (1, "x")):
            src = half_of(half, yh, x, yl, EVERY, c)
            q2.append(k.plan(src, src, p.step(axis, j)))
    for j in (1, 2, 3):
        src = half_of(0, EVERY, x, EVERY, EVERY, c)
        q3.append(k.plan(src, src, p.step("x", j)))
        src = half_of(1, yh, EVERY, yl, EVERY, c)
        q3.append(k.plan(src, src, p.step("y", j)))
    q4 = k.plan(WQ.at[whole], WQ.at[whole], sib)

    sent = []
    for copy in q1:
        copy.start()
    for j in (1, 3, 2):
        copy = remote(n2, rows.at[z, c], j, p.step("z", j))
        copy.start()
        sent.append(copy)
    remote(n2, rows.at[z, c], 4, sib).start()
    own = local(n2, rows.at[z, c], 0)
    get_wd = local(WD, wd80, 1)
    get_wg = local(WG, wgs, 2)
    get_og = local(OG, ogs, 3)
    get_wd.wait()

    @pl.loop(0, 8)
    def _(i):
        yl, x = i // 4, i % 4
        a, b = wd80[yl, x, 0].astype(F32), wd80[yl, x, 1].astype(F32)
        at = pl.ds(pl.multiple_of(i * 80, 80), 80)
        wds[at, :1024] = jnp.concatenate([a[:40], b[:40]], axis=0).astype(BF16)
        wds[at, 1024:] = jnp.concatenate([a[40:], b[40:]], axis=0).astype(BF16)

    own.wait()
    get_wg.wait()
    get_og.wait()
    own_wq.wait()

    @pl.loop(0, 4)
    def _(j):
        o = jnp.where(j == 2, 3, jnp.where(j == 3, 2, j))
        zz = (z + o) % 4
        at = pl.ds(pl.multiple_of(zz * 256, 256), 256)

        @pl.when(o > 0)
        def _():
            remote(n2, rows.at[zz, c], (4 - o) % 4, sib).wait_recv()
            remote(rows.at[zz, c], rows.at[zz, c], 4 + o, sib).start()

        remote(rows.at[zz, c], rows.at[zz, 1 - c], 4 + o, sib).wait_recv()
        r = rows[zz].reshape(256, D)
        din[...] = dot_last(ogs[zz].reshape(256, D), wds[...])
        for t in range(5):
            lo, hi = slice(t * 128, (t + 1) * 128), slice(FS + t * 128, FS + (t + 1) * 128)
            w = jnp.concatenate(
                [wgs[:, :, :, :, :, lo].reshape(D, 128), wgs[:, :, :, :, :, hi].reshape(D, 128)], axis=1
            )
            both = dot(r, w)
            gate, upper = both[:, :128], both[:, 128:]
            sig = jax.nn.sigmoid(gate)
            active = gate * sig
            d_inner = din[:, lo]
            inn[at, lo] = (active * upper).astype(BF16)
            dgu[at, lo] = (d_inner * upper * sig * (1.0 + gate * (1.0 - sig))).astype(BF16)
            dgu[at, hi] = (d_inner * active).astype(BF16)

        @pl.loop(0, 8)
        def _(t):
            w = wgs[t // 4, t % 4].reshape(256, 2 * FS)
            cols = pl.ds(pl.multiple_of(t * 256, 256), 256)
            part[zz, :, :, cols] = dot_last(dgu[at], w).astype(BF16).reshape(2, TOK, 256)

        remote(part.at[zz, 1 - c], r0.at[zz], 8 + o, sib).start()

        @pl.loop(0, 4)
        def _(t):
            cols = pl.ds(pl.multiple_of(t * 512, 512), 512)
            mixs[zz, :, :, cols] = dot(inn[at], wds[:, cols]).astype(BF16).reshape(2, TOK, 512)

        remote(mixs.at[zz, 1 - c], m0.at[zz], 16 + o, sib).start()
        remote(part.at[zz, 1 - c], r0.at[zz], 8 + o, sib).wait_recv()

        @pl.loop(0, TOK, step=16)
        def _(t):
            here = pl.ds(pl.multiple_of(t, 16), 16)
            s0[zz, here] = (part[zz, c, here].astype(F32) + r0[zz, here].astype(F32)).astype(BF16)

        @pl.when(o > 0)
        def _():
            remote(s0.at[zz], r1.at[o - 1], 12 + o, p.at(z=zz)).start()

        @pl.when(j == 0)
        def _():
            for copy in q1:
                copy.wait_recv()
            for copy in q2:
                copy.start()

        @pl.when(j == 1)
        def _():
            for copy in q2:
                copy.wait_recv()
            for copy in q3:
                copy.start()

    for o in range(4):
        remote(mixs.at[0, 0], m0.at[0], 16 + o, sib).wait_recv()

    @pl.loop(0, 4)
    def _(zz):
        @pl.loop(0, TOK, step=16)
        def _(t):
            here = pl.ds(pl.multiple_of(t, 16), 16)
            m0[zz, here] = (mixs[zz, c, here].astype(F32) + m0[zz, here].astype(F32)).astype(BF16)

    out_mix = local(m0, mix_out, 4)

    @pl.loop(0, 8)
    def _(t):
        cols = pl.ds(pl.multiple_of(t * 256, 256), 256)
        left = rows[:, :, :, cols].reshape(8 * TOK, 256)
        dwg[t // 4, t % 4] = dot_rows(left, dgu[...]).astype(BF16).reshape(2, TOK, 2 * FS)

    out_wg = local(dwg, dwg_out, 5)
    for copy in q3:
        copy.wait_recv()
    q4.start()

    @pl.loop(0, 5)
    def _(t):
        units = pl.ds(pl.multiple_of(t * 128, 128), 128)
        dwd32[units] = dot_rows(inn[:, units], ogs[...].reshape(8 * TOK, D))

    @pl.loop(0, 8)
    def _(i):
        yl, x = i // 4, i % 4
        at = pl.ds(pl.multiple_of(i * 80, 80), 80)
        lo, hi = dwd32[at, :1024], dwd32[at, 1024:]
        dwd[yl, x, 0] = jnp.concatenate([lo[:40], hi[:40]], axis=0).astype(BF16)
        dwd[yl, x, 1] = jnp.concatenate([lo[40:], hi[40:]], axis=0).astype(BF16)

    out_wd = local(dwd, dwd_out, 6)
    for o in (1, 2, 3):
        remote(s0.at[0], r1.at[o - 1], 12 + o, sib).wait_recv()

    @pl.loop(0, TOK, step=16)
    def _(t):
        here = pl.ds(pl.multiple_of(t, 16), 16)
        total = s0[z, here].astype(F32)
        for j in range(3):
            total = total + r1[j, here].astype(F32)
        dn[here] = total

    out_dn = local(dn, d_out, 7)
    q4.wait_recv()
    k.drain()
    for copy in sent:
        copy.wait_send()
    for o in range(4):
        remote(rows.at[0, 0], rows.at[0, 0], 4 + o, sib).wait_send()
        remote(part.at[0, 0], r0.at[0], 8 + o, sib).wait_send()
        remote(mixs.at[0, 0], m0.at[0], 16 + o, sib).wait_send()
    for o in (1, 2, 3):
        remote(s0.at[0], r1.at[o - 1], 12 + o, sib).wait_send()
    for copy in (out_mix, out_wg, out_wd, out_dn):
        copy.wait()


def ffn(n2, OG, WG, WD, wq):
    outs = [
        sds((TOK, D), F32),
        sds((4, TOK, D), BF16),
        sds((2, 4, 2, TOK, 2 * FS), BF16),
        sds((2, 4, 2, 80, 1024), BF16),
        sds((2, 4, 2, 4, 2, 16, 2048), BF16),
    ]
    scratch = [
        pltpu.VMEM((4, 2, TOK, D), BF16),
        pltpu.VMEM((4, 2, TOK, D), BF16),
        pltpu.VMEM((2, 4, 2, 8, 16, 2 * FS), BF16),
        pltpu.VMEM((2, 4, 2, 80, 1024), BF16),
        pltpu.VMEM((FS, D), BF16),
        pltpu.VMEM((8 * TOK, 2 * FS), BF16),
        pltpu.VMEM((8 * TOK, FS), BF16),
        pltpu.VMEM((256, FS), F32),
        pltpu.VMEM((4, 2, TOK, D), BF16),
        pltpu.VMEM((4, 2, TOK, D), BF16),
        pltpu.VMEM((4, TOK, D), BF16),
        pltpu.VMEM((4, TOK, D), BF16),
        pltpu.VMEM((3, TOK, D), BF16),
        pltpu.VMEM((4, TOK, D), BF16),
        pltpu.VMEM((2, 4, 2, TOK, 2 * FS), BF16),
        pltpu.VMEM((FS, D), F32),
        pltpu.VMEM((2, 4, 2, 80, 1024), BF16),
        pltpu.VMEM((TOK, D), F32),
        pltpu.SemaphoreType.DMA((20,)),
        pltpu.SemaphoreType.DMA((20,)),
        pltpu.SemaphoreType.DMA((8,)),
        pltpu.SemaphoreType.DMA((20,)),
        pltpu.SemaphoreType.DMA((20,)),
    ]
    return pl.pallas_call(
        ffn_body,
        out_shape=outs,
        in_specs=[ANY] * 5,
        out_specs=[ANY] * 5,
        scratch_shapes=scratch,
        name="ffn",
        compiler_params=pltpu.CompilerParams(
            collective_id=1, has_side_effects=True, vmem_limit_bytes=60 << 20
        ),
    )(n2, OG, WG, WD, wq)


def back_body(*refs):
    (DN, X_IN, OG_IN, RESID, ATT, PT, LSE, WQ, WO, KV, mix_part, dwg, dwd, NA) = refs[:14]
    (gains, segc, segq, cos_ref, sin_ref, qgain, kgain) = refs[14:21]
    (IN_GRAD, MIXED, GWG, GWD, GQ, GO, SMALL) = refs[21:28]
    (dn, xv, ogv, resid, pt, lse, in_grad, mixed, kvs, bias, qts, qns, dts, dns, dqt, dpt, datt, dres) = refs[28:46]
    (kpart, k0, k1, ks1, k2, kres, w2, wo2, low2, att2, do, dp, dpm, na2, dqm, mix1) = refs[46:62]
    scr = list(refs[62:])
    parts = []
    for shapes in PLANE_SHAPES + O_SHAPES:
        n = 2 * len(shapes)
        parts.append(scr[:n])
        scr = scr[n:]
    vec, vrecv, ssem, rsem = scr
    p = Place()
    k = Links(ssem, rsem)
    yl, z, c = p.yl, p.z, p.c
    m = z * 2 + c
    sib = p.step("c", 1)
    yl_partner = p.at(y=p.yh * 2 + 1 - yl)
    get = {
        "dn": k.local(DN, dn),
        "x": k.local(X_IN, xv),
        "og": k.local(OG_IN, ogv),
        "resid": k.local(RESID, resid),
        "att": k.local(ATT, att2.at[0]),
        "pt": k.local(PT, pt),
        "lse": k.local(LSE, lse),
        "kv": k.local(KV, kvs),
        "mix": k.local(mix_part.at[z], mix1.at[3]),
    }
    partners = [p.step(a, j) for a in "xyz" for j in (1, 2, 3)]
    partners += [p.at(z=(z + j) % 4, c=1 - c) for j in range(4)]
    slab_to, slab_from = slab_target(p), slab_source(p)
    own_slab = same(p, slab_to)
    greet_plane(p, partners, slab_to, slab_from, own_slab)
    plane = [
        staged_reduce(p, k, dwg, wg_stages(0), parts[0], 16),
        staged_reduce(p, k, dwg, wg_stages(1), parts[1], 16),
        staged_reduce(p, k, dwd, wd_stages(0), parts[2], 16),
        staged_reduce(p, k, dwd, wd_stages(1), parts[3], 16),
    ]
    for i in (0, 1, 3):
        next(plane[i])
    pair_att = k.send(ATT, att2.at[1], sib)
    mixing = [k.send(mix_part.at[p.pos("z", j)], mix1.at[j - 1], p.step("z", j)) for j in (1, 2, 3)]
    get_w = [k.local(WO.at[0, t], wo2.at[t]) for t in range(2)]
    fill_bias(bias, segc, segq, p.s * ROWS)
    cos, sin = cos_ref[...], sin_ref[...]
    get["pt"].wait()

    @pl.loop(0, KV_HEADS)
    def _(g):
        for mm, unit in enumerate(query_units(pt, g, cos, sin, qgain[...])):
            qts[g, mm] = unit.astype(BF16)
            qns[g, mm] = unit.T.astype(BF16)

    for name in ("dn", "og", "resid"):
        get[name].wait()
    value = resid[...]
    scale_two = rms_scale(value)
    norm_two = value * scale_two
    d_resid = ogv[...].astype(F32) + norm_back(dn[...], norm_two, scale_two, gains[1:2, :])
    dres[...] = d_resid
    low2[0] = d_resid.astype(BF16)
    pair_low = k.send(low2.at[0], low2.at[1], sib)
    for t in range(8):
        get_w[t].wait()
        term = dot(low2[0, :, t * 256 : (t + 1) * 256], wo2[t % 2].reshape(256, QD))
        datt[...] = term if t == 0 else datt[...] + term
        if t < 6:
            get_w.append(k.local(WO.at[(t + 2) // 4, (t + 2) % 4], wo2.at[t % 2]))
    for g in range(KV_HEADS):
        tiles = []
        for t in range(2):
            at = (g * GROUP + 2 * t) * HEAD
            both = low(datt[:, at : at + 128]).T
            tiles.append(swap(both[:HEAD], both[HEAD:]))
        for mm in range(MICRO):
            none = jnp.zeros((HEAD, 256), F32)
            unit = jnp.concatenate([none, jnp.concatenate([tiles[0][mm], tiles[1][mm]], axis=1)], axis=0)
            dts[g, mm] = unit.astype(BF16)
            dns[g, mm] = unit.T.astype(BF16)
    get["kv"].wait()
    get["lse"].wait()

    @pl.loop(0, 2 * KV_HEADS)
    def _(u):
        g, mm = u // 2, u % 2
        kv = unit_kv(kvs, mm, g)
        score = jnp.minimum(dot(kv, qts[g, mm]), unit_bias(bias, mm))
        again = jnp.exp(score - lse[u, 0:1, :])
        d_probs = dot(kv, dts[g, mm])
        inner = jnp.sum(again * d_probs, axis=0, keepdims=True)
        d_scores = (again * (d_probs - inner)).astype(BF16)
        d_kv = dot(d_scores, qns[g, mm]) + dot(again.astype(BF16), dns[g, mm])
        cols = pl.ds(pl.multiple_of(g * 128, 128), 128)
        kpart[mm, :, :, :, :, cols] = d_kv.astype(BF16).reshape(2, 4, 2, ROWS, 128)
        dqt[g, mm] = dot_rows(kv, d_scores)[:HEAD] * (HEAD ** -0.5)

    core = k.send(kpart.at[:, :, :, 1 - c], k0, sib)
    core.wait_recv()

    @pl.loop(0, 4)
    def _(zz):
        for a in range(2):
            for b in range(2):
                k0[a, b, zz] = (kpart[a, b, zz, c].astype(F32) + k0[a, b, zz].astype(F32)).astype(BF16)

    ring = [k.send(k0.at[:, :, p.pos("z", j)], k1.at[j - 1], p.step("z", j)) for j in (1, 2, 3)]

    get["att"].wait()
    pair_att.wait_recv()
    pair_low.wait_recv()
    att_cols = pl.ds(pl.multiple_of(c * 640, 128), 640)

    @pl.loop(0, 8)
    def _(t):
        cols = pl.ds(pl.multiple_of(t * 256, 256), 256)
        left = low2[:, :, cols].reshape(2 * TOK, 256)
        right = att2[:, :, att_cols].reshape(2 * TOK, 640)
        do[t // 4, t % 4] = dot_rows(left, right).astype(BF16).reshape(2, 4, 32, 640)

    outward = [staged_reduce(p, k, do, o_stages(i), parts[6 + i], 16) for i in range(3)]
    for step in outward:
        next(step)

    query_sum = jnp.zeros((HEAD, TOK), F32)
    for g in range(KV_HEADS):
        heads = []
        for t in range(2):
            cols = slice(t * 128, (t + 1) * 128)
            heads += list(swap(dqt[g, 0, :, cols], dqt[g, 1, :, cols]))
        for h in range(GROUP):
            at = (g * GROUP + h) * HEAD
            d_raw, term = head_back(pt[at : at + HEAD], heads[h], cos, sin, qgain[...])
            query_sum = query_sum + term
            dpt[at : at + HEAD] = d_raw

    for copy in ring:
        copy.wait_recv()
    for a in range(2):
        for b in range(2):
            total = k0[a, b, z].astype(F32)
            for j in range(3):
                total = total + k1[j, a, b].astype(F32)
            ks1[a, b] = total.astype(BF16)
    across = k.send(ks1.at[:, 1 - yl], k2, yl_partner)
    across.wait_recv()
    next(plane[2])
    for a in range(2):
        kres[pl.ds(a * ROWS, ROWS)] = ks1[a, yl].astype(F32) + k2[a].astype(F32)
    key_sum = jnp.zeros((HEAD, TOK), F32)
    for g in range(KV_HEADS):
        both = kres[:, g * 128 : (g + 1) * 128].T
        at = QD + g * HEAD
        d_raw, term = head_back(pt[at : at + HEAD], both[:HEAD], cos, sin, kgain[...])
        key_sum = key_sum + term
        dpt[at : at + HEAD] = d_raw
        dpt[at + KD : at + KD + HEAD] = both[HEAD:]
    get_q = [k.local(WQ.at[0, t], w2.at[t]) for t in range(2)]
    get_n = [k.local(NA.at[:, :, :, pl.ds(t * 256, 256)], na2.at[t]) for t in range(2)]
    for t in range(8):
        block = jnp.concatenate([dpt[t * 240 : (t + 1) * 240], jnp.zeros((16, TOK), F32)], axis=0)
        dp[t] = block.T.astype(BF16)
    members = []
    for dz in range(4):
        for dc in range(2):
            zz, cc = (z + dz) % 4, (c + dc) % 2
            src = dp.at[zz * 2 + cc]
            if dz == 0 and dc == 0:
                own_dp = k.local(src, dpm.at[z, c])
            else:
                members.append(k.send(src, dpm.at[z, c], p.at(z=zz, c=cc)))
    sums = jnp.concatenate(
        [jnp.sum(query_sum.T, axis=0, keepdims=True), jnp.sum(key_sum.T, axis=0, keepdims=True)], axis=1
    )
    vec[0] = jnp.broadcast_to(sums, (8, 128))
    small = small_reduce(p, k, vec, vrecv)
    next(small)
    for i in (0, 1, 3):
        next(plane[i])
    own_dp.wait()
    for copy in members:
        copy.wait_recv()
    for t in range(8):
        get_n[t].wait()
        total = dot_rows(na2[t % 2].reshape(8 * TOK, 256), dpm[...].reshape(8 * TOK, 256))
        dqm[t // 4, t % 4] = total.astype(BF16).reshape(2, TOK, 256)
        if t < 6:
            get_n.append(k.local(NA.at[:, :, :, pl.ds((t + 2) * 256, 256)], na2.at[t % 2]))
    inward = [staged_reduce(p, k, dqm, q_stages(i), parts[4 + i], 16) for i in range(2)]
    for step in inward:
        next(step)
    for step in outward:
        next(step)
    next(small)
    for t in range(8):
        get_q[t].wait()
        w = w2[t % 2].reshape(256, 2048)
        left = jnp.concatenate([dp[i] for i in range(8)], axis=1)
        in_grad[:, t * 256 : (t + 1) * 256] = dot_last(left, w)
        if t < 6:
            get_q.append(k.local(WQ.at[(t + 2) // 4, (t + 2) % 4], w2.at[t % 2]))
    next(plane[2])
    for step in inward:
        next(step)
    next(small)
    for step in outward:
        next(step)
    get["x"].wait()
    hidden = xv[...].astype(F32)
    scale_one = rms_scale(hidden)
    in_grad[...] = dres[...] + norm_back(in_grad[...], hidden * scale_one, scale_one, gains[0:1, :])
    keep = [k.local(in_grad, IN_GRAD)]
    for step in plane:
        next(step, None)
    next(small)

    last = []

    def to_owners(total, dst):
        for dz in range(4):
            for dc in range(2):
                zz, cc = (z + dz) % 4, (c + dc) % 2
                src = total.at[pl.ds(pl.multiple_of((zz * 2 + cc) * 16, 16), 16)]
                if dz == 0 and dc == 0:
                    keep.append(k.local(src, dst))
                else:
                    last.append(k.send(src, dst, p.at(z=zz, c=cc)))

    for half in range(2):
        to_owners(parts[half][-1], GWG.at[:, pl.ds(pl.multiple_of(half * FF + m * FS, 128), FS)])
    slabs = []
    for half in range(2):
        i = k.used
        k.used += 1
        src, dst = parts[2 + half][-1], GWD.at[:, pl.ds(half * 512, 512)]
        slabs.append((src, dst, i))

        @pl.when(own_slab)
        def _(src=src, dst=dst, i=i):
            pltpu.make_async_copy(src, dst, rsem.at[i]).start()

        @pl.when(jnp.logical_not(own_slab))
        def _(src=src, dst=dst, i=i):
            slab_copy(src, dst, ssem, rsem, i, slab_from).start()

    get["mix"].wait()
    for copy in mixing:
        copy.wait_recv()

    @pl.loop(0, TOK, step=16)
    def _(t):
        at = pl.ds(pl.multiple_of(t, 16), 16)
        total = resid[at]
        for j in range(4):
            total = total + mix1[j, at].astype(F32)
        mixed[at] = total.astype(BF16)

    keep.append(k.local(mixed, MIXED))
    for step in inward:
        next(step, None)
    for half in range(2):
        to_owners(parts[4 + half][-1], GQ.at[:, pl.ds(pl.multiple_of(m * 256 + half * 128, 128), 128)])
    for i, step in enumerate(outward):
        next(step, None)
        total = parts[6 + i][-1]
        dst = GO.at[c, :, pl.ds(*O_PARTS[i])]
        keep.append(k.local(total.at[pl.ds(pl.multiple_of(c * 16, 16), 16)], dst))
        last.append(k.send(total.at[pl.ds(pl.multiple_of((1 - c) * 16, 16), 16)], dst, sib))
    next(small, None)
    SMALL[...] = vec[4]
    for copy in keep:
        copy.wait()
    for copy in last:
        copy.wait_recv()
    for src, dst, i in slabs:

        @pl.when(own_slab)
        def _(src=src, dst=dst, i=i):
            pltpu.make_async_copy(src, dst, rsem.at[i]).wait()

        @pl.when(jnp.logical_not(own_slab))
        def _(src=src, dst=dst, i=i):
            slab_copy(src, dst, ssem, rsem, i, slab_from).wait()

    k.drain()


def head_back(raw, grad, cos, sin, gain):
    scale = head_scale(raw)
    normed = raw * scale
    d_head = grad * cos + half_back(grad * sin)
    scaled = d_head * gain
    inner = jnp.mean(scaled * normed, axis=0, keepdims=True)
    return scale * (scaled - normed * inner), d_head * normed


def back(dn, x, og, resid, att, pt, lse, WQ, WO, KV, mix, dwg, dwd, NA, gains, segc, segq, cos, sin, qgain, kgain):
    w = 2 * KD
    outs = [
        sds((TOK, D), F32),
        sds((TOK, D), BF16),
        sds((16, 2 * FF), BF16),
        sds((80, 1024), BF16),
        sds((16, 2048), BF16),
        sds((2, 16, 640), BF16),
        sds((8, 128), F32),
    ]
    scratch = [
        pltpu.VMEM((TOK, D), F32),
        pltpu.VMEM((TOK, D), BF16),
        pltpu.VMEM((TOK, D), BF16),
        pltpu.VMEM((TOK, D), F32),
        pltpu.VMEM((QKV, TOK), F32),
        pltpu.VMEM((2 * KV_HEADS, 8, 256), F32),
        pltpu.VMEM((TOK, D), F32),
        pltpu.VMEM((TOK, D), BF16),
        pltpu.VMEM((2, 2, 4, 2, ROWS, w), BF16),
        pltpu.VMEM((2, SEQ, 128), F32),
        pltpu.VMEM((KV_HEADS, 2, 128, 256), BF16),
        pltpu.VMEM((KV_HEADS, 2, 256, 128), BF16),
        pltpu.VMEM((KV_HEADS, 2, 128, 256), BF16),
        pltpu.VMEM((KV_HEADS, 2, 256, 128), BF16),
        pltpu.VMEM((KV_HEADS, 2, HEAD, 256), F32),
        pltpu.VMEM((QKV, TOK), F32),
        pltpu.VMEM((TOK, QD), F32),
        pltpu.VMEM((TOK, D), F32),
        pltpu.VMEM((2, 2, 4, 2, ROWS, w), BF16),
        pltpu.VMEM((2, 2, 4, ROWS, w), BF16),
        pltpu.VMEM((3, 2, 2, ROWS, w), BF16),
        pltpu.VMEM((2, 2, ROWS, w), BF16),
        pltpu.VMEM((2, ROWS, w), BF16),
        pltpu.VMEM((TOK, w), F32),
        pltpu.VMEM((2, 2, 4, 2, 16, 2048), BF16),
        pltpu.VMEM((2, 2, 4, 2, 16, QD), BF16),
        pltpu.VMEM((2, TOK, D), BF16),
        pltpu.VMEM((2, TOK, QD), BF16),
        pltpu.VMEM((2, 4, 2, 4, 32, 640), BF16),
        pltpu.VMEM((8, TOK, 256), BF16),
        pltpu.VMEM((4, 2, TOK, 256), BF16),
        pltpu.VMEM((2, 4, 2, TOK, 256), BF16),
        pltpu.VMEM((2, 4, 2, TOK, 256), BF16),
        pltpu.VMEM((4, TOK, D), BF16),
    ]
    for shapes in PLANE_SHAPES + O_SHAPES:
        scratch += staged_scratch(shapes)
    scratch += [
        pltpu.VMEM((5, 8, 128), F32),
        pltpu.VMEM((4, 3, 8, 128), F32),
        pltpu.SemaphoreType.DMA((180,)),
        pltpu.SemaphoreType.DMA((180,)),
    ]
    return pl.pallas_call(
        back_body,
        out_shape=outs,
        in_specs=[ANY] * 14 + [VMEM] * 7,
        out_specs=[ANY] * 6 + [VMEM],
        scratch_shapes=scratch,
        name="back",
        compiler_params=pltpu.CompilerParams(
            collective_id=2, has_side_effects=True, vmem_limit_bytes=60 << 20
        ),
    )(dn, x, og, resid, att, pt, lse, WQ, WO, KV, mix, dwg, dwd, NA, gains, segc, segq, cos, sin, qgain, kgain)


def rope_tables(start):
    half = HEAD // 2
    inverse = 10000.0 ** (-jnp.arange(half, dtype=F32) / half)
    positions = (start + jnp.arange(TOK) % ROWS).astype(F32)
    angles = inverse[:, None] * positions[None, :]
    angles = jnp.concatenate([angles, angles], axis=0)
    return jnp.cos(angles), jnp.sin(angles)


def per_device(
    tokens,
    segment_ids,
    w_qkv,
    w_out,
    w_gate_up,
    w_down,
    attn_gain,
    ffn_gain,
    query_gain,
    key_gain,
    out_grad,
):
    start = lax.axis_index("seq") * ROWS
    qgain = query_gain.astype(F32)[:, None]
    kgain = key_gain.astype(F32)[:, None]
    spare = jnp.stack([attn_gain, ffn_gain] + [jnp.zeros_like(attn_gain)] * 14, axis=1)
    spare = jnp.broadcast_to(spare[:, None, :], (16, 8, 16))
    wq_in = jnp.concatenate([w_qkv.reshape(16, 8, 240), spare], axis=2).reshape(16, 2048)
    wd_in = jnp.concatenate([w_down[:, :1024], w_down[:, 1024:]], axis=0)
    og_in = out_grad.reshape(TOK, D)
    x_in = tokens.reshape(TOK, D)
    segc = segment_ids.T
    query_ids = lax.dynamic_slice_in_dim(segment_ids, start, ROWS, axis=1)
    segq = jnp.tile(jnp.where(query_ids >= 0, query_ids, -2), (1, 2))
    cos, sin = rope_tables(start)
    (WO, WG, WD, OG, NA, KV, pt, lse, attended, resid, n2, gains) = front(
        x_in, wq_in, w_out.T, w_gate_up, wd_in, og_in, segc, segq, cos, sin, qgain, kgain
    )
    d_normed, mix_part, dwg, dwd, WQ = ffn(n2, OG, WG, WD, wq_in)
    input_grad, result, gwg, gwd, gq, go, sums = back(
        d_normed, x_in, og_in, resid, attended, pt, lse, WQ, WO, KV, mix_part, dwg, dwd, NA,
        gains, segc, segq, cos, sin, qgain, kgain,
    )
    w_qkv_grad = gq.reshape(16, 8, 256)[:, :, :240].reshape(16, QKV).astype(F32)
    w_out_grad = jnp.concatenate([go[0], go[1]], axis=1).T.astype(F32)
    w_gate_up_grad = gwg.astype(F32)
    attn_sum = jnp.sum(w_qkv.astype(F32) * w_qkv_grad, axis=1) / attn_gain.astype(F32)
    ffn_sum = jnp.sum(w_gate_up.astype(F32) * w_gate_up_grad, axis=1) / ffn_gain.astype(F32)
    return (
        result.reshape(MICRO, ROWS, D),
        input_grad.reshape(MICRO, ROWS, D),
        w_qkv_grad,
        w_out_grad,
        w_gate_up_grad,
        jnp.concatenate([gwd[:40], gwd[40:]], axis=1).astype(F32),
        attn_sum,
        ffn_sum,
        sums[0, :HEAD],
        sums[0, HEAD:],
    )


def solution(mesh):
    return jax.shard_map(
        per_device,
        mesh=mesh,
        in_specs=(
            P(None, ("grp", "seq"), None),
            P(None, "grp"),
            P(("grp", "seq"), None),
            P(None, ("grp", "seq")),
            P(("grp", "seq"), None),
            P(("grp", "seq"), None),
            P(("grp", "seq")),
            P(("grp", "seq")),
            P(),
            P(),
            P(None, ("grp", "seq"), None),
        ),
        out_specs=(
            P(None, ("grp", "seq"), None),
            P(None, ("grp", "seq"), None),
            P(("grp", "seq"), None),
            P(None, ("grp", "seq")),
            P(("grp", "seq"), None),
            P(("grp", "seq"), None),
            P(("grp", "seq")),
            P(("grp", "seq")),
            P(),
            P(),
        ),
        check_vma=False,
    )
```

```python
import jax
import jax.numpy as jnp
import numpy as np
from jax import lax
from jax.experimental import pallas as pl
from jax.experimental.pallas import tpu as pltpu
from jax.sharding import PartitionSpec as P

Q_HEADS = 20
KV_HEADS = 5
GROUP = 4
HEAD = 64
D = 2048
FF = 5120
QD = 1280
KD = 320
QKV = 1920
SEQ = 1024
MICRO = 2
ROWS = 64
TOK = 128
FS = 640
EPS = 1e-06
MESH = pl.DeviceIdType.MESH
F32 = jnp.float32
BF16 = jnp.bfloat16
ANY = pl.BlockSpec(memory_space=pl.ANY)


class Place:
    def __init__(self):
        g = lax.axis_index("grp")
        s = lax.axis_index("seq")
        self.g, self.s = g, s
        self.yh, self.x = g // 4, g % 4
        self.yl, self.z, self.c = s // 8, (s // 2) % 4, s % 2
        self.y = self.yh * 2 + self.yl

    def at(self, x=None, y=None, z=None, c=None):
        x = self.x if x is None else x
        y = self.y if y is None else y
        z = self.z if z is None else z
        c = self.c if c is None else c
        return ((y // 2) * 4 + x, (y % 2) * 8 + z * 2 + c)

    def step(self, axis, k):
        if axis == "x":
            return self.at(x=(self.x + k) % 4)
        if axis == "y":
            return self.at(y=(self.y + k) % 4)
        if axis == "z":
            return self.at(z=(self.z + k) % 4)
        return self.at(c=1 - self.c)

    def pos(self, axis, k):
        return (getattr(self, axis) + k) % 4


class Links:
    def __init__(self, send_sems, recv_sems, local_sems):
        self.send_sems, self.recv_sems, self.local_sems = send_sems, recv_sems, local_sems
        self.received = 0
        self.free = {"send": list(range(send_sems.shape[0]))[::-1], "local": list(range(local_sems.shape[0]))[::-1]}
        self.sent = {}

    def plan(self, src, dst, to):
        i = self.received
        self.received += 1
        slot = self.free["send"].pop()
        copy = pltpu.make_async_remote_copy(
            src_ref=src,
            dst_ref=dst,
            send_sem=self.send_sems.at[slot],
            recv_sem=self.recv_sems.at[i],
            device_id=to,
            device_id_type=MESH,
        )
        self.sent[id(copy)] = (copy, slot)
        return copy

    def send(self, src, dst, to):
        copy = self.plan(src, dst, to)
        copy.start()
        return copy

    def local(self, src, dst):
        slot = self.free["local"].pop()
        copy = pltpu.make_async_copy(src, dst, self.local_sems.at[slot])
        copy.start()
        return Local(self, copy, slot)

    def settle(self, copies):
        for copy in copies:
            copy, slot = self.sent.pop(id(copy))
            copy.wait_send()
            self.free["send"].append(slot)

    def drain(self):
        self.settle([copy for copy, _ in list(self.sent.values())])


class Local:
    def __init__(self, links, copy, slot):
        self.links, self.copy, self.slot = links, copy, slot

    def wait(self):
        self.copy.wait()
        self.links.free["local"].append(self.slot)


def greet(partners):
    barrier = pltpu.get_barrier_semaphore()
    for to in partners:
        pl.semaphore_signal(barrier, inc=1, device_id=to, device_id_type=MESH)
    pl.semaphore_wait(barrier, len(partners))


def sds(shape, dtype):
    return jax.ShapeDtypeStruct(shape, dtype)


def rms_scale(values):
    return lax.rsqrt(jnp.mean(values * values, axis=-1, keepdims=True) + EPS)


def norm_back(upstream, normed, scale, gain):
    scaled = upstream * gain
    inner = jnp.mean(scaled * normed, axis=-1, keepdims=True)
    return scale * (scaled - normed * inner)


def dot(left, right):
    return jnp.dot(left, right, preferred_element_type=F32)


def dot_last(left, right):
    return lax.dot_general(left, right, (((1,), (1,)), ((), ())), preferred_element_type=F32)


def dot_rows(left, right):
    return lax.dot_general(left, right, (((0,), (0,)), ((), ())), preferred_element_type=F32)


def slab_target(p):
    to = p.at(x=p.z, y=p.c * 2 + p.yl, z=p.g // 2, c=p.g % 2)
    return to


def slab_source(p):
    m = p.z * 2 + p.c
    return p.at(x=m % 4, y=(m // 4) * 2 + p.yl, z=p.x, c=p.yh)


def same(p, to):
    return (to[0] == p.g) & (to[1] == p.s)


def greet_plane(p, partners, slab_to, slab_from, own_slab):
    barrier = pltpu.get_barrier_semaphore()
    for to in partners:
        pl.semaphore_signal(barrier, inc=1, device_id=to, device_id_type=MESH)

    @pl.when(jnp.logical_not(own_slab))
    def _():
        pl.semaphore_signal(barrier, inc=1, device_id=slab_to, device_id_type=MESH)
        pl.semaphore_signal(barrier, inc=1, device_id=slab_from, device_id_type=MESH)
        pl.semaphore_wait(barrier, len(partners) + 2)

    @pl.when(own_slab)
    def _():
        pl.semaphore_wait(barrier, len(partners))


class Slab:
    def __init__(self, k, src, dst, to, own):
        self.own, self.src, self.dst = own, src, dst
        self.far = k.plan(src, dst, to)
        k.sent.pop(id(self.far))
        self.near = pltpu.make_async_copy(src, dst, k.recv_sems.at[k.received - 1])

    def start(self):
        @pl.when(self.own)
        def _():
            self.near.start()

        @pl.when(jnp.logical_not(self.own))
        def _():
            self.far.start()

    def wait_recv(self):
        @pl.when(self.own)
        def _():
            self.near.wait()

        @pl.when(jnp.logical_not(self.own))
        def _():
            self.far.wait_recv()

    def wait_send(self):
        @pl.when(jnp.logical_not(self.own))
        def _():
            self.far.wait_send()


def add_blocks(dst, own, recv, chunk):
    lead, rows = dst.shape[:-2], dst.shape[-2]
    count = 1
    for n in lead:
        count *= n

    @pl.loop(0, count)
    def _(i):
        at = []
        rest = i
        for n in reversed(lead):
            at.insert(0, rest % n)
            rest = rest // n

        @pl.loop(0, rows, step=chunk)
        def _(t):
            here = (*at, pl.ds(pl.multiple_of(t, chunk), chunk))
            total = own[here].astype(F32)
            for j in range(3):
                total = total + recv[(j, *here)].astype(F32)
            dst[here] = total.astype(dst.dtype)


def staged_reduce(p, k, src, stages, scr, chunk):
    own = scr[0]
    cur = src
    for n, (axis, pick) in enumerate(stages):
        recv = scr[1] if n == 0 else scr[2 * n]
        if n == 0:
            mine = k.local(pick(src, p.pos(axis, 0)), own)
        ring = [k.send(pick(cur, p.pos(axis, j)), recv.at[j - 1], p.step(axis, j)) for j in (1, 2, 3)]
        yield
        if n == 0:
            mine.wait()
        for copy in ring:
            copy.wait_recv()
        total = own if n == 0 else scr[2 * n + 1]
        add_blocks(total, own if n == 0 else pick(cur, p.pos(axis, 0)), recv, chunk)
        cur = total


def staged_scratch(shapes):
    out = [pltpu.VMEM(shapes[0], BF16), pltpu.VMEM((3, *shapes[0]), BF16)]
    for n, shape in enumerate(shapes[1:]):
        out.append(pltpu.VMEM((3, *shape), BF16))
        out.append(pltpu.VMEM(shape, BF16))
    return out


EVERY = slice(None)


def wg_stages(half):
    cols = pl.ds(half * FS, FS)
    if half == 0:
        return [
            ("y", lambda r, i: r.at[i // 2, :, i % 2, :, cols]),
            ("x", lambda r, i: r.at[i]),
        ]
    return [
        ("x", lambda r, i: r.at[:, i, :, :, cols]),
        ("y", lambda r, i: r.at[i // 2, i % 2]),
    ]


def wd_stages(half):
    cols = pl.ds(half * 512, 512)
    if half == 0:
        return [
            ("y", lambda r, i: r.at[i % 2, :, i // 2, :, cols]),
            ("x", lambda r, i: r.at[i]),
        ]
    return [
        ("x", lambda r, i: r.at[:, i, :, :, cols]),
        ("y", lambda r, i: r.at[i % 2, i // 2]),
    ]


def q_stages(half):
    cols = pl.ds(half * 128, 128)
    if half == 0:
        return [
            ("y", lambda r, i: r.at[i // 2, :, i % 2, :, cols]),
            ("x", lambda r, i: r.at[i]),
        ]
    return [
        ("x", lambda r, i: r.at[:, i, :, :, cols]),
        ("y", lambda r, i: r.at[i // 2, i % 2]),
    ]


def o_stages(part):
    cols = pl.ds((0, 256, 512)[part], (256, 256, 128)[part])
    if part == 0:
        return [
            ("x", lambda r, i: r.at[:, i, :, :, :, cols]),
            ("z", lambda r, i: r.at[:, :, i]),
            ("y", lambda r, i: r.at[i // 2, i % 2]),
        ]
    if part == 1:
        return [
            ("y", lambda r, i: r.at[i // 2, :, i % 2, :, :, cols]),
            ("x", lambda r, i: r.at[i]),
            ("z", lambda r, i: r.at[i]),
        ]
    return [
        ("z", lambda r, i: r.at[:, :, :, i, :, cols]),
        ("y", lambda r, i: r.at[i // 2, :, i % 2]),
        ("x", lambda r, i: r.at[i]),
    ]


O_PARTS = ((0, 256), (256, 256), (512, 128))
PLANE_SHAPES = [
    [(4, 128, FS), (128, FS)],
    [(2, 2, 128, FS), (128, FS)],
    [(4, 80, 512), (80, 512)],
    [(2, 2, 80, 512), (80, 512)],
    [(4, 128, 128), (128, 128)],
    [(2, 2, 128, 128), (128, 128)],
]
O_SHAPES = [
    [(2, 2, 4, 32, 256), (2, 2, 32, 256), (32, 256)],
    [(4, 4, 32, 256), (4, 32, 256), (32, 256)],
    [(2, 4, 2, 32, 128), (4, 32, 128), (32, 128)],
]


def small_reduce(p, k, vec, recv):
    for n, axis in enumerate("xyzc"):
        steps = (1,) if axis == "c" else (1, 2, 3)
        ring = [k.send(vec.at[n], recv.at[n, j - 1], p.step(axis, j)) for j in steps]
        yield
        for copy in ring:
            copy.wait_recv()
        total = vec[n]
        for j in range(len(steps)):
            total = total + recv[n, j]
        vec[n + 1] = total


def swap(a, b):
    left = lax.broadcasted_iota(jnp.int32, a.shape, 1) < ROWS
    return jnp.where(left, a, pltpu.roll(b, ROWS, 1)), jnp.where(left, pltpu.roll(a, ROWS, 1), b)


def head_scale(v):
    return lax.rsqrt(jnp.mean(v * v, axis=-2, keepdims=True) + EPS)


def half_turn(v):
    half = HEAD // 2
    return jnp.concatenate([-v[..., half:, :], v[..., :half, :]], axis=-2)


def half_back(v):
    half = HEAD // 2
    return jnp.concatenate([v[..., half:, :], -v[..., :half, :]], axis=-2)


def low(v):
    return v.astype(BF16).astype(F32)


def query_units(packed_t, g, cos, sin, gain):
    raw = packed_t[pl.ds(pl.multiple_of(g * 256, 256), 256)].reshape(GROUP, HEAD, TOK)
    head = raw * head_scale(raw) * gain
    turned = low(head * cos + half_turn(head) * sin) * (HEAD ** -0.5)
    a0, a1 = swap(turned[0], turned[1])
    b0, b1 = swap(turned[2], turned[3])
    none = jnp.zeros((HEAD, 256), F32)
    return [
        jnp.concatenate([jnp.concatenate([a, b], axis=1), none], axis=0) for a, b in ((a0, b0), (a1, b1))
    ]


def fill_bias(bias, seg, s):
    lane = lax.broadcasted_iota(jnp.int32, (128, 128), 1)
    query = lane % ROWS + s * ROWS
    around = pl.ds(pl.multiple_of((s // 2) * 128, 128), 128)
    for m in range(MICRO):
        ids = jnp.broadcast_to(seg[m : m + 1, around].astype(F32), (128, 128))
        turned = pltpu.roll(ids, ROWS, 1)
        ids = jnp.where((lane < ROWS) == (s % 2 == 0), ids, turned)
        ids = jnp.where(ids >= 0, ids, -2.0)

        @pl.loop(0, SEQ, step=128)
        def _(t):
            at = pl.ds(pl.multiple_of(t, 128), 128)
            key = lax.broadcasted_iota(jnp.int32, (128, 128), 0) + t
            keys = jnp.broadcast_to(seg[m : m + 1, at].astype(F32), (128, 128)).T
            ok = ((key <= query) & (keys == ids)) | (key == query)
            bias[m, at] = jnp.where(ok, 3e38, -1e30)


def rope_parts():
    inverse = 10000.0 ** (-(np.arange(HEAD) % (HEAD // 2)) / (HEAD // 2))
    begin = inverse[:, None] * (np.arange(128)[None, :] % 16 * ROWS)
    inside = inverse[:, None] * (np.arange(128)[None, :] % ROWS)
    return np.stack([np.cos(begin), np.sin(begin), np.cos(inside), np.sin(inside)]).astype(np.float32)


def rope_tables(parts, s):
    here = lax.broadcasted_iota(jnp.int32, (HEAD, 128), 1) == s
    c0 = jnp.sum(jnp.where(here, parts[0], 0.0), axis=1, keepdims=True)
    s0 = jnp.sum(jnp.where(here, parts[1], 0.0), axis=1, keepdims=True)
    return c0 * parts[2] - s0 * parts[3], s0 * parts[2] + c0 * parts[3]


def column(row):
    n = row.shape[1]
    place = lax.broadcasted_iota(jnp.int32, (n, n), 0) == lax.broadcasted_iota(jnp.int32, (n, n), 1)
    return jnp.sum(jnp.where(place, jnp.broadcast_to(row, (n, n)), 0.0), axis=1, keepdims=True)


def unit_bias(bias, m):
    half = bias[m]
    return jnp.concatenate([half, half], axis=1)


def unit_kv(KV, m, g):
    cols = pl.ds(pl.multiple_of(g * 128, 128), 128)
    return KV[m, :, :, :, :, cols].reshape(SEQ, 128)


def front_body(*refs):
    (x_in, w_qkv, wo, wg, w_down, og, seg, g1, g2, g3, g4, parts) = refs[:12]
    (WO, WG, WD, OG, NA, KV, PT, LSE, ATT, RESID, N2, WQIN, BIAS, ROPE, GAINS, QKGAIN) = refs[12:28]
    (wq, wd, ogv, gains_out, rope, qkgain) = refs[28:34]
    (xs, na, wqm, wos, pks, pk, pt, lse, att, resid, n2, kvl, kvs, bias, qts, ots) = refs[34:50]
    ssem, rsem, lsem = refs[50:]
    p = Place()
    k = Links(ssem, rsem, lsem)
    yh, x, yl, z, c = p.yh, p.x, p.yl, p.z, p.c
    m = z * 2 + c
    sib = p.step("c", 1)
    yl_partner = p.at(y=p.yh * 2 + 1 - yl)
    partners = [p.step(a, j) for a in "xyz" for j in (1, 2, 3)]
    partners += [p.at(z=(z + j) % 4, c=1 - c) for j in range(4)]
    slab_to, slab_from = slab_target(p), slab_source(p)
    own_slab = same(p, slab_to)

    spare = [column(row[...].astype(F32)) for row in (g1, g2)]
    wide = w_qkv[...].astype(F32)
    lane = lax.broadcasted_iota(jnp.int32, (16, 256), 1)
    rest = jnp.where(lane == 240, spare[0], jnp.where(lane == 241, spare[1], 0.0))
    for i in range(8):
        turned = pltpu.roll(wide, (QKV - 240 * i) % QKV, 1)[:, :256]
        wq[:, i * 256 : (i + 1) * 256] = jnp.where(lane < 240, turned, rest).astype(BF16)
    slab_rows = w_down[...].astype(F32)
    wd[...] = jnp.concatenate([slab_rows[:, :1024], slab_rows[:, 1024:]], axis=0).astype(BF16)
    greet_plane(p, partners, slab_to, slab_from, own_slab)

    def spread(src_of, dst_of):
        far, near = [], None
        for dz in range(4):
            for dc in range(2):
                zz, cc = (z + dz) % 4, (c + dc) % 2
                src, dst = src_of(zz * 2 + cc), dst_of(m)
                if dz == 0 and dc == 0:
                    near = k.local(src, dst)
                else:
                    far.append(k.send(src, dst, p.at(z=zz, c=cc)))
        return near, far

    q0 = spread(
        lambda i: wq.at[:, pl.ds(pl.multiple_of(i * 256, 256), 256)], lambda i: wqm.at[yh, x, yl, i]
    )
    own_x = k.local(x_in, xs.at[z, c])
    get_og = k.local(og, ogv)
    xcore = {0: k.send(x_in, xs.at[z, c], sib)}
    own_wo = k.local(wo, wos.at[yh, x, yl, z, c])

    def wo_at(part, *at):
        return wos.at[(*at, EVERY, pl.ds((0, 512, 1024)[part], (512, 512, 256)[part]))]

    def wo_own(part):
        return wo.at[:, pl.ds((0, 512, 1024)[part], (512, 512, 256)[part])]

    o1 = []
    for j in (1, 2, 3):
        for part, axis in ((0, "z"), (1, "z"), (2, "x")):
            o1.append(k.send(wo_own(part), wo_at(part, yh, x, yl, z, c), p.step(axis, j)))
    g0 = [
        spread(
            lambda i: wg.at[:, pl.ds(pl.multiple_of(half * FF + i * FS, 128), FS)],
            lambda i: WG.at[yh, x, yl, i, :, pl.ds(half * FS, FS)],
        )
        for half in range(2)
    ]
    slab_dst = WD.at[yl, z, c]
    slab = Slab(k, wd, slab_dst, slab_to, own_slab)
    slab.start()

    xring = {j: k.send(x_in, xs.at[z, c], p.step("z", j)) for j in (1, 3, 2)}

    def to_plane(blocks):
        return [k.send(b, b, p.step(axis, j)) for j in (1, 2, 3) for b, axis in blocks]

    ql, qh = pl.ds(0, 128), pl.ds(128, 128)
    lo, hi = pl.ds(0, FS), pl.ds(FS, FS)
    dlo, dhi = pl.ds(0, 512), pl.ds(512, 512)
    q0[0].wait()
    for copy in q0[1]:
        copy.wait_recv()
    q1 = to_plane(((wqm.at[yh, x, yl, :, :, ql], "x"), (wqm.at[yh, x, yl, :, :, qh], "y")))
    fill_bias(bias, seg, p.s)
    cos, sin = rope_tables(parts, p.s)
    rope[0], rope[1] = cos, sin
    qgain, kgain = column(g3[...].astype(F32)), column(g4[...].astype(F32))
    qkgain[...] = jnp.concatenate([jnp.broadcast_to(qgain, (HEAD, 128)), jnp.broadcast_to(kgain, (HEAD, 128))], axis=0)
    for copy in q1:
        copy.wait_recv()
    q2 = to_plane(((wqm.at[yh, :, yl, :, :, ql], "y"), (wqm.at[:, x, :, :, :, qh], "x")))
    for near, far in g0:
        near.wait()
        for copy in far:
            copy.wait_recv()

    slab.wait_recv()
    plane = to_plane(
        (
            (WG.at[yh, x, yl, :, :, lo], "x"),
            (WG.at[yh, x, yl, :, :, hi], "y"),
            (WD.at[yl, x, yh, :, dlo], "x"),
            (WD.at[yl, x, yh, :, dhi], "y"),
        ),
    )
    for copy in q2:
        copy.wait_recv()
    own_x.wait()
    own_wo.wait()
    pick = jnp.where(
        lax.broadcasted_iota(jnp.int32, (8, 128), 0) + 112 == lax.broadcasted_iota(jnp.int32, (8, 128), 1), 1.0, 0.0
    ).astype(BF16)
    gains_out[...] = dot_last(pick, wqm[:, :, :, :, :, pl.ds(128, 128)].reshape(D, 128))
    keep = [k.local(wq, WQIN), k.local(bias, BIAS), k.local(rope, ROPE), k.local(gains_out, GAINS), k.local(qkgain, QKGAIN)]
    k.settle(q0[1] + q1)
    packs = []
    plane2 = []
    for o in (0, 1, 3, 2):
        zz = (z + o) % 4
        if o:
            xring[(4 - o) % 4].wait_recv()
            xcore[o] = k.send(xs.at[zz, c], xs.at[zz, c], sib)
        xcore[o].wait_recv()
        rows = xs[zz].reshape(256, D).astype(F32)
        normed = (rows * rms_scale(rows) * gains_out[0:1, :]).astype(BF16)
        na[zz] = normed.reshape(2, TOK, D)
        pks[zz] = dot(normed, wqm[...].reshape(D, 256)).astype(BF16).reshape(2, TOK, 256)
        if o:
            packs.append(k.send(pks.at[zz, c], pk.at[m], p.at(z=zz)))
        else:
            own_pk = k.local(pks.at[z, c], pk.at[m])
        packs.append(k.send(pks.at[zz, 1 - c], pk.at[m], p.at(z=zz, c=1 - c)))
        if o == 1:
            for copy in o1:
                copy.wait_recv()
            o2 = to_plane(
                (
                    (wo_at(0, yh, x, yl, EVERY, c), "y"),
                    (wo_at(1, yh, x, yl, EVERY, c), "x"),
                    (wo_at(2, yh, EVERY, yl, z, c), "y"),
                ),
            )
        if o == 3:
            for copy in plane:
                copy.wait_recv()
            plane2 = to_plane(
                (
                    (WG.at[:, x, :, :, :, hi], "x"),
                    (WD.at[yl, :, yh, :, dlo], "y"),
                    (WD.at[:, x, :, :, dhi], "x"),
                ),
            )
    keep.append(k.local(na, NA))
    k.settle(q2 + o1 + [copy for _, far in g0 for copy in far])
    own_pk.wait()
    for copy in packs:
        copy.wait_recv()
    for i8 in range(8):
        pt[i8 * 240 : (i8 + 1) * 240] = pk[i8].astype(F32).T[:240]

    @pl.loop(0, KV_HEADS)
    def _(g):
        raw = pt[pl.ds(pl.multiple_of(QD + g * HEAD, HEAD), HEAD)]
        head = raw * head_scale(raw) * kgain
        key = head * cos + half_turn(head) * sin
        value = pt[pl.ds(pl.multiple_of(QD + KD + g * HEAD, HEAD), HEAD)]
        both = jnp.concatenate([key, value], axis=0).T.astype(BF16)
        cols = pl.ds(pl.multiple_of(g * 128, 128), 128)
        for mm in range(MICRO):
            kvl[mm, :, cols] = both[mm * ROWS : (mm + 1) * ROWS]

    own_kv = k.local(kvl, kvs.at[:, yl, z, c])
    across = k.send(kvl, kvs.at[:, yl, z, c], yl_partner)
    ring = [k.send(kvl, kvs.at[:, yl, z, c], p.step("z", j)) for j in (1, 2, 3)]
    keep.append(k.local(pt, PT))

    @pl.loop(0, KV_HEADS)
    def _(g):
        for mm, unit in enumerate(query_units(pt, g, cos, sin, qgain)):
            qts[g, mm] = unit.astype(BF16)

    across.wait_recv()
    src = kvs.at[:, 1 - yl, z, c]
    ring += [k.send(src, src, p.step("z", j)) for j in (1, 2, 3)]
    for copy in o2:
        copy.wait_recv()
    own_kv.wait()
    k.settle(packs + plane)

    def wo_third(part):
        out = []
        for j in (1, 2, 3):
            if part == 0:
                src, got = wo_at(0, EVERY, x, EVERY, EVERY, c), wo_at(0, EVERY, p.pos("x", -j), EVERY, EVERY, c)
            elif part == 1:
                yy = p.pos("y", -j)
                src, got = wo_at(1, yh, EVERY, yl, EVERY, c), wo_at(1, yy // 2, EVERY, yy % 2, EVERY, c)
            else:
                src, got = wo_at(2, EVERY, EVERY, EVERY, z, c), wo_at(2, EVERY, EVERY, EVERY, p.pos("z", -j), c)
            out.append((k.send(src, src, p.step("xyz"[part], j)), got))
        return out

    o3 = wo_third(0) + wo_third(1)
    plane2 += to_plane(((WG.at[yh, :, yl, :, :, lo], "y"),))
    oc = []
    for src in (
        wo_at(0, EVERY, x, EVERY, EVERY, c),
        wo_at(1, yh, EVERY, yl, EVERY, c),
        wo_at(2, EVERY, EVERY, EVERY, z, c),
    ):
        oc.append(k.send(src, src, sib))
    for copy in ring:
        copy.wait_recv()
    src = kvs.at[:, :, :, c]
    kvc = k.send(src, src, sib)
    o3 += wo_third(2)
    get_og.wait()
    keep.append(k.local(ogv, OG.at[z, c]))
    rows = [k.send(ogv, OG.at[z, c], p.step("z", j)) for j in (1, 3, 2)]
    last = [k.send(ogv, OG.at[z, c], sib)]
    k.settle(o2 + list(xring.values()) + list(xcore.values()))
    kvc.wait_recv()
    keep.append(k.local(kvs, KV))

    @pl.loop(0, 2 * KV_HEADS)
    def _(u):
        g, mm = u // 2, u % 2
        kv = unit_kv(kvs, mm, g)
        score = jnp.minimum(dot(kv, qts[g, mm]), unit_bias(bias, mm))
        peak = jnp.max(score, axis=0, keepdims=True)
        raised = jnp.exp(score - peak)
        total = jnp.sum(raised, axis=0, keepdims=True)
        probs = (raised * (1.0 / total)).astype(BF16)
        ots[g, mm] = dot_rows(kv, probs)[HEAD:]
        lse[u] = jnp.broadcast_to(peak + jnp.log(total), (8, 256))

    for g in range(KV_HEADS):
        for t in range(2):
            cols = slice(t * 128, (t + 1) * 128)
            a, b = swap(ots[g, 0, :, cols], ots[g, 1, :, cols])
            at = (g * GROUP + 2 * t) * HEAD
            att[:, at : at + 128] = jnp.concatenate([a, b], axis=0).T.astype(BF16)
    keep += [k.local(lse, LSE), k.local(att, ATT)]
    for copy, src in o3:
        copy.wait_recv()
        oc.append(k.send(src, src, sib))
    for copy in oc:
        copy.wait_recv()
    keep.append(k.local(wos, WO))

    @pl.loop(0, 8)
    def _(t):
        w = wos[t // 4, t % 4].reshape(256, QD)
        cols = pl.ds(pl.multiple_of(t * 256, 256), 256)
        resid[:, cols] = xs[z, c, :, cols].astype(F32) + dot_last(att[...], w)

    value = resid[...]
    n2[...] = (value * rms_scale(value) * gains_out[1:2, :]).astype(BF16)
    keep += [k.local(resid, RESID), k.local(n2, N2)]
    for j, copy in zip((1, 3, 2), rows):
        copy.wait_recv()
        src = OG.at[p.pos("z", -j), c]
        last.append(k.send(src, src, sib))
    for copy in plane2 + last:
        copy.wait_recv()
    for copy in keep:
        copy.wait()
    slab.wait_send()
    k.drain()


VMEM = pl.BlockSpec(memory_space=pltpu.VMEM)


def front(*args):
    hbm = [
        sds((2, 4, 2, 4, 2, 16, QD), BF16),
        sds((2, 4, 2, 8, 16, 2 * FS), BF16),
        sds((2, 4, 2, 80, 1024), BF16),
        sds((4, 2, TOK, D), BF16),
        sds((4, 2, TOK, D), BF16),
        sds((2, 2, 4, 2, ROWS, 2 * KD), BF16),
        sds((QKV, TOK), F32),
        sds((2 * KV_HEADS, 8, 256), F32),
        sds((TOK, QD), BF16),
        sds((TOK, D), F32),
        sds((TOK, D), BF16),
        sds((16, 2048), BF16),
        sds((2, SEQ, 128), F32),
        sds((2, HEAD, TOK), F32),
        sds((8, D), F32),
        sds((2 * HEAD, 128), F32),
    ]
    scratch = [
        pltpu.VMEM((16, 2048), BF16),
        pltpu.VMEM((80, 1024), BF16),
        pltpu.VMEM((TOK, D), BF16),
        pltpu.VMEM((8, D), F32),
        pltpu.VMEM((2, HEAD, TOK), F32),
        pltpu.VMEM((2 * HEAD, 128), F32),
        pltpu.VMEM((4, 2, TOK, D), BF16),
        pltpu.VMEM((4, 2, TOK, D), BF16),
        pltpu.VMEM((2, 4, 2, 8, 16, 256), BF16),
        pltpu.VMEM((2, 4, 2, 4, 2, 16, QD), BF16),
        pltpu.VMEM((4, 2, TOK, 256), BF16),
        pltpu.VMEM((8, TOK, 256), BF16),
        pltpu.VMEM((QKV, TOK), F32),
        pltpu.VMEM((2 * KV_HEADS, 8, 256), F32),
        pltpu.VMEM((TOK, QD), BF16),
        pltpu.VMEM((TOK, D), F32),
        pltpu.VMEM((TOK, D), BF16),
        pltpu.VMEM((2, ROWS, 2 * KD), BF16),
        pltpu.VMEM((2, 2, 4, 2, ROWS, 2 * KD), BF16),
        pltpu.VMEM((2, SEQ, 128), F32),
        pltpu.VMEM((KV_HEADS, 2, 128, 256), BF16),
        pltpu.VMEM((KV_HEADS, 2, HEAD, 256), F32),
        pltpu.SemaphoreType.DMA((80,)),
        pltpu.SemaphoreType.DMA((126,)),
        pltpu.SemaphoreType.DMA((26,)),
    ]
    return pl.pallas_call(
        front_body,
        out_shape=hbm,
        in_specs=[ANY, VMEM, VMEM, ANY, VMEM, ANY] + [VMEM] * 6,
        out_specs=[ANY] * len(hbm),
        scratch_shapes=scratch,
        name="front",
        compiler_params=pltpu.CompilerParams(
            collective_id=0, has_side_effects=True, vmem_limit_bytes=56 << 20
        ),
    )(*args)


def ffn_body(n2, OG, WG, WD, wq, d_out, mix_out, dwg_out, dwd_out, WQ, *scr):
    (rows, ogs, wgs, wd80, wds, dgu, inn, din, part, mixs, r0, s0, r1, m0, dwg, dwd32, dwd) = scr[:17]
    (dn, wqv, ssem, rsem, lsem, wsem, vsem, wlsem) = scr[17:]
    p = Place()
    k = Links(wsem, vsem, wlsem)
    yh, x, yl, z, c = p.yh, p.x, p.yl, p.z, p.c
    sib = p.step("c", 1)
    greet([p.step(a, j) for a in "xyz" for j in (1, 2, 3)] + [sib])

    def remote(src, dst, i, to):
        return pltpu.make_async_remote_copy(
            src_ref=src,
            dst_ref=dst,
            send_sem=ssem.at[i],
            recv_sem=rsem.at[i],
            device_id=to,
            device_id_type=MESH,
        )

    def local(src, dst, i):
        copy = pltpu.make_async_copy(src, dst, lsem.at[i])
        copy.start()
        return copy

    def half_of(half, *at):
        return WQ.at[(*at, EVERY, pl.ds(half * 1024, 1024))]

    whole = (EVERY, EVERY, EVERY, EVERY, c)
    get_wq = k.local(wq, wqv)
    q1 = [k.plan(wq, WQ.at[yh, x, yl, z, c], p.step("z", j)) for j in (1, 2, 3)]
    q2, q3 = [], []
    for j in (1, 2, 3):
        for half, axis in ((0, "y"), (1, "x")):
            src = half_of(half, yh, x, yl, EVERY, c)
            q2.append(k.plan(src, src, p.step(axis, j)))
    for j in (1, 2, 3):
        src = half_of(0, EVERY, x, EVERY, EVERY, c)
        q3.append(k.plan(src, src, p.step("x", j)))
        src = half_of(1, yh, EVERY, yl, EVERY, c)
        q3.append(k.plan(src, src, p.step("y", j)))
    q4 = k.plan(WQ.at[whole], WQ.at[whole], sib)

    sent = []
    for copy in q1:
        copy.start()
    for j in (1, 3, 2):
        copy = remote(n2, rows.at[z, c], j, p.step("z", j))
        copy.start()
        sent.append(copy)
    remote(n2, rows.at[z, c], 4, sib).start()
    own = local(n2, rows.at[z, c], 0)
    get_wd = local(WD, wd80, 1)
    get_wg = local(WG, wgs, 2)
    get_og = local(OG, ogs, 3)
    get_wd.wait()

    @pl.loop(0, 8)
    def _(i):
        yl, x = i // 4, i % 4
        a, b = wd80[yl, x, 0].astype(F32), wd80[yl, x, 1].astype(F32)
        at = pl.ds(pl.multiple_of(i * 80, 80), 80)
        wds[at, :1024] = jnp.concatenate([a[:40], b[:40]], axis=0).astype(BF16)
        wds[at, 1024:] = jnp.concatenate([a[40:], b[40:]], axis=0).astype(BF16)

    own.wait()
    get_wg.wait()
    get_og.wait()
    get_wq.wait()
    own_wq = k.local(wqv, WQ.at[yh, x, yl, z, c])

    @pl.loop(0, 4)
    def _(j):
        o = jnp.where(j == 2, 3, jnp.where(j == 3, 2, j))
        zz = (z + o) % 4
        at = pl.ds(pl.multiple_of(zz * 256, 256), 256)

        @pl.when(o > 0)
        def _():
            remote(n2, rows.at[zz, c], (4 - o) % 4, sib).wait_recv()
            remote(rows.at[zz, c], rows.at[zz, c], 4 + o, sib).start()

        remote(rows.at[zz, c], rows.at[zz, 1 - c], 4 + o, sib).wait_recv()
        r = rows[zz].reshape(256, D)
        din[...] = dot_last(ogs[zz].reshape(256, D), wds[...])
        for t in range(5):
            lo, hi = slice(t * 128, (t + 1) * 128), slice(FS + t * 128, FS + (t + 1) * 128)
            w = jnp.concatenate(
                [wgs[:, :, :, :, :, lo].reshape(D, 128), wgs[:, :, :, :, :, hi].reshape(D, 128)], axis=1
            )
            both = dot(r, w)
            gate, upper = both[:, :128], both[:, 128:]
            sig = jax.nn.sigmoid(gate)
            active = gate * sig
            d_inner = din[:, lo]
            inn[at, lo] = (active * upper).astype(BF16)
            dgu[at, lo] = (d_inner * upper * sig * (1.0 + gate * (1.0 - sig))).astype(BF16)
            dgu[at, hi] = (d_inner * active).astype(BF16)

        @pl.loop(0, 8)
        def _(t):
            w = wgs[t // 4, t % 4].reshape(256, 2 * FS)
            cols = pl.ds(pl.multiple_of(t * 256, 256), 256)
            part[zz, :, :, cols] = dot_last(dgu[at], w).astype(BF16).reshape(2, TOK, 256)

        remote(part.at[zz, 1 - c], r0.at[zz], 8 + o, sib).start()

        @pl.loop(0, 4)
        def _(t):
            cols = pl.ds(pl.multiple_of(t * 512, 512), 512)
            mixs[zz, :, :, cols] = dot(inn[at], wds[:, cols]).astype(BF16).reshape(2, TOK, 512)

        remote(mixs.at[zz, 1 - c], m0.at[zz], 16 + o, sib).start()
        remote(part.at[zz, 1 - c], r0.at[zz], 8 + o, sib).wait_recv()

        @pl.loop(0, TOK, step=16)
        def _(t):
            here = pl.ds(pl.multiple_of(t, 16), 16)
            s0[zz, here] = (part[zz, c, here].astype(F32) + r0[zz, here].astype(F32)).astype(BF16)

        @pl.when(o > 0)
        def _():
            remote(s0.at[zz], r1.at[o - 1], 12 + o, p.at(z=zz)).start()

        @pl.when(j == 0)
        def _():
            own_wq.wait()
            for copy in q1:
                copy.wait_recv()
            for copy in q2:
                copy.start()

        @pl.when(j == 1)
        def _():
            for copy in q2:
                copy.wait_recv()
            for copy in q3:
                copy.start()

    for o in range(4):
        remote(mixs.at[0, 0], m0.at[0], 16 + o, sib).wait_recv()

    @pl.loop(0, 4)
    def _(zz):
        @pl.loop(0, TOK, step=16)
        def _(t):
            here = pl.ds(pl.multiple_of(t, 16), 16)
            m0[zz, here] = (mixs[zz, c, here].astype(F32) + m0[zz, here].astype(F32)).astype(BF16)

    out_mix = local(m0, mix_out, 4)

    @pl.loop(0, 8)
    def _(t):
        cols = pl.ds(pl.multiple_of(t * 256, 256), 256)
        left = rows[:, :, :, cols].reshape(8 * TOK, 256)
        dwg[t // 4, t % 4] = dot_rows(left, dgu[...]).astype(BF16).reshape(2, TOK, 2 * FS)

    out_wg = local(dwg, dwg_out, 5)
    for copy in q3:
        copy.wait_recv()
    q4.start()

    @pl.loop(0, 5)
    def _(t):
        units = pl.ds(pl.multiple_of(t * 128, 128), 128)
        dwd32[units] = dot_rows(inn[:, units], ogs[...].reshape(8 * TOK, D))

    @pl.loop(0, 8)
    def _(i):
        yl, x = i // 4, i % 4
        at = pl.ds(pl.multiple_of(i * 80, 80), 80)
        lo, hi = dwd32[at, :1024], dwd32[at, 1024:]
        dwd[yl, x, 0] = jnp.concatenate([lo[:40], hi[:40]], axis=0).astype(BF16)
        dwd[yl, x, 1] = jnp.concatenate([lo[40:], hi[40:]], axis=0).astype(BF16)

    out_wd = local(dwd, dwd_out, 6)
    for o in (1, 2, 3):
        remote(s0.at[0], r1.at[o - 1], 12 + o, sib).wait_recv()

    @pl.loop(0, TOK, step=16)
    def _(t):
        here = pl.ds(pl.multiple_of(t, 16), 16)
        total = s0[z, here].astype(F32)
        for j in range(3):
            total = total + r1[j, here].astype(F32)
        dn[here] = total

    out_dn = local(dn, d_out, 7)
    q4.wait_recv()
    k.drain()
    for copy in sent:
        copy.wait_send()
    for o in range(4):
        remote(rows.at[0, 0], rows.at[0, 0], 4 + o, sib).wait_send()
        remote(part.at[0, 0], r0.at[0], 8 + o, sib).wait_send()
        remote(mixs.at[0, 0], m0.at[0], 16 + o, sib).wait_send()
    for o in (1, 2, 3):
        remote(s0.at[0], r1.at[o - 1], 12 + o, sib).wait_send()
    for copy in (out_mix, out_wg, out_wd, out_dn):
        copy.wait()


def ffn(n2, OG, WG, WD, wq):
    outs = [
        sds((TOK, D), F32),
        sds((4, TOK, D), BF16),
        sds((2, 4, 2, TOK, 2 * FS), BF16),
        sds((2, 4, 2, 80, 1024), BF16),
        sds((2, 4, 2, 4, 2, 16, 2048), BF16),
    ]
    scratch = [
        pltpu.VMEM((4, 2, TOK, D), BF16),
        pltpu.VMEM((4, 2, TOK, D), BF16),
        pltpu.VMEM((2, 4, 2, 8, 16, 2 * FS), BF16),
        pltpu.VMEM((2, 4, 2, 80, 1024), BF16),
        pltpu.VMEM((FS, D), BF16),
        pltpu.VMEM((8 * TOK, 2 * FS), BF16),
        pltpu.VMEM((8 * TOK, FS), BF16),
        pltpu.VMEM((256, FS), F32),
        pltpu.VMEM((4, 2, TOK, D), BF16),
        pltpu.VMEM((4, 2, TOK, D), BF16),
        pltpu.VMEM((4, TOK, D), BF16),
        pltpu.VMEM((4, TOK, D), BF16),
        pltpu.VMEM((3, TOK, D), BF16),
        pltpu.VMEM((4, TOK, D), BF16),
        pltpu.VMEM((2, 4, 2, TOK, 2 * FS), BF16),
        pltpu.VMEM((FS, D), F32),
        pltpu.VMEM((2, 4, 2, 80, 1024), BF16),
        pltpu.VMEM((TOK, D), F32),
        pltpu.VMEM((16, 2048), BF16),
        pltpu.SemaphoreType.DMA((20,)),
        pltpu.SemaphoreType.DMA((20,)),
        pltpu.SemaphoreType.DMA((8,)),
        pltpu.SemaphoreType.DMA((16,)),
        pltpu.SemaphoreType.DMA((16,)),
        pltpu.SemaphoreType.DMA((1,)),
    ]
    return pl.pallas_call(
        ffn_body,
        out_shape=outs,
        in_specs=[ANY] * 5,
        out_specs=[ANY] * 5,
        scratch_shapes=scratch,
        name="ffn",
        compiler_params=pltpu.CompilerParams(
            collective_id=1, has_side_effects=True, vmem_limit_bytes=60 << 20
        ),
    )(n2, OG, WG, WD, wq)


def back_body(*refs):
    (DN, X_IN, OG_IN, RESID, ATT, PT, LSE, WQ, WO, KV, mix_part, dwg, dwd, NA) = refs[:14]
    (BIAS, ROPE, GAINS, QKGAIN) = refs[14:18]
    (IN_GRAD, MIXED, GWG, GWD, GQ, GO, SMALL) = refs[18:25]
    (dn, xv, ogv, resid, pt, lse, in_grad, mixed, kvs, bias, qts, qns, dts, dns, dqt, dpt, datt, dres) = refs[25:43]
    (kpart, k0, k1, ks1, k2, kres, w2, wo2, low2, att2, do, dp, dpm, na2, dqm, mix1) = refs[43:59]
    (rope, gains, qkgain) = refs[59:62]
    scr = list(refs[62:])
    parts = []
    for shapes in PLANE_SHAPES + O_SHAPES:
        n = 2 * len(shapes)
        parts.append(scr[:n])
        scr = scr[n:]
    vec, vrecv, ssem, rsem, lsem = scr
    p = Place()
    k = Links(ssem, rsem, lsem)
    yl, z, c = p.yl, p.z, p.c
    m = z * 2 + c
    sib = p.step("c", 1)
    yl_partner = p.at(y=p.yh * 2 + 1 - yl)
    get = {
        "dn": k.local(DN, dn),
        "x": k.local(X_IN, xv),
        "og": k.local(OG_IN, ogv),
        "resid": k.local(RESID, resid),
        "att": k.local(ATT, att2.at[0]),
        "pt": k.local(PT, pt),
        "lse": k.local(LSE, lse),
        "kv": k.local(KV, kvs),
        "mix": k.local(mix_part.at[z], mix1.at[3]),
        "bias": k.local(BIAS, bias),
        "rope": k.local(ROPE, rope),
        "gains": k.local(GAINS, gains),
        "qkgain": k.local(QKGAIN, qkgain),
    }
    partners = [p.step(a, j) for a in "xyz" for j in (1, 2, 3)]
    partners += [p.at(z=(z + j) % 4, c=1 - c) for j in range(4)]
    slab_to, slab_from = slab_target(p), slab_source(p)
    own_slab = same(p, slab_to)
    greet_plane(p, partners, slab_to, slab_from, own_slab)
    plane = [
        staged_reduce(p, k, dwg, wg_stages(0), parts[0], 16),
        staged_reduce(p, k, dwg, wg_stages(1), parts[1], 16),
        staged_reduce(p, k, dwd, wd_stages(0), parts[2], 16),
        staged_reduce(p, k, dwd, wd_stages(1), parts[3], 16),
    ]
    for i in (0, 1, 3):
        next(plane[i])
    pair_att = k.send(ATT, att2.at[1], sib)
    mixing = [k.send(mix_part.at[p.pos("z", j)], mix1.at[j - 1], p.step("z", j)) for j in (1, 2, 3)]
    get_w = [k.local(WO.at[0, t], wo2.at[t]) for t in range(2)]
    for name in ("pt", "rope", "qkgain"):
        get[name].wait()
    cos, sin = rope[0], rope[1]
    qgain, kgain = qkgain[:HEAD], qkgain[HEAD:]

    @pl.loop(0, KV_HEADS)
    def _(g):
        for mm, unit in enumerate(query_units(pt, g, cos, sin, qgain)):
            qts[g, mm] = unit.astype(BF16)
            qns[g, mm] = unit.T.astype(BF16)

    for name in ("dn", "og", "resid", "gains"):
        get[name].wait()
    value = resid[...]
    scale_two = rms_scale(value)
    norm_two = value * scale_two
    d_resid = ogv[...].astype(F32) + norm_back(dn[...], norm_two, scale_two, gains[1:2, :])
    dres[...] = d_resid
    low2[0] = d_resid.astype(BF16)
    pair_low = k.send(low2.at[0], low2.at[1], sib)
    for t in range(8):
        get_w[t].wait()
        term = dot(low2[0, :, t * 256 : (t + 1) * 256], wo2[t % 2].reshape(256, QD))
        datt[...] = term if t == 0 else datt[...] + term
        if t < 6:
            get_w.append(k.local(WO.at[(t + 2) // 4, (t + 2) % 4], wo2.at[t % 2]))
    for g in range(KV_HEADS):
        tiles = []
        for t in range(2):
            at = (g * GROUP + 2 * t) * HEAD
            both = low(datt[:, at : at + 128]).T
            tiles.append(swap(both[:HEAD], both[HEAD:]))
        for mm in range(MICRO):
            none = jnp.zeros((HEAD, 256), F32)
            unit = jnp.concatenate([none, jnp.concatenate([tiles[0][mm], tiles[1][mm]], axis=1)], axis=0)
            dts[g, mm] = unit.astype(BF16)
            dns[g, mm] = unit.T.astype(BF16)
    get["kv"].wait()
    get["lse"].wait()
    get["bias"].wait()

    @pl.loop(0, 2 * KV_HEADS)
    def _(u):
        g, mm = u // 2, u % 2
        kv = unit_kv(kvs, mm, g)
        score = jnp.minimum(dot(kv, qts[g, mm]), unit_bias(bias, mm))
        again = jnp.exp(score - lse[u, 0:1, :])
        d_probs = dot(kv, dts[g, mm])
        inner = jnp.sum(again * d_probs, axis=0, keepdims=True)
        d_scores = (again * (d_probs - inner)).astype(BF16)
        d_kv = dot(d_scores, qns[g, mm]) + dot(again.astype(BF16), dns[g, mm])
        cols = pl.ds(pl.multiple_of(g * 128, 128), 128)
        kpart[mm, :, :, :, :, cols] = d_kv.astype(BF16).reshape(2, 4, 2, ROWS, 128)
        dqt[g, mm] = dot_rows(kv, d_scores)[:HEAD] * (HEAD ** -0.5)

    core = k.send(kpart.at[:, :, :, 1 - c], k0, sib)
    core.wait_recv()

    @pl.loop(0, 4)
    def _(zz):
        for a in range(2):
            for b in range(2):
                k0[a, b, zz] = (kpart[a, b, zz, c].astype(F32) + k0[a, b, zz].astype(F32)).astype(BF16)

    ring = [k.send(k0.at[:, :, p.pos("z", j)], k1.at[j - 1], p.step("z", j)) for j in (1, 2, 3)]

    get["att"].wait()
    pair_att.wait_recv()
    pair_low.wait_recv()
    att_cols = pl.ds(pl.multiple_of(c * 640, 128), 640)

    @pl.loop(0, 8)
    def _(t):
        cols = pl.ds(pl.multiple_of(t * 256, 256), 256)
        left = low2[:, :, cols].reshape(2 * TOK, 256)
        right = att2[:, :, att_cols].reshape(2 * TOK, 640)
        do[t // 4, t % 4] = dot_rows(left, right).astype(BF16).reshape(2, 4, 32, 640)

    outward = [staged_reduce(p, k, do, o_stages(i), parts[6 + i], 16) for i in range(3)]
    next(outward[0])

    query_sum = jnp.zeros((HEAD, TOK), F32)
    for g in range(KV_HEADS):
        heads = []
        for t in range(2):
            cols = slice(t * 128, (t + 1) * 128)
            heads += list(swap(dqt[g, 0, :, cols], dqt[g, 1, :, cols]))
        for h in range(GROUP):
            at = (g * GROUP + h) * HEAD
            d_raw, term = head_back(pt[at : at + HEAD], heads[h], cos, sin, qgain)
            query_sum = query_sum + term
            dpt[at : at + HEAD] = d_raw

    for copy in ring:
        copy.wait_recv()
    for a in range(2):
        for b in range(2):
            total = k0[a, b, z].astype(F32)
            for j in range(3):
                total = total + k1[j, a, b].astype(F32)
            ks1[a, b] = total.astype(BF16)
    across = k.send(ks1.at[:, 1 - yl], k2, yl_partner)
    across.wait_recv()
    next(plane[2])
    for a in range(2):
        kres[pl.ds(a * ROWS, ROWS)] = ks1[a, yl].astype(F32) + k2[a].astype(F32)
    key_sum = jnp.zeros((HEAD, TOK), F32)
    for g in range(KV_HEADS):
        both = kres[:, g * 128 : (g + 1) * 128].T
        at = QD + g * HEAD
        d_raw, term = head_back(pt[at : at + HEAD], both[:HEAD], cos, sin, kgain)
        key_sum = key_sum + term
        dpt[at : at + HEAD] = d_raw
        dpt[at + KD : at + KD + HEAD] = both[HEAD:]
    get_q = [k.local(WQ.at[0, t], w2.at[t]) for t in range(2)]
    get_n = [k.local(NA.at[:, :, :, pl.ds(t * 256, 256)], na2.at[t]) for t in range(2)]
    for t in range(8):
        block = jnp.concatenate([dpt[t * 240 : (t + 1) * 240], jnp.zeros((16, TOK), F32)], axis=0)
        dp[t] = block.T.astype(BF16)
    members = []
    for dz in range(4):
        for dc in range(2):
            zz, cc = (z + dz) % 4, (c + dc) % 2
            src = dp.at[zz * 2 + cc]
            if dz == 0 and dc == 0:
                own_dp = k.local(src, dpm.at[z, c])
            else:
                members.append(k.send(src, dpm.at[z, c], p.at(z=zz, c=cc)))
    sums = jnp.concatenate(
        [jnp.sum(query_sum.T, axis=0, keepdims=True), jnp.sum(key_sum.T, axis=0, keepdims=True)], axis=1
    )
    vec[0] = jnp.broadcast_to(sums, (8, 128))
    small = small_reduce(p, k, vec, vrecv)
    next(small)
    next(outward[1])
    next(outward[2])
    for i in (0, 1, 3):
        next(plane[i])
    own_dp.wait()
    for copy in members:
        copy.wait_recv()
    for t in range(8):
        get_n[t].wait()
        total = dot_rows(na2[t % 2].reshape(8 * TOK, 256), dpm[...].reshape(8 * TOK, 256))
        dqm[t // 4, t % 4] = total.astype(BF16).reshape(2, TOK, 256)
        if t < 6:
            get_n.append(k.local(NA.at[:, :, :, pl.ds((t + 2) * 256, 256)], na2.at[t % 2]))
    inward = [staged_reduce(p, k, dqm, q_stages(i), parts[4 + i], 16) for i in range(2)]
    for step in inward:
        next(step)
    for step in outward:
        next(step)
    next(small)
    for t in range(8):
        get_q[t].wait()
        w = w2[t % 2].reshape(256, 2048)
        left = jnp.concatenate([dp[i] for i in range(8)], axis=1)
        in_grad[:, t * 256 : (t + 1) * 256] = dot_last(left, w)
        if t < 6:
            get_q.append(k.local(WQ.at[(t + 2) // 4, (t + 2) % 4], w2.at[t % 2]))
    next(plane[2])
    for step in inward:
        next(step)
    next(small)
    for step in outward:
        next(step)
    get["x"].wait()
    hidden = xv[...].astype(F32)
    scale_one = rms_scale(hidden)
    in_grad[...] = dres[...] + norm_back(in_grad[...], hidden * scale_one, scale_one, gains[0:1, :])
    keep = [k.local(in_grad, IN_GRAD)]
    for step in plane:
        next(step, None)
    next(small)

    last = []

    def to_owners(total, dst):
        for dz in range(4):
            for dc in range(2):
                zz, cc = (z + dz) % 4, (c + dc) % 2
                src = total.at[pl.ds(pl.multiple_of((zz * 2 + cc) * 16, 16), 16)]
                if dz == 0 and dc == 0:
                    keep.append(k.local(src, dst))
                else:
                    last.append(k.send(src, dst, p.at(z=zz, c=cc)))

    for half in range(2):
        to_owners(parts[half][-1], GWG.at[:, pl.ds(pl.multiple_of(half * FF + m * FS, 128), FS)])
    slabs = [
        Slab(k, parts[2 + half][-1], GWD.at[:, pl.ds(half * 512, 512)], slab_from, own_slab) for half in range(2)
    ]
    for slab in slabs:
        slab.start()

    get["mix"].wait()
    for copy in mixing:
        copy.wait_recv()

    @pl.loop(0, TOK, step=16)
    def _(t):
        at = pl.ds(pl.multiple_of(t, 16), 16)
        total = resid[at]
        for j in range(4):
            total = total + mix1[j, at].astype(F32)
        mixed[at] = total.astype(BF16)

    keep.append(k.local(mixed, MIXED))
    for step in inward:
        next(step, None)
    for half in range(2):
        to_owners(parts[4 + half][-1], GQ.at[:, pl.ds(pl.multiple_of(m * 256 + half * 128, 128), 128)])
    for i, step in enumerate(outward):
        next(step, None)
        total = parts[6 + i][-1]
        dst = GO.at[c, :, pl.ds(*O_PARTS[i])]
        keep.append(k.local(total.at[pl.ds(pl.multiple_of(c * 16, 16), 16)], dst))
        last.append(k.send(total.at[pl.ds(pl.multiple_of((1 - c) * 16, 16), 16)], dst, sib))
    next(small, None)
    keep.append(k.local(vec.at[4], SMALL))
    for copy in keep:
        copy.wait()
    for copy in last:
        copy.wait_recv()
    for slab in slabs:
        slab.wait_recv()
        slab.wait_send()
    k.drain()


def head_back(raw, grad, cos, sin, gain):
    scale = head_scale(raw)
    normed = raw * scale
    d_head = grad * cos + half_back(grad * sin)
    scaled = d_head * gain
    inner = jnp.mean(scaled * normed, axis=0, keepdims=True)
    return scale * (scaled - normed * inner), d_head * normed


def back(*args):
    w = 2 * KD
    outs = [
        sds((TOK, D), F32),
        sds((TOK, D), BF16),
        sds((16, 2 * FF), BF16),
        sds((80, 1024), BF16),
        sds((16, 2048), BF16),
        sds((2, 16, 640), BF16),
        sds((8, 128), F32),
    ]
    scratch = [
        pltpu.VMEM((TOK, D), F32),
        pltpu.VMEM((TOK, D), BF16),
        pltpu.VMEM((TOK, D), BF16),
        pltpu.VMEM((TOK, D), F32),
        pltpu.VMEM((QKV, TOK), F32),
        pltpu.VMEM((2 * KV_HEADS, 8, 256), F32),
        pltpu.VMEM((TOK, D), F32),
        pltpu.VMEM((TOK, D), BF16),
        pltpu.VMEM((2, 2, 4, 2, ROWS, w), BF16),
        pltpu.VMEM((2, SEQ, 128), F32),
        pltpu.VMEM((KV_HEADS, 2, 128, 256), BF16),
        pltpu.VMEM((KV_HEADS, 2, 256, 128), BF16),
        pltpu.VMEM((KV_HEADS, 2, 128, 256), BF16),
        pltpu.VMEM((KV_HEADS, 2, 256, 128), BF16),
        pltpu.VMEM((KV_HEADS, 2, HEAD, 256), F32),
        pltpu.VMEM((QKV, TOK), F32),
        pltpu.VMEM((TOK, QD), F32),
        pltpu.VMEM((TOK, D), F32),
        pltpu.VMEM((2, 2, 4, 2, ROWS, w), BF16),
        pltpu.VMEM((2, 2, 4, ROWS, w), BF16),
        pltpu.VMEM((3, 2, 2, ROWS, w), BF16),
        pltpu.VMEM((2, 2, ROWS, w), BF16),
        pltpu.VMEM((2, ROWS, w), BF16),
        pltpu.VMEM((TOK, w), F32),
        pltpu.VMEM((2, 2, 4, 2, 16, 2048), BF16),
        pltpu.VMEM((2, 2, 4, 2, 16, QD), BF16),
        pltpu.VMEM((2, TOK, D), BF16),
        pltpu.VMEM((2, TOK, QD), BF16),
        pltpu.VMEM((2, 4, 2, 4, 32, 640), BF16),
        pltpu.VMEM((8, TOK, 256), BF16),
        pltpu.VMEM((4, 2, TOK, 256), BF16),
        pltpu.VMEM((2, 4, 2, TOK, 256), BF16),
        pltpu.VMEM((2, 4, 2, TOK, 256), BF16),
        pltpu.VMEM((4, TOK, D), BF16),
        pltpu.VMEM((2, HEAD, TOK), F32),
        pltpu.VMEM((8, D), F32),
        pltpu.VMEM((2 * HEAD, 128), F32),
    ]
    for shapes in PLANE_SHAPES + O_SHAPES:
        scratch += staged_scratch(shapes)
    scratch += [
        pltpu.VMEM((5, 8, 128), F32),
        pltpu.VMEM((4, 3, 8, 128), F32),
        pltpu.SemaphoreType.DMA((130,)),
        pltpu.SemaphoreType.DMA((130,)),
        pltpu.SemaphoreType.DMA((30,)),
    ]
    return pl.pallas_call(
        back_body,
        out_shape=outs,
        in_specs=[ANY] * 18,
        out_specs=[ANY] * 7,
        scratch_shapes=scratch,
        name="back",
        compiler_params=pltpu.CompilerParams(
            collective_id=2, has_side_effects=True, vmem_limit_bytes=60 << 20
        ),
    )(*args)


def finish_body(*refs):
    IN_GRAD, MIXED, GWG, GWD, GQ, GO, SUMS, WG, WQ, g1, g2 = refs[:11]
    in_out, mixed_out, Q, O, G, DOWN, ATTN, FFN, QG, KG = refs[11:21]
    (gwg, gwd, gq, go, sums, wg, wq, q, o, g, down, attn, ffn_, qg, kg, ing, mix, sem) = refs[21:]
    used = []

    def copy(src, dst):
        out = pltpu.make_async_copy(src, dst, sem.at[len(used)])
        out.start()
        used.append(out)
        return out

    rows = [copy(IN_GRAD, ing), copy(MIXED, mix)]
    through = []
    got = [copy(a, b) for a, b in ((GQ, gq), (WQ, wq), (GO, go), (SUMS, sums), (GWD, gwd), (GWG, gwg), (WG, wg))]
    for one in got[:5]:
        one.wait()
    for one, (src, dst) in zip(rows, ((ing, in_out), (mix, mixed_out))):
        one.wait()
        through.append(copy(src, dst))
    wide = gq[...].astype(F32)
    lane = lax.broadcasted_iota(jnp.int32, (16, QKV), 1)
    total = jnp.zeros((16, QKV), F32)
    for i in range(8):
        piece = jnp.concatenate([wide[:, i * 256 : (i + 1) * 256], jnp.zeros((16, QKV - 256), F32)], axis=1)
        here = (lane >= i * 240) & (lane < (i + 1) * 240)
        total = jnp.where(here, pltpu.roll(piece, 240 * i, 1) if i else piece, total)
    q[...] = total
    through.append(copy(q, Q))
    o[...] = jnp.concatenate([go[0].astype(F32), go[1].astype(F32)], axis=1)
    through.append(copy(o, O))
    slab = gwd[...].astype(F32)
    down[...] = jnp.concatenate([slab[:40], slab[40:]], axis=1)
    through.append(copy(down, DOWN))
    attn[...] = flat(jnp.sum(wq[...].astype(F32) * total, axis=1, keepdims=True)) / g1[...].astype(F32)
    through.append(copy(attn, ATTN))
    qg[...] = sums[0:1, :HEAD]
    kg[...] = pltpu.roll(sums[...], HEAD, 1)[0:1, :HEAD]
    through += [copy(qg, QG), copy(kg, KG)]
    for one in got[5:]:
        one.wait()
    grown = gwg[...].astype(F32)
    g[...] = grown
    through.append(copy(g, G))
    ffn_[...] = flat(jnp.sum(wg[...].astype(F32) * grown, axis=1, keepdims=True)) / g2[...].astype(F32)
    through.append(copy(ffn_, FFN))
    for one in through:
        one.wait()


def flat(col):
    n = col.shape[0]
    place = lax.broadcasted_iota(jnp.int32, (n, n), 0) == lax.broadcasted_iota(jnp.int32, (n, n), 1)
    return jnp.sum(jnp.where(place, jnp.broadcast_to(col, (n, n)), 0.0), axis=0, keepdims=True)


def finish(*args):
    outs = [
        sds((TOK, D), F32),
        sds((TOK, D), BF16),
        sds((16, QKV), F32),
        sds((16, QD), F32),
        sds((16, 2 * FF), F32),
        sds((40, D), F32),
        sds((1, 16), F32),
        sds((1, 16), F32),
        sds((1, HEAD), F32),
        sds((1, HEAD), F32),
    ]
    ins = [(16, 2 * FF), (80, 1024), (16, 2048), (2, 16, 640), (8, 128), (16, 2 * FF), (16, QKV)]
    scratch = [pltpu.VMEM(a, F32 if a == (8, 128) else BF16) for a in ins]
    scratch += [pltpu.VMEM(a.shape, a.dtype) for a in outs[2:] + outs[:2]]
    return pl.pallas_call(
        finish_body,
        out_shape=outs,
        in_specs=[ANY] * 9 + [VMEM] * 2,
        out_specs=[ANY] * 10,
        scratch_shapes=scratch + [pltpu.SemaphoreType.DMA((19,))],
        name="finish",
        compiler_params=pltpu.CompilerParams(vmem_limit_bytes=60 << 20),
    )(*args)


def per_device(
    tokens,
    segment_ids,
    w_qkv,
    w_out,
    w_gate_up,
    w_down,
    attn_gain,
    ffn_gain,
    query_gain,
    key_gain,
    out_grad,
):
    g1, g2, g3, g4 = [a.reshape(1, -1) for a in (attn_gain, ffn_gain, query_gain, key_gain)]
    og_in = out_grad.reshape(TOK, D)
    x_in = tokens.reshape(TOK, D)
    (WO, WG, WD, OG, NA, KV, pt, lse, attended, resid, n2, wq_in, bias, rope, gain_rows, head_gains) = front(
        x_in, w_qkv, w_out.T, w_gate_up, w_down, og_in, segment_ids, g1, g2, g3, g4, rope_parts()
    )
    d_normed, mix_part, dwg, dwd, WQ = ffn(n2, OG, WG, WD, wq_in)
    in_grad, mixed, gwg, gwd, gq, go, sums = back(
        d_normed, x_in, og_in, resid, attended, pt, lse, WQ, WO, KV, mix_part, dwg, dwd, NA,
        bias, rope, gain_rows, head_gains,
    )
    outs = finish(in_grad, mixed, gwg, gwd, gq, go, sums, w_gate_up, w_qkv, g1, g2)
    return (
        outs[1].reshape(MICRO, ROWS, D),
        outs[0].reshape(MICRO, ROWS, D),
        outs[2],
        outs[3].T,
        outs[4],
        outs[5],
        outs[6].reshape(16),
        outs[7].reshape(16),
        outs[8].reshape(HEAD),
        outs[9].reshape(HEAD),
    )


def solution(mesh):
    return jax.shard_map(
        per_device,
        mesh=mesh,
        in_specs=(
            P(None, ("grp", "seq"), None),
            P(None, "grp"),
            P(("grp", "seq"), None),
            P(None, ("grp", "seq")),
            P(("grp", "seq"), None),
            P(("grp", "seq"), None),
            P(("grp", "seq")),
            P(("grp", "seq")),
            P(),
            P(),
            P(None, ("grp", "seq"), None),
        ),
        out_specs=(
            P(None, ("grp", "seq"), None),
            P(None, ("grp", "seq"), None),
            P(("grp", "seq"), None),
            P(None, ("grp", "seq")),
            P(("grp", "seq"), None),
            P(("grp", "seq"), None),
            P(("grp", "seq")),
            P(("grp", "seq")),
            P(),
            P(),
        ),
        check_vma=False,
    )
```

```python
import jax
import jax.numpy as jnp
import numpy as np
from jax import lax
from jax.experimental import pallas as pl
from jax.experimental.pallas import tpu as pltpu
from jax.sharding import PartitionSpec as P

Q_HEADS = 20
KV_HEADS = 5
GROUP = 4
HEAD = 64
D = 2048
FF = 5120
QD = 1280
KD = 320
QKV = 1920
SEQ = 1024
MICRO = 2
ROWS = 64
TOK = 128
FS = 640
EPS = 1e-06
MESH = pl.DeviceIdType.MESH
F32 = jnp.float32
BF16 = jnp.bfloat16
ANY = pl.BlockSpec(memory_space=pl.ANY)


class Place:
    def __init__(self):
        g = lax.axis_index("grp")
        s = lax.axis_index("seq")
        self.g, self.s = g, s
        self.yh, self.x = g // 4, g % 4
        self.yl, self.z, self.c = s // 8, (s // 2) % 4, s % 2
        self.y = self.yh * 2 + self.yl

    def at(self, x=None, y=None, z=None, c=None):
        x = self.x if x is None else x
        y = self.y if y is None else y
        z = self.z if z is None else z
        c = self.c if c is None else c
        return ((y // 2) * 4 + x, (y % 2) * 8 + z * 2 + c)

    def step(self, axis, k):
        if axis == "x":
            return self.at(x=(self.x + k) % 4)
        if axis == "y":
            return self.at(y=(self.y + k) % 4)
        if axis == "z":
            return self.at(z=(self.z + k) % 4)
        return self.at(c=1 - self.c)

    def pos(self, axis, k):
        return (getattr(self, axis) + k) % 4


class Links:
    def __init__(self, send_sems, recv_sems, local_sems):
        self.send_sems, self.recv_sems, self.local_sems = send_sems, recv_sems, local_sems
        self.received = 0
        self.free = {"send": list(range(send_sems.shape[0]))[::-1], "local": list(range(local_sems.shape[0]))[::-1]}
        self.sent = {}

    def plan(self, src, dst, to):
        i = self.received
        self.received += 1
        assert i < self.recv_sems.shape[0], i
        slot = self.free["send"].pop()
        copy = pltpu.make_async_remote_copy(
            src_ref=src,
            dst_ref=dst,
            send_sem=self.send_sems.at[slot],
            recv_sem=self.recv_sems.at[i],
            device_id=to,
            device_id_type=MESH,
        )
        self.sent[id(copy)] = (copy, slot)
        return copy

    def send(self, src, dst, to):
        copy = self.plan(src, dst, to)
        copy.start()
        return copy

    def local(self, src, dst):
        slot = self.free["local"].pop()
        copy = pltpu.make_async_copy(src, dst, self.local_sems.at[slot])
        copy.start()
        return Local(self, copy, slot)

    def settle(self, copies):
        for copy in copies:
            copy, slot = self.sent.pop(id(copy))
            copy.wait_send()
            self.free["send"].append(slot)

    def drain(self):
        self.settle([copy for copy, _ in list(self.sent.values())])


class Local:
    def __init__(self, links, copy, slot):
        self.links, self.copy, self.slot = links, copy, slot

    def wait(self):
        self.copy.wait()
        self.links.free["local"].append(self.slot)


def halves(ref):
    n = ref.shape[0] // 2
    return ref.at[pl.ds(0, n)], ref.at[pl.ds(n, n)]


class RingGather:
    def __init__(self, p, k, axis, block, src=None):
        self.p, self.k, self.axis, self.block = p, k, axis, block
        dst = block(p.pos(axis, 0))
        src = dst if src is None else src
        self.right = k.send(src, dst, p.step(axis, 1))
        self.left = k.send(src, dst, p.step(axis, 3))

    def from_before(self):
        self.right.wait_recv()
        half = halves(self.block(self.p.pos(self.axis, 3)))[0]
        self.far_right = self.k.send(half, half, self.p.step(self.axis, 1))

    def from_after(self):
        self.left.wait_recv()
        half = halves(self.block(self.p.pos(self.axis, 1)))[1]
        self.far_left = self.k.send(half, half, self.p.step(self.axis, 3))

    def hand_on(self):
        self.from_before()
        self.from_after()

    def wait(self):
        self.far_right.wait_recv()
        self.far_left.wait_recv()

    def copies(self):
        return [self.right, self.left, self.far_right, self.far_left]


def greet(partners):
    barrier = pltpu.get_barrier_semaphore()
    for to in partners:
        pl.semaphore_signal(barrier, inc=1, device_id=to, device_id_type=MESH)
    pl.semaphore_wait(barrier, len(partners))


def sds(shape, dtype):
    return jax.ShapeDtypeStruct(shape, dtype)


def rms_scale(values):
    return lax.rsqrt(jnp.mean(values * values, axis=-1, keepdims=True) + EPS)


def norm_back(upstream, normed, scale, gain):
    scaled = upstream * gain
    inner = jnp.mean(scaled * normed, axis=-1, keepdims=True)
    return scale * (scaled - normed * inner)


def dot(left, right):
    return jnp.dot(left, right, preferred_element_type=F32)


def dot_last(left, right):
    return lax.dot_general(left, right, (((1,), (1,)), ((), ())), preferred_element_type=F32)


def dot_rows(left, right):
    return lax.dot_general(left, right, (((0,), (0,)), ((), ())), preferred_element_type=F32)


def slab_target(p):
    return p.at(x=(p.z + p.x) % 4, y=(p.c + p.yh) % 2 * 2 + p.yl, z=p.g // 2, c=p.g % 2)


def slab_place(p, x=None, y=None):
    m = p.z * 2 + p.c
    if x is not None:
        return (x + 4 - m % 4) % 4
    return (y // 2 + 2 - m // 4) % 2


def slab_source(p):
    m = p.z * 2 + p.c
    return p.at(x=m % 4, y=(m // 4) * 2 + p.yl, z=slab_place(p, x=p.x), c=slab_place(p, y=p.y))


def same(p, to):
    return (to[0] == p.g) & (to[1] == p.s)


def greet_plane(p, partners, slab_to, slab_from, own_slab):
    barrier = pltpu.get_barrier_semaphore()
    for to in partners:
        pl.semaphore_signal(barrier, inc=1, device_id=to, device_id_type=MESH)

    @pl.when(jnp.logical_not(own_slab))
    def _():
        pl.semaphore_signal(barrier, inc=1, device_id=slab_to, device_id_type=MESH)
        pl.semaphore_signal(barrier, inc=1, device_id=slab_from, device_id_type=MESH)
        pl.semaphore_wait(barrier, len(partners) + 2)

    @pl.when(own_slab)
    def _():
        pl.semaphore_wait(barrier, len(partners))


class Slab:
    def __init__(self, k, src, dst, to, own):
        self.own, self.src, self.dst = own, src, dst
        self.far = k.plan(src, dst, to)
        k.sent.pop(id(self.far))
        self.near = pltpu.make_async_copy(src, dst, k.recv_sems.at[k.received - 1])

    def start(self):
        @pl.when(self.own)
        def _():
            self.near.start()

        @pl.when(jnp.logical_not(self.own))
        def _():
            self.far.start()

    def wait_recv(self):
        @pl.when(self.own)
        def _():
            self.near.wait()

        @pl.when(jnp.logical_not(self.own))
        def _():
            self.far.wait_recv()

    def wait_send(self):
        @pl.when(jnp.logical_not(self.own))
        def _():
            self.far.wait_send()


def add_blocks(dst, terms, chunk):
    lead, rows = dst.shape[:-2], dst.shape[-2]
    count = 1
    for n in lead:
        count *= n

    @pl.loop(0, count)
    def _(i):
        at = []
        rest = i
        for n in reversed(lead):
            at.insert(0, rest % n)
            rest = rest // n

        @pl.loop(0, rows, step=chunk)
        def _(t):
            here = (*at, pl.ds(pl.multiple_of(t, chunk), chunk))
            total = terms[0][here].astype(F32)
            for term in terms[1:]:
                total = total + term[here].astype(F32)
            dst[here] = total.astype(dst.dtype)


def staged_reduce(p, k, src, stages, scr, chunk):
    own = scr[0]
    cur = src
    for n, (axis, pick) in enumerate(stages):
        recv = scr[1] if n == 0 else scr[2 * n]
        if n == 0:
            mine = k.local(pick(src, p.pos(axis, 0)), own)
        ring = [k.send(pick(cur, p.pos(axis, j)), recv.at[j - 1], p.step(axis, j)) for j in (1, 2, 3)]
        yield
        if n == 0:
            mine.wait()
        for copy in ring:
            copy.wait_recv()
        total = own if n == 0 else scr[2 * n + 1]
        add_blocks(total, [own if n == 0 else pick(cur, p.pos(axis, 0))] + [recv.at[j] for j in range(3)], chunk)
        cur = total


def ring_reduce(p, k, src, stages, scr, chunk):
    own, recv, held, recv2, total = scr
    axis, pick = stages[0]
    before, after, far = recv.at[0], recv.at[1], recv.at[2]
    far_a, far_b = halves(pick(src, p.pos(axis, 2)))
    right_a, right_b = halves(pick(src, p.pos(axis, 1)))
    left_a, left_b = halves(pick(src, p.pos(axis, 3)))
    right, left = p.step(axis, 1), p.step(axis, 3)
    on_right = k.send(far_a, halves(far)[0], right)
    on_left = k.send(far_b, halves(far)[1], left)
    get = [k.local(right_a, halves(held)[0]), k.local(left_b, halves(held)[1])]
    mine = k.local(pick(src, p.pos(axis, 0)), own)
    yield
    near = [k.send(right_b, halves(before)[1], right), k.send(left_a, halves(after)[0], left)]
    for i, (copy, to, dst) in enumerate(((on_right, right, before), (on_left, left, after))):
        get[i].wait()
        copy.wait_recv()
        here = halves(held)[i]
        add_blocks(here, [here, halves(far)[i]], chunk)
        near.append(k.send(here, halves(dst)[i], to))
    yield
    mine.wait()
    for copy in near:
        copy.wait_recv()
    add_blocks(own, [own, before, after], chunk)
    axis, pick = stages[1]
    ring = [k.send(pick(own, p.pos(axis, j)), recv2.at[j - 1], p.step(axis, j)) for j in (1, 2, 3)]
    yield
    for copy in ring:
        copy.wait_recv()
    add_blocks(total, [pick(own, p.pos(axis, 0))] + [recv2.at[j] for j in range(3)], chunk)


def staged_scratch(shapes, held=False):
    out = [pltpu.VMEM(shapes[0], BF16), pltpu.VMEM((3, *shapes[0]), BF16)]
    if held:
        out.append(pltpu.VMEM(shapes[0], BF16))
    for n, shape in enumerate(shapes[1:]):
        out.append(pltpu.VMEM((3, *shape), BF16))
        out.append(pltpu.VMEM(shape, BF16))
    return out


EVERY = slice(None)


def wg_stages(half):
    cols = pl.ds(half * FS, FS)
    if half == 0:
        return [
            ("y", lambda r, i: r.at[i // 2, :, i % 2, :, cols]),
            ("x", lambda r, i: r.at[i]),
        ]
    return [
        ("x", lambda r, i: r.at[:, i, :, :, cols]),
        ("y", lambda r, i: r.at[i // 2, i % 2]),
    ]


def wd_stages(p, half):
    cols = pl.ds(half * 512, 512)
    if half == 0:
        return [
            ("y", lambda r, i: r.at[i % 2, :, slab_place(p, y=i), :, cols]),
            ("x", lambda r, i: r.at[slab_place(p, x=i)]),
        ]
    return [
        ("x", lambda r, i: r.at[:, slab_place(p, x=i), :, :, cols]),
        ("y", lambda r, i: r.at[i % 2, slab_place(p, y=i)]),
    ]


def q_stages(half):
    cols = pl.ds(half * 128, 128)
    if half == 0:
        return [
            ("y", lambda r, i: r.at[i // 2, :, i % 2, :, cols]),
            ("x", lambda r, i: r.at[i]),
        ]
    return [
        ("x", lambda r, i: r.at[:, i, :, :, cols]),
        ("y", lambda r, i: r.at[i // 2, i % 2]),
    ]


def o_stages(part):
    cols = pl.ds(*O_PARTS[part])
    if part == 0:
        return [
            ("x", lambda r, i: r.at[:, i, :, :, :, cols]),
            ("z", lambda r, i: r.at[:, :, i]),
            ("y", lambda r, i: r.at[i // 2, i % 2]),
        ]
    if part == 1:
        return [
            ("y", lambda r, i: r.at[i // 2, :, i % 2, :, :, cols]),
            ("x", lambda r, i: r.at[i]),
            ("z", lambda r, i: r.at[i]),
        ]
    return [
        ("z", lambda r, i: r.at[:, :, :, i, :, cols]),
        ("y", lambda r, i: r.at[i // 2, :, i % 2]),
        ("x", lambda r, i: r.at[i]),
    ]


O_PARTS = ((0, 256), (256, 128), (384, 256))
PLANE_SHAPES = [
    [(4, 128, FS), (128, FS)],
    [(2, 2, 128, FS), (128, FS)],
    [(4, 80, 512), (80, 512)],
    [(2, 2, 80, 512), (80, 512)],
    [(4, 128, 128), (128, 128)],
    [(2, 2, 128, 128), (128, 128)],
]
O_SHAPES = [
    [(2, 2, 4, 32, 256), (2, 2, 32, 256), (32, 256)],
    [(4, 4, 32, 128), (4, 32, 128), (32, 128)],
    [(2, 4, 2, 32, 256), (4, 32, 256), (32, 256)],
]


def small_reduce(p, k, vec, recv):
    for n, axis in enumerate("xyzc"):
        steps = (1,) if axis == "c" else (1, 2, 3)
        ring = [k.send(vec.at[n], recv.at[n, j - 1], p.step(axis, j)) for j in steps]
        yield
        for copy in ring:
            copy.wait_recv()
        total = vec[n]
        for j in range(len(steps)):
            total = total + recv[n, j]
        vec[n + 1] = total


def swap(a, b):
    left = lax.broadcasted_iota(jnp.int32, a.shape, 1) < ROWS
    return jnp.where(left, a, pltpu.roll(b, ROWS, 1)), jnp.where(left, pltpu.roll(a, ROWS, 1), b)


def head_scale(v):
    return lax.rsqrt(jnp.mean(v * v, axis=-2, keepdims=True) + EPS)


def half_turn(v):
    half = HEAD // 2
    return jnp.concatenate([-v[..., half:, :], v[..., :half, :]], axis=-2)


def half_back(v):
    half = HEAD // 2
    return jnp.concatenate([v[..., half:, :], -v[..., :half, :]], axis=-2)


def low(v):
    return v.astype(BF16).astype(F32)


def query_units(packed_t, g, cos, sin, gain):
    raw = packed_t[pl.ds(pl.multiple_of(g * 256, 256), 256)].reshape(GROUP, HEAD, TOK)
    head = raw * head_scale(raw) * gain
    turned = low(head * cos + half_turn(head) * sin) * (HEAD ** -0.5)
    a0, a1 = swap(turned[0], turned[1])
    b0, b1 = swap(turned[2], turned[3])
    none = jnp.zeros((HEAD, 256), F32)
    return [
        jnp.concatenate([jnp.concatenate([a, b], axis=1), none], axis=0) for a, b in ((a0, b0), (a1, b1))
    ]


def fill_bias(bias, seg, s):
    lane = lax.broadcasted_iota(jnp.int32, (128, 128), 1)
    query = lane % ROWS + s * ROWS
    around = pl.ds(pl.multiple_of((s // 2) * 128, 128), 128)
    for m in range(MICRO):
        ids = jnp.broadcast_to(seg[m : m + 1, around].astype(F32), (128, 128))
        turned = pltpu.roll(ids, ROWS, 1)
        ids = jnp.where((lane < ROWS) == (s % 2 == 0), ids, turned)
        ids = jnp.where(ids >= 0, ids, -2.0)

        @pl.loop(0, SEQ, step=128)
        def _(t):
            at = pl.ds(pl.multiple_of(t, 128), 128)
            key = lax.broadcasted_iota(jnp.int32, (128, 128), 0) + t
            keys = jnp.broadcast_to(seg[m : m + 1, at].astype(F32), (128, 128)).T
            ok = ((key <= query) & (keys == ids)) | (key == query)
            bias[m, at] = jnp.where(ok, 3e38, -1e30)


def rope_parts():
    inverse = 10000.0 ** (-(np.arange(HEAD) % (HEAD // 2)) / (HEAD // 2))
    begin = inverse[:, None] * (np.arange(128)[None, :] % 16 * ROWS)
    inside = inverse[:, None] * (np.arange(128)[None, :] % ROWS)
    return np.stack([np.cos(begin), np.sin(begin), np.cos(inside), np.sin(inside)]).astype(np.float32)


def rope_tables(parts, s):
    here = lax.broadcasted_iota(jnp.int32, (HEAD, 128), 1) == s
    c0 = jnp.sum(jnp.where(here, parts[0], 0.0), axis=1, keepdims=True)
    s0 = jnp.sum(jnp.where(here, parts[1], 0.0), axis=1, keepdims=True)
    return c0 * parts[2] - s0 * parts[3], s0 * parts[2] + c0 * parts[3]


def column(row):
    n = row.shape[1]
    place = lax.broadcasted_iota(jnp.int32, (n, n), 0) == lax.broadcasted_iota(jnp.int32, (n, n), 1)
    return jnp.sum(jnp.where(place, jnp.broadcast_to(row, (n, n)), 0.0), axis=1, keepdims=True)


def unit_bias(bias, m):
    half = bias[m]
    return jnp.concatenate([half, half], axis=1)


def unit_kv(KV, m, g):
    cols = pl.ds(pl.multiple_of(g * 128, 128), 128)
    return KV[m, :, :, :, :, cols].reshape(SEQ, 128)


def front_body(*refs):
    (x_in, w_qkv, wo, wg, w_down, og, seg, g1, g2, g3, g4, parts) = refs[:12]
    (WO, WG, WD, OG, NA, KV, PT, LSE, ATT, RESID, N2, WQIN, BIAS, ROPE, GAINS, QKGAIN) = refs[12:28]
    (wq, wd, ogv, gains_out, rope, qkgain) = refs[28:34]
    (xs, na, wqm, wos, pks, pk, pt, lse, att, resid, n2, kvl, kvs, bias, qts, ots) = refs[34:50]
    ssem, rsem, lsem = refs[50:]
    p = Place()
    k = Links(ssem, rsem, lsem)
    yh, x, yl, z, c = p.yh, p.x, p.yl, p.z, p.c
    m = z * 2 + c
    sib = p.step("c", 1)
    yl_partner = p.at(y=p.yh * 2 + 1 - yl)
    partners = [p.step(a, j) for a in "xyz" for j in (1, 2, 3)]
    partners += [p.at(z=(z + j) % 4, c=1 - c) for j in range(4)]
    slab_to, slab_from = slab_target(p), slab_source(p)
    own_slab = same(p, slab_to)

    spare = [column(row[...].astype(F32)) for row in (g1, g2)]
    wide = w_qkv[...].astype(F32)
    lane = lax.broadcasted_iota(jnp.int32, (16, 256), 1)
    rest = jnp.where(lane == 240, spare[0], jnp.where(lane == 241, spare[1], 0.0))
    for i in range(8):
        turned = pltpu.roll(wide, (QKV - 240 * i) % QKV, 1)[:, :256]
        wq[:, i * 256 : (i + 1) * 256] = jnp.where(lane < 240, turned, rest).astype(BF16)
    greet_plane(p, partners, slab_to, slab_from, own_slab)

    def spread(src_of, dst_of):
        far, near = [], None
        for dz in range(4):
            for dc in range(2):
                zz, cc = (z + dz) % 4, (c + dc) % 2
                src, dst = src_of(zz * 2 + cc), dst_of(m)
                if dz == 0 and dc == 0:
                    near = k.local(src, dst)
                else:
                    far.append(k.send(src, dst, p.at(z=zz, c=cc)))
        return near, far

    q0 = spread(
        lambda i: wq.at[:, pl.ds(pl.multiple_of(i * 256, 256), 256)], lambda i: wqm.at[yh, x, yl, i]
    )
    own_x = k.local(x_in, xs.at[z, c])
    get_og = k.local(og, ogv)
    xcore = {0: k.send(x_in, xs.at[z, c], sib)}
    own_wo = k.local(wo, wos.at[yh, x, yl, z, c])

    def wo_at(part, *at):
        return wos.at[(*at, EVERY, pl.ds((0, 512, 1024)[part], (512, 512, 256)[part]))]

    def wo_own(part):
        return wo.at[:, pl.ds((0, 512, 1024)[part], (512, 512, 256)[part])]

    o1 = []
    for j in (1, 2, 3):
        for part, axis in ((0, "z"), (1, "z"), (2, "x")):
            o1.append(k.send(wo_own(part), wo_at(part, yh, x, yl, z, c), p.step(axis, j)))
    g0 = [
        spread(
            lambda i: wg.at[:, pl.ds(pl.multiple_of(half * FF + i * FS, 128), FS)],
            lambda i: WG.at[yh, x, yl, i, :, pl.ds(half * FS, FS)],
        )
        for half in range(2)
    ]
    xring = RingGather(p, k, "z", lambda i: xs.at[i, c], x_in)

    def to_plane(blocks):
        return [k.send(b, b, p.step(axis, j)) for j in (1, 2, 3) for b, axis in blocks]

    ql, qh = pl.ds(0, 128), pl.ds(128, 128)
    lo, hi = pl.ds(0, FS), pl.ds(FS, FS)
    dlo, dhi = pl.ds(0, 512), pl.ds(512, 512)
    q0[0].wait()
    for copy in q0[1]:
        copy.wait_recv()
    q1 = to_plane(((wqm.at[yh, x, yl, :, :, ql], "x"), (wqm.at[yh, x, yl, :, :, qh], "y")))
    fill_bias(bias, seg, p.s)
    cos, sin = rope_tables(parts, p.s)
    rope[0], rope[1] = cos, sin
    qgain, kgain = column(g3[...].astype(F32)), column(g4[...].astype(F32))
    qkgain[...] = jnp.concatenate([jnp.broadcast_to(qgain, (HEAD, 128)), jnp.broadcast_to(kgain, (HEAD, 128))], axis=0)
    for copy in q1:
        copy.wait_recv()
    q2 = to_plane(((wqm.at[yh, :, yl, :, :, ql], "y"), (wqm.at[:, x, :, :, :, qh], "x")))
    for near, far in g0:
        near.wait()
        for copy in far:
            copy.wait_recv()
    plane = to_plane(((WG.at[yh, x, yl, :, :, lo], "x"), (WG.at[yh, x, yl, :, :, hi], "y")))
    slab_rows = w_down[...].astype(F32)
    wd[...] = jnp.concatenate([slab_rows[:, :1024], slab_rows[:, 1024:]], axis=0).astype(BF16)
    slab = Slab(k, wd, WD.at[yl, z, c], slab_to, own_slab)
    slab.start()
    for copy in q2:
        copy.wait_recv()
    own_x.wait()
    own_wo.wait()
    pick = jnp.where(
        lax.broadcasted_iota(jnp.int32, (8, 128), 0) + 112 == lax.broadcasted_iota(jnp.int32, (8, 128), 1), 1.0, 0.0
    ).astype(BF16)
    gains_out[...] = dot_last(pick, wqm[:, :, :, :, :, pl.ds(128, 128)].reshape(D, 128))
    keep = [k.local(wq, WQIN), k.local(bias, BIAS), k.local(rope, ROPE), k.local(gains_out, GAINS), k.local(qkgain, QKGAIN)]
    k.settle(q0[1] + q1)
    xring.hand_on()
    for o in (1, 3):
        src = xs.at[(z + o) % 4, c]
        xcore[o] = k.send(src, src, sib)
    packs = []
    for o in (0, 1, 3, 2):
        zz = (z + o) % 4
        if o == 2:
            xring.wait()
            xcore[o] = k.send(xs.at[zz, c], xs.at[zz, c], sib)
        xcore[o].wait_recv()
        rows = xs[zz].reshape(256, D).astype(F32)
        normed = (rows * rms_scale(rows) * gains_out[0:1, :]).astype(BF16)
        na[zz] = normed.reshape(2, TOK, D)
        pks[zz] = dot(normed, wqm[...].reshape(D, 256)).astype(BF16).reshape(2, TOK, 256)
        if o:
            packs.append(k.send(pks.at[zz, c], pk.at[m], p.at(z=zz)))
        else:
            own_pk = k.local(pks.at[z, c], pk.at[m])
        packs.append(k.send(pks.at[zz, 1 - c], pk.at[m], p.at(z=zz, c=1 - c)))
        if o == 1:
            for copy in o1:
                copy.wait_recv()
            o2 = to_plane(
                (
                    (wo_at(0, yh, x, yl, EVERY, c), "y"),
                    (wo_at(1, yh, x, yl, EVERY, c), "x"),
                    (wo_at(2, yh, EVERY, yl, z, c), "y"),
                ),
            )
    slab.wait_recv()
    held = WD.at[yl, slab_place(p, x=x), slab_place(p, y=p.y)]
    plane += to_plane(((held.at[:, dlo], "x"), (held.at[:, dhi], "y")))
    for copy in o2:
        copy.wait_recv()
    o3 = [
        RingGather(p, k, "x", lambda i: wo_at(0, EVERY, i, EVERY, EVERY, c)),
        RingGather(p, k, "y", lambda i: wo_at(1, i // 2, EVERY, i % 2, EVERY, c)),
    ]
    keep.append(k.local(na, NA))
    k.settle(q2 + o1 + [copy for _, far in g0 for copy in far])
    own_pk.wait()
    for copy in packs:
        copy.wait_recv()
    for i8 in range(8):
        pt[i8 * 240 : (i8 + 1) * 240] = pk[i8].astype(F32).T[:240]

    @pl.loop(0, KV_HEADS)
    def _(g):
        raw = pt[pl.ds(pl.multiple_of(QD + g * HEAD, HEAD), HEAD)]
        head = raw * head_scale(raw) * kgain
        key = head * cos + half_turn(head) * sin
        value = pt[pl.ds(pl.multiple_of(QD + KD + g * HEAD, HEAD), HEAD)]
        both = jnp.concatenate([key, value], axis=0).T.astype(BF16)
        cols = pl.ds(pl.multiple_of(g * 128, 128), 128)
        for mm in range(MICRO):
            kvl[mm, :, cols] = both[mm * ROWS : (mm + 1) * ROWS]

    own_kv = k.local(kvl, kvs.at[:, yl, z, c])
    across = k.send(kvl, kvs.at[:, yl, z, c], yl_partner)
    ring = [k.send(kvl, kvs.at[:, yl, z, c], p.step("z", j)) for j in (1, 2, 3)]
    keep.append(k.local(pt, PT))

    @pl.loop(0, KV_HEADS)
    def _(g):
        for mm, unit in enumerate(query_units(pt, g, cos, sin, qgain)):
            qts[g, mm] = unit.astype(BF16)

    across.wait_recv()
    src = kvs.at[:, 1 - yl, z, c]
    ring += [k.send(src, src, p.step("z", j)) for j in (1, 2, 3)]
    own_kv.wait()
    for ring4 in o3:
        ring4.hand_on()
    for copy in plane:
        copy.wait_recv()
    k.settle(packs + plane)
    plane2 = [
        RingGather(p, k, "x", lambda i: WG.at[:, i, :, :, :, hi]),
        RingGather(p, k, "y", lambda i: WD.at[i % 2, :, slab_place(p, y=i), :, dlo]),
        RingGather(p, k, "x", lambda i: WD.at[:, slab_place(p, x=i), :, :, dhi]),
        RingGather(p, k, "y", lambda i: WG.at[i // 2, :, i % 2, :, :, lo]),
    ]
    oc = []
    for src in (
        wo_at(0, EVERY, x, EVERY, EVERY, c),
        wo_at(1, yh, EVERY, yl, EVERY, c),
        wo_at(2, EVERY, EVERY, EVERY, z, c),
    ):
        oc.append(k.send(src, src, sib))
    for copy in ring:
        copy.wait_recv()
    src = kvs.at[:, :, :, c]
    kvc = k.send(src, src, sib)
    o3.append(RingGather(p, k, "z", lambda i: wo_at(2, EVERY, EVERY, EVERY, i, c)))
    get_og.wait()
    keep.append(k.local(ogv, OG.at[z, c]))
    rows = RingGather(p, k, "z", lambda i: OG.at[i, c], ogv)
    last = [k.send(ogv, OG.at[z, c], sib)]
    k.settle(o2 + xring.copies() + list(xcore.values()))
    kvc.wait_recv()
    keep.append(k.local(kvs, KV))

    @pl.loop(0, 2 * KV_HEADS)
    def _(u):
        g, mm = u // 2, u % 2
        kv = unit_kv(kvs, mm, g)
        score = jnp.minimum(dot(kv, qts[g, mm]), unit_bias(bias, mm))
        peak = jnp.max(score, axis=0, keepdims=True)
        raised = jnp.exp(score - peak)
        total = jnp.sum(raised, axis=0, keepdims=True)
        probs = (raised * (1.0 / total)).astype(BF16)
        ots[g, mm] = dot_rows(kv, probs)[HEAD:]
        lse[u] = jnp.broadcast_to(peak + jnp.log(total), (8, 256))

    for g in range(KV_HEADS):
        for t in range(2):
            cols = slice(t * 128, (t + 1) * 128)
            a, b = swap(ots[g, 0, :, cols], ots[g, 1, :, cols])
            at = (g * GROUP + 2 * t) * HEAD
            att[:, at : at + 128] = jnp.concatenate([a, b], axis=0).T.astype(BF16)
    keep += [k.local(lse, LSE), k.local(att, ATT)]
    plane2[0].hand_on()
    plane2[1].hand_on()
    o3[2].hand_on()
    for axis, ring4 in zip("xyz", o3):
        ring4.wait()
        for j in (1, 2, 3):
            src = ring4.block(p.pos(axis, j))
            oc.append(k.send(src, src, sib))
    rows.hand_on()
    for copy in oc:
        copy.wait_recv()
    keep.append(k.local(wos, WO))

    @pl.loop(0, 8)
    def _(t):
        w = wos[t // 4, t % 4].reshape(256, QD)
        cols = pl.ds(pl.multiple_of(t * 256, 256), 256)
        resid[:, cols] = xs[z, c, :, cols].astype(F32) + dot_last(att[...], w)

    plane2[2].hand_on()
    plane2[3].hand_on()
    value = resid[...]
    n2[...] = (value * rms_scale(value) * gains_out[1:2, :]).astype(BF16)
    keep += [k.local(resid, RESID), k.local(n2, N2)]
    rows.wait()
    for j in (1, 2, 3):
        src = OG.at[p.pos("z", j), c]
        last.append(k.send(src, src, sib))
    for ring4 in plane2:
        ring4.wait()
    for copy in last:
        copy.wait_recv()
    for copy in keep:
        copy.wait()
    slab.wait_send()
    k.drain()


VMEM = pl.BlockSpec(memory_space=pltpu.VMEM)


def front(*args):
    hbm = [
        sds((2, 4, 2, 4, 2, 16, QD), BF16),
        sds((2, 4, 2, 8, 16, 2 * FS), BF16),
        sds((2, 4, 2, 80, 1024), BF16),
        sds((4, 2, TOK, D), BF16),
        sds((4, 2, TOK, D), BF16),
        sds((2, 2, 4, 2, ROWS, 2 * KD), BF16),
        sds((QKV, TOK), F32),
        sds((2 * KV_HEADS, 8, 256), F32),
        sds((TOK, QD), BF16),
        sds((TOK, D), F32),
        sds((TOK, D), BF16),
        sds((16, 2048), BF16),
        sds((2, SEQ, 128), F32),
        sds((2, HEAD, TOK), F32),
        sds((8, D), F32),
        sds((2 * HEAD, 128), F32),
    ]
    scratch = [
        pltpu.VMEM((16, 2048), BF16),
        pltpu.VMEM((80, 1024), BF16),
        pltpu.VMEM((TOK, D), BF16),
        pltpu.VMEM((8, D), F32),
        pltpu.VMEM((2, HEAD, TOK), F32),
        pltpu.VMEM((2 * HEAD, 128), F32),
        pltpu.VMEM((4, 2, TOK, D), BF16),
        pltpu.VMEM((4, 2, TOK, D), BF16),
        pltpu.VMEM((2, 4, 2, 8, 16, 256), BF16),
        pltpu.VMEM((2, 4, 2, 4, 2, 16, QD), BF16),
        pltpu.VMEM((4, 2, TOK, 256), BF16),
        pltpu.VMEM((8, TOK, 256), BF16),
        pltpu.VMEM((QKV, TOK), F32),
        pltpu.VMEM((2 * KV_HEADS, 8, 256), F32),
        pltpu.VMEM((TOK, QD), BF16),
        pltpu.VMEM((TOK, D), F32),
        pltpu.VMEM((TOK, D), BF16),
        pltpu.VMEM((2, ROWS, 2 * KD), BF16),
        pltpu.VMEM((2, 2, 4, 2, ROWS, 2 * KD), BF16),
        pltpu.VMEM((2, SEQ, 128), F32),
        pltpu.VMEM((KV_HEADS, 2, 128, 256), BF16),
        pltpu.VMEM((KV_HEADS, 2, HEAD, 256), F32),
        pltpu.SemaphoreType.DMA((84,)),
        pltpu.SemaphoreType.DMA((136,)),
        pltpu.SemaphoreType.DMA((26,)),
    ]
    return pl.pallas_call(
        front_body,
        out_shape=hbm,
        in_specs=[ANY, VMEM, VMEM, ANY, VMEM, ANY] + [VMEM] * 6,
        out_specs=[ANY] * len(hbm),
        scratch_shapes=scratch,
        name="front",
        compiler_params=pltpu.CompilerParams(
            collective_id=0, has_side_effects=True, vmem_limit_bytes=56 << 20
        ),
    )(*args)


def ffn_body(n2, OG, WG, WD, wq, d_out, mix_out, dwg_out, dwd_out, WQ, *scr):
    (rows, ogs, wgs, wd80, wds, dgu, inn, din, part, mixs, r0, s0, r1, m0, dwg, dwd32, dwd) = scr[:17]
    (dn, wqv, ssem, rsem, lsem, wsem, vsem, wlsem) = scr[17:]
    p = Place()
    k = Links(wsem, vsem, wlsem)
    yh, x, yl, z, c = p.yh, p.x, p.yl, p.z, p.c
    sib = p.step("c", 1)
    greet([p.step(a, j) for a in "xyz" for j in (1, 2, 3)] + [sib])

    def remote(src, dst, i, to):
        return pltpu.make_async_remote_copy(
            src_ref=src,
            dst_ref=dst,
            send_sem=ssem.at[i],
            recv_sem=rsem.at[i],
            device_id=to,
            device_id_type=MESH,
        )

    def local(src, dst, i):
        copy = pltpu.make_async_copy(src, dst, lsem.at[i])
        copy.start()
        return copy

    def half_of(half, *at):
        return WQ.at[(*at, EVERY, pl.ds(half * 1024, 1024))]

    whole = (EVERY, EVERY, EVERY, EVERY, c)
    get_wq = k.local(wq, wqv)
    q1 = [k.plan(wq, WQ.at[yh, x, yl, z, c], p.step("z", j)) for j in (1, 2, 3)]
    q2, q3 = [], []
    for j in (1, 2, 3):
        for half, axis in ((0, "y"), (1, "x")):
            src = half_of(half, yh, x, yl, EVERY, c)
            q2.append(k.plan(src, src, p.step(axis, j)))
    for j in (1, 2, 3):
        src = half_of(0, EVERY, x, EVERY, EVERY, c)
        q3.append(k.plan(src, src, p.step("x", j)))
        src = half_of(1, yh, EVERY, yl, EVERY, c)
        q3.append(k.plan(src, src, p.step("y", j)))
    q4 = k.plan(WQ.at[whole], WQ.at[whole], sib)

    sent = []
    for copy in q1:
        copy.start()
    for j in (1, 3):
        copy = remote(n2, rows.at[z, c], j, p.step("z", j))
        copy.start()
        sent.append(copy)
    half = halves(rows.at[p.pos("z", 1), c])[1], halves(rows.at[p.pos("z", 3), c])[0]
    on_left = remote(half[0], half[0], 0, p.step("z", 3))
    on_right = remote(half[1], half[1], 2, p.step("z", 1))
    sent += [on_left, on_right]
    remote(n2, rows.at[z, c], 4, sib).start()
    own = local(n2, rows.at[z, c], 0)
    get_wd = local(WD, wd80, 1)
    get_wg = local(WG, wgs, 2)
    get_og = local(OG, ogs, 3)
    get_wd.wait()

    @pl.loop(0, 8)
    def _(i):
        yl, x = i // 4, i % 4
        a, b = wd80[yl, x, 0].astype(F32), wd80[yl, x, 1].astype(F32)
        at = pl.ds(pl.multiple_of(i * 80, 80), 80)
        wds[at, :1024] = jnp.concatenate([a[:40], b[:40]], axis=0).astype(BF16)
        wds[at, 1024:] = jnp.concatenate([a[40:], b[40:]], axis=0).astype(BF16)

    own.wait()
    get_wg.wait()
    get_og.wait()
    get_wq.wait()
    own_wq = k.local(wqv, WQ.at[yh, x, yl, z, c])

    @pl.loop(0, 4)
    def _(j):
        o = jnp.where(j == 2, 3, jnp.where(j == 3, 2, j))
        zz = (z + o) % 4
        at = pl.ds(pl.multiple_of(zz * 256, 256), 256)

        @pl.when(j == 1)
        def _():
            remote(n2, rows.at[z, c], 3, sib).wait_recv()
            on_left.start()
            remote(n2, rows.at[z, c], 1, sib).wait_recv()
            on_right.start()

        @pl.when(j == 3)
        def _():
            on_left.wait_recv()
            on_right.wait_recv()

        @pl.when(o > 0)
        def _():
            remote(rows.at[zz, c], rows.at[zz, c], 4 + o, sib).start()

        remote(rows.at[zz, c], rows.at[zz, 1 - c], 4 + o, sib).wait_recv()
        r = rows[zz].reshape(256, D)
        din[...] = dot_last(ogs[zz].reshape(256, D), wds[...])
        for t in range(5):
            lo, hi = slice(t * 128, (t + 1) * 128), slice(FS + t * 128, FS + (t + 1) * 128)
            w = jnp.concatenate(
                [wgs[:, :, :, :, :, lo].reshape(D, 128), wgs[:, :, :, :, :, hi].reshape(D, 128)], axis=1
            )
            both = dot(r, w)
            gate, upper = both[:, :128], both[:, 128:]
            sig = jax.nn.sigmoid(gate)
            active = gate * sig
            d_inner = din[:, lo]
            inn[at, lo] = (active * upper).astype(BF16)
            dgu[at, lo] = (d_inner * upper * sig * (1.0 + gate * (1.0 - sig))).astype(BF16)
            dgu[at, hi] = (d_inner * active).astype(BF16)

        @pl.loop(0, 8)
        def _(t):
            w = wgs[t // 4, t % 4].reshape(256, 2 * FS)
            cols = pl.ds(pl.multiple_of(t * 256, 256), 256)
            part[zz, :, :, cols] = dot_last(dgu[at], w).astype(BF16).reshape(2, TOK, 256)

        remote(part.at[zz, 1 - c], r0.at[zz], 8 + o, sib).start()

        @pl.loop(0, 4)
        def _(t):
            cols = pl.ds(pl.multiple_of(t * 512, 512), 512)
            mixs[zz, :, :, cols] = dot(inn[at], wds[:, cols]).astype(BF16).reshape(2, TOK, 512)

        remote(mixs.at[zz, 1 - c], m0.at[zz], 16 + o, sib).start()
        remote(part.at[zz, 1 - c], r0.at[zz], 8 + o, sib).wait_recv()

        @pl.loop(0, TOK, step=16)
        def _(t):
            here = pl.ds(pl.multiple_of(t, 16), 16)
            s0[zz, here] = (part[zz, c, here].astype(F32) + r0[zz, here].astype(F32)).astype(BF16)

        @pl.when(o > 0)
        def _():
            remote(s0.at[zz], r1.at[o - 1], 12 + o, p.at(z=zz)).start()

        @pl.when(j == 0)
        def _():
            own_wq.wait()
            for copy in q1:
                copy.wait_recv()
            for copy in q2:
                copy.start()

        @pl.when(j == 1)
        def _():
            for copy in q2:
                copy.wait_recv()
            for copy in q3:
                copy.start()

    for o in range(4):
        remote(mixs.at[0, 0], m0.at[0], 16 + o, sib).wait_recv()

    @pl.loop(0, 4)
    def _(zz):
        @pl.loop(0, TOK, step=16)
        def _(t):
            here = pl.ds(pl.multiple_of(t, 16), 16)
            m0[zz, here] = (mixs[zz, c, here].astype(F32) + m0[zz, here].astype(F32)).astype(BF16)

    out_mix = local(m0, mix_out, 4)

    @pl.loop(0, 8)
    def _(t):
        cols = pl.ds(pl.multiple_of(t * 256, 256), 256)
        left = rows[:, :, :, cols].reshape(8 * TOK, 256)
        dwg[t // 4, t % 4] = dot_rows(left, dgu[...]).astype(BF16).reshape(2, TOK, 2 * FS)

    out_wg = local(dwg, dwg_out, 5)
    for copy in q3:
        copy.wait_recv()
    q4.start()

    @pl.loop(0, 5)
    def _(t):
        units = pl.ds(pl.multiple_of(t * 128, 128), 128)
        dwd32[units] = dot_rows(inn[:, units], ogs[...].reshape(8 * TOK, D))

    @pl.loop(0, 8)
    def _(i):
        yl, x = i // 4, i % 4
        at = pl.ds(pl.multiple_of(i * 80, 80), 80)
        lo, hi = dwd32[at, :1024], dwd32[at, 1024:]
        dwd[yl, x, 0] = jnp.concatenate([lo[:40], hi[:40]], axis=0).astype(BF16)
        dwd[yl, x, 1] = jnp.concatenate([lo[40:], hi[40:]], axis=0).astype(BF16)

    out_wd = local(dwd, dwd_out, 6)
    for o in (1, 2, 3):
        remote(s0.at[0], r1.at[o - 1], 12 + o, sib).wait_recv()

    @pl.loop(0, TOK, step=16)
    def _(t):
        here = pl.ds(pl.multiple_of(t, 16), 16)
        total = s0[z, here].astype(F32)
        for j in range(3):
            total = total + r1[j, here].astype(F32)
        dn[here] = total

    out_dn = local(dn, d_out, 7)
    q4.wait_recv()
    k.drain()
    for copy in sent:
        copy.wait_send()
    for o in range(4):
        remote(rows.at[0, 0], rows.at[0, 0], 4 + o, sib).wait_send()
        remote(part.at[0, 0], r0.at[0], 8 + o, sib).wait_send()
        remote(mixs.at[0, 0], m0.at[0], 16 + o, sib).wait_send()
    for o in (1, 2, 3):
        remote(s0.at[0], r1.at[o - 1], 12 + o, sib).wait_send()
    for copy in (out_mix, out_wg, out_wd, out_dn):
        copy.wait()


def ffn(n2, OG, WG, WD, wq):
    outs = [
        sds((TOK, D), F32),
        sds((4, TOK, D), BF16),
        sds((2, 4, 2, TOK, 2 * FS), BF16),
        sds((2, 4, 2, 80, 1024), BF16),
        sds((2, 4, 2, 4, 2, 16, 2048), BF16),
    ]
    scratch = [
        pltpu.VMEM((4, 2, TOK, D), BF16),
        pltpu.VMEM((4, 2, TOK, D), BF16),
        pltpu.VMEM((2, 4, 2, 8, 16, 2 * FS), BF16),
        pltpu.VMEM((2, 4, 2, 80, 1024), BF16),
        pltpu.VMEM((FS, D), BF16),
        pltpu.VMEM((8 * TOK, 2 * FS), BF16),
        pltpu.VMEM((8 * TOK, FS), BF16),
        pltpu.VMEM((256, FS), F32),
        pltpu.VMEM((4, 2, TOK, D), BF16),
        pltpu.VMEM((4, 2, TOK, D), BF16),
        pltpu.VMEM((4, TOK, D), BF16),
        pltpu.VMEM((4, TOK, D), BF16),
        pltpu.VMEM((3, TOK, D), BF16),
        pltpu.VMEM((4, TOK, D), BF16),
        pltpu.VMEM((2, 4, 2, TOK, 2 * FS), BF16),
        pltpu.VMEM((FS, D), F32),
        pltpu.VMEM((2, 4, 2, 80, 1024), BF16),
        pltpu.VMEM((TOK, D), F32),
        pltpu.VMEM((16, 2048), BF16),
        pltpu.SemaphoreType.DMA((20,)),
        pltpu.SemaphoreType.DMA((20,)),
        pltpu.SemaphoreType.DMA((8,)),
        pltpu.SemaphoreType.DMA((16,)),
        pltpu.SemaphoreType.DMA((16,)),
        pltpu.SemaphoreType.DMA((1,)),
    ]
    return pl.pallas_call(
        ffn_body,
        out_shape=outs,
        in_specs=[ANY] * 5,
        out_specs=[ANY] * 5,
        scratch_shapes=scratch,
        name="ffn",
        compiler_params=pltpu.CompilerParams(
            collective_id=1, has_side_effects=True, vmem_limit_bytes=60 << 20
        ),
    )(n2, OG, WG, WD, wq)


def back_body(*refs):
    (DN, X_IN, OG_IN, RESID, ATT, PT, LSE, WQ, WO, KV, mix_part, dwg, dwd, NA) = refs[:14]
    (BIAS, ROPE, GAINS, QKGAIN) = refs[14:18]
    (IN_GRAD, MIXED, GWG, GWD, GQ, GO, SMALL) = refs[18:25]
    (dn, xv, ogv, resid, pt, lse, in_grad, mixed, kvs, bias, qts, qns, dts, dns, dqt, dpt, datt, dres) = refs[25:43]
    (kpart, k0, k1, ks1, k2, kres, w2, wo2, low2, att2, do, dp, dpm, na2, dqm, mix1) = refs[43:59]
    (rope, gains, qkgain) = refs[59:62]
    scr = list(refs[62:])
    parts = []
    for i, shapes in enumerate(PLANE_SHAPES + O_SHAPES):
        n = 2 * len(shapes) + (i < 4)
        parts.append(scr[:n])
        scr = scr[n:]
    vec, vrecv, ssem, rsem, lsem = scr
    p = Place()
    k = Links(ssem, rsem, lsem)
    yl, z, c = p.yl, p.z, p.c
    m = z * 2 + c
    sib = p.step("c", 1)
    yl_partner = p.at(y=p.yh * 2 + 1 - yl)
    get = {
        "dn": k.local(DN, dn),
        "x": k.local(X_IN, xv),
        "og": k.local(OG_IN, ogv),
        "resid": k.local(RESID, resid),
        "att": k.local(ATT, att2.at[0]),
        "pt": k.local(PT, pt),
        "lse": k.local(LSE, lse),
        "kv": k.local(KV, kvs),
        "mix": k.local(mix_part.at[z], mix1.at[3]),
        "bias": k.local(BIAS, bias),
        "rope": k.local(ROPE, rope),
        "gains": k.local(GAINS, gains),
        "qkgain": k.local(QKGAIN, qkgain),
    }
    partners = [p.step(a, j) for a in "xyz" for j in (1, 2, 3)]
    partners += [p.at(z=(z + j) % 4, c=1 - c) for j in range(4)]
    slab_to, slab_from = slab_target(p), slab_source(p)
    own_slab = same(p, slab_to)
    greet_plane(p, partners, slab_to, slab_from, own_slab)
    plane = [
        ring_reduce(p, k, dwg, wg_stages(0), parts[0], 16),
        ring_reduce(p, k, dwg, wg_stages(1), parts[1], 16),
        ring_reduce(p, k, dwd, wd_stages(p, 0), parts[2], 16),
        ring_reduce(p, k, dwd, wd_stages(p, 1), parts[3], 16),
    ]
    for step in plane:
        next(step)
    pair_att = k.send(ATT, att2.at[1], sib)
    mixing = [k.send(mix_part.at[p.pos("z", j)], mix1.at[j - 1], p.step("z", j)) for j in (1, 2, 3)]
    get_w = [k.local(WO.at[0, t], wo2.at[t]) for t in range(2)]
    for name in ("pt", "rope", "qkgain"):
        get[name].wait()
    cos, sin = rope[0], rope[1]
    qgain, kgain = qkgain[:HEAD], qkgain[HEAD:]

    @pl.loop(0, KV_HEADS)
    def _(g):
        for mm, unit in enumerate(query_units(pt, g, cos, sin, qgain)):
            qts[g, mm] = unit.astype(BF16)
            qns[g, mm] = unit.T.astype(BF16)

    for name in ("dn", "og", "resid", "gains"):
        get[name].wait()
    value = resid[...]
    scale_two = rms_scale(value)
    norm_two = value * scale_two
    d_resid = ogv[...].astype(F32) + norm_back(dn[...], norm_two, scale_two, gains[1:2, :])
    dres[...] = d_resid
    low2[0] = d_resid.astype(BF16)
    pair_low = k.send(low2.at[0], low2.at[1], sib)
    for t in range(8):
        get_w[t].wait()
        term = dot(low2[0, :, t * 256 : (t + 1) * 256], wo2[t % 2].reshape(256, QD))
        datt[...] = term if t == 0 else datt[...] + term
        if t < 6:
            get_w.append(k.local(WO.at[(t + 2) // 4, (t + 2) % 4], wo2.at[t % 2]))
    for g in range(KV_HEADS):
        tiles = []
        for t in range(2):
            at = (g * GROUP + 2 * t) * HEAD
            both = low(datt[:, at : at + 128]).T
            tiles.append(swap(both[:HEAD], both[HEAD:]))
        for mm in range(MICRO):
            none = jnp.zeros((HEAD, 256), F32)
            unit = jnp.concatenate([none, jnp.concatenate([tiles[0][mm], tiles[1][mm]], axis=1)], axis=0)
            dts[g, mm] = unit.astype(BF16)
            dns[g, mm] = unit.T.astype(BF16)
    get["kv"].wait()
    get["lse"].wait()
    get["bias"].wait()

    def unit(u):
        g, mm = u // 2, u % 2
        kv = unit_kv(kvs, mm, g)
        score = jnp.minimum(dot(kv, qts[g, mm]), unit_bias(bias, mm))
        again = jnp.exp(score - lse[u, 0:1, :])
        d_probs = dot(kv, dts[g, mm])
        inner = jnp.sum(again * d_probs, axis=0, keepdims=True)
        d_scores = (again * (d_probs - inner)).astype(BF16)
        d_kv = dot(d_scores, qns[g, mm]) + dot(again.astype(BF16), dns[g, mm])
        cols = pl.ds(pl.multiple_of(g * 128, 128), 128)
        kpart[mm, :, :, :, :, cols] = d_kv.astype(BF16).reshape(2, 4, 2, ROWS, 128)
        dqt[g, mm] = dot_rows(kv, d_scores)[:HEAD] * (HEAD ** -0.5)

    pl.loop(0, KV_HEADS)(unit)
    for step in plane:
        next(step)
    pl.loop(KV_HEADS, 2 * KV_HEADS)(unit)

    core = k.send(kpart.at[:, :, :, 1 - c], k0, sib)
    core.wait_recv()

    @pl.loop(0, 4)
    def _(zz):
        for a in range(2):
            for b in range(2):
                k0[a, b, zz] = (kpart[a, b, zz, c].astype(F32) + k0[a, b, zz].astype(F32)).astype(BF16)

    ring = [k.send(k0.at[:, :, p.pos("z", j)], k1.at[j - 1], p.step("z", j)) for j in (1, 2, 3)]

    get["att"].wait()
    pair_att.wait_recv()
    pair_low.wait_recv()
    att_cols = pl.ds(pl.multiple_of(c * 640, 128), 640)

    @pl.loop(0, 8)
    def _(t):
        cols = pl.ds(pl.multiple_of(t * 256, 256), 256)
        left = low2[:, :, cols].reshape(2 * TOK, 256)
        right = att2[:, :, att_cols].reshape(2 * TOK, 640)
        do[t // 4, t % 4] = dot_rows(left, right).astype(BF16).reshape(2, 4, 32, 640)

    outward = [staged_reduce(p, k, do, o_stages(i), parts[6 + i], 16) for i in range(3)]
    next(outward[0])

    query_sum = jnp.zeros((HEAD, TOK), F32)
    for g in range(KV_HEADS):
        heads = []
        for t in range(2):
            cols = slice(t * 128, (t + 1) * 128)
            heads += list(swap(dqt[g, 0, :, cols], dqt[g, 1, :, cols]))
        for h in range(GROUP):
            at = (g * GROUP + h) * HEAD
            d_raw, term = head_back(pt[at : at + HEAD], heads[h], cos, sin, qgain)
            query_sum = query_sum + term
            dpt[at : at + HEAD] = d_raw

    for copy in ring:
        copy.wait_recv()
    for a in range(2):
        for b in range(2):
            total = k0[a, b, z].astype(F32)
            for j in range(3):
                total = total + k1[j, a, b].astype(F32)
            ks1[a, b] = total.astype(BF16)
    across = k.send(ks1.at[:, 1 - yl], k2, yl_partner)
    across.wait_recv()
    for step in plane:
        next(step)
    for a in range(2):
        kres[pl.ds(a * ROWS, ROWS)] = ks1[a, yl].astype(F32) + k2[a].astype(F32)
    key_sum = jnp.zeros((HEAD, TOK), F32)
    for g in range(KV_HEADS):
        both = kres[:, g * 128 : (g + 1) * 128].T
        at = QD + g * HEAD
        d_raw, term = head_back(pt[at : at + HEAD], both[:HEAD], cos, sin, kgain)
        key_sum = key_sum + term
        dpt[at : at + HEAD] = d_raw
        dpt[at + KD : at + KD + HEAD] = both[HEAD:]
    get_q = [k.local(WQ.at[0, t], w2.at[t]) for t in range(2)]
    get_n = [k.local(NA.at[:, :, :, pl.ds(t * 256, 256)], na2.at[t]) for t in range(2)]
    for t in range(8):
        block = jnp.concatenate([dpt[t * 240 : (t + 1) * 240], jnp.zeros((16, TOK), F32)], axis=0)
        dp[t] = block.T.astype(BF16)
    members = []
    for dz in range(4):
        for dc in range(2):
            zz, cc = (z + dz) % 4, (c + dc) % 2
            src = dp.at[zz * 2 + cc]
            if dz == 0 and dc == 0:
                own_dp = k.local(src, dpm.at[z, c])
            else:
                members.append(k.send(src, dpm.at[z, c], p.at(z=zz, c=cc)))
    sums = jnp.concatenate(
        [jnp.sum(query_sum.T, axis=0, keepdims=True), jnp.sum(key_sum.T, axis=0, keepdims=True)], axis=1
    )
    vec[0] = jnp.broadcast_to(sums, (8, 128))
    small = small_reduce(p, k, vec, vrecv)
    next(small)

    last, keep = [], []

    def to_owners(total, dst):
        for dz in range(4):
            for dc in range(2):
                zz, cc = (z + dz) % 4, (c + dc) % 2
                src = total.at[pl.ds(pl.multiple_of((zz * 2 + cc) * 16, 16), 16)]
                if dz == 0 and dc == 0:
                    keep.append(k.local(src, dst))
                else:
                    last.append(k.send(src, dst, p.at(z=zz, c=cc)))

    def slab_home(half):
        slab = Slab(k, parts[2 + half][-1], GWD.at[:, pl.ds(half * 512, 512)], slab_from, own_slab)
        slab.start()
        return slab

    own_dp.wait()
    for copy in members:
        copy.wait_recv()
    for t in range(8):
        get_n[t].wait()
        total = dot_rows(na2[t % 2].reshape(8 * TOK, 256), dpm[...].reshape(8 * TOK, 256))
        dqm[t // 4, t % 4] = total.astype(BF16).reshape(2, TOK, 256)
        if t < 6:
            get_n.append(k.local(NA.at[:, :, :, pl.ds((t + 2) * 256, 256)], na2.at[t % 2]))
    inward = [staged_reduce(p, k, dqm, q_stages(i), parts[4 + i], 16) for i in range(2)]
    for step in inward:
        next(step)
    next(small)
    next(outward[1])
    next(outward[2])
    for half in range(2):
        next(plane[half], None)
        to_owners(parts[half][-1], GWG.at[:, pl.ds(pl.multiple_of(half * FF + m * FS, 128), FS)])
    slabs = []
    for half in range(2):
        next(plane[2 + half], None)
        slabs.append(slab_home(half))
    get["mix"].wait()
    for copy in mixing:
        copy.wait_recv()

    @pl.loop(0, TOK, step=16)
    def _(t):
        at = pl.ds(pl.multiple_of(t, 16), 16)
        total = resid[at]
        for j in range(4):
            total = total + mix1[j, at].astype(F32)
        mixed[at] = total.astype(BF16)

    keep.append(k.local(mixed, MIXED))
    for t in range(8):
        get_q[t].wait()
        w = w2[t % 2].reshape(256, 2048)
        left = jnp.concatenate([dp[i] for i in range(8)], axis=1)
        in_grad[:, t * 256 : (t + 1) * 256] = dot_last(left, w)
        if t < 6:
            get_q.append(k.local(WQ.at[(t + 2) // 4, (t + 2) % 4], w2.at[t % 2]))
    for step in inward:
        next(step)
    next(small)
    for step in outward:
        next(step)
    get["x"].wait()
    hidden = xv[...].astype(F32)
    scale_one = rms_scale(hidden)
    in_grad[...] = dres[...] + norm_back(in_grad[...], hidden * scale_one, scale_one, gains[0:1, :])
    keep.append(k.local(in_grad, IN_GRAD))
    next(small)
    for half, step in enumerate(inward):
        next(step, None)
        to_owners(parts[4 + half][-1], GQ.at[:, pl.ds(pl.multiple_of(m * 256 + half * 128, 128), 128)])
    for step in outward:
        next(step)
    next(small, None)
    keep.append(k.local(vec.at[4], SMALL))
    for i, step in enumerate(outward):
        next(step, None)
        total = parts[6 + i][-1]
        dst = GO.at[c, :, pl.ds(*O_PARTS[i])]
        keep.append(k.local(total.at[pl.ds(pl.multiple_of(c * 16, 16), 16)], dst))
        last.append(k.send(total.at[pl.ds(pl.multiple_of((1 - c) * 16, 16), 16)], dst, sib))
    for copy in keep:
        copy.wait()
    for copy in last:
        copy.wait_recv()
    for slab in slabs:
        slab.wait_recv()
        slab.wait_send()
    k.drain()


def head_back(raw, grad, cos, sin, gain):
    scale = head_scale(raw)
    normed = raw * scale
    d_head = grad * cos + half_back(grad * sin)
    scaled = d_head * gain
    inner = jnp.mean(scaled * normed, axis=0, keepdims=True)
    return scale * (scaled - normed * inner), d_head * normed


def back(*args):
    w = 2 * KD
    outs = [
        sds((TOK, D), F32),
        sds((TOK, D), BF16),
        sds((16, 2 * FF), BF16),
        sds((80, 1024), BF16),
        sds((16, 2048), BF16),
        sds((2, 16, 640), BF16),
        sds((8, 128), F32),
    ]
    scratch = [
        pltpu.VMEM((TOK, D), F32),
        pltpu.VMEM((TOK, D), BF16),
        pltpu.VMEM((TOK, D), BF16),
        pltpu.VMEM((TOK, D), F32),
        pltpu.VMEM((QKV, TOK), F32),
        pltpu.VMEM((2 * KV_HEADS, 8, 256), F32),
        pltpu.VMEM((TOK, D), F32),
        pltpu.VMEM((TOK, D), BF16),
        pltpu.VMEM((2, 2, 4, 2, ROWS, w), BF16),
        pltpu.VMEM((2, SEQ, 128), F32),
        pltpu.VMEM((KV_HEADS, 2, 128, 256), BF16),
        pltpu.VMEM((KV_HEADS, 2, 256, 128), BF16),
        pltpu.VMEM((KV_HEADS, 2, 128, 256), BF16),
        pltpu.VMEM((KV_HEADS, 2, 256, 128), BF16),
        pltpu.VMEM((KV_HEADS, 2, HEAD, 256), F32),
        pltpu.VMEM((QKV, TOK), F32),
        pltpu.VMEM((TOK, QD), F32),
        pltpu.VMEM((TOK, D), F32),
        pltpu.VMEM((2, 2, 4, 2, ROWS, w), BF16),
        pltpu.VMEM((2, 2, 4, ROWS, w), BF16),
        pltpu.VMEM((3, 2, 2, ROWS, w), BF16),
        pltpu.VMEM((2, 2, ROWS, w), BF16),
        pltpu.VMEM((2, ROWS, w), BF16),
        pltpu.VMEM((TOK, w), F32),
        pltpu.VMEM((2, 2, 4, 2, 16, 2048), BF16),
        pltpu.VMEM((2, 2, 4, 2, 16, QD), BF16),
        pltpu.VMEM((2, TOK, D), BF16),
        pltpu.VMEM((2, TOK, QD), BF16),
        pltpu.VMEM((2, 4, 2, 4, 32, 640), BF16),
        pltpu.VMEM((8, TOK, 256), BF16),
        pltpu.VMEM((4, 2, TOK, 256), BF16),
        pltpu.VMEM((2, 4, 2, TOK, 256), BF16),
        pltpu.VMEM((2, 4, 2, TOK, 256), BF16),
        pltpu.VMEM((4, TOK, D), BF16),
        pltpu.VMEM((2, HEAD, TOK), F32),
        pltpu.VMEM((8, D), F32),
        pltpu.VMEM((2 * HEAD, 128), F32),
    ]
    for i, shapes in enumerate(PLANE_SHAPES + O_SHAPES):
        scratch += staged_scratch(shapes, i < 4)
    scratch += [
        pltpu.VMEM((5, 8, 128), F32),
        pltpu.VMEM((4, 3, 8, 128), F32),
        pltpu.SemaphoreType.DMA((150,)),
        pltpu.SemaphoreType.DMA((150,)),
        pltpu.SemaphoreType.DMA((36,)),
    ]
    return pl.pallas_call(
        back_body,
        out_shape=outs,
        in_specs=[ANY] * 18,
        out_specs=[ANY] * 7,
        scratch_shapes=scratch,
        name="back",
        compiler_params=pltpu.CompilerParams(
            collective_id=2, has_side_effects=True, vmem_limit_bytes=60 << 20
        ),
    )(*args)


def finish_body(*refs):
    IN_GRAD, MIXED, GWG, GWD, GQ, GO, SUMS, WG, WQ, g1, g2 = refs[:11]
    in_out, mixed_out, Q, O, G, DOWN, ATTN, FFN, QG, KG = refs[11:21]
    (gwg, gwd, gq, go, sums, wg, wq, q, o, g, down, attn, ffn_, qg, kg, ing, mix, sem) = refs[21:]
    used = []

    def copy(src, dst):
        out = pltpu.make_async_copy(src, dst, sem.at[len(used)])
        out.start()
        used.append(out)
        return out

    rows = [copy(IN_GRAD, ing), copy(MIXED, mix)]
    through = []
    got = [copy(a, b) for a, b in ((GQ, gq), (WQ, wq), (GO, go), (SUMS, sums), (GWD, gwd), (GWG, gwg), (WG, wg))]
    for one in got[:5]:
        one.wait()
    for one, (src, dst) in zip(rows, ((ing, in_out), (mix, mixed_out))):
        one.wait()
        through.append(copy(src, dst))
    wide = gq[...].astype(F32)
    lane = lax.broadcasted_iota(jnp.int32, (16, QKV), 1)
    total = jnp.zeros((16, QKV), F32)
    for i in range(8):
        piece = jnp.concatenate([wide[:, i * 256 : (i + 1) * 256], jnp.zeros((16, QKV - 256), F32)], axis=1)
        here = (lane >= i * 240) & (lane < (i + 1) * 240)
        total = jnp.where(here, pltpu.roll(piece, 240 * i, 1) if i else piece, total)
    q[...] = total
    through.append(copy(q, Q))
    o[...] = jnp.concatenate([go[0].astype(F32), go[1].astype(F32)], axis=1)
    through.append(copy(o, O))
    slab = gwd[...].astype(F32)
    down[...] = jnp.concatenate([slab[:40], slab[40:]], axis=1)
    through.append(copy(down, DOWN))
    attn[...] = flat(jnp.sum(wq[...].astype(F32) * total, axis=1, keepdims=True)) / g1[...].astype(F32)
    through.append(copy(attn, ATTN))
    qg[...] = sums[0:1, :HEAD]
    kg[...] = pltpu.roll(sums[...], HEAD, 1)[0:1, :HEAD]
    through += [copy(qg, QG), copy(kg, KG)]
    for one in got[5:]:
        one.wait()
    grown = gwg[...].astype(F32)
    g[...] = grown
    through.append(copy(g, G))
    ffn_[...] = flat(jnp.sum(wg[...].astype(F32) * grown, axis=1, keepdims=True)) / g2[...].astype(F32)
    through.append(copy(ffn_, FFN))
    for one in through:
        one.wait()


def flat(col):
    n = col.shape[0]
    place = lax.broadcasted_iota(jnp.int32, (n, n), 0) == lax.broadcasted_iota(jnp.int32, (n, n), 1)
    return jnp.sum(jnp.where(place, jnp.broadcast_to(col, (n, n)), 0.0), axis=0, keepdims=True)


def finish(*args):
    outs = [
        sds((TOK, D), F32),
        sds((TOK, D), BF16),
        sds((16, QKV), F32),
        sds((16, QD), F32),
        sds((16, 2 * FF), F32),
        sds((40, D), F32),
        sds((1, 16), F32),
        sds((1, 16), F32),
        sds((1, HEAD), F32),
        sds((1, HEAD), F32),
    ]
    ins = [(16, 2 * FF), (80, 1024), (16, 2048), (2, 16, 640), (8, 128), (16, 2 * FF), (16, QKV)]
    scratch = [pltpu.VMEM(a, F32 if a == (8, 128) else BF16) for a in ins]
    scratch += [pltpu.VMEM(a.shape, a.dtype) for a in outs[2:] + outs[:2]]
    return pl.pallas_call(
        finish_body,
        out_shape=outs,
        in_specs=[ANY] * 9 + [VMEM] * 2,
        out_specs=[ANY] * 10,
        scratch_shapes=scratch + [pltpu.SemaphoreType.DMA((19,))],
        name="finish",
        compiler_params=pltpu.CompilerParams(vmem_limit_bytes=60 << 20),
    )(*args)


def per_device(
    tokens,
    segment_ids,
    w_qkv,
    w_out,
    w_gate_up,
    w_down,
    attn_gain,
    ffn_gain,
    query_gain,
    key_gain,
    out_grad,
):
    g1, g2, g3, g4 = [a.reshape(1, -1) for a in (attn_gain, ffn_gain, query_gain, key_gain)]
    og_in = out_grad.reshape(TOK, D)
    x_in = tokens.reshape(TOK, D)
    (WO, WG, WD, OG, NA, KV, pt, lse, attended, resid, n2, wq_in, bias, rope, gain_rows, head_gains) = front(
        x_in, w_qkv, w_out.T, w_gate_up, w_down, og_in, segment_ids, g1, g2, g3, g4, rope_parts()
    )
    d_normed, mix_part, dwg, dwd, WQ = ffn(n2, OG, WG, WD, wq_in)
    in_grad, mixed, gwg, gwd, gq, go, sums = back(
        d_normed, x_in, og_in, resid, attended, pt, lse, WQ, WO, KV, mix_part, dwg, dwd, NA,
        bias, rope, gain_rows, head_gains,
    )
    outs = finish(in_grad, mixed, gwg, gwd, gq, go, sums, w_gate_up, w_qkv, g1, g2)
    return (
        outs[1].reshape(MICRO, ROWS, D),
        outs[0].reshape(MICRO, ROWS, D),
        outs[2],
        outs[3].T,
        outs[4],
        outs[5],
        outs[6].reshape(16),
        outs[7].reshape(16),
        outs[8].reshape(HEAD),
        outs[9].reshape(HEAD),
    )


def solution(mesh):
    return jax.shard_map(
        per_device,
        mesh=mesh,
        in_specs=(
            P(None, ("grp", "seq"), None),
            P(None, "grp"),
            P(("grp", "seq"), None),
            P(None, ("grp", "seq")),
            P(("grp", "seq"), None),
            P(("grp", "seq"), None),
            P(("grp", "seq")),
            P(("grp", "seq")),
            P(),
            P(),
            P(None, ("grp", "seq"), None),
        ),
        out_specs=(
            P(None, ("grp", "seq"), None),
            P(None, ("grp", "seq"), None),
            P(("grp", "seq"), None),
            P(None, ("grp", "seq")),
            P(("grp", "seq"), None),
            P(("grp", "seq"), None),
            P(("grp", "seq")),
            P(("grp", "seq")),
            P(),
            P(),
        ),
        check_vma=False,
    )
```

```python
import jax
import jax.numpy as jnp
import numpy as np
from jax import lax
from jax.experimental import pallas as pl
from jax.experimental.pallas import tpu as pltpu
from jax.sharding import PartitionSpec as P

Q_HEADS = 20
KV_HEADS = 5
GROUP = 4
HEAD = 64
D = 2048
FF = 5120
QD = 1280
KD = 320
QKV = 1920
SEQ = 1024
MICRO = 2
ROWS = 64
TOK = 128
FS = 640
EPS = 1e-06
MESH = pl.DeviceIdType.MESH
F32 = jnp.float32
BF16 = jnp.bfloat16
ANY = pl.BlockSpec(memory_space=pl.ANY)


class Place:
    def __init__(self):
        g = lax.axis_index("grp")
        s = lax.axis_index("seq")
        self.g, self.s = g, s
        self.yh, self.x = g // 4, g % 4
        self.yl, self.z, self.c = s // 8, (s // 2) % 4, s % 2
        self.y = self.yh * 2 + self.yl

    def at(self, x=None, y=None, z=None, c=None):
        x = self.x if x is None else x
        y = self.y if y is None else y
        z = self.z if z is None else z
        c = self.c if c is None else c
        return ((y // 2) * 4 + x, (y % 2) * 8 + z * 2 + c)

    def step(self, axis, k):
        if axis == "x":
            return self.at(x=(self.x + k) % 4)
        if axis == "y":
            return self.at(y=(self.y + k) % 4)
        if axis == "z":
            return self.at(z=(self.z + k) % 4)
        return self.at(c=1 - self.c)

    def pos(self, axis, k):
        return (getattr(self, axis) + k) % 4


class Links:
    def __init__(self, send_sems, recv_sems, local_sems):
        self.send_sems, self.recv_sems, self.local_sems = send_sems, recv_sems, local_sems
        self.received = 0
        self.free = {"send": list(range(send_sems.shape[0]))[::-1], "local": list(range(local_sems.shape[0]))[::-1]}
        self.sent = {}

    def plan(self, src, dst, to):
        i = self.received
        self.received += 1
        assert i < self.recv_sems.shape[0], i
        slot = self.free["send"].pop()
        copy = pltpu.make_async_remote_copy(
            src_ref=src,
            dst_ref=dst,
            send_sem=self.send_sems.at[slot],
            recv_sem=self.recv_sems.at[i],
            device_id=to,
            device_id_type=MESH,
        )
        self.sent[id(copy)] = (copy, slot)
        return copy

    def send(self, src, dst, to):
        copy = self.plan(src, dst, to)
        copy.start()
        return copy

    def local(self, src, dst):
        slot = self.free["local"].pop()
        copy = pltpu.make_async_copy(src, dst, self.local_sems.at[slot])
        copy.start()
        return Local(self, copy, slot)

    def settle(self, copies):
        for copy in copies:
            copy, slot = self.sent.pop(id(copy))
            copy.wait_send()
            self.free["send"].append(slot)

    def drain(self):
        self.settle([copy for copy, _ in list(self.sent.values())])


class Local:
    def __init__(self, links, copy, slot):
        self.links, self.copy, self.slot = links, copy, slot

    def wait(self):
        self.copy.wait()
        self.links.free["local"].append(self.slot)


def halves(ref):
    n = ref.shape[0] // 2
    return ref.at[pl.ds(0, n)], ref.at[pl.ds(n, n)]


class RingGather:
    def __init__(self, p, k, axis, block, src=None):
        self.p, self.k, self.axis, self.block = p, k, axis, block
        dst = block(p.pos(axis, 0))
        src = dst if src is None else src
        self.right = k.send(src, dst, p.step(axis, 1))
        self.left = k.send(src, dst, p.step(axis, 3))

    def from_before(self):
        self.right.wait_recv()
        half = halves(self.block(self.p.pos(self.axis, 3)))[0]
        self.far_right = self.k.send(half, half, self.p.step(self.axis, 1))

    def from_after(self):
        self.left.wait_recv()
        half = halves(self.block(self.p.pos(self.axis, 1)))[1]
        self.far_left = self.k.send(half, half, self.p.step(self.axis, 3))

    def hand_on(self):
        self.from_before()
        self.from_after()

    def wait(self):
        self.far_right.wait_recv()
        self.far_left.wait_recv()

    def copies(self):
        return [self.right, self.left, self.far_right, self.far_left]


def greet(partners):
    barrier = pltpu.get_barrier_semaphore()
    for to in partners:
        pl.semaphore_signal(barrier, inc=1, device_id=to, device_id_type=MESH)
    pl.semaphore_wait(barrier, len(partners))


def sds(shape, dtype):
    return jax.ShapeDtypeStruct(shape, dtype)


def rms_scale(values):
    return lax.rsqrt(jnp.mean(values * values, axis=-1, keepdims=True) + EPS)


def norm_back(upstream, normed, scale, gain):
    scaled = upstream * gain
    inner = jnp.mean(scaled * normed, axis=-1, keepdims=True)
    return scale * (scaled - normed * inner)


def dot(left, right):
    return jnp.dot(left, right, preferred_element_type=F32)


def dot_last(left, right):
    return lax.dot_general(left, right, (((1,), (1,)), ((), ())), preferred_element_type=F32)


def dot_rows(left, right):
    return lax.dot_general(left, right, (((0,), (0,)), ((), ())), preferred_element_type=F32)


def slab_target(p):
    return p.at(x=(p.z + p.x) % 4, y=(p.c + p.yh) % 2 * 2 + p.yl, z=p.g // 2, c=p.g % 2)


def slab_place(p, x=None, y=None):
    m = p.z * 2 + p.c
    if x is not None:
        return (x + 4 - m % 4) % 4
    return (y // 2 + 2 - m // 4) % 2


def slab_source(p):
    m = p.z * 2 + p.c
    return p.at(x=m % 4, y=(m // 4) * 2 + p.yl, z=slab_place(p, x=p.x), c=slab_place(p, y=p.y))


def same(p, to):
    return (to[0] == p.g) & (to[1] == p.s)


def greet_plane(p, partners, slab_to, slab_from, own_slab):
    barrier = pltpu.get_barrier_semaphore()
    for to in partners:
        pl.semaphore_signal(barrier, inc=1, device_id=to, device_id_type=MESH)

    @pl.when(jnp.logical_not(own_slab))
    def _():
        pl.semaphore_signal(barrier, inc=1, device_id=slab_to, device_id_type=MESH)
        pl.semaphore_signal(barrier, inc=1, device_id=slab_from, device_id_type=MESH)
        pl.semaphore_wait(barrier, len(partners) + 2)

    @pl.when(own_slab)
    def _():
        pl.semaphore_wait(barrier, len(partners))


class Slab:
    def __init__(self, k, src, dst, to, own):
        self.own, self.src, self.dst = own, src, dst
        self.far = k.plan(src, dst, to)
        k.sent.pop(id(self.far))
        self.near = pltpu.make_async_copy(src, dst, k.recv_sems.at[k.received - 1])

    def start(self):
        @pl.when(self.own)
        def _():
            self.near.start()

        @pl.when(jnp.logical_not(self.own))
        def _():
            self.far.start()

    def wait_recv(self):
        @pl.when(self.own)
        def _():
            self.near.wait()

        @pl.when(jnp.logical_not(self.own))
        def _():
            self.far.wait_recv()

    def wait_send(self):
        @pl.when(jnp.logical_not(self.own))
        def _():
            self.far.wait_send()


def add_blocks(dst, terms, chunk):
    lead, rows = dst.shape[:-2], dst.shape[-2]
    count = 1
    for n in lead:
        count *= n

    @pl.loop(0, count)
    def _(i):
        at = []
        rest = i
        for n in reversed(lead):
            at.insert(0, rest % n)
            rest = rest // n

        @pl.loop(0, rows, step=chunk)
        def _(t):
            here = (*at, pl.ds(pl.multiple_of(t, chunk), chunk))
            total = terms[0][here].astype(F32)
            for term in terms[1:]:
                total = total + term[here].astype(F32)
            dst[here] = total.astype(dst.dtype)


def staged_reduce(p, k, src, stages, scr, chunk):
    own = scr[0]
    cur = src
    for n, (axis, pick) in enumerate(stages):
        recv = scr[1] if n == 0 else scr[2 * n]
        if n == 0:
            mine = k.local(pick(src, p.pos(axis, 0)), own)
        ring = [k.send(pick(cur, p.pos(axis, j)), recv.at[j - 1], p.step(axis, j)) for j in (1, 2, 3)]
        yield
        if n == 0:
            mine.wait()
        for copy in ring:
            copy.wait_recv()
        total = own if n == 0 else scr[2 * n + 1]
        add_blocks(total, [own if n == 0 else pick(cur, p.pos(axis, 0))] + [recv.at[j] for j in range(3)], chunk)
        cur = total


def ring_reduce(p, k, src, stages, scr, chunk):
    own, recv, held, recv2, total = scr
    axis, pick = stages[0]
    before, after, far = recv.at[0], recv.at[1], recv.at[2]
    far_a, far_b = halves(pick(src, p.pos(axis, 2)))
    right_a, right_b = halves(pick(src, p.pos(axis, 1)))
    left_a, left_b = halves(pick(src, p.pos(axis, 3)))
    right, left = p.step(axis, 1), p.step(axis, 3)
    on_right = k.send(far_a, halves(far)[0], right)
    on_left = k.send(far_b, halves(far)[1], left)
    get = [k.local(right_a, halves(held)[0]), k.local(left_b, halves(held)[1])]
    mine = k.local(pick(src, p.pos(axis, 0)), own)
    yield
    near = [k.send(right_b, halves(before)[1], right), k.send(left_a, halves(after)[0], left)]
    yield
    for i, (copy, to, dst) in enumerate(((on_right, right, before), (on_left, left, after))):
        get[i].wait()
        copy.wait_recv()
        here = halves(held)[i]
        add_blocks(here, [here, halves(far)[i]], chunk)
        near.append(k.send(here, halves(dst)[i], to))
    yield
    mine.wait()
    for copy in near:
        copy.wait_recv()
    add_blocks(own, [own, before, after], chunk)
    axis, pick = stages[1]
    ring = [k.send(pick(own, p.pos(axis, j)), recv2.at[j - 1], p.step(axis, j)) for j in (1, 2, 3)]
    yield
    for copy in ring:
        copy.wait_recv()
    add_blocks(total, [pick(own, p.pos(axis, 0))] + [recv2.at[j] for j in range(3)], chunk)


def staged_scratch(shapes, held=False):
    out = [pltpu.VMEM(shapes[0], BF16), pltpu.VMEM((3, *shapes[0]), BF16)]
    if held:
        out.append(pltpu.VMEM(shapes[0], BF16))
    for n, shape in enumerate(shapes[1:]):
        out.append(pltpu.VMEM((3, *shape), BF16))
        out.append(pltpu.VMEM(shape, BF16))
    return out


EVERY = slice(None)


def wg_stages(half):
    cols = pl.ds(half * FS, FS)
    if half == 0:
        return [
            ("y", lambda r, i: r.at[i // 2, :, i % 2, :, cols]),
            ("x", lambda r, i: r.at[i]),
        ]
    return [
        ("x", lambda r, i: r.at[:, i, :, :, cols]),
        ("y", lambda r, i: r.at[i // 2, i % 2]),
    ]


def wd_stages(p, half):
    cols = pl.ds(half * 512, 512)
    if half == 0:
        return [
            ("y", lambda r, i: r.at[i % 2, :, slab_place(p, y=i), :, cols]),
            ("x", lambda r, i: r.at[slab_place(p, x=i)]),
        ]
    return [
        ("x", lambda r, i: r.at[:, slab_place(p, x=i), :, :, cols]),
        ("y", lambda r, i: r.at[i % 2, slab_place(p, y=i)]),
    ]


def q_stages(half):
    cols = pl.ds(half * 128, 128)
    if half == 0:
        return [
            ("y", lambda r, i: r.at[i // 2, :, i % 2, :, cols]),
            ("x", lambda r, i: r.at[i]),
        ]
    return [
        ("x", lambda r, i: r.at[:, i, :, :, cols]),
        ("y", lambda r, i: r.at[i // 2, i % 2]),
    ]


def o_stages(part):
    cols = pl.ds(*O_PARTS[part])
    if part == 0:
        return [
            ("x", lambda r, i: r.at[:, i, :, :, :, cols]),
            ("z", lambda r, i: r.at[:, :, i]),
            ("y", lambda r, i: r.at[i // 2, i % 2]),
        ]
    if part == 1:
        return [
            ("y", lambda r, i: r.at[i // 2, :, i % 2, :, :, cols]),
            ("x", lambda r, i: r.at[i]),
            ("z", lambda r, i: r.at[i]),
        ]
    return [
        ("z", lambda r, i: r.at[:, :, :, i, :, cols]),
        ("y", lambda r, i: r.at[i // 2, :, i % 2]),
        ("x", lambda r, i: r.at[i]),
    ]


O_PARTS = ((0, 384), (384, 128), (512, 128))
PLANE_SHAPES = [
    [(4, 128, FS), (128, FS)],
    [(2, 2, 128, FS), (128, FS)],
    [(4, 80, 512), (80, 512)],
    [(2, 2, 80, 512), (80, 512)],
    [(4, 128, 128), (128, 128)],
    [(2, 2, 128, 128), (128, 128)],
]
O_SHAPES = [
    [(2, 2, 4, 32, 384), (2, 2, 32, 384), (32, 384)],
    [(4, 4, 32, 128), (4, 32, 128), (32, 128)],
    [(2, 4, 2, 32, 128), (4, 32, 128), (32, 128)],
]


def small_reduce(p, k, vec, recv):
    for n, axis in enumerate("zyxc"):
        steps = (1,) if axis == "c" else (1, 2, 3)
        ring = [k.send(vec.at[n], recv.at[n, j - 1], p.step(axis, j)) for j in steps]
        yield
        for copy in ring:
            copy.wait_recv()
        total = vec[n]
        for j in range(len(steps)):
            total = total + recv[n, j]
        vec[n + 1] = total


def swap(a, b):
    left = lax.broadcasted_iota(jnp.int32, a.shape, 1) < ROWS
    return jnp.where(left, a, pltpu.roll(b, ROWS, 1)), jnp.where(left, pltpu.roll(a, ROWS, 1), b)


def head_scale(v):
    return lax.rsqrt(jnp.mean(v * v, axis=-2, keepdims=True) + EPS)


def half_turn(v):
    half = HEAD // 2
    return jnp.concatenate([-v[..., half:, :], v[..., :half, :]], axis=-2)


def half_back(v):
    half = HEAD // 2
    return jnp.concatenate([v[..., half:, :], -v[..., :half, :]], axis=-2)


def low(v):
    return v.astype(BF16).astype(F32)


def query_units(packed_t, g, cos, sin, gain):
    raw = packed_t[pl.ds(pl.multiple_of(g * 256, 256), 256)].reshape(GROUP, HEAD, TOK)
    head = raw * head_scale(raw) * gain
    turned = low(head * cos + half_turn(head) * sin) * (HEAD ** -0.5)
    a0, a1 = swap(turned[0], turned[1])
    b0, b1 = swap(turned[2], turned[3])
    none = jnp.zeros((HEAD, 256), F32)
    return [
        jnp.concatenate([jnp.concatenate([a, b], axis=1), none], axis=0) for a, b in ((a0, b0), (a1, b1))
    ]


def fill_bias(bias, seg, s):
    lane = lax.broadcasted_iota(jnp.int32, (128, 128), 1)
    query = lane % ROWS + s * ROWS
    around = pl.ds(pl.multiple_of((s // 2) * 128, 128), 128)
    for m in range(MICRO):
        ids = jnp.broadcast_to(seg[m : m + 1, around].astype(F32), (128, 128))
        turned = pltpu.roll(ids, ROWS, 1)
        ids = jnp.where((lane < ROWS) == (s % 2 == 0), ids, turned)
        ids = jnp.where(ids >= 0, ids, -2.0)

        @pl.loop(0, SEQ, step=128)
        def _(t):
            at = pl.ds(pl.multiple_of(t, 128), 128)
            key = lax.broadcasted_iota(jnp.int32, (128, 128), 0) + t
            keys = jnp.broadcast_to(seg[m : m + 1, at].astype(F32), (128, 128)).T
            ok = ((key <= query) & (keys == ids)) | (key == query)
            bias[m, at] = jnp.where(ok, 3e38, -1e30)


def rope_parts():
    inverse = 10000.0 ** (-(np.arange(HEAD) % (HEAD // 2)) / (HEAD // 2))
    begin = inverse[:, None] * (np.arange(128)[None, :] % 16 * ROWS)
    inside = inverse[:, None] * (np.arange(128)[None, :] % ROWS)
    return np.stack([np.cos(begin), np.sin(begin), np.cos(inside), np.sin(inside)]).astype(np.float32)


def rope_tables(parts, s):
    here = lax.broadcasted_iota(jnp.int32, (HEAD, 128), 1) == s
    c0 = jnp.sum(jnp.where(here, parts[0], 0.0), axis=1, keepdims=True)
    s0 = jnp.sum(jnp.where(here, parts[1], 0.0), axis=1, keepdims=True)
    return c0 * parts[2] - s0 * parts[3], s0 * parts[2] + c0 * parts[3]


def column(row):
    n = row.shape[1]
    place = lax.broadcasted_iota(jnp.int32, (n, n), 0) == lax.broadcasted_iota(jnp.int32, (n, n), 1)
    return jnp.sum(jnp.where(place, jnp.broadcast_to(row, (n, n)), 0.0), axis=1, keepdims=True)


KV_PARTS = (pl.ds(0, 384), pl.ds(384, 256))


def unit_bias(bias, m):
    half = bias[m]
    return jnp.concatenate([half, half], axis=1)


def unit_kv(KV, m, g):
    cols = pl.ds(pl.multiple_of(g * 128, 128), 128)
    return KV[m, :, :, :, :, cols].reshape(SEQ, 128)


def front_body(*refs):
    (x_in, w_qkv, wo, wg, w_down, og, seg, g1, g2, g3, g4, parts) = refs[:12]
    (WO, WG, WD, OG, NA, KV, PT, LSE, ATT, RESID, N2, WQIN, BIAS, ROPE, GAINS, QKGAIN) = refs[12:28]
    (wq, wd, ogv, gains_out, rope, qkgain) = refs[28:34]
    (xs, na, wqm, wos, pks, pk, pt, lse, att, resid, n2, kvl, kvs, bias, qts, ots) = refs[34:50]
    ssem, rsem, lsem = refs[50:]
    p = Place()
    k = Links(ssem, rsem, lsem)
    yh, x, yl, z, c = p.yh, p.x, p.yl, p.z, p.c
    m = z * 2 + c
    sib = p.step("c", 1)
    yl_partner = p.at(y=p.yh * 2 + 1 - yl)
    partners = [p.step(a, j) for a in "xyz" for j in (1, 2, 3)]
    partners += [p.at(z=(z + j) % 4, c=1 - c) for j in range(4)]
    slab_to, slab_from = slab_target(p), slab_source(p)
    own_slab = same(p, slab_to)

    spare = [column(row[...].astype(F32)) for row in (g1, g2)]
    wide = w_qkv[...].astype(F32)
    lane = lax.broadcasted_iota(jnp.int32, (16, 256), 1)
    rest = jnp.where(lane == 240, spare[0], jnp.where(lane == 241, spare[1], 0.0))
    for i in range(8):
        turned = pltpu.roll(wide, (QKV - 240 * i) % QKV, 1)[:, :256]
        wq[:, i * 256 : (i + 1) * 256] = jnp.where(lane < 240, turned, rest).astype(BF16)
    greet_plane(p, partners, slab_to, slab_from, own_slab)

    def spread(src_of, dst_of):
        far, near = [], None
        for dz in range(4):
            for dc in range(2):
                zz, cc = (z + dz) % 4, (c + dc) % 2
                src, dst = src_of(zz * 2 + cc), dst_of(m)
                if dz == 0 and dc == 0:
                    near = k.local(src, dst)
                else:
                    far.append(k.send(src, dst, p.at(z=zz, c=cc)))
        return near, far

    q0 = spread(
        lambda i: wq.at[:, pl.ds(pl.multiple_of(i * 256, 256), 256)], lambda i: wqm.at[yh, x, yl, i]
    )
    own_x = k.local(x_in, xs.at[z, c])
    get_og = k.local(og, ogv)
    xcore = {0: k.send(x_in, xs.at[z, c], sib)}
    own_wo = k.local(wo, wos.at[yh, x, yl, z, c])

    def wo_at(part, *at):
        return wos.at[(*at, EVERY, pl.ds(part * 640, 640))]

    o1 = [k.send(wo, wos.at[yh, x, yl, z, c], p.step("z", j)) for j in (1, 2, 3)]
    g0 = [
        spread(
            lambda i: wg.at[:, pl.ds(pl.multiple_of(half * FF + i * FS, 128), FS)],
            lambda i: WG.at[yh, x, yl, i, :, pl.ds(half * FS, FS)],
        )
        for half in range(2)
    ]
    xring = RingGather(p, k, "z", lambda i: xs.at[i, c], x_in)

    def to_plane(blocks):
        return [k.send(b, b, p.step(axis, j)) for j in (1, 2, 3) for b, axis in blocks]

    ql, qh = pl.ds(0, 128), pl.ds(128, 128)
    lo, hi = pl.ds(0, FS), pl.ds(FS, FS)
    dlo, dhi = pl.ds(0, 384), pl.ds(384, 640)
    q0[0].wait()
    for copy in q0[1]:
        copy.wait_recv()
    q1 = to_plane(((wqm.at[yh, x, yl, :, :, ql], "x"), (wqm.at[yh, x, yl, :, :, qh], "y")))
    fill_bias(bias, seg, p.s)
    cos, sin = rope_tables(parts, p.s)
    rope[0], rope[1] = cos, sin
    qgain, kgain = column(g3[...].astype(F32)), column(g4[...].astype(F32))
    qkgain[...] = jnp.concatenate([jnp.broadcast_to(qgain, (HEAD, 128)), jnp.broadcast_to(kgain, (HEAD, 128))], axis=0)
    for copy in q1:
        copy.wait_recv()
    q2 = to_plane(((wqm.at[yh, :, yl, :, :, ql], "y"), (wqm.at[:, x, :, :, :, qh], "x")))
    for near, far in g0:
        near.wait()
        for copy in far:
            copy.wait_recv()
    plane = to_plane(((WG.at[yh, x, yl, :, :, lo], "x"), (WG.at[yh, x, yl, :, :, hi], "y")))
    slab_rows = w_down[...].astype(F32)
    wd[...] = jnp.concatenate([slab_rows[:, :1024], slab_rows[:, 1024:]], axis=0).astype(BF16)
    slab = Slab(k, wd, WD.at[yl, z, c], slab_to, own_slab)
    slab.start()
    for copy in q2:
        copy.wait_recv()
    own_x.wait()
    own_wo.wait()
    pick = jnp.where(
        lax.broadcasted_iota(jnp.int32, (8, 128), 0) + 112 == lax.broadcasted_iota(jnp.int32, (8, 128), 1), 1.0, 0.0
    ).astype(BF16)
    gains_out[...] = dot_last(pick, wqm[:, :, :, :, :, pl.ds(128, 128)].reshape(D, 128))
    keep = [k.local(wq, WQIN), k.local(bias, BIAS), k.local(rope, ROPE), k.local(gains_out, GAINS), k.local(qkgain, QKGAIN)]
    k.settle(q0[1] + q1)
    xring.hand_on()
    for o in (1, 3):
        src = xs.at[(z + o) % 4, c]
        xcore[o] = k.send(src, src, sib)
    packs = []
    for o in (0, 1, 3, 2):
        zz = (z + o) % 4
        if o == 2:
            xring.wait()
            xcore[o] = k.send(xs.at[zz, c], xs.at[zz, c], sib)
        xcore[o].wait_recv()
        rows = xs[zz].reshape(256, D).astype(F32)
        normed = (rows * rms_scale(rows) * gains_out[0:1, :]).astype(BF16)
        na[zz] = normed.reshape(2, TOK, D)
        pks[zz] = dot(normed, wqm[...].reshape(D, 256)).astype(BF16).reshape(2, TOK, 256)
        if o:
            packs.append(k.send(pks.at[zz, c], pk.at[m], p.at(z=zz)))
        else:
            own_pk = k.local(pks.at[z, c], pk.at[m])
        packs.append(k.send(pks.at[zz, 1 - c], pk.at[m], p.at(z=zz, c=1 - c)))
        if o == 1:
            for copy in o1:
                copy.wait_recv()
            o2 = to_plane(
                (
                    (wo_at(0, yh, x, yl, EVERY, c), "y"),
                    (wo_at(1, yh, x, yl, EVERY, c), "x"),
                ),
            )
        if o == 3:
            for copy in plane:
                copy.wait_recv()
            plane2 = [
                RingGather(p, k, "x", lambda i: WG.at[:, i, :, :, :, hi]),
                RingGather(p, k, "y", lambda i: WG.at[i // 2, :, i % 2, pl.ds(0, 4), :, lo]),
            ]
    slab.wait_recv()
    held = WD.at[yl, slab_place(p, x=x), slab_place(p, y=p.y)]
    plane_d = to_plane(((held.at[:, dlo], "x"), (held.at[:, dhi], "y")))
    for copy in o2:
        copy.wait_recv()
    o3 = [RingGather(p, k, "x", lambda i: wo_at(0, EVERY, i, EVERY, EVERY, c))]
    keep.append(k.local(na, NA))
    k.settle(q2 + o1 + [copy for _, far in g0 for copy in far])
    own_pk.wait()
    for copy in packs:
        copy.wait_recv()
    for i8 in range(8):
        pt[i8 * 240 : (i8 + 1) * 240] = pk[i8].astype(F32).T[:240]

    @pl.loop(0, KV_HEADS)
    def _(g):
        raw = pt[pl.ds(pl.multiple_of(QD + g * HEAD, HEAD), HEAD)]
        head = raw * head_scale(raw) * kgain
        key = head * cos + half_turn(head) * sin
        value = pt[pl.ds(pl.multiple_of(QD + KD + g * HEAD, HEAD), HEAD)]
        both = jnp.concatenate([key, value], axis=0).T.astype(BF16)
        cols = pl.ds(pl.multiple_of(g * 128, 128), 128)
        for mm in range(MICRO):
            kvl[mm, :, cols] = both[mm * ROWS : (mm + 1) * ROWS]

    own_kv = k.local(kvl, kvs.at[:, yl, z, c])
    across, ring = [], []
    for cols in KV_PARTS:
        across.append(k.send(kvl.at[:, :, cols], kvs.at[:, yl, z, c, :, cols], yl_partner))
        ring.append([k.send(kvl.at[:, :, cols], kvs.at[:, yl, z, c, :, cols], p.step("z", j)) for j in (1, 2, 3)])
    keep.append(k.local(pt, PT))

    @pl.loop(0, KV_HEADS)
    def _(g):
        for mm, unit in enumerate(query_units(pt, g, cos, sin, qgain)):
            qts[g, mm] = unit.astype(BF16)

    for copy, group, cols in zip(across, ring, KV_PARTS):
        copy.wait_recv()
        src = kvs.at[:, 1 - yl, z, c, :, cols]
        group += [k.send(src, src, p.step("z", j)) for j in (1, 2, 3)]
    get_og.wait()
    keep.append(k.local(ogv, OG.at[z, c]))
    rows = RingGather(p, k, "z", lambda i: OG.at[i, c], ogv)
    last = [k.send(ogv, OG.at[z, c], sib)]
    own_kv.wait()
    o3.append(RingGather(p, k, "y", lambda i: wo_at(1, i // 2, EVERY, i % 2, EVERY, c)))
    for ring4 in plane2:
        ring4.hand_on()
    oc = []
    for src in (
        wo_at(0, EVERY, x, EVERY, EVERY, c),
        wo_at(1, yh, EVERY, yl, EVERY, c),
    ):
        oc.append(k.send(src, src, sib))
    for copy in ring[0]:
        copy.wait_recv()
    src = kvs.at[:, :, :, c, :, KV_PARTS[0]]
    kvc = [k.send(src, src, sib)]
    o3[0].hand_on()
    o3[1].hand_on()
    for copy in plane_d:
        copy.wait_recv()
    plane2.append(RingGather(p, k, "x", lambda i: WD.at[:, slab_place(p, x=i), :, :, dhi]))
    plane2 += [
        RingGather(p, k, "y", lambda i: WD.at[i % 2, :, slab_place(p, y=i), :, dlo]),
        RingGather(p, k, "y", lambda i: WG.at[i // 2, :, i % 2, pl.ds(4, 4), :, lo]),
    ]
    for axis, ring4 in zip("xy", o3):
        for j in (1, 3):
            src = ring4.block(p.pos(axis, j))
            oc.append(k.send(src, src, sib))
    kvc[0].wait_recv()

    def unit(u):
        g, mm = u // 2, u % 2
        kv = unit_kv(kvs, mm, g)
        score = jnp.minimum(dot(kv, qts[g, mm]), unit_bias(bias, mm))
        peak = jnp.max(score, axis=0, keepdims=True)
        raised = jnp.exp(score - peak)
        total = jnp.sum(raised, axis=0, keepdims=True)
        probs = (raised * (1.0 / total)).astype(BF16)
        ots[g, mm] = dot_rows(kv, probs)[HEAD:]
        lse[u] = jnp.broadcast_to(peak + jnp.log(total), (8, 256))

    k.settle(packs + plane + plane_d)
    pl.loop(0, 6)(unit)
    for copy in ring[1]:
        copy.wait_recv()
    src = kvs.at[:, :, :, c, :, KV_PARTS[1]]
    kvc.append(k.send(src, src, sib))
    k.settle(o2 + xring.copies() + list(xcore.values()))
    kvc[1].wait_recv()
    keep.append(k.local(kvs, KV))
    for axis, ring4 in zip("xy", o3):
        ring4.wait()
        src = ring4.block(p.pos(axis, 2))
        oc.append(k.send(src, src, sib))
    pl.loop(6, 2 * KV_HEADS)(unit)
    for g in range(KV_HEADS):
        for t in range(2):
            cols = slice(t * 128, (t + 1) * 128)
            a, b = swap(ots[g, 0, :, cols], ots[g, 1, :, cols])
            at = (g * GROUP + 2 * t) * HEAD
            att[:, at : at + 128] = jnp.concatenate([a, b], axis=0).T.astype(BF16)
    keep += [k.local(lse, LSE), k.local(att, ATT)]
    rows.hand_on()
    for j in (1, 3):
        src = OG.at[p.pos("z", j), c]
        last.append(k.send(src, src, sib))
    for copy in oc:
        copy.wait_recv()
    keep.append(k.local(wos, WO))

    @pl.loop(0, 8)
    def _(t):
        w = wos[t // 4, t % 4].reshape(256, QD)
        cols = pl.ds(pl.multiple_of(t * 256, 256), 256)
        resid[:, cols] = xs[z, c, :, cols].astype(F32) + dot_last(att[...], w)

    plane2[2].hand_on()
    plane2[3].hand_on()
    plane2[4].hand_on()
    value = resid[...]
    n2[...] = (value * rms_scale(value) * gains_out[1:2, :]).astype(BF16)
    keep += [k.local(resid, RESID), k.local(n2, N2)]
    rows.wait()
    src = OG.at[p.pos("z", 2), c]
    last.append(k.send(src, src, sib))
    for ring4 in plane2:
        ring4.wait()
    for copy in last:
        copy.wait_recv()
    for copy in keep:
        copy.wait()
    slab.wait_send()
    k.drain()


VMEM = pl.BlockSpec(memory_space=pltpu.VMEM)


def front(*args):
    hbm = [
        sds((2, 4, 2, 4, 2, 16, QD), BF16),
        sds((2, 4, 2, 8, 16, 2 * FS), BF16),
        sds((2, 4, 2, 80, 1024), BF16),
        sds((4, 2, TOK, D), BF16),
        sds((4, 2, TOK, D), BF16),
        sds((2, 2, 4, 2, ROWS, 2 * KD), BF16),
        sds((QKV, TOK), F32),
        sds((2 * KV_HEADS, 8, 256), F32),
        sds((TOK, QD), BF16),
        sds((TOK, D), F32),
        sds((TOK, D), BF16),
        sds((16, 2048), BF16),
        sds((2, SEQ, 128), F32),
        sds((2, HEAD, TOK), F32),
        sds((8, D), F32),
        sds((2 * HEAD, 128), F32),
    ]
    scratch = [
        pltpu.VMEM((16, 2048), BF16),
        pltpu.VMEM((80, 1024), BF16),
        pltpu.VMEM((TOK, D), BF16),
        pltpu.VMEM((8, D), F32),
        pltpu.VMEM((2, HEAD, TOK), F32),
        pltpu.VMEM((2 * HEAD, 128), F32),
        pltpu.VMEM((4, 2, TOK, D), BF16),
        pltpu.VMEM((4, 2, TOK, D), BF16),
        pltpu.VMEM((2, 4, 2, 8, 16, 256), BF16),
        pltpu.VMEM((2, 4, 2, 4, 2, 16, QD), BF16),
        pltpu.VMEM((4, 2, TOK, 256), BF16),
        pltpu.VMEM((8, TOK, 256), BF16),
        pltpu.VMEM((QKV, TOK), F32),
        pltpu.VMEM((2 * KV_HEADS, 8, 256), F32),
        pltpu.VMEM((TOK, QD), BF16),
        pltpu.VMEM((TOK, D), F32),
        pltpu.VMEM((TOK, D), BF16),
        pltpu.VMEM((2, ROWS, 2 * KD), BF16),
        pltpu.VMEM((2, 2, 4, 2, ROWS, 2 * KD), BF16),
        pltpu.VMEM((2, SEQ, 128), F32),
        pltpu.VMEM((KV_HEADS, 2, 128, 256), BF16),
        pltpu.VMEM((KV_HEADS, 2, HEAD, 256), F32),
        pltpu.SemaphoreType.DMA((84,)),
        pltpu.SemaphoreType.DMA((150,)),
        pltpu.SemaphoreType.DMA((26,)),
    ]
    return pl.pallas_call(
        front_body,
        out_shape=hbm,
        in_specs=[ANY, VMEM, VMEM, ANY, VMEM, ANY] + [VMEM] * 6,
        out_specs=[ANY] * len(hbm),
        scratch_shapes=scratch,
        name="front",
        compiler_params=pltpu.CompilerParams(
            collective_id=0, has_side_effects=True, vmem_limit_bytes=56 << 20
        ),
    )(*args)


def ffn_body(n2, OG, WG, WD, wq, d_out, mix_out, dwg_out, dwd_out, WQ, *scr):
    (rows, ogs, wgs, wd80, wds, dgu, inn, din, part, mixs, r0, s0, r1, m0, dwg, dwd32, dwd) = scr[:17]
    (dn, wqv, ssem, rsem, lsem, wsem, vsem, wlsem) = scr[17:]
    p = Place()
    k = Links(wsem, vsem, wlsem)
    yh, x, yl, z, c = p.yh, p.x, p.yl, p.z, p.c
    sib = p.step("c", 1)
    greet([p.step(a, j) for a in "xyz" for j in (1, 2, 3)] + [sib])

    def remote(src, dst, i, to):
        return pltpu.make_async_remote_copy(
            src_ref=src,
            dst_ref=dst,
            send_sem=ssem.at[i],
            recv_sem=rsem.at[i],
            device_id=to,
            device_id_type=MESH,
        )

    def local(src, dst, i):
        copy = pltpu.make_async_copy(src, dst, lsem.at[i])
        copy.start()
        return copy

    def half_of(half, *at):
        return WQ.at[(*at, EVERY, pl.ds(half * 1024, 1024))]

    whole = (EVERY, EVERY, EVERY, EVERY, c)
    get_wq = k.local(wq, wqv)
    q1 = [k.plan(wq, WQ.at[yh, x, yl, z, c], p.step("z", j)) for j in (1, 2, 3)]
    q2, q3 = [], []
    for j in (1, 2, 3):
        for half, axis in ((0, "y"), (1, "x")):
            src = half_of(half, yh, x, yl, EVERY, c)
            q2.append(k.plan(src, src, p.step(axis, j)))
    for j in (1, 2, 3):
        src = half_of(0, EVERY, x, EVERY, EVERY, c)
        q3.append(k.plan(src, src, p.step("x", j)))
        src = half_of(1, yh, EVERY, yl, EVERY, c)
        q3.append(k.plan(src, src, p.step("y", j)))
    q4 = k.plan(WQ.at[whole], WQ.at[whole], sib)

    sent = []
    for copy in q1:
        copy.start()
    for j in (1, 3):
        copy = remote(n2, rows.at[z, c], j, p.step("z", j))
        copy.start()
        sent.append(copy)
    half = halves(rows.at[p.pos("z", 1), c])[1], halves(rows.at[p.pos("z", 3), c])[0]
    on_left = remote(half[0], half[0], 0, p.step("z", 3))
    on_right = remote(half[1], half[1], 2, p.step("z", 1))
    sent += [on_left, on_right]
    remote(n2, rows.at[z, c], 4, sib).start()
    own = local(n2, rows.at[z, c], 0)
    get_wd = local(WD, wd80, 1)
    get_wg = local(WG, wgs, 2)
    get_og = local(OG, ogs, 3)
    get_wd.wait()

    @pl.loop(0, 8)
    def _(i):
        yl, x = i // 4, i % 4
        a, b = wd80[yl, x, 0].astype(F32), wd80[yl, x, 1].astype(F32)
        at = pl.ds(pl.multiple_of(i * 80, 80), 80)
        wds[at, :1024] = jnp.concatenate([a[:40], b[:40]], axis=0).astype(BF16)
        wds[at, 1024:] = jnp.concatenate([a[40:], b[40:]], axis=0).astype(BF16)

    own.wait()
    get_wg.wait()
    get_og.wait()
    get_wq.wait()
    own_wq = k.local(wqv, WQ.at[yh, x, yl, z, c])

    def ring_step(j):
        return jnp.where(j == 2, 3, jnp.where(j == 3, 2, j))

    def d_inner_of(zz):
        din[...] = dot_last(ogs[zz].reshape(256, D), wds[...])

    d_inner_of(z)

    @pl.loop(0, 4)
    def _(j):
        o = ring_step(j)
        zz = (z + o) % 4
        at = pl.ds(pl.multiple_of(zz * 256, 256), 256)

        @pl.when(j == 1)
        def _():
            remote(n2, rows.at[z, c], 3, sib).wait_recv()
            on_left.start()
            remote(n2, rows.at[z, c], 1, sib).wait_recv()
            on_right.start()

        @pl.when(j == 3)
        def _():
            on_left.wait_recv()
            on_right.wait_recv()

        @pl.when(o > 0)
        def _():
            remote(rows.at[zz, c], rows.at[zz, c], 4 + o, sib).start()

        remote(rows.at[zz, c], rows.at[zz, 1 - c], 4 + o, sib).wait_recv()
        r = rows[zz].reshape(256, D)
        for t in range(5):
            lo, hi = slice(t * 128, (t + 1) * 128), slice(FS + t * 128, FS + (t + 1) * 128)
            w = jnp.concatenate(
                [wgs[:, :, :, :, :, lo].reshape(D, 128), wgs[:, :, :, :, :, hi].reshape(D, 128)], axis=1
            )
            both = dot(r, w)
            gate, upper = both[:, :128], both[:, 128:]
            sig = jax.nn.sigmoid(gate)
            active = gate * sig
            d_inner = din[:, lo]
            inn[at, lo] = (active * upper).astype(BF16)
            dgu[at, lo] = (d_inner * upper * sig * (1.0 + gate * (1.0 - sig))).astype(BF16)
            dgu[at, hi] = (d_inner * active).astype(BF16)

        for h in range(2):
            turned = dot_last(wgs[h].reshape(1024, 2 * FS), dgu[at]).astype(BF16)
            for cc in range(2):
                part[zz, cc, h * 1024 : (h + 1) * 1024] = turned[:, cc * TOK : (cc + 1) * TOK]

        remote(part.at[zz, 1 - c], r0.at[zz], 8 + o, sib).start()
        d_inner_of((z + ring_step((j + 1) % 4)) % 4)
        remote(part.at[zz, 1 - c], r0.at[zz], 8 + o, sib).wait_recv()

        @pl.loop(0, D, step=128)
        def _(t):
            here = pl.ds(pl.multiple_of(t, 128), 128)
            s0[zz, here] = (part[zz, c, here].astype(F32) + r0[zz, here].astype(F32)).astype(BF16)

        @pl.when(o > 0)
        def _():
            remote(s0.at[zz], r1.at[o - 1], 12 + o, p.at(z=zz)).start()

        @pl.when(j == 0)
        def _():
            own_wq.wait()
            for copy in q1:
                copy.wait_recv()
            for copy in q2:
                copy.start()

        @pl.when(j == 1)
        def _():
            for copy in q2:
                copy.wait_recv()
            for copy in q3:
                copy.start()

    @pl.loop(0, 4)
    def _(t):
        cols = pl.ds(pl.multiple_of(t * 512, 512), 512)
        mixs[:, :, :, cols] = dot(inn[...], wds[:, cols]).astype(BF16).reshape(4, 2, TOK, 512)

    mix_core = remote(mixs.at[:, 1 - c], m0, 16, sib)
    mix_core.start()

    @pl.loop(0, 8)
    def _(t):
        cols = pl.ds(pl.multiple_of(t * 256, 256), 256)
        left = rows[:, :, :, cols].reshape(8 * TOK, 256)
        dwg[t // 4, t % 4] = dot_rows(left, dgu[...]).astype(BF16).reshape(2, TOK, 2 * FS)

    out_wg = local(dwg, dwg_out, 5)
    mix_core.wait_recv()

    @pl.loop(0, 4)
    def _(zz):
        @pl.loop(0, TOK, step=16)
        def _(t):
            here = pl.ds(pl.multiple_of(t, 16), 16)
            m0[zz, here] = (mixs[zz, c, here].astype(F32) + m0[zz, here].astype(F32)).astype(BF16)

    out_mix = local(m0, mix_out, 4)
    for copy in q3:
        copy.wait_recv()
    q4.start()

    @pl.loop(0, 5)
    def _(t):
        units = pl.ds(pl.multiple_of(t * 128, 128), 128)
        dwd32[units] = dot_rows(inn[:, units], ogs[...].reshape(8 * TOK, D))

    @pl.loop(0, 8)
    def _(i):
        yl, x = i // 4, i % 4
        at = pl.ds(pl.multiple_of(i * 80, 80), 80)
        lo, hi = dwd32[at, :1024], dwd32[at, 1024:]
        dwd[yl, x, 0] = jnp.concatenate([lo[:40], hi[:40]], axis=0).astype(BF16)
        dwd[yl, x, 1] = jnp.concatenate([lo[40:], hi[40:]], axis=0).astype(BF16)

    out_wd = local(dwd, dwd_out, 6)
    for o in (1, 2, 3):
        remote(s0.at[0], r1.at[o - 1], 12 + o, sib).wait_recv()

    for t in range(0, D, 128):
        here = slice(t, t + 128)
        total = s0[z, here].astype(F32)
        for j in range(3):
            total = total + r1[j, here].astype(F32)
        dn[:, here] = total.T

    out_dn = local(dn, d_out, 7)
    q4.wait_recv()
    k.drain()
    for copy in sent:
        copy.wait_send()
    for o in range(4):
        remote(rows.at[0, 0], rows.at[0, 0], 4 + o, sib).wait_send()
        remote(part.at[0, 0], r0.at[0], 8 + o, sib).wait_send()
    for o in (1, 2, 3):
        remote(s0.at[0], r1.at[o - 1], 12 + o, sib).wait_send()
    mix_core.wait_send()
    for copy in (out_mix, out_wg, out_wd, out_dn):
        copy.wait()


def ffn(n2, OG, WG, WD, wq):
    outs = [
        sds((TOK, D), F32),
        sds((4, TOK, D), BF16),
        sds((2, 4, 2, TOK, 2 * FS), BF16),
        sds((2, 4, 2, 80, 1024), BF16),
        sds((2, 4, 2, 4, 2, 16, 2048), BF16),
    ]
    scratch = [
        pltpu.VMEM((4, 2, TOK, D), BF16),
        pltpu.VMEM((4, 2, TOK, D), BF16),
        pltpu.VMEM((2, 4, 2, 8, 16, 2 * FS), BF16),
        pltpu.VMEM((2, 4, 2, 80, 1024), BF16),
        pltpu.VMEM((FS, D), BF16),
        pltpu.VMEM((8 * TOK, 2 * FS), BF16),
        pltpu.VMEM((8 * TOK, FS), BF16),
        pltpu.VMEM((256, FS), F32),
        pltpu.VMEM((4, 2, D, TOK), BF16),
        pltpu.VMEM((4, 2, TOK, D), BF16),
        pltpu.VMEM((4, D, TOK), BF16),
        pltpu.VMEM((4, D, TOK), BF16),
        pltpu.VMEM((3, D, TOK), BF16),
        pltpu.VMEM((4, TOK, D), BF16),
        pltpu.VMEM((2, 4, 2, TOK, 2 * FS), BF16),
        pltpu.VMEM((FS, D), F32),
        pltpu.VMEM((2, 4, 2, 80, 1024), BF16),
        pltpu.VMEM((TOK, D), F32),
        pltpu.VMEM((16, 2048), BF16),
        pltpu.SemaphoreType.DMA((17,)),
        pltpu.SemaphoreType.DMA((17,)),
        pltpu.SemaphoreType.DMA((8,)),
        pltpu.SemaphoreType.DMA((24,)),
        pltpu.SemaphoreType.DMA((24,)),
        pltpu.SemaphoreType.DMA((4,)),
    ]
    return pl.pallas_call(
        ffn_body,
        out_shape=outs,
        in_specs=[ANY] * 5,
        out_specs=[ANY] * 5,
        scratch_shapes=scratch,
        name="ffn",
        compiler_params=pltpu.CompilerParams(
            collective_id=1, has_side_effects=True, vmem_limit_bytes=60 << 20
        ),
    )(n2, OG, WG, WD, wq)


def back_body(*refs):
    (DN, X_IN, OG_IN, RESID, ATT, PT, LSE, WQ, WO, KV, mix_part, dwg, dwd, NA) = refs[:14]
    (BIAS, ROPE, GAINS, QKGAIN) = refs[14:18]
    (IN_GRAD, MIXED, GWG, GWD, GQ, GO, SMALL) = refs[18:25]
    (dn, xv, ogv, resid, pt, lse, in_grad, mixed, kvs, bias, qts, qns, dts, dns, dqt, dpt, datt, dres) = refs[25:43]
    (kpart, k0, k1, ks1, k2, kres, w2, wo2, low2, att2, do, dp, dpm, na2, dqm, mix1) = refs[43:59]
    (rope, gains, qkgain) = refs[59:62]
    scr = list(refs[62:])
    parts = []
    for i, shapes in enumerate(PLANE_SHAPES + O_SHAPES):
        n = 2 * len(shapes) + (i < 4)
        parts.append(scr[:n])
        scr = scr[n:]
    vec, vrecv, ssem, rsem, lsem = scr
    p = Place()
    k = Links(ssem, rsem, lsem)
    yl, z, c = p.yl, p.z, p.c
    m = z * 2 + c
    sib = p.step("c", 1)
    yl_partner = p.at(y=p.yh * 2 + 1 - yl)
    get = {}

    def fetch(**pairs):
        for name, (src, dst) in pairs.items():
            get[name] = k.local(src, dst)

    fetch(dn=(DN, dn), og=(OG_IN, ogv), resid=(RESID, resid), gains=(GAINS, gains))
    get_w = [k.local(WO.at[t // 4, t % 4], wo2.at[t]) for t in range(8)]
    fetch(pt=(PT, pt), rope=(ROPE, rope), qkgain=(QKGAIN, qkgain), att=(ATT, att2.at[0]))
    partners = [p.step(a, j) for a in "xyz" for j in (1, 2, 3)]
    partners += [p.at(z=(z + j) % 4, c=1 - c) for j in range(4)]
    slab_to, slab_from = slab_target(p), slab_source(p)
    own_slab = same(p, slab_to)
    greet_plane(p, partners, slab_to, slab_from, own_slab)
    plane = [
        ring_reduce(p, k, dwg, wg_stages(0), parts[0], 16),
        ring_reduce(p, k, dwg, wg_stages(1), parts[1], 16),
        ring_reduce(p, k, dwd, wd_stages(p, 0), parts[2], 16),
        ring_reduce(p, k, dwd, wd_stages(p, 1), parts[3], 16),
    ]
    for step in plane + plane:
        next(step)
    pair_att = k.send(ATT, att2.at[1], sib)

    def mix_send(part):
        at = pl.ds((0, 80)[part], (80, 48)[part])
        return [k.send(mix_part.at[p.pos("z", j), at], mix1.at[j - 1, at], p.step("z", j)) for j in (1, 2, 3)]

    mixing = mix_send(0)
    for name in ("dn", "og", "resid", "gains"):
        get[name].wait()
    value = resid[...]
    scale_two = rms_scale(value)
    norm_two = value * scale_two
    d_resid = ogv[...].astype(F32) + norm_back(dn[...], norm_two, scale_two, gains[1:2, :])
    dres[...] = d_resid
    low2[0] = d_resid.astype(BF16)
    pair_low = k.send(low2.at[0], low2.at[1], sib)
    fetch(kv=(KV, kvs), lse=(LSE, lse), bias=(BIAS, bias))
    for name in ("pt", "rope", "qkgain"):
        get[name].wait()
    cos, sin = rope[0], rope[1]
    qgain, kgain = qkgain[:HEAD], qkgain[HEAD:]

    @pl.loop(0, KV_HEADS)
    def _(g):
        for mm, unit in enumerate(query_units(pt, g, cos, sin, qgain)):
            qts[g, mm] = unit.astype(BF16)
            qns[g, mm] = unit.T.astype(BF16)

    for t in range(8):
        get_w[t].wait()
        term = dot(low2[0, :, t * 256 : (t + 1) * 256], wo2[t].reshape(256, QD))
        datt[...] = term if t == 0 else datt[...] + term
    for g in range(KV_HEADS):
        tiles = []
        for t in range(2):
            at = (g * GROUP + 2 * t) * HEAD
            both = low(datt[:, at : at + 128]).T
            tiles.append(swap(both[:HEAD], both[HEAD:]))
        for mm in range(MICRO):
            none = jnp.zeros((HEAD, 256), F32)
            unit = jnp.concatenate([none, jnp.concatenate([tiles[0][mm], tiles[1][mm]], axis=1)], axis=0)
            dts[g, mm] = unit.astype(BF16)
            dns[g, mm] = unit.T.astype(BF16)
    fetch(x=(X_IN, xv), mix=(mix_part.at[z], mix1.at[3]))
    get["kv"].wait()
    get["lse"].wait()
    get["bias"].wait()

    def unit(u):
        g, mm = u // 2, u % 2
        kv = unit_kv(kvs, mm, g)
        score = jnp.minimum(dot(kv, qts[g, mm]), unit_bias(bias, mm))
        again = jnp.exp(score - lse[u, 0:1, :])
        d_probs = dot(kv, dts[g, mm])
        inner = jnp.sum(again * d_probs, axis=0, keepdims=True)
        d_scores = (again * (d_probs - inner)).astype(BF16)
        d_kv = dot(d_scores, qns[g, mm]) + dot(again.astype(BF16), dns[g, mm])
        cols = pl.ds(pl.multiple_of(g * 128, 128), 128)
        kpart[mm, :, :, :, :, cols] = d_kv.astype(BF16).reshape(2, 4, 2, ROWS, 128)
        dqt[g, mm] = dot_rows(kv, d_scores)[:HEAD] * (HEAD ** -0.5)

    def core_send(cols):
        return k.send(kpart.at[:, :, :, 1 - c, :, cols], k0.at[:, :, :, :, cols], sib)

    def ring_send(core, cols):
        core.wait_recv()

        @pl.loop(0, 4)
        def _(zz):
            for a in range(2):
                for b in range(2):
                    here = (a, b, zz, EVERY, cols)
                    both = kpart[a, b, zz, c, :, cols].astype(F32) + k0[here].astype(F32)
                    k0[here] = both.astype(BF16)

        return [
            k.send(k0.at[:, :, p.pos("z", j), :, cols], k1.at[j - 1, :, :, :, cols], p.step("z", j))
            for j in (1, 2, 3)
        ]

    pl.loop(0, 6)(unit)
    core = core_send(KV_PARTS[0])
    for step in plane:
        next(step)
    ring = ring_send(core, KV_PARTS[0])
    pl.loop(6, 2 * KV_HEADS)(unit)
    core = core_send(KV_PARTS[1])
    ring += ring_send(core, KV_PARTS[1])
    get["att"].wait()
    pair_att.wait_recv()
    pair_low.wait_recv()
    att_cols = pl.ds(pl.multiple_of(c * 640, 128), 640)

    @pl.loop(0, 8)
    def _(t):
        cols = pl.ds(pl.multiple_of(t * 256, 256), 256)
        left = low2[:, :, cols].reshape(2 * TOK, 256)
        right = att2[:, :, att_cols].reshape(2 * TOK, 640)
        do[t // 4, t % 4] = dot_rows(left, right).astype(BF16).reshape(2, 4, 32, 640)

    outward = [staged_reduce(p, k, do, o_stages(i), parts[6 + i], 16) for i in range(3)]
    next(outward[0])

    query_sum = jnp.zeros((HEAD, TOK), F32)
    for g in range(KV_HEADS):
        heads = []
        for t in range(2):
            cols = slice(t * 128, (t + 1) * 128)
            heads += list(swap(dqt[g, 0, :, cols], dqt[g, 1, :, cols]))
        for h in range(GROUP):
            at = (g * GROUP + h) * HEAD
            d_raw, term = head_back(pt[at : at + HEAD], heads[h], cos, sin, qgain)
            query_sum = query_sum + term
            dpt[at : at + HEAD] = d_raw

    for copy in ring:
        copy.wait_recv()
    for a in range(2):
        for b in range(2):
            total = k0[a, b, z].astype(F32)
            for j in range(3):
                total = total + k1[j, a, b].astype(F32)
            ks1[a, b] = total.astype(BF16)
    across = k.send(ks1.at[:, 1 - yl], k2, yl_partner)
    next(outward[1])
    next(outward[2])
    next(plane[0])
    next(plane[2])
    across.wait_recv()
    next(plane[1])
    next(plane[3])
    for a in range(2):
        kres[pl.ds(a * ROWS, ROWS)] = ks1[a, yl].astype(F32) + k2[a].astype(F32)
    key_sum = jnp.zeros((HEAD, TOK), F32)
    for g in range(KV_HEADS):
        both = kres[:, g * 128 : (g + 1) * 128].T
        at = QD + g * HEAD
        d_raw, term = head_back(pt[at : at + HEAD], both[:HEAD], cos, sin, kgain)
        key_sum = key_sum + term
        dpt[at : at + HEAD] = d_raw
        dpt[at + KD : at + KD + HEAD] = both[HEAD:]
    get_q = [k.local(WQ.at[0, t], w2.at[t]) for t in range(2)]
    get_n = [k.local(NA.at[:, :, :, pl.ds(t * 256, 256)], na2.at[t]) for t in range(2)]
    for t in range(8):
        block = jnp.concatenate([dpt[t * 240 : (t + 1) * 240], jnp.zeros((16, TOK), F32)], axis=0)
        dp[t] = block.T.astype(BF16)
    sums = jnp.concatenate(
        [jnp.sum(query_sum.T, axis=0, keepdims=True), jnp.sum(key_sum.T, axis=0, keepdims=True)], axis=1
    )
    vec[0] = jnp.broadcast_to(sums, (8, 128))
    small = small_reduce(p, k, vec, vrecv)
    next(small)

    last, keep = [], []

    def to_owners(total, dst):
        for dz in range(4):
            for dc in range(2):
                zz, cc = (z + dz) % 4, (c + dc) % 2
                src = total.at[pl.ds(pl.multiple_of((zz * 2 + cc) * 16, 16), 16)]
                if dz == 0 and dc == 0:
                    keep.append(k.local(src, dst))
                else:
                    last.append(k.send(src, dst, p.at(z=zz, c=cc)))

    def slab_home(half):
        slab = Slab(k, parts[2 + half][-1], GWD.at[:, pl.ds(half * 512, 512)], slab_from, own_slab)
        slab.start()
        return slab

    members = []
    for dz in range(4):
        for dc in range(2):
            zz, cc = (z + dz) % 4, (c + dc) % 2
            src = dp.at[zz * 2 + cc]
            if dz == 0 and dc == 0:
                own_dp = k.local(src, dpm.at[z, c])
            else:
                members.append(k.send(src, dpm.at[z, c], p.at(z=zz, c=cc)))
    mixing += mix_send(1)
    own_dp.wait()
    for copy in members:
        copy.wait_recv()
    next(small)
    for t in range(8):
        get_n[t].wait()
        total = dot_rows(na2[t % 2].reshape(8 * TOK, 256), dpm[...].reshape(8 * TOK, 256))
        dqm[t // 4, t % 4] = total.astype(BF16).reshape(2, TOK, 256)
        if t < 6:
            get_n.append(k.local(NA.at[:, :, :, pl.ds((t + 2) * 256, 256)], na2.at[t % 2]))
    inward = [staged_reduce(p, k, dqm, q_stages(i), parts[4 + i], 16) for i in range(2)]
    for step in inward:
        next(step)
    next(small)
    for half in range(2):
        next(plane[half], None)
        to_owners(parts[half][-1], GWG.at[:, pl.ds(pl.multiple_of(half * FF + m * FS, 128), FS)])
    slabs = []
    for half in range(2):
        next(plane[2 + half], None)
        slabs.append(slab_home(half))
    next(outward[0])
    next(outward[1])
    left = jnp.concatenate([dp[i] for i in range(8)], axis=1)

    def d_normed_block(t):
        get_q[t].wait()
        w = w2[t % 2].reshape(256, 2048)
        in_grad[:, t * 256 : (t + 1) * 256] = dot_last(left, w)
        if t < 6:
            get_q.append(k.local(WQ.at[(t + 2) // 4, (t + 2) % 4], w2.at[t % 2]))

    for t in range(4):
        d_normed_block(t)
    for step in inward:
        next(step)
    next(outward[2])
    next(small)
    for t in range(4, 8):
        d_normed_block(t)
    for half, step in enumerate(inward):
        next(step, None)
        to_owners(parts[4 + half][-1], GQ.at[:, pl.ds(pl.multiple_of(m * 256 + half * 128, 128), 128)])
    get["x"].wait()
    hidden = xv[...].astype(F32)
    scale_one = rms_scale(hidden)
    in_grad[...] = dres[...] + norm_back(in_grad[...], hidden * scale_one, scale_one, gains[0:1, :])
    keep.append(k.local(in_grad, IN_GRAD))
    next(small, None)
    keep.append(k.local(vec.at[4], SMALL))
    get["mix"].wait()
    for copy in mixing:
        copy.wait_recv()

    @pl.loop(0, TOK, step=16)
    def _(t):
        at = pl.ds(pl.multiple_of(t, 16), 16)
        total = resid[at]
        for j in range(4):
            total = total + mix1[j, at].astype(F32)
        mixed[at] = total.astype(BF16)

    keep.append(k.local(mixed, MIXED))
    for step in outward:
        next(step)
    for i, step in enumerate(outward):
        next(step, None)
        total = parts[6 + i][-1]
        dst = GO.at[c, :, pl.ds(*O_PARTS[i])]
        keep.append(k.local(total.at[pl.ds(pl.multiple_of(c * 16, 16), 16)], dst))
        last.append(k.send(total.at[pl.ds(pl.multiple_of((1 - c) * 16, 16), 16)], dst, sib))
    for copy in keep:
        copy.wait()
    for copy in last:
        copy.wait_recv()
    for slab in slabs:
        slab.wait_recv()
        slab.wait_send()
    k.drain()


def head_back(raw, grad, cos, sin, gain):
    scale = head_scale(raw)
    normed = raw * scale
    d_head = grad * cos + half_back(grad * sin)
    scaled = d_head * gain
    inner = jnp.mean(scaled * normed, axis=0, keepdims=True)
    return scale * (scaled - normed * inner), d_head * normed


def back(*args):
    w = 2 * KD
    outs = [
        sds((TOK, D), F32),
        sds((TOK, D), BF16),
        sds((16, 2 * FF), BF16),
        sds((80, 1024), BF16),
        sds((16, 2048), BF16),
        sds((2, 16, 640), BF16),
        sds((8, 128), F32),
    ]
    scratch = [
        pltpu.VMEM((TOK, D), F32),
        pltpu.VMEM((TOK, D), BF16),
        pltpu.VMEM((TOK, D), BF16),
        pltpu.VMEM((TOK, D), F32),
        pltpu.VMEM((QKV, TOK), F32),
        pltpu.VMEM((2 * KV_HEADS, 8, 256), F32),
        pltpu.VMEM((TOK, D), F32),
        pltpu.VMEM((TOK, D), BF16),
        pltpu.VMEM((2, 2, 4, 2, ROWS, w), BF16),
        pltpu.VMEM((2, SEQ, 128), F32),
        pltpu.VMEM((KV_HEADS, 2, 128, 256), BF16),
        pltpu.VMEM((KV_HEADS, 2, 256, 128), BF16),
        pltpu.VMEM((KV_HEADS, 2, 128, 256), BF16),
        pltpu.VMEM((KV_HEADS, 2, 256, 128), BF16),
        pltpu.VMEM((KV_HEADS, 2, HEAD, 256), F32),
        pltpu.VMEM((QKV, TOK), F32),
        pltpu.VMEM((TOK, QD), F32),
        pltpu.VMEM((TOK, D), F32),
        pltpu.VMEM((2, 2, 4, 2, ROWS, w), BF16),
        pltpu.VMEM((2, 2, 4, ROWS, w), BF16),
        pltpu.VMEM((3, 2, 2, ROWS, w), BF16),
        pltpu.VMEM((2, 2, ROWS, w), BF16),
        pltpu.VMEM((2, ROWS, w), BF16),
        pltpu.VMEM((TOK, w), F32),
        pltpu.VMEM((2, 2, 4, 2, 16, 2048), BF16),
        pltpu.VMEM((8, 2, 4, 2, 16, QD), BF16),
        pltpu.VMEM((2, TOK, D), BF16),
        pltpu.VMEM((2, TOK, QD), BF16),
        pltpu.VMEM((2, 4, 2, 4, 32, 640), BF16),
        pltpu.VMEM((8, TOK, 256), BF16),
        pltpu.VMEM((4, 2, TOK, 256), BF16),
        pltpu.VMEM((2, 4, 2, TOK, 256), BF16),
        pltpu.VMEM((2, 4, 2, TOK, 256), BF16),
        pltpu.VMEM((4, TOK, D), BF16),
        pltpu.VMEM((2, HEAD, TOK), F32),
        pltpu.VMEM((8, D), F32),
        pltpu.VMEM((2 * HEAD, 128), F32),
    ]
    for i, shapes in enumerate(PLANE_SHAPES + O_SHAPES):
        scratch += staged_scratch(shapes, i < 4)
    scratch += [
        pltpu.VMEM((5, 8, 128), F32),
        pltpu.VMEM((4, 3, 8, 128), F32),
        pltpu.SemaphoreType.DMA((150,)),
        pltpu.SemaphoreType.DMA((150,)),
        pltpu.SemaphoreType.DMA((36,)),
    ]
    return pl.pallas_call(
        back_body,
        out_shape=outs,
        in_specs=[ANY] * 18,
        out_specs=[ANY] * 7,
        scratch_shapes=scratch,
        name="back",
        compiler_params=pltpu.CompilerParams(
            collective_id=2, has_side_effects=True, vmem_limit_bytes=60 << 20
        ),
    )(*args)


def finish_body(*refs):
    IN_GRAD, MIXED, GWG, GWD, GQ, GO, SUMS, WG, WQ, g1, g2 = refs[:11]
    in_out, mixed_out, Q, O, G, DOWN, ATTN, FFN, QG, KG = refs[11:21]
    (gwg, gwd, gq, go, sums, wg, wq, q, o, g, down, attn, ffn_, qg, kg, ing, mix, sem) = refs[21:]
    used = []

    def copy(src, dst):
        out = pltpu.make_async_copy(src, dst, sem.at[len(used)])
        out.start()
        used.append(out)
        return out

    rows = [copy(IN_GRAD, ing), copy(MIXED, mix)]
    through = []
    got = [copy(a, b) for a, b in ((GQ, gq), (WQ, wq), (GO, go), (SUMS, sums), (GWD, gwd), (GWG, gwg), (WG, wg))]
    for one in got[:5]:
        one.wait()
    for one, (src, dst) in zip(rows, ((ing, in_out), (mix, mixed_out))):
        one.wait()
        through.append(copy(src, dst))
    wide = gq[...].astype(F32)
    lane = lax.broadcasted_iota(jnp.int32, (16, QKV), 1)
    total = jnp.zeros((16, QKV), F32)
    for i in range(8):
        piece = jnp.concatenate([wide[:, i * 256 : (i + 1) * 256], jnp.zeros((16, QKV - 256), F32)], axis=1)
        here = (lane >= i * 240) & (lane < (i + 1) * 240)
        total = jnp.where(here, pltpu.roll(piece, 240 * i, 1) if i else piece, total)
    q[...] = total
    through.append(copy(q, Q))
    o[...] = jnp.concatenate([go[0].astype(F32), go[1].astype(F32)], axis=1)
    through.append(copy(o, O))
    slab = gwd[...].astype(F32)
    down[...] = jnp.concatenate([slab[:40], slab[40:]], axis=1)
    through.append(copy(down, DOWN))
    attn[...] = flat(jnp.sum(wq[...].astype(F32) * total, axis=1, keepdims=True)) / g1[...].astype(F32)
    through.append(copy(attn, ATTN))
    qg[...] = sums[0:1, :HEAD]
    kg[...] = pltpu.roll(sums[...], HEAD, 1)[0:1, :HEAD]
    through += [copy(qg, QG), copy(kg, KG)]
    for one in got[5:]:
        one.wait()
    grown = gwg[...].astype(F32)
    g[...] = grown
    through.append(copy(g, G))
    ffn_[...] = flat(jnp.sum(wg[...].astype(F32) * grown, axis=1, keepdims=True)) / g2[...].astype(F32)
    through.append(copy(ffn_, FFN))
    for one in through:
        one.wait()


def flat(col):
    n = col.shape[0]
    place = lax.broadcasted_iota(jnp.int32, (n, n), 0) == lax.broadcasted_iota(jnp.int32, (n, n), 1)
    return jnp.sum(jnp.where(place, jnp.broadcast_to(col, (n, n)), 0.0), axis=0, keepdims=True)


def finish(*args):
    outs = [
        sds((TOK, D), F32),
        sds((TOK, D), BF16),
        sds((16, QKV), F32),
        sds((16, QD), F32),
        sds((16, 2 * FF), F32),
        sds((40, D), F32),
        sds((1, 16), F32),
        sds((1, 16), F32),
        sds((1, HEAD), F32),
        sds((1, HEAD), F32),
    ]
    ins = [(16, 2 * FF), (80, 1024), (16, 2048), (2, 16, 640), (8, 128), (16, 2 * FF), (16, QKV)]
    scratch = [pltpu.VMEM(a, F32 if a == (8, 128) else BF16) for a in ins]
    scratch += [pltpu.VMEM(a.shape, a.dtype) for a in outs[2:] + outs[:2]]
    return pl.pallas_call(
        finish_body,
        out_shape=outs,
        in_specs=[ANY] * 9 + [VMEM] * 2,
        out_specs=[ANY] * 10,
        scratch_shapes=scratch + [pltpu.SemaphoreType.DMA((19,))],
        name="finish",
        compiler_params=pltpu.CompilerParams(vmem_limit_bytes=60 << 20),
    )(*args)


def per_device(
    tokens,
    segment_ids,
    w_qkv,
    w_out,
    w_gate_up,
    w_down,
    attn_gain,
    ffn_gain,
    query_gain,
    key_gain,
    out_grad,
):
    g1, g2, g3, g4 = [a.reshape(1, -1) for a in (attn_gain, ffn_gain, query_gain, key_gain)]
    og_in = out_grad.reshape(TOK, D)
    x_in = tokens.reshape(TOK, D)
    (WO, WG, WD, OG, NA, KV, pt, lse, attended, resid, n2, wq_in, bias, rope, gain_rows, head_gains) = front(
        x_in, w_qkv, w_out.T, w_gate_up, w_down, og_in, segment_ids, g1, g2, g3, g4, rope_parts()
    )
    d_normed, mix_part, dwg, dwd, WQ = ffn(n2, OG, WG, WD, wq_in)
    in_grad, mixed, gwg, gwd, gq, go, sums = back(
        d_normed, x_in, og_in, resid, attended, pt, lse, WQ, WO, KV, mix_part, dwg, dwd, NA,
        bias, rope, gain_rows, head_gains,
    )
    outs = finish(in_grad, mixed, gwg, gwd, gq, go, sums, w_gate_up, w_qkv, g1, g2)
    return (
        outs[1].reshape(MICRO, ROWS, D),
        outs[0].reshape(MICRO, ROWS, D),
        outs[2],
        outs[3].T,
        outs[4],
        outs[5],
        outs[6].reshape(16),
        outs[7].reshape(16),
        outs[8].reshape(HEAD),
        outs[9].reshape(HEAD),
    )


def solution(mesh):
    return jax.shard_map(
        per_device,
        mesh=mesh,
        in_specs=(
            P(None, ("grp", "seq"), None),
            P(None, "grp"),
            P(("grp", "seq"), None),
            P(None, ("grp", "seq")),
            P(("grp", "seq"), None),
            P(("grp", "seq"), None),
            P(("grp", "seq")),
            P(("grp", "seq")),
            P(),
            P(),
            P(None, ("grp", "seq"), None),
        ),
        out_specs=(
            P(None, ("grp", "seq"), None),
            P(None, ("grp", "seq"), None),
            P(("grp", "seq"), None),
            P(None, ("grp", "seq")),
            P(("grp", "seq"), None),
            P(("grp", "seq"), None),
            P(("grp", "seq")),
            P(("grp", "seq")),
            P(),
            P(),
        ),
        check_vma=False,
    )
```

```python
import jax
import jax.numpy as jnp
import numpy as np
from jax import lax
from jax.experimental import pallas as pl
from jax.experimental.pallas import tpu as pltpu
from jax.sharding import PartitionSpec as P

Q_HEADS = 20
KV_HEADS = 5
GROUP = 4
HEAD = 64
D = 2048
FF = 5120
QD = 1280
KD = 320
QKV = 1920
SEQ = 1024
MICRO = 2
ROWS = 64
TOK = 128
FS = 640
EPS = 1e-06
MESH = pl.DeviceIdType.MESH
F32 = jnp.float32
BF16 = jnp.bfloat16
ANY = pl.BlockSpec(memory_space=pl.ANY)


class Place:
    def __init__(self):
        g = lax.axis_index("grp")
        s = lax.axis_index("seq")
        self.g, self.s = g, s
        self.yh, self.x = g // 4, g % 4
        self.yl, self.z, self.c = s // 8, (s // 2) % 4, s % 2
        self.y = self.yh * 2 + self.yl

    def at(self, x=None, y=None, z=None, c=None):
        x = self.x if x is None else x
        y = self.y if y is None else y
        z = self.z if z is None else z
        c = self.c if c is None else c
        return ((y // 2) * 4 + x, (y % 2) * 8 + z * 2 + c)

    def step(self, axis, k):
        if axis == "x":
            return self.at(x=(self.x + k) % 4)
        if axis == "y":
            return self.at(y=(self.y + k) % 4)
        if axis == "z":
            return self.at(z=(self.z + k) % 4)
        return self.at(c=1 - self.c)

    def pos(self, axis, k):
        return (getattr(self, axis) + k) % 4


class Links:
    def __init__(self, send_sems, recv_sems, local_sems):
        self.send_sems, self.recv_sems, self.local_sems = send_sems, recv_sems, local_sems
        self.received = 0
        self.free = {"send": list(range(send_sems.shape[0]))[::-1], "local": list(range(local_sems.shape[0]))[::-1]}
        self.sent = {}

    def plan(self, src, dst, to):
        i = self.received
        self.received += 1
        assert i < self.recv_sems.shape[0], i
        slot = self.free["send"].pop()
        copy = pltpu.make_async_remote_copy(
            src_ref=src,
            dst_ref=dst,
            send_sem=self.send_sems.at[slot],
            recv_sem=self.recv_sems.at[i],
            device_id=to,
            device_id_type=MESH,
        )
        self.sent[id(copy)] = (copy, slot)
        return copy

    def send(self, src, dst, to):
        copy = self.plan(src, dst, to)
        copy.start()
        return copy

    def local(self, src, dst):
        slot = self.free["local"].pop()
        copy = pltpu.make_async_copy(src, dst, self.local_sems.at[slot])
        copy.start()
        return Local(self, copy, slot)

    def settle(self, copies):
        for copy in copies:
            copy, slot = self.sent.pop(id(copy))
            copy.wait_send()
            self.free["send"].append(slot)

    def drain(self):
        self.settle([copy for copy, _ in list(self.sent.values())])


class Local:
    def __init__(self, links, copy, slot):
        self.links, self.copy, self.slot = links, copy, slot

    def wait(self):
        self.copy.wait()
        self.links.free["local"].append(self.slot)


def halves(ref):
    n = ref.shape[0] // 2
    return ref.at[pl.ds(0, n)], ref.at[pl.ds(n, n)]


class RingGather:
    def __init__(self, p, k, axis, block, src=None):
        self.p, self.k, self.axis, self.block = p, k, axis, block
        dst = block(p.pos(axis, 0))
        src = dst if src is None else src
        self.right = k.send(src, dst, p.step(axis, 1))
        self.left = k.send(src, dst, p.step(axis, 3))

    def from_before(self):
        self.right.wait_recv()
        half = halves(self.block(self.p.pos(self.axis, 3)))[0]
        self.far_right = self.k.send(half, half, self.p.step(self.axis, 1))

    def from_after(self):
        self.left.wait_recv()
        half = halves(self.block(self.p.pos(self.axis, 1)))[1]
        self.far_left = self.k.send(half, half, self.p.step(self.axis, 3))

    def hand_on(self):
        self.from_before()
        self.from_after()

    def wait(self):
        self.far_right.wait_recv()
        self.far_left.wait_recv()

    def copies(self):
        return [self.right, self.left, self.far_right, self.far_left]


def greet(partners):
    barrier = pltpu.get_barrier_semaphore()
    for to in partners:
        pl.semaphore_signal(barrier, inc=1, device_id=to, device_id_type=MESH)
    pl.semaphore_wait(barrier, len(partners))


def sds(shape, dtype):
    return jax.ShapeDtypeStruct(shape, dtype)


def rms_scale(values):
    return lax.rsqrt(jnp.mean(values * values, axis=-1, keepdims=True) + EPS)


def norm_back(upstream, normed, scale, gain):
    scaled = upstream * gain
    inner = jnp.mean(scaled * normed, axis=-1, keepdims=True)
    return scale * (scaled - normed * inner)


def dot(left, right):
    return jnp.dot(left, right, preferred_element_type=F32)


def dot_last(left, right):
    return lax.dot_general(left, right, (((1,), (1,)), ((), ())), preferred_element_type=F32)


def dot_rows(left, right):
    return lax.dot_general(left, right, (((0,), (0,)), ((), ())), preferred_element_type=F32)


def slab_target(p):
    return p.at(x=(p.z + p.x) % 4, y=(p.c + p.yh) % 2 * 2 + p.yl, z=p.g // 2, c=p.g % 2)


def slab_place(p, x=None, y=None):
    m = p.z * 2 + p.c
    if x is not None:
        return (x + 4 - m % 4) % 4
    return (y // 2 + 2 - m // 4) % 2


def slab_source(p):
    m = p.z * 2 + p.c
    return p.at(x=m % 4, y=(m // 4) * 2 + p.yl, z=slab_place(p, x=p.x), c=slab_place(p, y=p.y))


def same(p, to):
    return (to[0] == p.g) & (to[1] == p.s)


def greet_plane(p, partners, slab_to, slab_from, own_slab):
    barrier = pltpu.get_barrier_semaphore()
    for to in partners:
        pl.semaphore_signal(barrier, inc=1, device_id=to, device_id_type=MESH)

    @pl.when(jnp.logical_not(own_slab))
    def _():
        pl.semaphore_signal(barrier, inc=1, device_id=slab_to, device_id_type=MESH)
        pl.semaphore_signal(barrier, inc=1, device_id=slab_from, device_id_type=MESH)
        pl.semaphore_wait(barrier, len(partners) + 2)

    @pl.when(own_slab)
    def _():
        pl.semaphore_wait(barrier, len(partners))


class Slab:
    def __init__(self, k, src, dst, to, own):
        self.own, self.src, self.dst = own, src, dst
        self.far = k.plan(src, dst, to)
        k.sent.pop(id(self.far))
        self.near = pltpu.make_async_copy(src, dst, k.recv_sems.at[k.received - 1])

    def start(self):
        @pl.when(self.own)
        def _():
            self.near.start()

        @pl.when(jnp.logical_not(self.own))
        def _():
            self.far.start()

    def wait_recv(self):
        @pl.when(self.own)
        def _():
            self.near.wait()

        @pl.when(jnp.logical_not(self.own))
        def _():
            self.far.wait_recv()

    def wait_send(self):
        @pl.when(jnp.logical_not(self.own))
        def _():
            self.far.wait_send()


def add_blocks(dst, terms, chunk):
    lead, rows = dst.shape[:-2], dst.shape[-2]
    count = 1
    for n in lead:
        count *= n

    @pl.loop(0, count)
    def _(i):
        at = []
        rest = i
        for n in reversed(lead):
            at.insert(0, rest % n)
            rest = rest // n

        @pl.loop(0, rows, step=chunk)
        def _(t):
            here = (*at, pl.ds(pl.multiple_of(t, chunk), chunk))
            total = terms[0][here].astype(F32)
            for term in terms[1:]:
                total = total + term[here].astype(F32)
            dst[here] = total.astype(dst.dtype)


def staged_reduce(p, k, src, stages, scr, chunk):
    own = scr[0]
    cur = src
    for n, (axis, pick) in enumerate(stages):
        recv = scr[1] if n == 0 else scr[2 * n]
        if n == 0:
            mine = k.local(pick(src, p.pos(axis, 0)), own)
        ring = [k.send(pick(cur, p.pos(axis, j)), recv.at[j - 1], p.step(axis, j)) for j in (1, 2, 3)]
        yield
        if n == 0:
            mine.wait()
        for copy in ring:
            copy.wait_recv()
        total = own if n == 0 else scr[2 * n + 1]
        add_blocks(total, [own if n == 0 else pick(cur, p.pos(axis, 0))] + [recv.at[j] for j in range(3)], chunk)
        cur = total


def ring_reduce(p, k, src, stages, scr, chunk):
    own, recv, held, recv2, total = scr
    axis, pick = stages[0]
    before, after, far = recv.at[0], recv.at[1], recv.at[2]
    far_a, far_b = halves(pick(src, p.pos(axis, 2)))
    right_a, right_b = halves(pick(src, p.pos(axis, 1)))
    left_a, left_b = halves(pick(src, p.pos(axis, 3)))
    right, left = p.step(axis, 1), p.step(axis, 3)
    on_right = k.send(far_a, halves(far)[0], right)
    on_left = k.send(far_b, halves(far)[1], left)
    get = [k.local(right_a, halves(held)[0]), k.local(left_b, halves(held)[1])]
    mine = k.local(pick(src, p.pos(axis, 0)), own)
    yield
    near = [k.send(right_b, halves(before)[1], right), k.send(left_a, halves(after)[0], left)]
    yield
    for i, (copy, to, dst) in enumerate(((on_right, right, before), (on_left, left, after))):
        get[i].wait()
        copy.wait_recv()
        here = halves(held)[i]
        add_blocks(here, [here, halves(far)[i]], chunk)
        near.append(k.send(here, halves(dst)[i], to))
    yield
    mine.wait()
    for copy in near:
        copy.wait_recv()
    add_blocks(own, [own, before, after], chunk)
    axis, pick = stages[1]
    ring = [k.send(pick(own, p.pos(axis, j)), recv2.at[j - 1], p.step(axis, j)) for j in (1, 2, 3)]
    yield
    for copy in ring:
        copy.wait_recv()
    add_blocks(total, [pick(own, p.pos(axis, 0))] + [recv2.at[j] for j in range(3)], chunk)


def staged_scratch(shapes, held=False):
    out = [pltpu.VMEM(shapes[0], BF16), pltpu.VMEM((3, *shapes[0]), BF16)]
    if held:
        out.append(pltpu.VMEM(shapes[0], BF16))
    for n, shape in enumerate(shapes[1:]):
        out.append(pltpu.VMEM((3, *shape), BF16))
        out.append(pltpu.VMEM(shape, BF16))
    return out


EVERY = slice(None)


def wg_stages(half):
    cols = pl.ds(half * FS, FS)
    if half == 0:
        return [
            ("y", lambda r, i: r.at[i // 2, :, i % 2, :, cols]),
            ("x", lambda r, i: r.at[i]),
        ]
    return [
        ("x", lambda r, i: r.at[:, i, :, :, cols]),
        ("y", lambda r, i: r.at[i // 2, i % 2]),
    ]


def wd_stages(p, half):
    cols = pl.ds(half * 512, 512)
    if half == 0:
        return [
            ("y", lambda r, i: r.at[i % 2, :, slab_place(p, y=i), :, cols]),
            ("x", lambda r, i: r.at[slab_place(p, x=i)]),
        ]
    return [
        ("x", lambda r, i: r.at[:, slab_place(p, x=i), :, :, cols]),
        ("y", lambda r, i: r.at[i % 2, slab_place(p, y=i)]),
    ]


def q_stages(half):
    cols = pl.ds(half * 128, 128)
    if half == 0:
        return [
            ("y", lambda r, i: r.at[i // 2, :, i % 2, :, cols]),
            ("x", lambda r, i: r.at[i]),
        ]
    return [
        ("x", lambda r, i: r.at[:, i, :, :, cols]),
        ("y", lambda r, i: r.at[i // 2, i % 2]),
    ]


def o_stages(part):
    cols = pl.ds(*O_PARTS[part])
    if part == 0:
        return [
            ("x", lambda r, i: r.at[:, i, :, :, :, cols]),
            ("z", lambda r, i: r.at[:, :, i]),
            ("y", lambda r, i: r.at[i // 2, i % 2]),
        ]
    if part == 1:
        return [
            ("y", lambda r, i: r.at[i // 2, :, i % 2, :, :, cols]),
            ("x", lambda r, i: r.at[i]),
            ("z", lambda r, i: r.at[i]),
        ]
    return [
        ("z", lambda r, i: r.at[:, :, :, i, :, cols]),
        ("y", lambda r, i: r.at[i // 2, :, i % 2]),
        ("x", lambda r, i: r.at[i]),
    ]


O_PARTS = ((0, 256), (256, 128), (384, 256))
PLANE_SHAPES = [
    [(4, 128, FS), (128, FS)],
    [(2, 2, 128, FS), (128, FS)],
    [(4, 80, 512), (80, 512)],
    [(2, 2, 80, 512), (80, 512)],
    [(4, 128, 128), (128, 128)],
    [(2, 2, 128, 128), (128, 128)],
]
O_SHAPES = [
    [(2, 2, 4, 32, 256), (2, 2, 32, 256), (32, 256)],
    [(4, 4, 32, 128), (4, 32, 128), (32, 128)],
    [(2, 4, 2, 32, 256), (4, 32, 256), (32, 256)],
]


def small_reduce(p, k, vec, recv):
    for n, axis in enumerate("zyxc"):
        steps = (1,) if axis == "c" else (1, 2, 3)
        ring = [k.send(vec.at[n], recv.at[n, j - 1], p.step(axis, j)) for j in steps]
        yield
        for copy in ring:
            copy.wait_recv()
        total = vec[n]
        for j in range(len(steps)):
            total = total + recv[n, j]
        vec[n + 1] = total


def swap(a, b):
    left = lax.broadcasted_iota(jnp.int32, a.shape, 1) < ROWS
    return jnp.where(left, a, pltpu.roll(b, ROWS, 1)), jnp.where(left, pltpu.roll(a, ROWS, 1), b)


def head_scale(v):
    return lax.rsqrt(jnp.mean(v * v, axis=-2, keepdims=True) + EPS)


def half_turn(v):
    half = HEAD // 2
    return jnp.concatenate([-v[..., half:, :], v[..., :half, :]], axis=-2)


def half_back(v):
    half = HEAD // 2
    return jnp.concatenate([v[..., half:, :], -v[..., :half, :]], axis=-2)


def low(v):
    return v.astype(BF16).astype(F32)


def query_units(packed_t, g, cos, sin, gain):
    raw = packed_t[pl.ds(pl.multiple_of(g * 256, 256), 256)].reshape(GROUP, HEAD, TOK)
    head = raw * head_scale(raw) * gain
    turned = low(head * cos + half_turn(head) * sin) * (HEAD ** -0.5)
    a0, a1 = swap(turned[0], turned[1])
    b0, b1 = swap(turned[2], turned[3])
    none = jnp.zeros((HEAD, 256), F32)
    return [
        jnp.concatenate([jnp.concatenate([a, b], axis=1), none], axis=0) for a, b in ((a0, b0), (a1, b1))
    ]


def fill_bias(bias, seg, s):
    lane = lax.broadcasted_iota(jnp.int32, (128, 128), 1)
    query = lane % ROWS + s * ROWS
    around = pl.ds(pl.multiple_of((s // 2) * 128, 128), 128)
    for m in range(MICRO):
        ids = jnp.broadcast_to(seg[m : m + 1, around].astype(F32), (128, 128))
        turned = pltpu.roll(ids, ROWS, 1)
        ids = jnp.where((lane < ROWS) == (s % 2 == 0), ids, turned)
        ids = jnp.where(ids >= 0, ids, -2.0)

        @pl.loop(0, SEQ, step=128)
        def _(t):
            at = pl.ds(pl.multiple_of(t, 128), 128)
            key = lax.broadcasted_iota(jnp.int32, (128, 128), 0) + t
            keys = jnp.broadcast_to(seg[m : m + 1, at].astype(F32), (128, 128)).T
            ok = ((key <= query) & (keys == ids)) | (key == query)
            bias[m, at] = jnp.where(ok, 3e38, -1e30)


def rope_parts():
    inverse = 10000.0 ** (-(np.arange(HEAD) % (HEAD // 2)) / (HEAD // 2))
    begin = inverse[:, None] * (np.arange(128)[None, :] % 16 * ROWS)
    inside = inverse[:, None] * (np.arange(128)[None, :] % ROWS)
    return np.stack([np.cos(begin), np.sin(begin), np.cos(inside), np.sin(inside)]).astype(np.float32)


def rope_tables(parts, s):
    here = lax.broadcasted_iota(jnp.int32, (HEAD, 128), 1) == s
    c0 = jnp.sum(jnp.where(here, parts[0], 0.0), axis=1, keepdims=True)
    s0 = jnp.sum(jnp.where(here, parts[1], 0.0), axis=1, keepdims=True)
    return c0 * parts[2] - s0 * parts[3], s0 * parts[2] + c0 * parts[3]


def column(row):
    n = row.shape[1]
    place = lax.broadcasted_iota(jnp.int32, (n, n), 0) == lax.broadcasted_iota(jnp.int32, (n, n), 1)
    return jnp.sum(jnp.where(place, jnp.broadcast_to(row, (n, n)), 0.0), axis=1, keepdims=True)


KV_PARTS = (pl.ds(0, 384), pl.ds(384, 256))


def unit_bias(bias, m):
    half = bias[m]
    return jnp.concatenate([half, half], axis=1)


def unit_kv(KV, m, g):
    cols = pl.ds(pl.multiple_of(g * 128, 128), 128)
    return KV[m, :, :, :, :, cols].reshape(SEQ, 128)


def front_body(*refs):
    (x_in, w_qkv, wo, wg, w_down, og, seg, g1, g2, g3, g4, parts) = refs[:12]
    (WO, WG, WD, OG, NA, KV, PT, LSE, ATT, RESID, N2, WQIN, BIAS, ROPE, GAINS, QKGAIN) = refs[12:28]
    (wq, wd, ogv, gains_out, rope, qkgain) = refs[28:34]
    (xs, na, wqm, wos, pks, pk, pt, lse, att, resid, n2, kvl, kvs, bias, qts, ots) = refs[34:50]
    ssem, rsem, lsem = refs[50:]
    p = Place()
    k = Links(ssem, rsem, lsem)
    yh, x, yl, z, c = p.yh, p.x, p.yl, p.z, p.c
    m = z * 2 + c
    sib = p.step("c", 1)
    yl_partner = p.at(y=p.yh * 2 + 1 - yl)
    partners = [p.step(a, j) for a in "xyz" for j in (1, 2, 3)]
    partners += [p.at(z=(z + j) % 4, c=1 - c) for j in range(4)]
    slab_to, slab_from = slab_target(p), slab_source(p)
    own_slab = same(p, slab_to)

    spare = [column(row[...].astype(F32)) for row in (g1, g2)]
    wide = w_qkv[...].astype(F32)
    lane = lax.broadcasted_iota(jnp.int32, (16, 256), 1)
    rest = jnp.where(lane == 240, spare[0], jnp.where(lane == 241, spare[1], 0.0))
    for i in range(8):
        turned = pltpu.roll(wide, (QKV - 240 * i) % QKV, 1)[:, :256]
        wq[:, i * 256 : (i + 1) * 256] = jnp.where(lane < 240, turned, rest).astype(BF16)
    greet_plane(p, partners, slab_to, slab_from, own_slab)

    def spread(src_of, dst_of):
        far, near = [], None
        for dz in range(4):
            for dc in range(2):
                zz, cc = (z + dz) % 4, (c + dc) % 2
                src, dst = src_of(zz * 2 + cc), dst_of(m)
                if dz == 0 and dc == 0:
                    near = k.local(src, dst)
                else:
                    far.append(k.send(src, dst, p.at(z=zz, c=cc)))
        return near, far

    q0 = spread(
        lambda i: wq.at[:, pl.ds(pl.multiple_of(i * 256, 256), 256)], lambda i: wqm.at[yh, x, yl, i]
    )
    own_x = k.local(x_in, xs.at[z, c])
    get_og = k.local(og, ogv)
    xcore = {0: k.send(x_in, xs.at[z, c], sib)}
    own_wo = k.local(wo, wos.at[yh, x, yl, z, c])

    def wo_at(part, *at):
        return wos.at[(*at, EVERY, pl.ds(part * 640, 640))]

    o1 = [k.send(wo, wos.at[yh, x, yl, z, c], p.step("z", j)) for j in (1, 2, 3)]
    g0 = [
        spread(
            lambda i: wg.at[:, pl.ds(pl.multiple_of(half * FF + i * FS, 128), FS)],
            lambda i: WG.at[yh, x, yl, i, :, pl.ds(half * FS, FS)],
        )
        for half in range(2)
    ]
    xring = RingGather(p, k, "z", lambda i: xs.at[i, c], x_in)

    def to_plane(blocks):
        return [k.send(b, b, p.step(axis, j)) for j in (1, 2, 3) for b, axis in blocks]

    ql, qh = pl.ds(0, 128), pl.ds(128, 128)
    lo, hi = pl.ds(0, FS), pl.ds(FS, FS)
    dlo, dhi = pl.ds(0, 384), pl.ds(384, 640)
    q0[0].wait()
    for copy in q0[1]:
        copy.wait_recv()
    q1 = to_plane(((wqm.at[yh, x, yl, :, :, ql], "x"), (wqm.at[yh, x, yl, :, :, qh], "y")))
    fill_bias(bias, seg, p.s)
    cos, sin = rope_tables(parts, p.s)
    rope[0], rope[1] = cos, sin
    qgain, kgain = column(g3[...].astype(F32)), column(g4[...].astype(F32))
    qkgain[...] = jnp.concatenate([jnp.broadcast_to(qgain, (HEAD, 128)), jnp.broadcast_to(kgain, (HEAD, 128))], axis=0)
    for copy in q1:
        copy.wait_recv()
    q2 = to_plane(((wqm.at[yh, :, yl, :, :, ql], "y"), (wqm.at[:, x, :, :, :, qh], "x")))
    for near, far in g0:
        near.wait()
        for copy in far:
            copy.wait_recv()
    plane = to_plane(((WG.at[yh, x, yl, :, :, lo], "x"), (WG.at[yh, x, yl, :, :, hi], "y")))
    slab_rows = w_down[...].astype(F32)
    wd[...] = jnp.concatenate([slab_rows[:, :1024], slab_rows[:, 1024:]], axis=0).astype(BF16)
    slab = Slab(k, wd, WD.at[yl, z, c], slab_to, own_slab)
    slab.start()
    for copy in q2:
        copy.wait_recv()
    own_x.wait()
    own_wo.wait()
    pick = jnp.where(
        lax.broadcasted_iota(jnp.int32, (8, 128), 0) + 112 == lax.broadcasted_iota(jnp.int32, (8, 128), 1), 1.0, 0.0
    ).astype(BF16)
    gains_out[...] = dot_last(pick, wqm[:, :, :, :, :, pl.ds(128, 128)].reshape(D, 128))
    keep = [k.local(wq, WQIN), k.local(bias, BIAS), k.local(rope, ROPE), k.local(gains_out, GAINS), k.local(qkgain, QKGAIN)]
    k.settle(q0[1] + q1)
    xring.hand_on()
    for o in (1, 3):
        src = xs.at[(z + o) % 4, c]
        xcore[o] = k.send(src, src, sib)
    packs = []
    for o in (0, 1, 3, 2):
        zz = (z + o) % 4
        if o == 2:
            xring.wait()
            xcore[o] = k.send(xs.at[zz, c], xs.at[zz, c], sib)
        xcore[o].wait_recv()
        rows = xs[zz].reshape(256, D).astype(F32)
        normed = (rows * rms_scale(rows) * gains_out[0:1, :]).astype(BF16)
        na[zz] = normed.reshape(2, TOK, D)
        pks[zz] = dot(normed, wqm[...].reshape(D, 256)).astype(BF16).reshape(2, TOK, 256)
        if o:
            packs.append(k.send(pks.at[zz, c], pk.at[m], p.at(z=zz)))
        else:
            own_pk = k.local(pks.at[z, c], pk.at[m])
        packs.append(k.send(pks.at[zz, 1 - c], pk.at[m], p.at(z=zz, c=1 - c)))
        if o == 1:
            for copy in o1:
                copy.wait_recv()
            o2 = to_plane(
                (
                    (wo_at(0, yh, x, yl, EVERY, c), "y"),
                    (wo_at(1, yh, x, yl, EVERY, c), "x"),
                ),
            )
        if o == 3:
            for copy in plane:
                copy.wait_recv()
            plane2 = [
                RingGather(p, k, "x", lambda i: WG.at[:, i, :, :, :, hi]),
                RingGather(p, k, "y", lambda i: WG.at[i // 2, :, i % 2, pl.ds(0, 4), :, lo]),
            ]
    slab.wait_recv()
    held = WD.at[yl, slab_place(p, x=x), slab_place(p, y=p.y)]
    plane_d = to_plane(((held.at[:, dlo], "x"), (held.at[:, dhi], "y")))
    for copy in o2:
        copy.wait_recv()
    o3 = [RingGather(p, k, "x", lambda i: wo_at(0, EVERY, i, EVERY, EVERY, c))]
    keep.append(k.local(na, NA))
    k.settle(q2 + o1 + [copy for _, far in g0 for copy in far])
    own_pk.wait()
    for copy in packs:
        copy.wait_recv()
    for i8 in range(8):
        pt[i8 * 240 : (i8 + 1) * 240] = pk[i8].astype(F32).T[:240]

    @pl.loop(0, KV_HEADS)
    def _(g):
        raw = pt[pl.ds(pl.multiple_of(QD + g * HEAD, HEAD), HEAD)]
        head = raw * head_scale(raw) * kgain
        key = head * cos + half_turn(head) * sin
        value = pt[pl.ds(pl.multiple_of(QD + KD + g * HEAD, HEAD), HEAD)]
        both = jnp.concatenate([key, value], axis=0).T.astype(BF16)
        cols = pl.ds(pl.multiple_of(g * 128, 128), 128)
        for mm in range(MICRO):
            kvl[mm, :, cols] = both[mm * ROWS : (mm + 1) * ROWS]

    own_kv = k.local(kvl, kvs.at[:, yl, z, c])
    across, ring = [], []
    for cols in KV_PARTS:
        across.append(k.send(kvl.at[:, :, cols], kvs.at[:, yl, z, c, :, cols], yl_partner))
        ring.append([k.send(kvl.at[:, :, cols], kvs.at[:, yl, z, c, :, cols], p.step("z", j)) for j in (1, 2, 3)])
    keep.append(k.local(pt, PT))

    @pl.loop(0, KV_HEADS)
    def _(g):
        for mm, unit in enumerate(query_units(pt, g, cos, sin, qgain)):
            qts[g, mm] = unit.astype(BF16)

    for copy, group, cols in zip(across, ring, KV_PARTS):
        copy.wait_recv()
        src = kvs.at[:, 1 - yl, z, c, :, cols]
        group += [k.send(src, src, p.step("z", j)) for j in (1, 2, 3)]
    get_og.wait()
    keep.append(k.local(ogv, OG.at[z, c]))
    rows = RingGather(p, k, "z", lambda i: OG.at[i, c], ogv)
    last = [k.send(ogv, OG.at[z, c], sib)]
    own_kv.wait()
    o3.append(RingGather(p, k, "y", lambda i: wo_at(1, i // 2, EVERY, i % 2, EVERY, c)))
    for ring4 in plane2:
        ring4.hand_on()
    oc = []
    for src in (
        wo_at(0, EVERY, x, EVERY, EVERY, c),
        wo_at(1, yh, EVERY, yl, EVERY, c),
    ):
        oc.append(k.send(src, src, sib))
    for copy in ring[0]:
        copy.wait_recv()
    src = kvs.at[:, :, :, c, :, KV_PARTS[0]]
    kvc = [k.send(src, src, sib)]
    o3[0].hand_on()
    o3[1].hand_on()
    for copy in plane_d:
        copy.wait_recv()
    plane2.append(RingGather(p, k, "x", lambda i: WD.at[:, slab_place(p, x=i), :, :, dhi]))
    plane2 += [
        RingGather(p, k, "y", lambda i: WD.at[i % 2, :, slab_place(p, y=i), :, dlo]),
        RingGather(p, k, "y", lambda i: WG.at[i // 2, :, i % 2, pl.ds(4, 4), :, lo]),
    ]
    for axis, ring4 in zip("xy", o3):
        for j in (1, 3):
            src = ring4.block(p.pos(axis, j))
            oc.append(k.send(src, src, sib))
    kvc[0].wait_recv()

    def unit(u):
        g, mm = u // 2, u % 2
        kv = unit_kv(kvs, mm, g)
        score = jnp.minimum(dot(kv, qts[g, mm]), unit_bias(bias, mm))
        peak = jnp.max(score, axis=0, keepdims=True)
        raised = jnp.exp(score - peak)
        total = jnp.sum(raised, axis=0, keepdims=True)
        probs = (raised * (1.0 / total)).astype(BF16)
        ots[g, mm] = dot_rows(kv, probs)[HEAD:]
        lse[u] = jnp.broadcast_to(peak + jnp.log(total), (8, 256))

    k.settle(packs + plane + plane_d)
    pl.loop(0, 6)(unit)
    for copy in ring[1]:
        copy.wait_recv()
    src = kvs.at[:, :, :, c, :, KV_PARTS[1]]
    kvc.append(k.send(src, src, sib))
    k.settle(o2 + xring.copies() + list(xcore.values()))
    kvc[1].wait_recv()
    keep.append(k.local(kvs, KV))
    for axis, ring4 in zip("xy", o3):
        ring4.wait()
        src = ring4.block(p.pos(axis, 2))
        oc.append(k.send(src, src, sib))
    pl.loop(6, 2 * KV_HEADS)(unit)
    for g in range(KV_HEADS):
        for t in range(2):
            cols = slice(t * 128, (t + 1) * 128)
            a, b = swap(ots[g, 0, :, cols], ots[g, 1, :, cols])
            at = (g * GROUP + 2 * t) * HEAD
            att[:, at : at + 128] = jnp.concatenate([a, b], axis=0).T.astype(BF16)
    keep += [k.local(lse, LSE), k.local(att, ATT)]
    rows.hand_on()
    for j in (1, 3):
        src = OG.at[p.pos("z", j), c]
        last.append(k.send(src, src, sib))
    for copy in oc:
        copy.wait_recv()
    keep.append(k.local(wos, WO))

    @pl.loop(0, 8)
    def _(t):
        w = wos[t // 4, t % 4].reshape(256, QD)
        cols = pl.ds(pl.multiple_of(t * 256, 256), 256)
        resid[:, cols] = xs[z, c, :, cols].astype(F32) + dot_last(att[...], w)

    plane2[2].hand_on()
    plane2[3].hand_on()
    plane2[4].hand_on()
    value = resid[...]
    n2[...] = (value * rms_scale(value) * gains_out[1:2, :]).astype(BF16)
    keep += [k.local(resid, RESID), k.local(n2, N2)]
    rows.wait()
    src = OG.at[p.pos("z", 2), c]
    last.append(k.send(src, src, sib))
    for ring4 in plane2:
        ring4.wait()
    for copy in last:
        copy.wait_recv()
    for copy in keep:
        copy.wait()
    slab.wait_send()
    k.drain()


VMEM = pl.BlockSpec(memory_space=pltpu.VMEM)


def front(*args):
    hbm = [
        sds((2, 4, 2, 4, 2, 16, QD), BF16),
        sds((2, 4, 2, 8, 16, 2 * FS), BF16),
        sds((2, 4, 2, 80, 1024), BF16),
        sds((4, 2, TOK, D), BF16),
        sds((4, 2, TOK, D), BF16),
        sds((2, 2, 4, 2, ROWS, 2 * KD), BF16),
        sds((QKV, TOK), F32),
        sds((2 * KV_HEADS, 8, 256), F32),
        sds((TOK, QD), BF16),
        sds((TOK, D), F32),
        sds((TOK, D), BF16),
        sds((16, 2048), BF16),
        sds((2, SEQ, 128), F32),
        sds((2, HEAD, TOK), F32),
        sds((8, D), F32),
        sds((2 * HEAD, 128), F32),
    ]
    scratch = [
        pltpu.VMEM((16, 2048), BF16),
        pltpu.VMEM((80, 1024), BF16),
        pltpu.VMEM((TOK, D), BF16),
        pltpu.VMEM((8, D), F32),
        pltpu.VMEM((2, HEAD, TOK), F32),
        pltpu.VMEM((2 * HEAD, 128), F32),
        pltpu.VMEM((4, 2, TOK, D), BF16),
        pltpu.VMEM((4, 2, TOK, D), BF16),
        pltpu.VMEM((2, 4, 2, 8, 16, 256), BF16),
        pltpu.VMEM((2, 4, 2, 4, 2, 16, QD), BF16),
        pltpu.VMEM((4, 2, TOK, 256), BF16),
        pltpu.VMEM((8, TOK, 256), BF16),
        pltpu.VMEM((QKV, TOK), F32),
        pltpu.VMEM((2 * KV_HEADS, 8, 256), F32),
        pltpu.VMEM((TOK, QD), BF16),
        pltpu.VMEM((TOK, D), F32),
        pltpu.VMEM((TOK, D), BF16),
        pltpu.VMEM((2, ROWS, 2 * KD), BF16),
        pltpu.VMEM((2, 2, 4, 2, ROWS, 2 * KD), BF16),
        pltpu.VMEM((2, SEQ, 128), F32),
        pltpu.VMEM((KV_HEADS, 2, 128, 256), BF16),
        pltpu.VMEM((KV_HEADS, 2, HEAD, 256), F32),
        pltpu.SemaphoreType.DMA((84,)),
        pltpu.SemaphoreType.DMA((150,)),
        pltpu.SemaphoreType.DMA((26,)),
    ]
    return pl.pallas_call(
        front_body,
        out_shape=hbm,
        in_specs=[ANY, VMEM, VMEM, ANY, VMEM, ANY] + [VMEM] * 6,
        out_specs=[ANY] * len(hbm),
        scratch_shapes=scratch,
        name="front",
        compiler_params=pltpu.CompilerParams(
            collective_id=0, has_side_effects=True, vmem_limit_bytes=56 << 20
        ),
    )(*args)


def ffn_body(n2, OG, WG, WD, wq, d_out, mix_out, dwg_out, dwd_out, WQ, *scr):
    (rows, ogs, wgs, wd80, wds, dgu, inn, din, part, mixs, r0, s0, r1, m0, dwg, dwd32, dwd) = scr[:17]
    (dn, wqv, ssem, rsem, lsem, wsem, vsem, wlsem) = scr[17:]
    p = Place()
    k = Links(wsem, vsem, wlsem)
    yh, x, yl, z, c = p.yh, p.x, p.yl, p.z, p.c
    sib = p.step("c", 1)
    greet([p.step(a, j) for a in "xyz" for j in (1, 2, 3)] + [sib])

    def remote(src, dst, i, to):
        return pltpu.make_async_remote_copy(
            src_ref=src,
            dst_ref=dst,
            send_sem=ssem.at[i],
            recv_sem=rsem.at[i],
            device_id=to,
            device_id_type=MESH,
        )

    def local(src, dst, i):
        copy = pltpu.make_async_copy(src, dst, lsem.at[i])
        copy.start()
        return copy

    def half_of(half, *at):
        return WQ.at[(*at, EVERY, pl.ds(half * 1024, 1024))]

    whole = (EVERY, EVERY, EVERY, EVERY, c)
    get_wq = k.local(wq, wqv)
    q1 = [k.plan(wq, WQ.at[yh, x, yl, z, c], p.step("z", j)) for j in (1, 2, 3)]
    q2, q3 = [], []
    for j in (1, 2, 3):
        for half, axis in ((0, "y"), (1, "x")):
            src = half_of(half, yh, x, yl, EVERY, c)
            q2.append(k.plan(src, src, p.step(axis, j)))
    for j in (1, 2, 3):
        src = half_of(0, EVERY, x, EVERY, EVERY, c)
        q3.append(k.plan(src, src, p.step("x", j)))
        src = half_of(1, yh, EVERY, yl, EVERY, c)
        q3.append(k.plan(src, src, p.step("y", j)))
    q4 = k.plan(WQ.at[whole], WQ.at[whole], sib)

    sent = []
    for copy in q1:
        copy.start()
    for j in (1, 3):
        copy = remote(n2, rows.at[z, c], j, p.step("z", j))
        copy.start()
        sent.append(copy)
    half = halves(rows.at[p.pos("z", 1), c])[1], halves(rows.at[p.pos("z", 3), c])[0]
    on_left = remote(half[0], half[0], 0, p.step("z", 3))
    on_right = remote(half[1], half[1], 2, p.step("z", 1))
    sent += [on_left, on_right]
    remote(n2, rows.at[z, c], 4, sib).start()
    own = local(n2, rows.at[z, c], 0)
    get_wd = local(WD, wd80, 1)
    get_wg = local(WG, wgs, 2)
    get_og = local(OG, ogs, 3)
    get_wd.wait()

    @pl.loop(0, 8)
    def _(i):
        yl, x = i // 4, i % 4
        a, b = wd80[yl, x, 0].astype(F32), wd80[yl, x, 1].astype(F32)
        at = pl.ds(pl.multiple_of(i * 80, 80), 80)
        wds[at, :1024] = jnp.concatenate([a[:40], b[:40]], axis=0).astype(BF16)
        wds[at, 1024:] = jnp.concatenate([a[40:], b[40:]], axis=0).astype(BF16)

    own.wait()
    get_wg.wait()
    get_og.wait()
    get_wq.wait()
    own_wq = k.local(wqv, WQ.at[yh, x, yl, z, c])

    def ring_step(j):
        return jnp.where(j == 2, 3, jnp.where(j == 3, 2, j))

    def d_inner_of(zz):
        din[...] = dot_last(ogs[zz].reshape(256, D), wds[...])

    d_inner_of(z)
    own_wq.wait()
    for copy in q1:
        copy.wait_recv()
    for copy in q2:
        copy.start()

    top, end = pl.ds(0, D // 2), pl.ds(D // 2, D // 2)
    right, left = p.step("z", 1), p.step("z", 3)
    to_right, to_left, to_far = s0.at[p.pos("z", 1)], s0.at[p.pos("z", 3)], s0.at[p.pos("z", 2)]
    near_right = remote(to_right.at[end], r1.at[0, end], 12, right)
    near_left = remote(to_left.at[top], r1.at[1, top], 13, left)
    far_right = remote(to_far.at[top], r1.at[2, top], 14, right)
    far_left = remote(to_far.at[end], r1.at[2, end], 15, left)
    sum_right = remote(to_right.at[top], r1.at[0, top], 17, right)
    sum_left = remote(to_left.at[end], r1.at[1, end], 18, left)
    ring_sums = [near_right, near_left, far_right, far_left, sum_right, sum_left]

    @pl.loop(0, 4)
    def _(j):
        o = ring_step(j)
        zz = (z + o) % 4
        at = pl.ds(pl.multiple_of(zz * 256, 256), 256)

        @pl.when(j == 1)
        def _():
            remote(n2, rows.at[z, c], 3, sib).wait_recv()
            on_left.start()
            remote(n2, rows.at[z, c], 1, sib).wait_recv()
            on_right.start()
            for o_near in (1, 3):
                near = rows.at[(z + o_near) % 4, c]
                remote(near, near, 4 + o_near, sib).start()

        @pl.when(j == 2)
        def _():
            on_left.wait_recv()
            on_right.wait_recv()
            far = rows.at[(z + 2) % 4, c]
            remote(far, far, 4 + 2, sib).start()

        remote(rows.at[zz, c], rows.at[zz, 1 - c], 4 + o, sib).wait_recv()
        r = rows[zz].reshape(256, D)
        for t in range(5):
            lo, hi = slice(t * 128, (t + 1) * 128), slice(FS + t * 128, FS + (t + 1) * 128)
            w = jnp.concatenate(
                [wgs[:, :, :, :, :, lo].reshape(D, 128), wgs[:, :, :, :, :, hi].reshape(D, 128)], axis=1
            )
            both = dot(r, w)
            gate, upper = both[:, :128], both[:, 128:]
            sig = jax.nn.sigmoid(gate)
            active = gate * sig
            d_inner = din[:, lo]
            inn[at, lo] = (active * upper).astype(BF16)
            dgu[at, lo] = (d_inner * upper * sig * (1.0 + gate * (1.0 - sig))).astype(BF16)
            dgu[at, hi] = (d_inner * active).astype(BF16)

        for h in range(2):
            turned = dot_last(wgs[h].reshape(1024, 2 * FS), dgu[at]).astype(BF16)
            for cc in range(2):
                part[zz, cc, h * 1024 : (h + 1) * 1024] = turned[:, cc * TOK : (cc + 1) * TOK]

        remote(part.at[zz, 1 - c], r0.at[zz], 8 + o, sib).start()
        d_inner_of((z + ring_step((j + 1) % 4)) % 4)
        remote(part.at[zz, 1 - c], r0.at[zz], 8 + o, sib).wait_recv()

        @pl.loop(0, D, step=128)
        def _(t):
            here = pl.ds(pl.multiple_of(t, 128), 128)
            s0[zz, here] = (part[zz, c, here].astype(F32) + r0[zz, here].astype(F32)).astype(BF16)

        @pl.when(j == 1)
        def _():
            near_right.start()

        @pl.when(j == 2)
        def _():
            near_left.start()

        @pl.when(j == 3)
        def _():
            far_right.start()
            far_left.start()

        @pl.when(j == 0)
        def _():
            for t in range(8):
                left = rows[z, :, :, t * 256 : (t + 1) * 256].reshape(256, D // 8)
                dwg[t // 4, t % 4] = dot_rows(left, dgu[at]).astype(BF16).reshape(2, TOK, 2 * FS)
            for copy in q2:
                copy.wait_recv()
            for copy in q3:
                copy.start()

    @pl.loop(0, 4)
    def _(t):
        cols = pl.ds(pl.multiple_of(t * 512, 512), 512)
        mixs[:, :, :, cols] = dot(inn[...], wds[:, cols]).astype(BF16).reshape(4, 2, TOK, 512)

    mix_core = remote(mixs.at[:, 1 - c], m0, 16, sib)
    mix_core.start()
    others = [((z + o) % 4, pl.ds(pl.multiple_of((z + o) % 4 * 256, 256), 256)) for o in (1, 2, 3)]

    def gate_up_block(t):
        cols = pl.ds(pl.multiple_of(t * 256, 256), 256)
        total = dwg[t // 4, t % 4].reshape(256, 2 * FS).astype(F32)
        for zz, at in others:
            total = total + dot_rows(rows[zz, :, :, cols].reshape(256, 256), dgu[at])
        dwg[t // 4, t % 4] = total.astype(BF16).reshape(2, TOK, 2 * FS)

    pl.loop(0, 4)(gate_up_block)
    for first, over, add, at in ((far_right, sum_right, to_right, 0), (far_left, sum_left, to_left, D // 2)):
        first.wait_recv()

        @pl.loop(0, D // 2, step=128)
        def _(t, add=add, at=at):
            here = pl.ds(pl.multiple_of(t + at, 128), 128)
            add[here] = (add[here].astype(F32) + r1[2, here].astype(F32)).astype(BF16)

        over.start()
    pl.loop(4, 8)(gate_up_block)
    out_wg = local(dwg, dwg_out, 5)
    for copy in q3:
        copy.wait_recv()
    q4.start()

    @pl.loop(0, 5)
    def _(t):
        units = pl.ds(pl.multiple_of(t * 128, 128), 128)
        dwd32[units] = dot_rows(inn[:, units], ogs[...].reshape(8 * TOK, D))

    @pl.loop(0, 8)
    def _(i):
        yl, x = i // 4, i % 4
        at = pl.ds(pl.multiple_of(i * 80, 80), 80)
        lo, hi = dwd32[at, :1024], dwd32[at, 1024:]
        dwd[yl, x, 0] = jnp.concatenate([lo[:40], hi[:40]], axis=0).astype(BF16)
        dwd[yl, x, 1] = jnp.concatenate([lo[40:], hi[40:]], axis=0).astype(BF16)

    out_wd = local(dwd, dwd_out, 6)
    mix_core.wait_recv()

    @pl.loop(0, 4)
    def _(zz):
        @pl.loop(0, TOK, step=16)
        def _(t):
            here = pl.ds(pl.multiple_of(t, 16), 16)
            m0[zz, here] = (mixs[zz, c, here].astype(F32) + m0[zz, here].astype(F32)).astype(BF16)

    out_mix = local(m0, mix_out, 4)
    for copy in (near_right, near_left, sum_right, sum_left):
        copy.wait_recv()
    for t in range(0, D, 128):
        here = slice(t, t + 128)
        total = s0[z, here].astype(F32)
        for j in range(2):
            total = total + r1[j, here].astype(F32)
        dn[:, here] = total.T

    out_dn = local(dn, d_out, 7)
    q4.wait_recv()
    k.drain()
    for copy in sent:
        copy.wait_send()
    for o in range(4):
        remote(rows.at[0, 0], rows.at[0, 0], 4 + o, sib).wait_send()
        remote(part.at[0, 0], r0.at[0], 8 + o, sib).wait_send()
    for copy in ring_sums:
        copy.wait_send()
    mix_core.wait_send()
    for copy in (out_mix, out_wg, out_wd, out_dn):
        copy.wait()


def ffn(n2, OG, WG, WD, wq):
    outs = [
        sds((TOK, D), F32),
        sds((4, TOK, D), BF16),
        sds((2, 4, 2, TOK, 2 * FS), BF16),
        sds((2, 4, 2, 80, 1024), BF16),
        sds((2, 4, 2, 4, 2, 16, 2048), BF16),
    ]
    scratch = [
        pltpu.VMEM((4, 2, TOK, D), BF16),
        pltpu.VMEM((4, 2, TOK, D), BF16),
        pltpu.VMEM((2, 4, 2, 8, 16, 2 * FS), BF16),
        pltpu.VMEM((2, 4, 2, 80, 1024), BF16),
        pltpu.VMEM((FS, D), BF16),
        pltpu.VMEM((8 * TOK, 2 * FS), BF16),
        pltpu.VMEM((8 * TOK, FS), BF16),
        pltpu.VMEM((256, FS), F32),
        pltpu.VMEM((4, 2, D, TOK), BF16),
        pltpu.VMEM((4, 2, TOK, D), BF16),
        pltpu.VMEM((4, D, TOK), BF16),
        pltpu.VMEM((4, D, TOK), BF16),
        pltpu.VMEM((3, D, TOK), BF16),
        pltpu.VMEM((4, TOK, D), BF16),
        pltpu.VMEM((2, 4, 2, TOK, 2 * FS), BF16),
        pltpu.VMEM((FS, D), F32),
        pltpu.VMEM((2, 4, 2, 80, 1024), BF16),
        pltpu.VMEM((TOK, D), F32),
        pltpu.VMEM((16, 2048), BF16),
        pltpu.SemaphoreType.DMA((19,)),
        pltpu.SemaphoreType.DMA((19,)),
        pltpu.SemaphoreType.DMA((8,)),
        pltpu.SemaphoreType.DMA((24,)),
        pltpu.SemaphoreType.DMA((24,)),
        pltpu.SemaphoreType.DMA((4,)),
    ]
    return pl.pallas_call(
        ffn_body,
        out_shape=outs,
        in_specs=[ANY] * 5,
        out_specs=[ANY] * 5,
        scratch_shapes=scratch,
        name="ffn",
        compiler_params=pltpu.CompilerParams(
            collective_id=1, has_side_effects=True, vmem_limit_bytes=60 << 20
        ),
    )(n2, OG, WG, WD, wq)


def back_body(*refs):
    (DN, X_IN, OG_IN, RESID, ATT, PT, LSE, WQ, WO, KV, mix_part, dwg, dwd, NA) = refs[:14]
    (BIAS, ROPE, GAINS, QKGAIN) = refs[14:18]
    (IN_GRAD, MIXED, GWG, GWD, GQ, GO, SMALL) = refs[18:25]
    (dn, xv, ogv, resid, pt, lse, in_grad, mixed, kvs, bias, qts, qns, dts, dns, dqt, dpt, datt, dres) = refs[25:43]
    (kpart, k0, k1, ks1, k2, kres, w2, wo2, low2, att2, do, dp, dpm, na2, dqm, mix1) = refs[43:59]
    (rope, gains, qkgain) = refs[59:62]
    scr = list(refs[62:])
    parts = []
    for i, shapes in enumerate(PLANE_SHAPES + O_SHAPES):
        n = 2 * len(shapes) + (i < 4)
        parts.append(scr[:n])
        scr = scr[n:]
    vec, vrecv, ssem, rsem, lsem = scr
    p = Place()
    k = Links(ssem, rsem, lsem)
    yl, z, c = p.yl, p.z, p.c
    m = z * 2 + c
    sib = p.step("c", 1)
    yl_partner = p.at(y=p.yh * 2 + 1 - yl)
    get = {}

    def fetch(**pairs):
        for name, (src, dst) in pairs.items():
            get[name] = k.local(src, dst)

    fetch(dn=(DN, dn), og=(OG_IN, ogv), resid=(RESID, resid), gains=(GAINS, gains))
    get_w = [k.local(WO.at[t // 4, t % 4], wo2.at[t]) for t in range(8)]
    fetch(pt=(PT, pt), rope=(ROPE, rope), qkgain=(QKGAIN, qkgain), att=(ATT, att2.at[0]))
    partners = [p.step(a, j) for a in "xyz" for j in (1, 2, 3)]
    partners += [p.at(z=(z + j) % 4, c=1 - c) for j in range(4)]
    slab_to, slab_from = slab_target(p), slab_source(p)
    own_slab = same(p, slab_to)
    greet_plane(p, partners, slab_to, slab_from, own_slab)
    plane = [
        ring_reduce(p, k, dwg, wg_stages(0), parts[0], 16),
        ring_reduce(p, k, dwg, wg_stages(1), parts[1], 16),
        ring_reduce(p, k, dwd, wd_stages(p, 0), parts[2], 16),
        ring_reduce(p, k, dwd, wd_stages(p, 1), parts[3], 16),
    ]
    for step in plane + plane:
        next(step)
    pair_att = k.send(ATT, att2.at[1], sib)

    def mix_send(part):
        at = pl.ds((0, 80)[part], (80, 48)[part])
        return [k.send(mix_part.at[p.pos("z", j), at], mix1.at[j - 1, at], p.step("z", j)) for j in (1, 2, 3)]

    mixing = mix_send(0)
    for name in ("dn", "og", "resid", "gains"):
        get[name].wait()
    value = resid[...]
    scale_two = rms_scale(value)
    norm_two = value * scale_two
    d_resid = ogv[...].astype(F32) + norm_back(dn[...], norm_two, scale_two, gains[1:2, :])
    dres[...] = d_resid
    low2[0] = d_resid.astype(BF16)
    pair_low = k.send(low2.at[0], low2.at[1], sib)
    fetch(kv=(KV, kvs), lse=(LSE, lse), bias=(BIAS, bias))
    for name in ("pt", "rope", "qkgain"):
        get[name].wait()
    cos, sin = rope[0], rope[1]
    qgain, kgain = qkgain[:HEAD], qkgain[HEAD:]

    @pl.loop(0, KV_HEADS)
    def _(g):
        for mm, unit in enumerate(query_units(pt, g, cos, sin, qgain)):
            qts[g, mm] = unit.astype(BF16)
            qns[g, mm] = unit.T.astype(BF16)

    for t in range(8):
        get_w[t].wait()
        term = dot(low2[0, :, t * 256 : (t + 1) * 256], wo2[t].reshape(256, QD))
        datt[...] = term if t == 0 else datt[...] + term
    for g in range(KV_HEADS):
        tiles = []
        for t in range(2):
            at = (g * GROUP + 2 * t) * HEAD
            both = low(datt[:, at : at + 128]).T
            tiles.append(swap(both[:HEAD], both[HEAD:]))
        for mm in range(MICRO):
            none = jnp.zeros((HEAD, 256), F32)
            unit = jnp.concatenate([none, jnp.concatenate([tiles[0][mm], tiles[1][mm]], axis=1)], axis=0)
            dts[g, mm] = unit.astype(BF16)
            dns[g, mm] = unit.T.astype(BF16)
    fetch(x=(X_IN, xv), mix=(mix_part.at[z], mix1.at[3]))
    get["kv"].wait()
    get["lse"].wait()
    get["bias"].wait()

    def unit(u):
        g, mm = u // 2, u % 2
        kv = unit_kv(kvs, mm, g)
        score = jnp.minimum(dot(kv, qts[g, mm]), unit_bias(bias, mm))
        again = jnp.exp(score - lse[u, 0:1, :])
        d_probs = dot(kv, dts[g, mm])
        inner = jnp.sum(again * d_probs, axis=0, keepdims=True)
        d_scores = (again * (d_probs - inner)).astype(BF16)
        d_kv = dot(d_scores, qns[g, mm]) + dot(again.astype(BF16), dns[g, mm])
        cols = pl.ds(pl.multiple_of(g * 128, 128), 128)
        kpart[mm, :, :, :, :, cols] = d_kv.astype(BF16).reshape(2, 4, 2, ROWS, 128)
        dqt[g, mm] = dot_rows(kv, d_scores)[:HEAD] * (HEAD ** -0.5)

    def core_send(cols):
        return k.send(kpart.at[:, :, :, 1 - c, :, cols], k0.at[:, :, :, :, cols], sib)

    def ring_send(core, cols):
        core.wait_recv()

        @pl.loop(0, 4)
        def _(zz):
            for a in range(2):
                for b in range(2):
                    here = (a, b, zz, EVERY, cols)
                    both = kpart[a, b, zz, c, :, cols].astype(F32) + k0[here].astype(F32)
                    k0[here] = both.astype(BF16)

        return [
            k.send(k0.at[:, :, p.pos("z", j), :, cols], k1.at[j - 1, :, :, :, cols], p.step("z", j))
            for j in (1, 2, 3)
        ]

    pl.loop(0, 6)(unit)
    core = core_send(KV_PARTS[0])
    for step in plane:
        next(step)
    ring = ring_send(core, KV_PARTS[0])
    pl.loop(6, 2 * KV_HEADS)(unit)
    core = core_send(KV_PARTS[1])
    ring += ring_send(core, KV_PARTS[1])
    get["att"].wait()
    pair_att.wait_recv()
    pair_low.wait_recv()
    att_cols = pl.ds(pl.multiple_of(c * 640, 128), 640)

    @pl.loop(0, 8)
    def _(t):
        cols = pl.ds(pl.multiple_of(t * 256, 256), 256)
        left = low2[:, :, cols].reshape(2 * TOK, 256)
        right = att2[:, :, att_cols].reshape(2 * TOK, 640)
        do[t // 4, t % 4] = dot_rows(left, right).astype(BF16).reshape(2, 4, 32, 640)

    outward = [staged_reduce(p, k, do, o_stages(i), parts[6 + i], 16) for i in range(3)]
    next(outward[0])

    query_sum = jnp.zeros((HEAD, TOK), F32)
    for g in range(KV_HEADS):
        heads = []
        for t in range(2):
            cols = slice(t * 128, (t + 1) * 128)
            heads += list(swap(dqt[g, 0, :, cols], dqt[g, 1, :, cols]))
        for h in range(GROUP):
            at = (g * GROUP + h) * HEAD
            d_raw, term = head_back(pt[at : at + HEAD], heads[h], cos, sin, qgain)
            query_sum = query_sum + term
            dpt[at : at + HEAD] = d_raw

    for copy in ring:
        copy.wait_recv()
    for a in range(2):
        for b in range(2):
            total = k0[a, b, z].astype(F32)
            for j in range(3):
                total = total + k1[j, a, b].astype(F32)
            ks1[a, b] = total.astype(BF16)
    across = k.send(ks1.at[:, 1 - yl], k2, yl_partner)
    next(outward[1])
    next(plane[0])
    next(plane[2])
    across.wait_recv()
    for a in range(2):
        kres[pl.ds(a * ROWS, ROWS)] = ks1[a, yl].astype(F32) + k2[a].astype(F32)
    key_sum = jnp.zeros((HEAD, TOK), F32)
    for g in range(KV_HEADS):
        both = kres[:, g * 128 : (g + 1) * 128].T
        at = QD + g * HEAD
        d_raw, term = head_back(pt[at : at + HEAD], both[:HEAD], cos, sin, kgain)
        key_sum = key_sum + term
        dpt[at : at + HEAD] = d_raw
        dpt[at + KD : at + KD + HEAD] = both[HEAD:]
    get_q = [k.local(WQ.at[0, t], w2.at[t]) for t in range(2)]
    get_n = [k.local(NA.at[:, :, :, pl.ds(t * 256, 256)], na2.at[t]) for t in range(2)]
    for t in range(8):
        block = jnp.concatenate([dpt[t * 240 : (t + 1) * 240], jnp.zeros((16, TOK), F32)], axis=0)
        dp[t] = block.T.astype(BF16)
    sums = jnp.concatenate(
        [jnp.sum(query_sum.T, axis=0, keepdims=True), jnp.sum(key_sum.T, axis=0, keepdims=True)], axis=1
    )
    vec[0] = jnp.broadcast_to(sums, (8, 128))
    small = small_reduce(p, k, vec, vrecv)
    next(small)

    last, keep = [], []

    def to_owners(total, dst):
        for dz in range(4):
            for dc in range(2):
                zz, cc = (z + dz) % 4, (c + dc) % 2
                src = total.at[pl.ds(pl.multiple_of((zz * 2 + cc) * 16, 16), 16)]
                if dz == 0 and dc == 0:
                    keep.append(k.local(src, dst))
                else:
                    last.append(k.send(src, dst, p.at(z=zz, c=cc)))

    def slab_home(half):
        slab = Slab(k, parts[2 + half][-1], GWD.at[:, pl.ds(half * 512, 512)], slab_from, own_slab)
        slab.start()
        return slab

    members = []
    for dz in range(4):
        for dc in range(2):
            zz, cc = (z + dz) % 4, (c + dc) % 2
            src = dp.at[zz * 2 + cc]
            if dz == 0 and dc == 0:
                own_dp = k.local(src, dpm.at[z, c])
            else:
                members.append(k.send(src, dpm.at[z, c], p.at(z=zz, c=cc)))
    next(plane[1])
    next(plane[3])
    next(outward[2])
    own_dp.wait()
    for copy in members:
        copy.wait_recv()
    next(small)
    for t in range(8):
        get_n[t].wait()
        total = dot_rows(na2[t % 2].reshape(8 * TOK, 256), dpm[...].reshape(8 * TOK, 256))
        dqm[t // 4, t % 4] = total.astype(BF16).reshape(2, TOK, 256)
        if t < 6:
            get_n.append(k.local(NA.at[:, :, :, pl.ds((t + 2) * 256, 256)], na2.at[t % 2]))
    inward = [staged_reduce(p, k, dqm, q_stages(i), parts[4 + i], 16) for i in range(2)]
    for step in inward:
        next(step)
    next(outward[0])
    next(outward[1])
    left = jnp.concatenate([dp[i] for i in range(8)], axis=1)

    def d_normed_block(t):
        get_q[t].wait()
        w = w2[t % 2].reshape(256, 2048)
        in_grad[:, t * 256 : (t + 1) * 256] = dot_last(left, w)
        if t < 6:
            get_q.append(k.local(WQ.at[(t + 2) // 4, (t + 2) % 4], w2.at[t % 2]))

    for t in range(4):
        d_normed_block(t)
    next(small)
    for half in range(2):
        next(plane[half], None)
        to_owners(parts[half][-1], GWG.at[:, pl.ds(pl.multiple_of(half * FF + m * FS, 128), FS)])
    slabs = []
    for half in range(2):
        next(plane[2 + half], None)
        slabs.append(slab_home(half))
    mixing += mix_send(1)
    for step in inward:
        next(step)
    for t in range(4, 8):
        d_normed_block(t)
    next(small)
    next(outward[2])
    for step in outward:
        next(step)
    for half, step in enumerate(inward):
        next(step, None)
        to_owners(parts[4 + half][-1], GQ.at[:, pl.ds(pl.multiple_of(m * 256 + half * 128, 128), 128)])
    get["x"].wait()
    hidden = xv[...].astype(F32)
    scale_one = rms_scale(hidden)
    in_grad[...] = dres[...] + norm_back(in_grad[...], hidden * scale_one, scale_one, gains[0:1, :])
    keep.append(k.local(in_grad, IN_GRAD))
    next(small, None)
    keep.append(k.local(vec.at[4], SMALL))
    get["mix"].wait()
    for copy in mixing:
        copy.wait_recv()

    @pl.loop(0, TOK, step=16)
    def _(t):
        at = pl.ds(pl.multiple_of(t, 16), 16)
        total = resid[at]
        for j in range(4):
            total = total + mix1[j, at].astype(F32)
        mixed[at] = total.astype(BF16)

    keep.append(k.local(mixed, MIXED))
    for i, step in enumerate(outward):
        next(step, None)
        total = parts[6 + i][-1]
        dst = GO.at[c, :, pl.ds(*O_PARTS[i])]
        keep.append(k.local(total.at[pl.ds(pl.multiple_of(c * 16, 16), 16)], dst))
        last.append(k.send(total.at[pl.ds(pl.multiple_of((1 - c) * 16, 16), 16)], dst, sib))
    for copy in keep:
        copy.wait()
    for copy in last:
        copy.wait_recv()
    for slab in slabs:
        slab.wait_recv()
        slab.wait_send()
    k.drain()


def head_back(raw, grad, cos, sin, gain):
    scale = head_scale(raw)
    normed = raw * scale
    d_head = grad * cos + half_back(grad * sin)
    scaled = d_head * gain
    inner = jnp.mean(scaled * normed, axis=0, keepdims=True)
    return scale * (scaled - normed * inner), d_head * normed


def back(*args):
    w = 2 * KD
    outs = [
        sds((TOK, D), F32),
        sds((TOK, D), BF16),
        sds((16, 2 * FF), BF16),
        sds((80, 1024), BF16),
        sds((16, 2048), BF16),
        sds((2, 16, 640), BF16),
        sds((8, 128), F32),
    ]
    scratch = [
        pltpu.VMEM((TOK, D), F32),
        pltpu.VMEM((TOK, D), BF16),
        pltpu.VMEM((TOK, D), BF16),
        pltpu.VMEM((TOK, D), F32),
        pltpu.VMEM((QKV, TOK), F32),
        pltpu.VMEM((2 * KV_HEADS, 8, 256), F32),
        pltpu.VMEM((TOK, D), F32),
        pltpu.VMEM((TOK, D), BF16),
        pltpu.VMEM((2, 2, 4, 2, ROWS, w), BF16),
        pltpu.VMEM((2, SEQ, 128), F32),
        pltpu.VMEM((KV_HEADS, 2, 128, 256), BF16),
        pltpu.VMEM((KV_HEADS, 2, 256, 128), BF16),
        pltpu.VMEM((KV_HEADS, 2, 128, 256), BF16),
        pltpu.VMEM((KV_HEADS, 2, 256, 128), BF16),
        pltpu.VMEM((KV_HEADS, 2, HEAD, 256), F32),
        pltpu.VMEM((QKV, TOK), F32),
        pltpu.VMEM((TOK, QD), F32),
        pltpu.VMEM((TOK, D), F32),
        pltpu.VMEM((2, 2, 4, 2, ROWS, w), BF16),
        pltpu.VMEM((2, 2, 4, ROWS, w), BF16),
        pltpu.VMEM((3, 2, 2, ROWS, w), BF16),
        pltpu.VMEM((2, 2, ROWS, w), BF16),
        pltpu.VMEM((2, ROWS, w), BF16),
        pltpu.VMEM((TOK, w), F32),
        pltpu.VMEM((2, 2, 4, 2, 16, 2048), BF16),
        pltpu.VMEM((8, 2, 4, 2, 16, QD), BF16),
        pltpu.VMEM((2, TOK, D), BF16),
        pltpu.VMEM((2, TOK, QD), BF16),
        pltpu.VMEM((2, 4, 2, 4, 32, 640), BF16),
        pltpu.VMEM((8, TOK, 256), BF16),
        pltpu.VMEM((4, 2, TOK, 256), BF16),
        pltpu.VMEM((2, 4, 2, TOK, 256), BF16),
        pltpu.VMEM((2, 4, 2, TOK, 256), BF16),
        pltpu.VMEM((4, TOK, D), BF16),
        pltpu.VMEM((2, HEAD, TOK), F32),
        pltpu.VMEM((8, D), F32),
        pltpu.VMEM((2 * HEAD, 128), F32),
    ]
    for i, shapes in enumerate(PLANE_SHAPES + O_SHAPES):
        scratch += staged_scratch(shapes, i < 4)
    scratch += [
        pltpu.VMEM((5, 8, 128), F32),
        pltpu.VMEM((4, 3, 8, 128), F32),
        pltpu.SemaphoreType.DMA((150,)),
        pltpu.SemaphoreType.DMA((150,)),
        pltpu.SemaphoreType.DMA((36,)),
    ]
    return pl.pallas_call(
        back_body,
        out_shape=outs,
        in_specs=[ANY] * 18,
        out_specs=[ANY] * 7,
        scratch_shapes=scratch,
        name="back",
        compiler_params=pltpu.CompilerParams(
            collective_id=2, has_side_effects=True, vmem_limit_bytes=60 << 20
        ),
    )(*args)


def finish_body(*refs):
    IN_GRAD, MIXED, GWG, GWD, GQ, GO, SUMS, WG, WQ, g1, g2 = refs[:11]
    in_out, mixed_out, Q, O, G, DOWN, ATTN, FFN, QG, KG = refs[11:21]
    (gwg, gwd, gq, go, sums, wg, wq, q, o, g, down, attn, ffn_, qg, kg, ing, mix, sem) = refs[21:]
    used = []

    def copy(src, dst):
        out = pltpu.make_async_copy(src, dst, sem.at[len(used)])
        out.start()
        used.append(out)
        return out

    rows = [copy(IN_GRAD, ing), copy(MIXED, mix)]
    through = []
    got = [copy(a, b) for a, b in ((GQ, gq), (WQ, wq), (GO, go), (SUMS, sums), (GWD, gwd), (GWG, gwg), (WG, wg))]
    for one in got[:5]:
        one.wait()
    for one, (src, dst) in zip(rows, ((ing, in_out), (mix, mixed_out))):
        one.wait()
        through.append(copy(src, dst))
    wide = gq[...].astype(F32)
    lane = lax.broadcasted_iota(jnp.int32, (16, QKV), 1)
    total = jnp.zeros((16, QKV), F32)
    for i in range(8):
        piece = jnp.concatenate([wide[:, i * 256 : (i + 1) * 256], jnp.zeros((16, QKV - 256), F32)], axis=1)
        here = (lane >= i * 240) & (lane < (i + 1) * 240)
        total = jnp.where(here, pltpu.roll(piece, 240 * i, 1) if i else piece, total)
    q[...] = total
    through.append(copy(q, Q))
    o[...] = jnp.concatenate([go[0].astype(F32), go[1].astype(F32)], axis=1)
    through.append(copy(o, O))
    slab = gwd[...].astype(F32)
    down[...] = jnp.concatenate([slab[:40], slab[40:]], axis=1)
    through.append(copy(down, DOWN))
    attn[...] = flat(jnp.sum(wq[...].astype(F32) * total, axis=1, keepdims=True)) / g1[...].astype(F32)
    through.append(copy(attn, ATTN))
    qg[...] = sums[0:1, :HEAD]
    kg[...] = pltpu.roll(sums[...], HEAD, 1)[0:1, :HEAD]
    through += [copy(qg, QG), copy(kg, KG)]
    for one in got[5:]:
        one.wait()
    grown = gwg[...].astype(F32)
    g[...] = grown
    through.append(copy(g, G))
    ffn_[...] = flat(jnp.sum(wg[...].astype(F32) * grown, axis=1, keepdims=True)) / g2[...].astype(F32)
    through.append(copy(ffn_, FFN))
    for one in through:
        one.wait()


def flat(col):
    n = col.shape[0]
    place = lax.broadcasted_iota(jnp.int32, (n, n), 0) == lax.broadcasted_iota(jnp.int32, (n, n), 1)
    return jnp.sum(jnp.where(place, jnp.broadcast_to(col, (n, n)), 0.0), axis=0, keepdims=True)


def finish(*args):
    outs = [
        sds((TOK, D), F32),
        sds((TOK, D), BF16),
        sds((16, QKV), F32),
        sds((16, QD), F32),
        sds((16, 2 * FF), F32),
        sds((40, D), F32),
        sds((1, 16), F32),
        sds((1, 16), F32),
        sds((1, HEAD), F32),
        sds((1, HEAD), F32),
    ]
    ins = [(16, 2 * FF), (80, 1024), (16, 2048), (2, 16, 640), (8, 128), (16, 2 * FF), (16, QKV)]
    scratch = [pltpu.VMEM(a, F32 if a == (8, 128) else BF16) for a in ins]
    scratch += [pltpu.VMEM(a.shape, a.dtype) for a in outs[2:] + outs[:2]]
    return pl.pallas_call(
        finish_body,
        out_shape=outs,
        in_specs=[ANY] * 9 + [VMEM] * 2,
        out_specs=[ANY] * 10,
        scratch_shapes=scratch + [pltpu.SemaphoreType.DMA((19,))],
        name="finish",
        compiler_params=pltpu.CompilerParams(vmem_limit_bytes=60 << 20),
    )(*args)


def per_device(
    tokens,
    segment_ids,
    w_qkv,
    w_out,
    w_gate_up,
    w_down,
    attn_gain,
    ffn_gain,
    query_gain,
    key_gain,
    out_grad,
):
    g1, g2, g3, g4 = [a.reshape(1, -1) for a in (attn_gain, ffn_gain, query_gain, key_gain)]
    og_in = out_grad.reshape(TOK, D)
    x_in = tokens.reshape(TOK, D)
    (WO, WG, WD, OG, NA, KV, pt, lse, attended, resid, n2, wq_in, bias, rope, gain_rows, head_gains) = front(
        x_in, w_qkv, w_out.T, w_gate_up, w_down, og_in, segment_ids, g1, g2, g3, g4, rope_parts()
    )
    d_normed, mix_part, dwg, dwd, WQ = ffn(n2, OG, WG, WD, wq_in)
    in_grad, mixed, gwg, gwd, gq, go, sums = back(
        d_normed, x_in, og_in, resid, attended, pt, lse, WQ, WO, KV, mix_part, dwg, dwd, NA,
        bias, rope, gain_rows, head_gains,
    )
    outs = finish(in_grad, mixed, gwg, gwd, gq, go, sums, w_gate_up, w_qkv, g1, g2)
    return (
        outs[1].reshape(MICRO, ROWS, D),
        outs[0].reshape(MICRO, ROWS, D),
        outs[2],
        outs[3].T,
        outs[4],
        outs[5],
        outs[6].reshape(16),
        outs[7].reshape(16),
        outs[8].reshape(HEAD),
        outs[9].reshape(HEAD),
    )


def solution(mesh):
    return jax.shard_map(
        per_device,
        mesh=mesh,
        in_specs=(
            P(None, ("grp", "seq"), None),
            P(None, "grp"),
            P(("grp", "seq"), None),
            P(None, ("grp", "seq")),
            P(("grp", "seq"), None),
            P(("grp", "seq"), None),
            P(("grp", "seq")),
            P(("grp", "seq")),
            P(),
            P(),
            P(None, ("grp", "seq"), None),
        ),
        out_specs=(
            P(None, ("grp", "seq"), None),
            P(None, ("grp", "seq"), None),
            P(("grp", "seq"), None),
            P(None, ("grp", "seq")),
            P(("grp", "seq"), None),
            P(("grp", "seq"), None),
            P(("grp", "seq")),
            P(("grp", "seq")),
            P(),
            P(),
        ),
        check_vma=False,
    )
```

```python
import jax
import jax.numpy as jnp
import numpy as np
from jax import lax
from jax.experimental import pallas as pl
from jax.experimental.pallas import tpu as pltpu
from jax.sharding import PartitionSpec as P

Q_HEADS = 20
KV_HEADS = 5
GROUP = 4
HEAD = 64
D = 2048
FF = 5120
QD = 1280
KD = 320
QKV = 1920
SEQ = 1024
MICRO = 2
ROWS = 64
TOK = 128
FS = 640
EPS = 1e-06
MESH = pl.DeviceIdType.MESH
F32 = jnp.float32
BF16 = jnp.bfloat16
ANY = pl.BlockSpec(memory_space=pl.ANY)


class Place:
    def __init__(self):
        g = lax.axis_index("grp")
        s = lax.axis_index("seq")
        self.g, self.s = g, s
        self.yh, self.x = g // 4, g % 4
        self.yl, self.z, self.c = s // 8, (s // 2) % 4, s % 2
        self.y = self.yh * 2 + self.yl

    def at(self, x=None, y=None, z=None, c=None):
        x = self.x if x is None else x
        y = self.y if y is None else y
        z = self.z if z is None else z
        c = self.c if c is None else c
        return ((y // 2) * 4 + x, (y % 2) * 8 + z * 2 + c)

    def step(self, axis, k):
        if axis == "x":
            return self.at(x=(self.x + k) % 4)
        if axis == "y":
            return self.at(y=(self.y + k) % 4)
        if axis == "z":
            return self.at(z=(self.z + k) % 4)
        return self.at(c=1 - self.c)

    def pos(self, axis, k):
        return (getattr(self, axis) + k) % 4


class Links:
    def __init__(self, send_sems, recv_sems, local_sems):
        self.send_sems, self.recv_sems, self.local_sems = send_sems, recv_sems, local_sems
        self.received = 0
        self.free = {"send": list(range(send_sems.shape[0]))[::-1], "local": list(range(local_sems.shape[0]))[::-1]}
        self.sent = {}

    def plan(self, src, dst, to):
        i = self.received
        self.received += 1
        assert i < self.recv_sems.shape[0], i
        slot = self.free["send"].pop()
        copy = pltpu.make_async_remote_copy(
            src_ref=src,
            dst_ref=dst,
            send_sem=self.send_sems.at[slot],
            recv_sem=self.recv_sems.at[i],
            device_id=to,
            device_id_type=MESH,
        )
        self.sent[id(copy)] = (copy, slot)
        return copy

    def send(self, src, dst, to):
        copy = self.plan(src, dst, to)
        copy.start()
        return copy

    def local(self, src, dst):
        slot = self.free["local"].pop()
        copy = pltpu.make_async_copy(src, dst, self.local_sems.at[slot])
        copy.start()
        return Local(self, copy, slot)

    def settle(self, copies):
        for copy in copies:
            copy, slot = self.sent.pop(id(copy))
            copy.wait_send()
            self.free["send"].append(slot)

    def drain(self):
        self.settle([copy for copy, _ in list(self.sent.values())])


class Local:
    def __init__(self, links, copy, slot):
        self.links, self.copy, self.slot = links, copy, slot

    def wait(self):
        self.copy.wait()
        self.links.free["local"].append(self.slot)


def halves(ref):
    n = ref.shape[0] // 2
    return ref.at[pl.ds(0, n)], ref.at[pl.ds(n, n)]


class RingGather:
    def __init__(self, p, k, axis, block, src=None):
        self.p, self.k, self.axis, self.block = p, k, axis, block
        dst = block(p.pos(axis, 0))
        src = dst if src is None else src
        self.right = k.send(src, dst, p.step(axis, 1))
        self.left = k.send(src, dst, p.step(axis, 3))

    def from_before(self):
        self.right.wait_recv()
        half = halves(self.block(self.p.pos(self.axis, 3)))[0]
        self.far_right = self.k.send(half, half, self.p.step(self.axis, 1))

    def from_after(self):
        self.left.wait_recv()
        half = halves(self.block(self.p.pos(self.axis, 1)))[1]
        self.far_left = self.k.send(half, half, self.p.step(self.axis, 3))

    def hand_on(self):
        self.from_before()
        self.from_after()

    def wait(self):
        self.far_right.wait_recv()
        self.far_left.wait_recv()

    def copies(self):
        return [self.right, self.left, self.far_right, self.far_left]


def greet(partners):
    barrier = pltpu.get_barrier_semaphore()
    for to in partners:
        pl.semaphore_signal(barrier, inc=1, device_id=to, device_id_type=MESH)
    pl.semaphore_wait(barrier, len(partners))


def sds(shape, dtype):
    return jax.ShapeDtypeStruct(shape, dtype)


def rms_scale(values):
    return lax.rsqrt(jnp.mean(values * values, axis=-1, keepdims=True) + EPS)


def norm_back(upstream, normed, scale, gain):
    scaled = upstream * gain
    inner = jnp.mean(scaled * normed, axis=-1, keepdims=True)
    return scale * (scaled - normed * inner)


def dot(left, right):
    return jnp.dot(left, right, preferred_element_type=F32)


def dot_last(left, right):
    return lax.dot_general(left, right, (((1,), (1,)), ((), ())), preferred_element_type=F32)


def dot_rows(left, right):
    return lax.dot_general(left, right, (((0,), (0,)), ((), ())), preferred_element_type=F32)


def slab_target(p):
    return p.at(x=(p.z + p.x) % 4, y=(p.c + p.yh) % 2 * 2 + p.yl, z=p.g // 2, c=p.g % 2)


def slab_place(p, x=None, y=None):
    m = p.z * 2 + p.c
    if x is not None:
        return (x + 4 - m % 4) % 4
    return (y // 2 + 2 - m // 4) % 2


def slab_source(p):
    m = p.z * 2 + p.c
    return p.at(x=m % 4, y=(m // 4) * 2 + p.yl, z=slab_place(p, x=p.x), c=slab_place(p, y=p.y))


def same(p, to):
    return (to[0] == p.g) & (to[1] == p.s)


def greet_plane(partners, slab_to, slab_from, own_slab):
    barrier = pltpu.get_barrier_semaphore()
    for to in partners:
        pl.semaphore_signal(barrier, inc=1, device_id=to, device_id_type=MESH)

    @pl.when(jnp.logical_not(own_slab))
    def _():
        pl.semaphore_signal(barrier, inc=1, device_id=slab_to, device_id_type=MESH)
        pl.semaphore_signal(barrier, inc=1, device_id=slab_from, device_id_type=MESH)

    def wait():
        @pl.when(jnp.logical_not(own_slab))
        def _():
            pl.semaphore_wait(barrier, len(partners) + 2)

        @pl.when(own_slab)
        def _():
            pl.semaphore_wait(barrier, len(partners))

    return wait


class Slab:
    def __init__(self, k, src, dst, to, own):
        self.own, self.src, self.dst = own, src, dst
        self.far = k.plan(src, dst, to)
        k.sent.pop(id(self.far))
        self.near = pltpu.make_async_copy(src, dst, k.recv_sems.at[k.received - 1])

    def start(self):
        @pl.when(self.own)
        def _():
            self.near.start()

        @pl.when(jnp.logical_not(self.own))
        def _():
            self.far.start()

    def wait_recv(self):
        @pl.when(self.own)
        def _():
            self.near.wait()

        @pl.when(jnp.logical_not(self.own))
        def _():
            self.far.wait_recv()

    def wait_send(self):
        @pl.when(jnp.logical_not(self.own))
        def _():
            self.far.wait_send()


def add_blocks(dst, terms, chunk):
    lead, rows = dst.shape[:-2], dst.shape[-2]
    count = 1
    for n in lead:
        count *= n

    @pl.loop(0, count)
    def _(i):
        at = []
        rest = i
        for n in reversed(lead):
            at.insert(0, rest % n)
            rest = rest // n

        @pl.loop(0, rows, step=chunk)
        def _(t):
            here = (*at, pl.ds(pl.multiple_of(t, chunk), chunk))
            total = terms[0][here].astype(F32)
            for term in terms[1:]:
                total = total + term[here].astype(F32)
            dst[here] = total.astype(dst.dtype)


def staged_reduce(p, k, src, stages, scr, chunk):
    own = scr[0]
    cur = src
    for n, (axis, pick) in enumerate(stages):
        recv = scr[1] if n == 0 else scr[2 * n]
        if n == 0:
            mine = k.local(pick(src, p.pos(axis, 0)), own)
        ring = [k.send(pick(cur, p.pos(axis, j)), recv.at[j - 1], p.step(axis, j)) for j in (1, 2, 3)]
        yield
        if n == 0:
            mine.wait()
        for copy in ring:
            copy.wait_recv()
        total = own if n == 0 else scr[2 * n + 1]
        add_blocks(total, [own if n == 0 else pick(cur, p.pos(axis, 0))] + [recv.at[j] for j in range(3)], chunk)
        cur = total


def ring_reduce(p, k, src, stages, scr, chunk):
    own, recv, held, recv2, total = scr
    axis, pick = stages[0]
    before, after, far = recv.at[0], recv.at[1], recv.at[2]
    far_a, far_b = halves(pick(src, p.pos(axis, 2)))
    right_a, right_b = halves(pick(src, p.pos(axis, 1)))
    left_a, left_b = halves(pick(src, p.pos(axis, 3)))
    right, left = p.step(axis, 1), p.step(axis, 3)
    on_right = k.send(far_a, halves(far)[0], right)
    on_left = k.send(far_b, halves(far)[1], left)
    get = [k.local(right_a, halves(held)[0]), k.local(left_b, halves(held)[1])]
    mine = k.local(pick(src, p.pos(axis, 0)), own)
    yield
    near = [k.send(right_b, halves(before)[1], right), k.send(left_a, halves(after)[0], left)]
    yield
    for i, (copy, to, dst) in enumerate(((on_right, right, before), (on_left, left, after))):
        get[i].wait()
        copy.wait_recv()
        here = halves(held)[i]
        add_blocks(here, [here, halves(far)[i]], chunk)
        near.append(k.send(here, halves(dst)[i], to))
    yield
    mine.wait()
    for copy in near:
        copy.wait_recv()
    add_blocks(own, [own, before, after], chunk)
    axis, pick = stages[1]
    ring = [k.send(pick(own, p.pos(axis, j)), recv2.at[j - 1], p.step(axis, j)) for j in (1, 2, 3)]
    yield
    for copy in ring:
        copy.wait_recv()
    add_blocks(total, [pick(own, p.pos(axis, 0))] + [recv2.at[j] for j in range(3)], chunk)


def mix_reduce(p, k, part, bufs, held):
    right, left = p.step("z", 1), p.step("z", 3)
    far_a, far_b = halves(part.at[p.pos("z", 2)])
    right_a, right_b = halves(part.at[p.pos("z", 1)])
    left_a, left_b = halves(part.at[p.pos("z", 3)])
    far = halves(bufs.at[2])
    first = [k.send(far_a, far[0], right), k.send(far_b, far[1], left)]
    near = [k.send(right_b, halves(bufs.at[0])[1], right), k.send(left_a, halves(bufs.at[1])[0], left)]
    get = [k.local(right_a, halves(held)[0]), k.local(left_b, halves(held)[1])]
    yield
    for i, to in enumerate((right, left)):
        get[i].wait()
        first[i].wait_recv()
        here = halves(held)[i]
        add_blocks(here, [here, far[i]], 16)
        near.append(k.send(here, halves(bufs.at[i])[i], to))
    yield
    for copy in near:
        copy.wait_recv()


def staged_scratch(shapes, held=False):
    out = [pltpu.VMEM(shapes[0], BF16), pltpu.VMEM((3, *shapes[0]), BF16)]
    if held:
        out.append(pltpu.VMEM(shapes[0], BF16))
    for n, shape in enumerate(shapes[1:]):
        out.append(pltpu.VMEM((3, *shape), BF16))
        out.append(pltpu.VMEM(shape, BF16))
    return out


EVERY = slice(None)


def wg_stages(half):
    cols = pl.ds(half * FS, FS)
    if half == 0:
        return [
            ("y", lambda r, i: r.at[i // 2, :, i % 2, :, cols]),
            ("x", lambda r, i: r.at[i]),
        ]
    return [
        ("x", lambda r, i: r.at[:, i, :, :, cols]),
        ("y", lambda r, i: r.at[i // 2, i % 2]),
    ]


def wd_stages(p, half):
    cols = pl.ds(half * 512, 512)
    if half == 0:
        return [
            ("y", lambda r, i: r.at[i % 2, :, slab_place(p, y=i), :, cols]),
            ("x", lambda r, i: r.at[slab_place(p, x=i)]),
        ]
    return [
        ("x", lambda r, i: r.at[:, slab_place(p, x=i), :, :, cols]),
        ("y", lambda r, i: r.at[i % 2, slab_place(p, y=i)]),
    ]


def q_stages(half):
    cols = pl.ds(half * 128, 128)
    if half == 0:
        return [
            ("y", lambda r, i: r.at[i // 2, :, i % 2, :, cols]),
            ("x", lambda r, i: r.at[i]),
        ]
    return [
        ("x", lambda r, i: r.at[:, i, :, :, cols]),
        ("y", lambda r, i: r.at[i // 2, i % 2]),
    ]


def o_stages(part):
    cols = pl.ds(*O_PARTS[part])
    if part == 0:
        return [
            ("x", lambda r, i: r.at[:, i, :, :, :, cols]),
            ("z", lambda r, i: r.at[:, :, i]),
            ("y", lambda r, i: r.at[i // 2, i % 2]),
        ]
    if part == 1:
        return [
            ("y", lambda r, i: r.at[i // 2, :, i % 2, :, :, cols]),
            ("x", lambda r, i: r.at[i]),
            ("z", lambda r, i: r.at[i]),
        ]
    return [
        ("z", lambda r, i: r.at[:, :, :, i, :, cols]),
        ("y", lambda r, i: r.at[i // 2, :, i % 2]),
        ("x", lambda r, i: r.at[i]),
    ]


O_PARTS = ((0, 256), (256, 128), (384, 256))
PLANE_SHAPES = [
    [(4, 128, FS), (128, FS)],
    [(2, 2, 128, FS), (128, FS)],
    [(4, 80, 512), (80, 512)],
    [(2, 2, 80, 512), (80, 512)],
    [(4, 128, 128), (128, 128)],
    [(2, 2, 128, 128), (128, 128)],
]
O_SHAPES = [
    [(2, 2, 4, 32, 256), (2, 2, 32, 256), (32, 256)],
    [(4, 4, 32, 128), (4, 32, 128), (32, 128)],
    [(2, 4, 2, 32, 256), (4, 32, 256), (32, 256)],
]


def small_reduce(p, k, vec, recv):
    for n, axis in enumerate("zyxc"):
        steps = (1,) if axis == "c" else (1, 2, 3)
        ring = [k.send(vec.at[n], recv.at[n, j - 1], p.step(axis, j)) for j in steps]
        yield
        for copy in ring:
            copy.wait_recv()
        total = vec[n]
        for j in range(len(steps)):
            total = total + recv[n, j]
        vec[n + 1] = total


def swap(a, b):
    left = lax.broadcasted_iota(jnp.int32, a.shape, 1) < ROWS
    return jnp.where(left, a, pltpu.roll(b, ROWS, 1)), jnp.where(left, pltpu.roll(a, ROWS, 1), b)


def head_scale(v):
    return lax.rsqrt(jnp.mean(v * v, axis=-2, keepdims=True) + EPS)


def half_turn(v):
    half = HEAD // 2
    return jnp.concatenate([-v[..., half:, :], v[..., :half, :]], axis=-2)


def half_back(v):
    half = HEAD // 2
    return jnp.concatenate([v[..., half:, :], -v[..., :half, :]], axis=-2)


def low(v):
    return v.astype(BF16).astype(F32)


def query_units(packed_t, g, cos, sin, gain):
    raw = packed_t[pl.ds(pl.multiple_of(g * 256, 256), 256)].reshape(GROUP, HEAD, TOK)
    head = raw * head_scale(raw) * gain
    turned = low(head * cos + half_turn(head) * sin) * (HEAD ** -0.5)
    a0, a1 = swap(turned[0], turned[1])
    b0, b1 = swap(turned[2], turned[3])
    none = jnp.zeros((HEAD, 256), F32)
    return [
        jnp.concatenate([jnp.concatenate([a, b], axis=1), none], axis=0) for a, b in ((a0, b0), (a1, b1))
    ]


def fill_bias(bias, seg, s):
    lane = lax.broadcasted_iota(jnp.int32, (128, 128), 1)
    query = lane % ROWS + s * ROWS
    around = pl.ds(pl.multiple_of((s // 2) * 128, 128), 128)
    for m in range(MICRO):
        ids = jnp.broadcast_to(seg[m : m + 1, around].astype(F32), (128, 128))
        turned = pltpu.roll(ids, ROWS, 1)
        ids = jnp.where((lane < ROWS) == (s % 2 == 0), ids, turned)
        ids = jnp.where(ids >= 0, ids, -2.0)

        @pl.loop(0, SEQ, step=128)
        def _(t):
            at = pl.ds(pl.multiple_of(t, 128), 128)
            key = lax.broadcasted_iota(jnp.int32, (128, 128), 0) + t
            keys = jnp.broadcast_to(seg[m : m + 1, at].astype(F32), (128, 128)).T
            ok = ((key <= query) & (keys == ids)) | (key == query)
            bias[m, at] = jnp.where(ok, 3e38, -1e30)


def rope_parts():
    inverse = 10000.0 ** (-(np.arange(HEAD) % (HEAD // 2)) / (HEAD // 2))
    begin = inverse[:, None] * (np.arange(128)[None, :] % 16 * ROWS)
    inside = inverse[:, None] * (np.arange(128)[None, :] % ROWS)
    return np.stack([np.cos(begin), np.sin(begin), np.cos(inside), np.sin(inside)]).astype(np.float32)


def rope_tables(parts, s):
    here = lax.broadcasted_iota(jnp.int32, (HEAD, 128), 1) == s
    c0 = jnp.sum(jnp.where(here, parts[0], 0.0), axis=1, keepdims=True)
    s0 = jnp.sum(jnp.where(here, parts[1], 0.0), axis=1, keepdims=True)
    return c0 * parts[2] - s0 * parts[3], s0 * parts[2] + c0 * parts[3]


def column(row):
    n = row.shape[1]
    place = lax.broadcasted_iota(jnp.int32, (n, n), 0) == lax.broadcasted_iota(jnp.int32, (n, n), 1)
    return jnp.sum(jnp.where(place, jnp.broadcast_to(row, (n, n)), 0.0), axis=1, keepdims=True)


KV_PARTS = (pl.ds(0, 384), pl.ds(384, 256))


def unit_bias(bias, m):
    half = bias[m]
    return jnp.concatenate([half, half], axis=1)


def unit_kv(KV, m, g):
    cols = pl.ds(pl.multiple_of(g * 128, 128), 128)
    return KV[m, :, :, :, :, cols].reshape(SEQ, 128)


def front_body(*refs):
    (x_in, w_qkv, wo, wg, w_down, og, seg, g1, g2, g3, g4, parts) = refs[:12]
    (WO, WG, WD, OG, NA, KV, PT, LSE, ATT, RESID, N2, WQIN, BIAS, ROPE, GAINS, QKGAIN) = refs[12:28]
    (wq, wd, ogv, gains_out, rope, qkgain) = refs[28:34]
    (xs, na, wqm, wos, pks, pk, pt, lse, att, resid, n2, kvl, kvs, bias, qts, ots) = refs[34:50]
    ssem, rsem, lsem = refs[50:]
    p = Place()
    k = Links(ssem, rsem, lsem)
    yh, x, yl, z, c = p.yh, p.x, p.yl, p.z, p.c
    m = z * 2 + c
    sib = p.step("c", 1)
    yl_partner = p.at(y=p.yh * 2 + 1 - yl)
    partners = [p.step(a, j) for a in "xyz" for j in (1, 2, 3)]
    partners += [p.at(z=(z + j) % 4, c=1 - c) for j in range(4)]
    slab_to, slab_from = slab_target(p), slab_source(p)
    own_slab = same(p, slab_to)

    met = greet_plane(partners, slab_to, slab_from, own_slab)
    own_x = k.local(x_in, xs.at[z, c])
    get_og = k.local(og, ogv)
    spare = [column(row[...].astype(F32)) for row in (g1, g2)]
    wide = w_qkv[...].astype(F32)
    lane = lax.broadcasted_iota(jnp.int32, (16, 256), 1)
    rest = jnp.where(lane == 240, spare[0], jnp.where(lane == 241, spare[1], 0.0))
    for i in range(8):
        turned = pltpu.roll(wide, (QKV - 240 * i) % QKV, 1)[:, :256]
        wq[:, i * 256 : (i + 1) * 256] = jnp.where(lane < 240, turned, rest).astype(BF16)
    met()

    def spread(src_of, dst_of):
        far, near = [], None
        for dz in range(4):
            for dc in range(2):
                zz, cc = (z + dz) % 4, (c + dc) % 2
                src, dst = src_of(zz * 2 + cc), dst_of(m)
                if dz == 0 and dc == 0:
                    near = k.local(src, dst)
                else:
                    far.append(k.send(src, dst, p.at(z=zz, c=cc)))
        return near, far

    q0 = spread(
        lambda i: wq.at[:, pl.ds(pl.multiple_of(i * 256, 256), 256)], lambda i: wqm.at[yh, x, yl, i]
    )
    xcore = {0: k.send(x_in, xs.at[z, c], sib)}
    own_wo = k.local(wo, wos.at[yh, x, yl, z, c])

    def wo_at(part, *at):
        return wos.at[(*at, EVERY, pl.ds(part * 640, 640))]

    o1 = [k.send(wo, wos.at[yh, x, yl, z, c], p.step("z", j)) for j in (1, 2, 3)]
    g0 = [
        spread(
            lambda i: wg.at[:, pl.ds(pl.multiple_of(half * FF + i * FS, 128), FS)],
            lambda i: WG.at[yh, x, yl, i, :, pl.ds(half * FS, FS)],
        )
        for half in range(2)
    ]
    xring = RingGather(p, k, "z", lambda i: xs.at[i, c], x_in)

    def to_plane(blocks):
        return [k.send(b, b, p.step(axis, j)) for j in (1, 2, 3) for b, axis in blocks]

    ql, qh = pl.ds(0, 128), pl.ds(128, 128)
    lo, hi = pl.ds(0, FS), pl.ds(FS, FS)
    dlo, dhi = pl.ds(0, 384), pl.ds(384, 640)
    q0[0].wait()
    for copy in q0[1]:
        copy.wait_recv()
    q1 = to_plane(((wqm.at[yh, x, yl, :, :, ql], "x"), (wqm.at[yh, x, yl, :, :, qh], "y")))
    fill_bias(bias, seg, p.s)
    cos, sin = rope_tables(parts, p.s)
    rope[0], rope[1] = cos, sin
    qgain, kgain = column(g3[...].astype(F32)), column(g4[...].astype(F32))
    qkgain[...] = jnp.concatenate([jnp.broadcast_to(qgain, (HEAD, 128)), jnp.broadcast_to(kgain, (HEAD, 128))], axis=0)
    for copy in q1:
        copy.wait_recv()
    q2 = to_plane(((wqm.at[yh, :, yl, :, :, ql], "y"), (wqm.at[:, x, :, :, :, qh], "x")))
    for near, far in g0:
        near.wait()
        for copy in far:
            copy.wait_recv()
    plane = to_plane(((WG.at[yh, x, yl, :, :, lo], "x"), (WG.at[yh, x, yl, :, :, hi], "y")))
    slab_rows = w_down[...].astype(F32)
    wd[...] = jnp.concatenate([slab_rows[:, :1024], slab_rows[:, 1024:]], axis=0).astype(BF16)
    slab = Slab(k, wd, WD.at[yl, z, c], slab_to, own_slab)
    slab.start()
    xring.hand_on()
    for o in (1, 3):
        src = xs.at[(z + o) % 4, c]
        xcore[o] = k.send(src, src, sib)
    for copy in q2:
        copy.wait_recv()
    own_x.wait()
    own_wo.wait()
    pick = jnp.where(
        lax.broadcasted_iota(jnp.int32, (8, 128), 0) + 112 == lax.broadcasted_iota(jnp.int32, (8, 128), 1), 1.0, 0.0
    ).astype(BF16)
    gains_out[...] = dot_last(pick, wqm[:, :, :, :, :, pl.ds(128, 128)].reshape(D, 128))
    keep = [k.local(wq, WQIN), k.local(bias, BIAS), k.local(rope, ROPE), k.local(gains_out, GAINS), k.local(qkgain, QKGAIN)]
    k.settle(q0[1] + q1)
    packs = []
    for o in (0, 1, 3, 2):
        zz = (z + o) % 4
        if o == 2:
            xring.wait()
            xcore[o] = k.send(xs.at[zz, c], xs.at[zz, c], sib)
        xcore[o].wait_recv()
        rows = xs[zz].reshape(256, D).astype(F32)
        normed = (rows * rms_scale(rows) * gains_out[0:1, :]).astype(BF16)
        na[zz] = normed.reshape(2, TOK, D)
        pks[zz] = dot(normed, wqm[...].reshape(D, 256)).astype(BF16).reshape(2, TOK, 256)
        if o:
            packs.append(k.send(pks.at[zz, c], pk.at[m], p.at(z=zz)))
        else:
            own_pk = k.local(pks.at[z, c], pk.at[m])
        packs.append(k.send(pks.at[zz, 1 - c], pk.at[m], p.at(z=zz, c=1 - c)))
        if o == 1:
            for copy in o1:
                copy.wait_recv()
            o2 = to_plane(
                (
                    (wo_at(0, yh, x, yl, EVERY, c), "y"),
                    (wo_at(1, yh, x, yl, EVERY, c), "x"),
                ),
            )
        if o == 3:
            for copy in plane:
                copy.wait_recv()
            plane2 = [
                RingGather(p, k, "x", lambda i: WG.at[:, i, :, :, :, hi]),
                RingGather(p, k, "y", lambda i: WG.at[i // 2, :, i % 2, pl.ds(0, 4), :, lo]),
            ]
    slab.wait_recv()
    held = WD.at[yl, slab_place(p, x=x), slab_place(p, y=p.y)]
    plane_d = to_plane(((held.at[:, dlo], "x"), (held.at[:, dhi], "y")))
    for copy in o2:
        copy.wait_recv()
    o3 = [RingGather(p, k, "x", lambda i: wo_at(0, EVERY, i, EVERY, EVERY, c))]
    keep.append(k.local(na, NA))
    k.settle(q2 + o1 + [copy for _, far in g0 for copy in far])
    own_pk.wait()
    for copy in packs:
        copy.wait_recv()
    for i8 in range(8):
        pt[i8 * 240 : (i8 + 1) * 240] = pk[i8].astype(F32).T[:240]

    @pl.loop(0, KV_HEADS)
    def _(g):
        raw = pt[pl.ds(pl.multiple_of(QD + g * HEAD, HEAD), HEAD)]
        head = raw * head_scale(raw) * kgain
        key = head * cos + half_turn(head) * sin
        value = pt[pl.ds(pl.multiple_of(QD + KD + g * HEAD, HEAD), HEAD)]
        both = jnp.concatenate([key, value], axis=0).T.astype(BF16)
        cols = pl.ds(pl.multiple_of(g * 128, 128), 128)
        for mm in range(MICRO):
            kvl[mm, :, cols] = both[mm * ROWS : (mm + 1) * ROWS]

    own_kv = k.local(kvl, kvs.at[:, yl, z, c])
    across, ring = [], []
    for cols in KV_PARTS:
        across.append(k.send(kvl.at[:, :, cols], kvs.at[:, yl, z, c, :, cols], yl_partner))
        ring.append([k.send(kvl.at[:, :, cols], kvs.at[:, yl, z, c, :, cols], p.step("z", j)) for j in (1, 2, 3)])
    keep.append(k.local(pt, PT))

    @pl.loop(0, KV_HEADS)
    def _(g):
        for mm, unit in enumerate(query_units(pt, g, cos, sin, qgain)):
            qts[g, mm] = unit.astype(BF16)

    for copy, group, cols in zip(across, ring, KV_PARTS):
        copy.wait_recv()
        src = kvs.at[:, 1 - yl, z, c, :, cols]
        group += [k.send(src, src, p.step("z", j)) for j in (1, 2, 3)]
    get_og.wait()
    keep.append(k.local(ogv, OG.at[z, c]))
    rows = RingGather(p, k, "z", lambda i: OG.at[i, c], ogv)
    last = [k.send(ogv, OG.at[z, c], sib)]
    own_kv.wait()
    o3.append(RingGather(p, k, "y", lambda i: wo_at(1, i // 2, EVERY, i % 2, EVERY, c)))
    for ring4 in plane2:
        ring4.hand_on()
    oc = []
    for src in (
        wo_at(0, EVERY, x, EVERY, EVERY, c),
        wo_at(1, yh, EVERY, yl, EVERY, c),
    ):
        oc.append(k.send(src, src, sib))
    for copy in ring[0]:
        copy.wait_recv()
    src = kvs.at[:, :, :, c, :, KV_PARTS[0]]
    kvc = [k.send(src, src, sib)]
    o3[0].hand_on()
    o3[1].hand_on()
    for copy in plane_d:
        copy.wait_recv()
    plane2.append(RingGather(p, k, "x", lambda i: WD.at[:, slab_place(p, x=i), :, :, dhi]))
    plane2 += [
        RingGather(p, k, "y", lambda i: WD.at[i % 2, :, slab_place(p, y=i), :, dlo]),
        RingGather(p, k, "y", lambda i: WG.at[i // 2, :, i % 2, pl.ds(4, 4), :, lo]),
    ]
    for axis, ring4 in zip("xy", o3):
        for j in (1, 3):
            src = ring4.block(p.pos(axis, j))
            oc.append(k.send(src, src, sib))
    kvc[0].wait_recv()

    def unit(u):
        g, mm = u // 2, u % 2
        kv = unit_kv(kvs, mm, g)
        score = jnp.minimum(dot(kv, qts[g, mm]), unit_bias(bias, mm))
        peak = jnp.max(score, axis=0, keepdims=True)
        raised = jnp.exp(score - peak)
        total = jnp.sum(raised, axis=0, keepdims=True)
        probs = (raised * (1.0 / total)).astype(BF16)
        ots[g, mm] = dot_rows(kv, probs)[HEAD:]
        lse[u] = jnp.broadcast_to(peak + jnp.log(total), (8, 256))

    k.settle(packs + plane + plane_d)
    pl.loop(0, 6)(unit)
    for copy in ring[1]:
        copy.wait_recv()
    src = kvs.at[:, :, :, c, :, KV_PARTS[1]]
    kvc.append(k.send(src, src, sib))
    k.settle(o2 + xring.copies() + list(xcore.values()))
    kvc[1].wait_recv()
    keep.append(k.local(kvs, KV))
    for axis, ring4 in zip("xy", o3):
        ring4.wait()
        src = ring4.block(p.pos(axis, 2))
        oc.append(k.send(src, src, sib))
    pl.loop(6, 2 * KV_HEADS)(unit)
    for g in range(KV_HEADS):
        for t in range(2):
            cols = slice(t * 128, (t + 1) * 128)
            a, b = swap(ots[g, 0, :, cols], ots[g, 1, :, cols])
            at = (g * GROUP + 2 * t) * HEAD
            att[:, at : at + 128] = jnp.concatenate([a, b], axis=0).T.astype(BF16)
    keep += [k.local(lse, LSE), k.local(att, ATT)]
    rows.hand_on()
    for j in (1, 3):
        src = OG.at[p.pos("z", j), c]
        last.append(k.send(src, src, sib))
    for copy in oc:
        copy.wait_recv()
    keep.append(k.local(wos, WO))

    @pl.loop(0, 8)
    def _(t):
        w = wos[t // 4, t % 4].reshape(256, QD)
        cols = pl.ds(pl.multiple_of(t * 256, 256), 256)
        resid[:, cols] = xs[z, c, :, cols].astype(F32) + dot_last(att[...], w)

    plane2[2].hand_on()
    plane2[3].hand_on()
    plane2[4].hand_on()
    value = resid[...]
    n2[...] = (value * rms_scale(value) * gains_out[1:2, :]).astype(BF16)
    keep += [k.local(resid, RESID), k.local(n2, N2)]
    rows.wait()
    src = OG.at[p.pos("z", 2), c]
    last.append(k.send(src, src, sib))
    for ring4 in plane2:
        ring4.wait()
    for copy in last:
        copy.wait_recv()
    for copy in keep:
        copy.wait()
    slab.wait_send()
    k.drain()


VMEM = pl.BlockSpec(memory_space=pltpu.VMEM)


def front(*args):
    hbm = [
        sds((2, 4, 2, 4, 2, 16, QD), BF16),
        sds((2, 4, 2, 8, 16, 2 * FS), BF16),
        sds((2, 4, 2, 80, 1024), BF16),
        sds((4, 2, TOK, D), BF16),
        sds((4, 2, TOK, D), BF16),
        sds((2, 2, 4, 2, ROWS, 2 * KD), BF16),
        sds((QKV, TOK), F32),
        sds((2 * KV_HEADS, 8, 256), F32),
        sds((TOK, QD), BF16),
        sds((TOK, D), F32),
        sds((TOK, D), BF16),
        sds((16, 2048), BF16),
        sds((2, SEQ, 128), F32),
        sds((2, HEAD, TOK), F32),
        sds((8, D), F32),
        sds((2 * HEAD, 128), F32),
    ]
    scratch = [
        pltpu.VMEM((16, 2048), BF16),
        pltpu.VMEM((80, 1024), BF16),
        pltpu.VMEM((TOK, D), BF16),
        pltpu.VMEM((8, D), F32),
        pltpu.VMEM((2, HEAD, TOK), F32),
        pltpu.VMEM((2 * HEAD, 128), F32),
        pltpu.VMEM((4, 2, TOK, D), BF16),
        pltpu.VMEM((4, 2, TOK, D), BF16),
        pltpu.VMEM((2, 4, 2, 8, 16, 256), BF16),
        pltpu.VMEM((2, 4, 2, 4, 2, 16, QD), BF16),
        pltpu.VMEM((4, 2, TOK, 256), BF16),
        pltpu.VMEM((8, TOK, 256), BF16),
        pltpu.VMEM((QKV, TOK), F32),
        pltpu.VMEM((2 * KV_HEADS, 8, 256), F32),
        pltpu.VMEM((TOK, QD), BF16),
        pltpu.VMEM((TOK, D), F32),
        pltpu.VMEM((TOK, D), BF16),
        pltpu.VMEM((2, ROWS, 2 * KD), BF16),
        pltpu.VMEM((2, 2, 4, 2, ROWS, 2 * KD), BF16),
        pltpu.VMEM((2, SEQ, 128), F32),
        pltpu.VMEM((KV_HEADS, 2, 128, 256), BF16),
        pltpu.VMEM((KV_HEADS, 2, HEAD, 256), F32),
        pltpu.SemaphoreType.DMA((80,)),
        pltpu.SemaphoreType.DMA((130,)),
        pltpu.SemaphoreType.DMA((14,)),
    ]
    return pl.pallas_call(
        front_body,
        out_shape=hbm,
        in_specs=[ANY, VMEM, VMEM, ANY, VMEM, ANY] + [VMEM] * 6,
        out_specs=[ANY] * len(hbm),
        scratch_shapes=scratch,
        name="front",
        compiler_params=pltpu.CompilerParams(
            collective_id=0, has_side_effects=True, vmem_limit_bytes=56 << 20
        ),
    )(*args)


def ffn_body(n2, OG, WG, WD, wq, d_out, mix_out, dwg_out, dwd_out, WQ, *scr):
    (rows, ogs, wgs, wd80, wds, dgu, inn, din, part, mixs, r0, s0, r1, m0, dwg, dwd32, dwd) = scr[:17]
    (dn, wqv, ssem, rsem, lsem, wsem, vsem, wlsem) = scr[17:]
    p = Place()
    k = Links(wsem, vsem, wlsem)
    yh, x, yl, z, c = p.yh, p.x, p.yl, p.z, p.c
    sib = p.step("c", 1)
    greet([p.step(a, j) for a in "xyz" for j in (1, 2, 3)] + [sib])

    def remote(src, dst, i, to):
        return pltpu.make_async_remote_copy(
            src_ref=src,
            dst_ref=dst,
            send_sem=ssem.at[i],
            recv_sem=rsem.at[i],
            device_id=to,
            device_id_type=MESH,
        )

    def local(src, dst, i):
        copy = pltpu.make_async_copy(src, dst, lsem.at[i])
        copy.start()
        return copy

    def half_of(half, *at):
        return WQ.at[(*at, EVERY, pl.ds(half * 1024, 1024))]

    whole = (EVERY, EVERY, EVERY, EVERY, c)
    get_wq = k.local(wq, wqv)
    q1 = [k.plan(wq, WQ.at[yh, x, yl, z, c], p.step("z", j)) for j in (1, 2, 3)]
    q2, q3 = [], []
    for j in (1, 2, 3):
        for half, axis in ((0, "y"), (1, "x")):
            src = half_of(half, yh, x, yl, EVERY, c)
            q2.append(k.plan(src, src, p.step(axis, j)))
    for j in (1, 2, 3):
        src = half_of(0, EVERY, x, EVERY, EVERY, c)
        q3.append(k.plan(src, src, p.step("x", j)))
        src = half_of(1, yh, EVERY, yl, EVERY, c)
        q3.append(k.plan(src, src, p.step("y", j)))
    q4 = k.plan(WQ.at[whole], WQ.at[whole], sib)

    sent = []
    for copy in q1:
        copy.start()
    for j in (1, 3):
        copy = remote(n2, rows.at[z, c], j, p.step("z", j))
        copy.start()
        sent.append(copy)
    half = halves(rows.at[p.pos("z", 1), c])[1], halves(rows.at[p.pos("z", 3), c])[0]
    on_left = remote(half[0], half[0], 0, p.step("z", 3))
    on_right = remote(half[1], half[1], 2, p.step("z", 1))
    sent += [on_left, on_right]
    remote(n2, rows.at[z, c], 4, sib).start()
    own = local(n2, rows.at[z, c], 0)
    get_wd = local(WD, wd80, 1)
    get_wg = local(WG, wgs, 2)
    get_og = local(OG, ogs, 3)
    get_wd.wait()

    @pl.loop(0, 8)
    def _(i):
        yl, x = i // 4, i % 4
        a, b = wd80[yl, x, 0].astype(F32), wd80[yl, x, 1].astype(F32)
        at = pl.ds(pl.multiple_of(i * 80, 80), 80)
        wds[at, :1024] = jnp.concatenate([a[:40], b[:40]], axis=0).astype(BF16)
        wds[at, 1024:] = jnp.concatenate([a[40:], b[40:]], axis=0).astype(BF16)

    own.wait()
    get_wg.wait()
    get_og.wait()
    get_wq.wait()
    own_wq = k.local(wqv, WQ.at[yh, x, yl, z, c])

    def ring_step(j):
        return jnp.where(j == 2, 3, jnp.where(j == 3, 2, j))

    def d_inner_of(zz):
        din[...] = dot_last(ogs[zz].reshape(256, D), wds[...])

    d_inner_of(z)
    own_wq.wait()
    for copy in q1:
        copy.wait_recv()
    for copy in q2:
        copy.start()

    top, end = pl.ds(0, D // 2), pl.ds(D // 2, D // 2)
    right, left = p.step("z", 1), p.step("z", 3)
    to_right, to_left, to_far = s0.at[p.pos("z", 1)], s0.at[p.pos("z", 3)], s0.at[p.pos("z", 2)]
    near_right = remote(to_right.at[end], r1.at[0, end], 12, right)
    near_left = remote(to_left.at[top], r1.at[1, top], 13, left)
    far_right = remote(to_far.at[top], r1.at[2, top], 14, right)
    far_left = remote(to_far.at[end], r1.at[2, end], 15, left)
    sum_right = remote(to_right.at[top], r1.at[0, top], 17, right)
    sum_left = remote(to_left.at[end], r1.at[1, end], 18, left)
    ring_sums = [near_right, near_left, far_right, far_left, sum_right, sum_left]

    @pl.loop(0, 4)
    def _(j):
        o = ring_step(j)
        zz = (z + o) % 4
        at = pl.ds(pl.multiple_of(zz * 256, 256), 256)

        @pl.when(j == 1)
        def _():
            remote(n2, rows.at[z, c], 3, sib).wait_recv()
            on_left.start()
            remote(n2, rows.at[z, c], 1, sib).wait_recv()
            on_right.start()
            for o_near in (1, 3):
                near = rows.at[(z + o_near) % 4, c]
                remote(near, near, 4 + o_near, sib).start()

        @pl.when(j == 2)
        def _():
            on_left.wait_recv()
            on_right.wait_recv()
            far = rows.at[(z + 2) % 4, c]
            remote(far, far, 4 + 2, sib).start()

        remote(rows.at[zz, c], rows.at[zz, 1 - c], 4 + o, sib).wait_recv()
        r = rows[zz].reshape(256, D)
        for t in range(5):
            lo, hi = slice(t * 128, (t + 1) * 128), slice(FS + t * 128, FS + (t + 1) * 128)
            w = jnp.concatenate(
                [wgs[:, :, :, :, :, lo].reshape(D, 128), wgs[:, :, :, :, :, hi].reshape(D, 128)], axis=1
            )
            both = dot(r, w)
            gate, upper = both[:, :128], both[:, 128:]
            sig = jax.nn.sigmoid(gate)
            active = gate * sig
            d_inner = din[:, lo]
            inn[at, lo] = (active * upper).astype(BF16)
            dgu[at, lo] = (d_inner * upper * sig * (1.0 + gate * (1.0 - sig))).astype(BF16)
            dgu[at, hi] = (d_inner * active).astype(BF16)

        for h in range(2):
            turned = dot_last(wgs[h].reshape(1024, 2 * FS), dgu[at]).astype(BF16)
            for cc in range(2):
                part[zz, cc, h * 1024 : (h + 1) * 1024] = turned[:, cc * TOK : (cc + 1) * TOK]

        remote(part.at[zz, 1 - c], r0.at[zz], 8 + o, sib).start()
        d_inner_of((z + ring_step((j + 1) % 4)) % 4)
        remote(part.at[zz, 1 - c], r0.at[zz], 8 + o, sib).wait_recv()

        @pl.loop(0, D, step=128)
        def _(t):
            here = pl.ds(pl.multiple_of(t, 128), 128)
            s0[zz, here] = (part[zz, c, here].astype(F32) + r0[zz, here].astype(F32)).astype(BF16)

        @pl.when(j == 1)
        def _():
            near_right.start()

        @pl.when(j == 2)
        def _():
            near_left.start()

        @pl.when(j == 3)
        def _():
            far_right.start()
            far_left.start()

        @pl.when(j == 0)
        def _():
            for t in range(8):
                left = rows[z, :, :, t * 256 : (t + 1) * 256].reshape(256, D // 8)
                dwg[t // 4, t % 4] = dot_rows(left, dgu[at]).astype(BF16).reshape(2, TOK, 2 * FS)
            for copy in q2:
                copy.wait_recv()
            for copy in q3:
                copy.start()

    @pl.loop(0, 4)
    def _(t):
        cols = pl.ds(pl.multiple_of(t * 512, 512), 512)
        mixs[:, :, :, cols] = dot(inn[...], wds[:, cols]).astype(BF16).reshape(4, 2, TOK, 512)

    mix_core = remote(mixs.at[:, 1 - c], m0, 16, sib)
    mix_core.start()
    others = [((z + o) % 4, pl.ds(pl.multiple_of((z + o) % 4 * 256, 256), 256)) for o in (1, 2, 3)]

    def gate_up_block(t):
        cols = pl.ds(pl.multiple_of(t * 256, 256), 256)
        total = dwg[t // 4, t % 4].reshape(256, 2 * FS).astype(F32)
        for zz, at in others:
            total = total + dot_rows(rows[zz, :, :, cols].reshape(256, 256), dgu[at])
        dwg[t // 4, t % 4] = total.astype(BF16).reshape(2, TOK, 2 * FS)

    pl.loop(0, 4)(gate_up_block)
    for first, over, add, at in ((far_right, sum_right, to_right, 0), (far_left, sum_left, to_left, D // 2)):
        first.wait_recv()

        @pl.loop(0, D // 2, step=128)
        def _(t, add=add, at=at):
            here = pl.ds(pl.multiple_of(t + at, 128), 128)
            add[here] = (add[here].astype(F32) + r1[2, here].astype(F32)).astype(BF16)

        over.start()
    pl.loop(4, 8)(gate_up_block)
    out_wg = local(dwg, dwg_out, 5)
    for copy in q3:
        copy.wait_recv()
    q4.start()

    @pl.loop(0, 5)
    def _(t):
        units = pl.ds(pl.multiple_of(t * 128, 128), 128)
        dwd32[units] = dot_rows(inn[:, units], ogs[...].reshape(8 * TOK, D))

    @pl.loop(0, 8)
    def _(i):
        yl, x = i // 4, i % 4
        at = pl.ds(pl.multiple_of(i * 80, 80), 80)
        lo, hi = dwd32[at, :1024], dwd32[at, 1024:]
        dwd[yl, x, 0] = jnp.concatenate([lo[:40], hi[:40]], axis=0).astype(BF16)
        dwd[yl, x, 1] = jnp.concatenate([lo[40:], hi[40:]], axis=0).astype(BF16)

    out_wd = local(dwd, dwd_out, 6)
    mix_core.wait_recv()

    @pl.loop(0, 4)
    def _(zz):
        @pl.loop(0, TOK, step=16)
        def _(t):
            here = pl.ds(pl.multiple_of(t, 16), 16)
            m0[zz, here] = (mixs[zz, c, here].astype(F32) + m0[zz, here].astype(F32)).astype(BF16)

    out_mix = local(m0, mix_out, 4)
    for copy in (near_right, near_left, sum_right, sum_left):
        copy.wait_recv()
    for t in range(0, D, 128):
        here = slice(t, t + 128)
        total = s0[z, here].astype(F32)
        for j in range(2):
            total = total + r1[j, here].astype(F32)
        dn[:, here] = total.T

    out_dn = local(dn, d_out, 7)
    q4.wait_recv()
    k.drain()
    for copy in sent:
        copy.wait_send()
    for o in range(4):
        remote(rows.at[0, 0], rows.at[0, 0], 4 + o, sib).wait_send()
        remote(part.at[0, 0], r0.at[0], 8 + o, sib).wait_send()
    for copy in ring_sums:
        copy.wait_send()
    mix_core.wait_send()
    for copy in (out_mix, out_wg, out_wd, out_dn):
        copy.wait()


def ffn(n2, OG, WG, WD, wq):
    outs = [
        sds((TOK, D), F32),
        sds((4, TOK, D), BF16),
        sds((2, 4, 2, TOK, 2 * FS), BF16),
        sds((2, 4, 2, 80, 1024), BF16),
        sds((2, 4, 2, 4, 2, 16, 2048), BF16),
    ]
    scratch = [
        pltpu.VMEM((4, 2, TOK, D), BF16),
        pltpu.VMEM((4, 2, TOK, D), BF16),
        pltpu.VMEM((2, 4, 2, 8, 16, 2 * FS), BF16),
        pltpu.VMEM((2, 4, 2, 80, 1024), BF16),
        pltpu.VMEM((FS, D), BF16),
        pltpu.VMEM((8 * TOK, 2 * FS), BF16),
        pltpu.VMEM((8 * TOK, FS), BF16),
        pltpu.VMEM((256, FS), F32),
        pltpu.VMEM((4, 2, D, TOK), BF16),
        pltpu.VMEM((4, 2, TOK, D), BF16),
        pltpu.VMEM((4, D, TOK), BF16),
        pltpu.VMEM((4, D, TOK), BF16),
        pltpu.VMEM((3, D, TOK), BF16),
        pltpu.VMEM((4, TOK, D), BF16),
        pltpu.VMEM((2, 4, 2, TOK, 2 * FS), BF16),
        pltpu.VMEM((FS, D), F32),
        pltpu.VMEM((2, 4, 2, 80, 1024), BF16),
        pltpu.VMEM((TOK, D), F32),
        pltpu.VMEM((16, 2048), BF16),
        pltpu.SemaphoreType.DMA((19,)),
        pltpu.SemaphoreType.DMA((19,)),
        pltpu.SemaphoreType.DMA((8,)),
        pltpu.SemaphoreType.DMA((16,)),
        pltpu.SemaphoreType.DMA((16,)),
        pltpu.SemaphoreType.DMA((1,)),
    ]
    return pl.pallas_call(
        ffn_body,
        out_shape=outs,
        in_specs=[ANY] * 5,
        out_specs=[ANY] * 5,
        scratch_shapes=scratch,
        name="ffn",
        compiler_params=pltpu.CompilerParams(
            collective_id=1, has_side_effects=True, vmem_limit_bytes=60 << 20
        ),
    )(n2, OG, WG, WD, wq)


def back_body(*refs):
    (DN, X_IN, OG_IN, RESID, ATT, PT, LSE, WQ, WO, KV, mix_part, dwg, dwd, NA) = refs[:14]
    (BIAS, ROPE, GAINS, QKGAIN) = refs[14:18]
    (IN_GRAD, MIXED, GWG, GWD, GQ, GO, SMALL) = refs[18:25]
    (dn, xv, ogv, resid, pt, lse, in_grad, mixed, kvs, bias, qts, qns, dts, dns, dqt, dpt, datt, dres) = refs[25:43]
    (kpart, k0, k1, ks1, k2, kres, w2, wo2, low2, att2, do, dp, dpm, na2, dqm, mix1) = refs[43:59]
    (rope, gains, qkgain, mix_held) = refs[59:63]
    scr = list(refs[63:])
    parts = []
    for i, shapes in enumerate(PLANE_SHAPES + O_SHAPES):
        n = 2 * len(shapes) + (i < 4)
        parts.append(scr[:n])
        scr = scr[n:]
    vec, vrecv, ssem, rsem, lsem = scr
    p = Place()
    k = Links(ssem, rsem, lsem)
    yl, z, c = p.yl, p.z, p.c
    m = z * 2 + c
    sib = p.step("c", 1)
    yl_partner = p.at(y=p.yh * 2 + 1 - yl)
    partners = [p.step(a, j) for a in "xyz" for j in (1, 2, 3)]
    partners += [p.at(z=(z + j) % 4, c=1 - c) for j in range(4)]
    slab_to, slab_from = slab_target(p), slab_source(p)
    own_slab = same(p, slab_to)
    met = greet_plane(partners, slab_to, slab_from, own_slab)
    get = {}

    def fetch(**pairs):
        for name, (src, dst) in pairs.items():
            get[name] = k.local(src, dst)

    fetch(dn=(DN, dn), og=(OG_IN, ogv), resid=(RESID, resid), gains=(GAINS, gains))
    get_w = [k.local(WO.at[t // 4, t % 4], wo2.at[t]) for t in range(8)]
    fetch(pt=(PT, pt), rope=(ROPE, rope), qkgain=(QKGAIN, qkgain), att=(ATT, att2.at[0]))
    met()
    plane = [
        ring_reduce(p, k, dwg, wg_stages(0), parts[0], 16),
        ring_reduce(p, k, dwg, wg_stages(1), parts[1], 16),
        ring_reduce(p, k, dwd, wd_stages(p, 0), parts[2], 16),
        ring_reduce(p, k, dwd, wd_stages(p, 1), parts[3], 16),
    ]
    for step in plane + plane:
        next(step)
    pair_att = k.send(ATT, att2.at[1], sib)

    mixing = mix_reduce(p, k, mix_part, mix1, mix_held)
    next(mixing)
    for name in ("dn", "og", "resid", "gains"):
        get[name].wait()
    value = resid[...]
    scale_two = rms_scale(value)
    norm_two = value * scale_two
    d_resid = ogv[...].astype(F32) + norm_back(dn[...], norm_two, scale_two, gains[1:2, :])
    dres[...] = d_resid
    low2[0] = d_resid.astype(BF16)
    pair_low = k.send(low2.at[0], low2.at[1], sib)
    fetch(kv=(KV, kvs), lse=(LSE, lse), bias=(BIAS, bias))
    for name in ("pt", "rope", "qkgain"):
        get[name].wait()
    cos, sin = rope[0], rope[1]
    qgain, kgain = qkgain[:HEAD], qkgain[HEAD:]

    @pl.loop(0, KV_HEADS)
    def _(g):
        for mm, unit in enumerate(query_units(pt, g, cos, sin, qgain)):
            qts[g, mm] = unit.astype(BF16)
            qns[g, mm] = unit.T.astype(BF16)

    for t in range(8):
        get_w[t].wait()
        term = dot(low2[0, :, t * 256 : (t + 1) * 256], wo2[t].reshape(256, QD))
        datt[...] = term if t == 0 else datt[...] + term
    for g in range(KV_HEADS):
        tiles = []
        for t in range(2):
            at = (g * GROUP + 2 * t) * HEAD
            both = low(datt[:, at : at + 128]).T
            tiles.append(swap(both[:HEAD], both[HEAD:]))
        for mm in range(MICRO):
            none = jnp.zeros((HEAD, 256), F32)
            unit = jnp.concatenate([none, jnp.concatenate([tiles[0][mm], tiles[1][mm]], axis=1)], axis=0)
            dts[g, mm] = unit.astype(BF16)
            dns[g, mm] = unit.T.astype(BF16)
    fetch(x=(X_IN, xv), mix=(mix_part.at[z], mix1.at[3]))
    get["kv"].wait()
    get["lse"].wait()
    get["bias"].wait()

    def unit(u):
        g, mm = u // 2, u % 2
        kv = unit_kv(kvs, mm, g)
        score = jnp.minimum(dot(kv, qts[g, mm]), unit_bias(bias, mm))
        again = jnp.exp(score - lse[u, 0:1, :])
        d_probs = dot(kv, dts[g, mm])
        inner = jnp.sum(again * d_probs, axis=0, keepdims=True)
        d_scores = (again * (d_probs - inner)).astype(BF16)
        d_kv = dot(d_scores, qns[g, mm]) + dot(again.astype(BF16), dns[g, mm])
        cols = pl.ds(pl.multiple_of(g * 128, 128), 128)
        kpart[mm, :, :, :, :, cols] = d_kv.astype(BF16).reshape(2, 4, 2, ROWS, 128)
        dqt[g, mm] = dot_rows(kv, d_scores)[:HEAD] * (HEAD ** -0.5)

    def core_send(cols):
        return k.send(kpart.at[:, :, :, 1 - c, :, cols], k0.at[:, :, :, :, cols], sib)

    def ring_send(core, cols):
        core.wait_recv()

        @pl.loop(0, 4)
        def _(zz):
            for a in range(2):
                for b in range(2):
                    here = (a, b, zz, EVERY, cols)
                    both = kpart[a, b, zz, c, :, cols].astype(F32) + k0[here].astype(F32)
                    k0[here] = both.astype(BF16)

        return [
            k.send(k0.at[:, :, p.pos("z", j), :, cols], k1.at[j - 1, :, :, :, cols], p.step("z", j))
            for j in (1, 2, 3)
        ]

    pl.loop(0, 6)(unit)
    core = core_send(KV_PARTS[0])
    for step in plane:
        next(step)
    ring = ring_send(core, KV_PARTS[0])
    early = [copy for copy, _ in k.sent.values()]
    pl.loop(6, 2 * KV_HEADS)(unit)
    core = core_send(KV_PARTS[1])
    ring += ring_send(core, KV_PARTS[1])
    next(mixing)
    get["att"].wait()
    pair_att.wait_recv()
    pair_low.wait_recv()
    att_cols = pl.ds(pl.multiple_of(c * 640, 128), 640)

    @pl.loop(0, 8)
    def _(t):
        cols = pl.ds(pl.multiple_of(t * 256, 256), 256)
        left = low2[:, :, cols].reshape(2 * TOK, 256)
        right = att2[:, :, att_cols].reshape(2 * TOK, 640)
        do[t // 4, t % 4] = dot_rows(left, right).astype(BF16).reshape(2, 4, 32, 640)

    outward = [staged_reduce(p, k, do, o_stages(i), parts[6 + i], 16) for i in range(3)]
    next(outward[0])

    query_sum = jnp.zeros((HEAD, TOK), F32)
    for g in range(KV_HEADS):
        heads = []
        for t in range(2):
            cols = slice(t * 128, (t + 1) * 128)
            heads += list(swap(dqt[g, 0, :, cols], dqt[g, 1, :, cols]))
        for h in range(GROUP):
            at = (g * GROUP + h) * HEAD
            d_raw, term = head_back(pt[at : at + HEAD], heads[h], cos, sin, qgain)
            query_sum = query_sum + term
            dpt[at : at + HEAD] = d_raw

    for copy in ring:
        copy.wait_recv()
    for a in range(2):
        for b in range(2):
            total = k0[a, b, z].astype(F32)
            for j in range(3):
                total = total + k1[j, a, b].astype(F32)
            ks1[a, b] = total.astype(BF16)
    across = k.send(ks1.at[:, 1 - yl], k2, yl_partner)
    next(outward[1])
    next(plane[0])
    next(plane[2])
    across.wait_recv()
    for a in range(2):
        kres[pl.ds(a * ROWS, ROWS)] = ks1[a, yl].astype(F32) + k2[a].astype(F32)
    key_sum = jnp.zeros((HEAD, TOK), F32)
    for g in range(KV_HEADS):
        both = kres[:, g * 128 : (g + 1) * 128].T
        at = QD + g * HEAD
        d_raw, term = head_back(pt[at : at + HEAD], both[:HEAD], cos, sin, kgain)
        key_sum = key_sum + term
        dpt[at : at + HEAD] = d_raw
        dpt[at + KD : at + KD + HEAD] = both[HEAD:]
    get_q = [k.local(WQ.at[0, t], w2.at[t]) for t in range(2)]
    get_n = [k.local(NA.at[:, :, :, pl.ds(t * 256, 256)], na2.at[t]) for t in range(2)]
    for t in range(8):
        block = jnp.concatenate([dpt[t * 240 : (t + 1) * 240], jnp.zeros((16, TOK), F32)], axis=0)
        dp[t] = block.T.astype(BF16)
    sums = jnp.concatenate(
        [jnp.sum(query_sum.T, axis=0, keepdims=True), jnp.sum(key_sum.T, axis=0, keepdims=True)], axis=1
    )
    vec[0] = jnp.broadcast_to(sums, (8, 128))
    small = small_reduce(p, k, vec, vrecv)
    next(small)

    last, keep = [], []

    def to_owners(total, dst):
        for dz in range(4):
            for dc in range(2):
                zz, cc = (z + dz) % 4, (c + dc) % 2
                src = total.at[pl.ds(pl.multiple_of((zz * 2 + cc) * 16, 16), 16)]
                if dz == 0 and dc == 0:
                    keep.append(k.local(src, dst))
                else:
                    last.append(k.send(src, dst, p.at(z=zz, c=cc)))

    def slab_home(half):
        slab = Slab(k, parts[2 + half][-1], GWD.at[:, pl.ds(half * 512, 512)], slab_from, own_slab)
        slab.start()
        return slab

    members = []
    for dz in range(4):
        for dc in range(2):
            zz, cc = (z + dz) % 4, (c + dc) % 2
            src = dp.at[zz * 2 + cc]
            if dz == 0 and dc == 0:
                own_dp = k.local(src, dpm.at[z, c])
            else:
                members.append(k.send(src, dpm.at[z, c], p.at(z=zz, c=cc)))
    next(outward[2])
    next(plane[1])
    next(plane[3])
    k.settle(early)
    own_dp.wait()
    for copy in members:
        copy.wait_recv()
    next(small)
    for t in range(8):
        get_n[t].wait()
        total = dot_rows(na2[t % 2].reshape(8 * TOK, 256), dpm[...].reshape(8 * TOK, 256))
        dqm[t // 4, t % 4] = total.astype(BF16).reshape(2, TOK, 256)
        if t < 6:
            get_n.append(k.local(NA.at[:, :, :, pl.ds((t + 2) * 256, 256)], na2.at[t % 2]))
    inward = [staged_reduce(p, k, dqm, q_stages(i), parts[4 + i], 16) for i in range(2)]
    for step in inward:
        next(step)
    get["mix"].wait()
    next(mixing, None)

    @pl.loop(0, TOK, step=16)
    def _(t):
        at = pl.ds(pl.multiple_of(t, 16), 16)
        total = resid[at]
        for j in (3, 0, 1):
            total = total + mix1[j, at].astype(F32)
        mixed[at] = total.astype(BF16)

    keep.append(k.local(mixed, MIXED))
    next(outward[0])
    next(outward[1])
    for half in range(2):
        next(plane[half], None)
        to_owners(parts[half][-1], GWG.at[:, pl.ds(pl.multiple_of(half * FF + m * FS, 128), FS)])
    slabs = []
    for half in range(2):
        next(plane[2 + half], None)
        slabs.append(slab_home(half))
    left = jnp.concatenate([dp[i] for i in range(8)], axis=1)

    def d_normed_block(t):
        get_q[t].wait()
        w = w2[t % 2].reshape(256, 2048)
        in_grad[:, t * 256 : (t + 1) * 256] = dot_last(left, w)
        if t < 6:
            get_q.append(k.local(WQ.at[(t + 2) // 4, (t + 2) % 4], w2.at[t % 2]))

    for t in range(4):
        d_normed_block(t)
    next(small)
    for step in inward:
        next(step)
    next(outward[2])
    for t in range(4, 8):
        d_normed_block(t)
    next(small)
    for step in outward:
        next(step)
    for half, step in enumerate(inward):
        next(step, None)
        to_owners(parts[4 + half][-1], GQ.at[:, pl.ds(pl.multiple_of(m * 256 + half * 128, 128), 128)])
    get["x"].wait()
    hidden = xv[...].astype(F32)
    scale_one = rms_scale(hidden)
    in_grad[...] = dres[...] + norm_back(in_grad[...], hidden * scale_one, scale_one, gains[0:1, :])
    keep.append(k.local(in_grad, IN_GRAD))
    next(small, None)
    keep.append(k.local(vec.at[4], SMALL))
    for i, step in enumerate(outward):
        next(step, None)
        total = parts[6 + i][-1]
        dst = GO.at[c, :, pl.ds(*O_PARTS[i])]
        keep.append(k.local(total.at[pl.ds(pl.multiple_of(c * 16, 16), 16)], dst))
        last.append(k.send(total.at[pl.ds(pl.multiple_of((1 - c) * 16, 16), 16)], dst, sib))
    for copy in keep:
        copy.wait()
    for copy in last:
        copy.wait_recv()
    for slab in slabs:
        slab.wait_recv()
        slab.wait_send()
    k.drain()


def head_back(raw, grad, cos, sin, gain):
    scale = head_scale(raw)
    normed = raw * scale
    d_head = grad * cos + half_back(grad * sin)
    scaled = d_head * gain
    inner = jnp.mean(scaled * normed, axis=0, keepdims=True)
    return scale * (scaled - normed * inner), d_head * normed


def back(*args):
    w = 2 * KD
    outs = [
        sds((TOK, D), F32),
        sds((TOK, D), BF16),
        sds((16, 2 * FF), BF16),
        sds((80, 1024), BF16),
        sds((16, 2048), BF16),
        sds((2, 16, 640), BF16),
        sds((8, 128), F32),
    ]
    scratch = [
        pltpu.VMEM((TOK, D), F32),
        pltpu.VMEM((TOK, D), BF16),
        pltpu.VMEM((TOK, D), BF16),
        pltpu.VMEM((TOK, D), F32),
        pltpu.VMEM((QKV, TOK), F32),
        pltpu.VMEM((2 * KV_HEADS, 8, 256), F32),
        pltpu.VMEM((TOK, D), F32),
        pltpu.VMEM((TOK, D), BF16),
        pltpu.VMEM((2, 2, 4, 2, ROWS, w), BF16),
        pltpu.VMEM((2, SEQ, 128), F32),
        pltpu.VMEM((KV_HEADS, 2, 128, 256), BF16),
        pltpu.VMEM((KV_HEADS, 2, 256, 128), BF16),
        pltpu.VMEM((KV_HEADS, 2, 128, 256), BF16),
        pltpu.VMEM((KV_HEADS, 2, 256, 128), BF16),
        pltpu.VMEM((KV_HEADS, 2, HEAD, 256), F32),
        pltpu.VMEM((QKV, TOK), F32),
        pltpu.VMEM((TOK, QD), F32),
        pltpu.VMEM((TOK, D), F32),
        pltpu.VMEM((2, 2, 4, 2, ROWS, w), BF16),
        pltpu.VMEM((2, 2, 4, ROWS, w), BF16),
        pltpu.VMEM((3, 2, 2, ROWS, w), BF16),
        pltpu.VMEM((2, 2, ROWS, w), BF16),
        pltpu.VMEM((2, ROWS, w), BF16),
        pltpu.VMEM((TOK, w), F32),
        pltpu.VMEM((2, 2, 4, 2, 16, 2048), BF16),
        pltpu.VMEM((8, 2, 4, 2, 16, QD), BF16),
        pltpu.VMEM((2, TOK, D), BF16),
        pltpu.VMEM((2, TOK, QD), BF16),
        pltpu.VMEM((2, 4, 2, 4, 32, 640), BF16),
        pltpu.VMEM((8, TOK, 256), BF16),
        pltpu.VMEM((4, 2, TOK, 256), BF16),
        pltpu.VMEM((2, 4, 2, TOK, 256), BF16),
        pltpu.VMEM((2, 4, 2, TOK, 256), BF16),
        pltpu.VMEM((4, TOK, D), BF16),
        pltpu.VMEM((2, HEAD, TOK), F32),
        pltpu.VMEM((8, D), F32),
        pltpu.VMEM((2 * HEAD, 128), F32),
        pltpu.VMEM((TOK, D), BF16),
    ]
    for i, shapes in enumerate(PLANE_SHAPES + O_SHAPES):
        scratch += staged_scratch(shapes, i < 4)
    scratch += [
        pltpu.VMEM((5, 8, 128), F32),
        pltpu.VMEM((4, 3, 8, 128), F32),
        pltpu.SemaphoreType.DMA((108,)),
        pltpu.SemaphoreType.DMA((142,)),
        pltpu.SemaphoreType.DMA((30,)),
    ]
    return pl.pallas_call(
        back_body,
        out_shape=outs,
        in_specs=[ANY] * 18,
        out_specs=[ANY] * 7,
        scratch_shapes=scratch,
        name="back",
        compiler_params=pltpu.CompilerParams(
            collective_id=2, has_side_effects=True, vmem_limit_bytes=60 << 20
        ),
    )(*args)


def finish_body(*refs):
    IN_GRAD, MIXED, GWG, GWD, GQ, GO, SUMS, WG, WQ, g1, g2 = refs[:11]
    in_out, mixed_out, Q, O, G, DOWN, ATTN, FFN, QG, KG = refs[11:21]
    (gwg, gwd, gq, go, sums, wg, wq, q, o, g, down, attn, ffn_, qg, kg, ing, mix, sem) = refs[21:]
    used = []

    def copy(src, dst):
        out = pltpu.make_async_copy(src, dst, sem.at[len(used)])
        out.start()
        used.append(out)
        return out

    rows = [copy(IN_GRAD, ing), copy(MIXED, mix)]
    through = []
    got = [copy(a, b) for a, b in ((GQ, gq), (WQ, wq), (GO, go), (SUMS, sums), (GWD, gwd), (GWG, gwg), (WG, wg))]
    for one in got[:5]:
        one.wait()
    for one, (src, dst) in zip(rows, ((ing, in_out), (mix, mixed_out))):
        one.wait()
        through.append(copy(src, dst))
    wide = gq[...].astype(F32)
    lane = lax.broadcasted_iota(jnp.int32, (16, QKV), 1)
    total = jnp.zeros((16, QKV), F32)
    for i in range(8):
        piece = jnp.concatenate([wide[:, i * 256 : (i + 1) * 256], jnp.zeros((16, QKV - 256), F32)], axis=1)
        here = (lane >= i * 240) & (lane < (i + 1) * 240)
        total = jnp.where(here, pltpu.roll(piece, 240 * i, 1) if i else piece, total)
    q[...] = total
    through.append(copy(q, Q))
    o[...] = jnp.concatenate([go[0].astype(F32), go[1].astype(F32)], axis=1)
    through.append(copy(o, O))
    slab = gwd[...].astype(F32)
    down[...] = jnp.concatenate([slab[:40], slab[40:]], axis=1)
    through.append(copy(down, DOWN))
    attn[...] = flat(jnp.sum(wq[...].astype(F32) * total, axis=1, keepdims=True)) / g1[...].astype(F32)
    through.append(copy(attn, ATTN))
    qg[...] = sums[0:1, :HEAD]
    kg[...] = pltpu.roll(sums[...], HEAD, 1)[0:1, :HEAD]
    through += [copy(qg, QG), copy(kg, KG)]
    for one in got[5:]:
        one.wait()
    grown = gwg[...].astype(F32)
    g[...] = grown
    through.append(copy(g, G))
    ffn_[...] = flat(jnp.sum(wg[...].astype(F32) * grown, axis=1, keepdims=True)) / g2[...].astype(F32)
    through.append(copy(ffn_, FFN))
    for one in through:
        one.wait()


def flat(col):
    n = col.shape[0]
    place = lax.broadcasted_iota(jnp.int32, (n, n), 0) == lax.broadcasted_iota(jnp.int32, (n, n), 1)
    return jnp.sum(jnp.where(place, jnp.broadcast_to(col, (n, n)), 0.0), axis=0, keepdims=True)


def finish(*args):
    outs = [
        sds((TOK, D), F32),
        sds((TOK, D), BF16),
        sds((16, QKV), F32),
        sds((16, QD), F32),
        sds((16, 2 * FF), F32),
        sds((40, D), F32),
        sds((1, 16), F32),
        sds((1, 16), F32),
        sds((1, HEAD), F32),
        sds((1, HEAD), F32),
    ]
    ins = [(16, 2 * FF), (80, 1024), (16, 2048), (2, 16, 640), (8, 128), (16, 2 * FF), (16, QKV)]
    scratch = [pltpu.VMEM(a, F32 if a == (8, 128) else BF16) for a in ins]
    scratch += [pltpu.VMEM(a.shape, a.dtype) for a in outs[2:] + outs[:2]]
    return pl.pallas_call(
        finish_body,
        out_shape=outs,
        in_specs=[ANY] * 9 + [VMEM] * 2,
        out_specs=[ANY] * 10,
        scratch_shapes=scratch + [pltpu.SemaphoreType.DMA((19,))],
        name="finish",
        compiler_params=pltpu.CompilerParams(vmem_limit_bytes=60 << 20),
    )(*args)


def per_device(
    tokens,
    segment_ids,
    w_qkv,
    w_out,
    w_gate_up,
    w_down,
    attn_gain,
    ffn_gain,
    query_gain,
    key_gain,
    out_grad,
):
    g1, g2, g3, g4 = [a.reshape(1, -1) for a in (attn_gain, ffn_gain, query_gain, key_gain)]
    og_in = out_grad.reshape(TOK, D)
    x_in = tokens.reshape(TOK, D)
    (WO, WG, WD, OG, NA, KV, pt, lse, attended, resid, n2, wq_in, bias, rope, gain_rows, head_gains) = front(
        x_in, w_qkv, w_out.T, w_gate_up, w_down, og_in, segment_ids, g1, g2, g3, g4, rope_parts()
    )
    d_normed, mix_part, dwg, dwd, WQ = ffn(n2, OG, WG, WD, wq_in)
    in_grad, mixed, gwg, gwd, gq, go, sums = back(
        d_normed, x_in, og_in, resid, attended, pt, lse, WQ, WO, KV, mix_part, dwg, dwd, NA,
        bias, rope, gain_rows, head_gains,
    )
    outs = finish(in_grad, mixed, gwg, gwd, gq, go, sums, w_gate_up, w_qkv, g1, g2)
    return (
        outs[1].reshape(MICRO, ROWS, D),
        outs[0].reshape(MICRO, ROWS, D),
        outs[2],
        outs[3].T,
        outs[4],
        outs[5],
        outs[6].reshape(16),
        outs[7].reshape(16),
        outs[8].reshape(HEAD),
        outs[9].reshape(HEAD),
    )


def solution(mesh):
    return jax.shard_map(
        per_device,
        mesh=mesh,
        in_specs=(
            P(None, ("grp", "seq"), None),
            P(None, "grp"),
            P(("grp", "seq"), None),
            P(None, ("grp", "seq")),
            P(("grp", "seq"), None),
            P(("grp", "seq"), None),
            P(("grp", "seq")),
            P(("grp", "seq")),
            P(),
            P(),
            P(None, ("grp", "seq"), None),
        ),
        out_specs=(
            P(None, ("grp", "seq"), None),
            P(None, ("grp", "seq"), None),
            P(("grp", "seq"), None),
            P(None, ("grp", "seq")),
            P(("grp", "seq"), None),
            P(("grp", "seq"), None),
            P(("grp", "seq")),
            P(("grp", "seq")),
            P(),
            P(),
        ),
        check_vma=False,
    )
```

```python
import jax
import jax.numpy as jnp
import numpy as np
from jax import lax
from jax.experimental import pallas as pl
from jax.experimental.pallas import tpu as pltpu
from jax.sharding import PartitionSpec as P

Q_HEADS = 20
KV_HEADS = 5
GROUP = 4
HEAD = 64
D = 2048
FF = 5120
QD = 1280
KD = 320
QKV = 1920
SEQ = 1024
MICRO = 2
ROWS = 64
TOK = 128
FS = 640
EPS = 1e-06
MESH = pl.DeviceIdType.MESH
F32 = jnp.float32
BF16 = jnp.bfloat16
ANY = pl.BlockSpec(memory_space=pl.ANY)


class Place:
    def __init__(self):
        g = lax.axis_index("grp")
        s = lax.axis_index("seq")
        self.g, self.s = g, s
        self.yh, self.x = g // 4, g % 4
        self.yl, self.z, self.c = s // 8, (s // 2) % 4, s % 2
        self.y = self.yh * 2 + self.yl

    def at(self, x=None, y=None, z=None, c=None):
        x = self.x if x is None else x
        y = self.y if y is None else y
        z = self.z if z is None else z
        c = self.c if c is None else c
        return ((y // 2) * 4 + x, (y % 2) * 8 + z * 2 + c)

    def step(self, axis, k):
        if axis == "x":
            return self.at(x=(self.x + k) % 4)
        if axis == "y":
            return self.at(y=(self.y + k) % 4)
        if axis == "z":
            return self.at(z=(self.z + k) % 4)
        return self.at(c=1 - self.c)

    def pos(self, axis, k):
        return (getattr(self, axis) + k) % 4


class Links:
    def __init__(self, send_sems, recv_sems, local_sems):
        self.send_sems, self.recv_sems, self.local_sems = send_sems, recv_sems, local_sems
        self.received = 0
        self.free = {"send": list(range(send_sems.shape[0]))[::-1], "local": list(range(local_sems.shape[0]))[::-1]}
        self.sent = {}

    def plan(self, src, dst, to):
        i = self.received
        self.received += 1
        assert i < self.recv_sems.shape[0], i
        slot = self.free["send"].pop()
        copy = pltpu.make_async_remote_copy(
            src_ref=src,
            dst_ref=dst,
            send_sem=self.send_sems.at[slot],
            recv_sem=self.recv_sems.at[i],
            device_id=to,
            device_id_type=MESH,
        )
        self.sent[id(copy)] = (copy, slot)
        return copy

    def send(self, src, dst, to):
        copy = self.plan(src, dst, to)
        copy.start()
        return copy

    def together(self, copies, region):
        i = self.received
        self.received += 1
        slot = self.free["send"].pop()
        for src, dst, to in copies:
            pltpu.make_async_remote_copy(
                src_ref=src,
                dst_ref=dst,
                send_sem=self.send_sems.at[slot],
                recv_sem=self.recv_sems.at[i],
                device_id=to,
                device_id_type=MESH,
            ).start()
        group = Group(self.send_sems.at[slot], self.recv_sems.at[i], region)
        self.sent[id(group)] = (group, slot)
        return group

    def local(self, src, dst):
        slot = self.free["local"].pop()
        copy = pltpu.make_async_copy(src, dst, self.local_sems.at[slot])
        copy.start()
        return Local(self, copy, slot)

    def settle(self, copies):
        for copy in copies:
            copy, slot = self.sent.pop(id(copy))
            copy.wait_send()
            self.free["send"].append(slot)

    def drain(self):
        self.settle([copy for copy, _ in list(self.sent.values())])


class Group:
    def __init__(self, send_sem, recv_sem, region):
        self.send_sem, self.recv_sem, self.region = send_sem, recv_sem, region

    def wait_recv(self):
        pltpu.make_async_copy(self.region, self.region, self.recv_sem).wait()

    def wait_send(self):
        pltpu.make_async_copy(self.region, self.region, self.send_sem).wait()


class Local:
    def __init__(self, links, copy, slot):
        self.links, self.copy, self.slot = links, copy, slot

    def wait(self):
        self.copy.wait()
        self.links.free["local"].append(self.slot)


def halves(ref):
    n = ref.shape[0] // 2
    return ref.at[pl.ds(0, n)], ref.at[pl.ds(n, n)]


class RingGather:
    def __init__(self, p, k, axis, block, src=None):
        self.p, self.k, self.axis, self.block = p, k, axis, block
        dst = block(p.pos(axis, 0))
        src = dst if src is None else src
        self.right = k.send(src, dst, p.step(axis, 1))
        self.left = k.send(src, dst, p.step(axis, 3))

    def from_before(self):
        self.right.wait_recv()
        half = halves(self.block(self.p.pos(self.axis, 3)))[0]
        self.far_right = self.k.send(half, half, self.p.step(self.axis, 1))

    def from_after(self):
        self.left.wait_recv()
        half = halves(self.block(self.p.pos(self.axis, 1)))[1]
        self.far_left = self.k.send(half, half, self.p.step(self.axis, 3))

    def hand_on(self):
        self.from_before()
        self.from_after()

    def wait(self):
        self.far_right.wait_recv()
        self.far_left.wait_recv()

    def copies(self):
        return [self.right, self.left, self.far_right, self.far_left]


def greet(partners):
    barrier = pltpu.get_barrier_semaphore()
    for to in partners:
        pl.semaphore_signal(barrier, inc=1, device_id=to, device_id_type=MESH)
    pl.semaphore_wait(barrier, len(partners))


def sds(shape, dtype):
    return jax.ShapeDtypeStruct(shape, dtype)


def rms_scale(values):
    return lax.rsqrt(jnp.mean(values * values, axis=-1, keepdims=True) + EPS)


def norm_back(upstream, normed, scale, gain):
    scaled = upstream * gain
    inner = jnp.mean(scaled * normed, axis=-1, keepdims=True)
    return scale * (scaled - normed * inner)


def dot(left, right):
    return jnp.dot(left, right, preferred_element_type=F32)


def dot_last(left, right):
    return lax.dot_general(left, right, (((1,), (1,)), ((), ())), preferred_element_type=F32)


def dot_rows(left, right):
    return lax.dot_general(left, right, (((0,), (0,)), ((), ())), preferred_element_type=F32)


def slab_target(p):
    return p.at(x=(p.z + p.x) % 4, y=(p.c + p.yh) % 2 * 2 + p.yl, z=p.g // 2, c=p.g % 2)


def slab_place(p, x=None, y=None):
    m = p.z * 2 + p.c
    if x is not None:
        return (x + 4 - m % 4) % 4
    return (y // 2 + 2 - m // 4) % 2


def slab_source(p):
    m = p.z * 2 + p.c
    return p.at(x=m % 4, y=(m // 4) * 2 + p.yl, z=slab_place(p, x=p.x), c=slab_place(p, y=p.y))


def same(p, to):
    return (to[0] == p.g) & (to[1] == p.s)


def greet_plane(partners, slab_to, slab_from, own_slab):
    barrier = pltpu.get_barrier_semaphore()
    for to in partners:
        pl.semaphore_signal(barrier, inc=1, device_id=to, device_id_type=MESH)

    @pl.when(jnp.logical_not(own_slab))
    def _():
        pl.semaphore_signal(barrier, inc=1, device_id=slab_to, device_id_type=MESH)
        pl.semaphore_signal(barrier, inc=1, device_id=slab_from, device_id_type=MESH)

    def wait():
        @pl.when(jnp.logical_not(own_slab))
        def _():
            pl.semaphore_wait(barrier, len(partners) + 2)

        @pl.when(own_slab)
        def _():
            pl.semaphore_wait(barrier, len(partners))

    return wait


class Slab:
    def __init__(self, k, src, dst, to, own):
        self.own, self.src, self.dst = own, src, dst
        self.far = k.plan(src, dst, to)
        k.sent.pop(id(self.far))
        self.near = pltpu.make_async_copy(src, dst, k.recv_sems.at[k.received - 1])

    def start(self):
        @pl.when(self.own)
        def _():
            self.near.start()

        @pl.when(jnp.logical_not(self.own))
        def _():
            self.far.start()

    def wait_recv(self):
        @pl.when(self.own)
        def _():
            self.near.wait()

        @pl.when(jnp.logical_not(self.own))
        def _():
            self.far.wait_recv()

    def wait_send(self):
        @pl.when(jnp.logical_not(self.own))
        def _():
            self.far.wait_send()


def add_blocks(dst, terms, chunk):
    lead, rows = dst.shape[:-2], dst.shape[-2]
    count = 1
    for n in lead:
        count *= n

    @pl.loop(0, count)
    def _(i):
        at = []
        rest = i
        for n in reversed(lead):
            at.insert(0, rest % n)
            rest = rest // n

        @pl.loop(0, rows, step=chunk)
        def _(t):
            here = (*at, pl.ds(pl.multiple_of(t, chunk), chunk))
            total = terms[0][here].astype(F32)
            for term in terms[1:]:
                total = total + term[here].astype(F32)
            dst[here] = total.astype(dst.dtype)


def staged_reduce(p, k, src, stages, scr, chunk):
    own = scr[0]
    cur = src
    for n, (axis, pick) in enumerate(stages):
        recv = scr[1] if n == 0 else scr[2 * n]
        if n == 0:
            mine = k.local(pick(src, p.pos(axis, 0)), own)
        ring = k.together(
            [(pick(cur, p.pos(axis, j)), recv.at[j - 1], p.step(axis, j)) for j in (1, 2, 3)], recv
        )
        yield
        if n == 0:
            mine.wait()
        ring.wait_recv()
        total = own if n == 0 else scr[2 * n + 1]
        add_blocks(total, [own if n == 0 else pick(cur, p.pos(axis, 0))] + [recv.at[j] for j in range(3)], chunk)
        cur = total


def ring_reduce(p, k, src, stages, scr, chunk):
    own, recv, held, recv2, total = scr
    axis, pick = stages[0]
    before, after, far = recv.at[0], recv.at[1], recv.at[2]
    far_a, far_b = halves(pick(src, p.pos(axis, 2)))
    right_a, right_b = halves(pick(src, p.pos(axis, 1)))
    left_a, left_b = halves(pick(src, p.pos(axis, 3)))
    right, left = p.step(axis, 1), p.step(axis, 3)
    on_right = k.send(far_a, halves(far)[0], right)
    on_left = k.send(far_b, halves(far)[1], left)
    get = [k.local(right_a, halves(held)[0]), k.local(left_b, halves(held)[1])]
    mine = k.local(pick(src, p.pos(axis, 0)), own)
    yield
    near = [k.send(right_b, halves(before)[1], right), k.send(left_a, halves(after)[0], left)]
    yield
    for i, (copy, to, dst) in enumerate(((on_right, right, before), (on_left, left, after))):
        get[i].wait()
        copy.wait_recv()
        here = halves(held)[i]
        add_blocks(here, [here, halves(far)[i]], chunk)
        near.append(k.send(here, halves(dst)[i], to))
    yield
    mine.wait()
    for copy in near:
        copy.wait_recv()
    add_blocks(own, [own, before, after], chunk)
    axis, pick = stages[1]
    ring = k.together([(pick(own, p.pos(axis, j)), recv2.at[j - 1], p.step(axis, j)) for j in (1, 2, 3)], recv2)
    yield
    ring.wait_recv()
    add_blocks(total, [pick(own, p.pos(axis, 0))] + [recv2.at[j] for j in range(3)], chunk)


def mix_reduce(p, k, part, bufs, held):
    right, left = p.step("z", 1), p.step("z", 3)
    far_a, far_b = halves(part.at[p.pos("z", 2)])
    right_a, right_b = halves(part.at[p.pos("z", 1)])
    left_a, left_b = halves(part.at[p.pos("z", 3)])
    far = halves(bufs.at[2])
    first = [k.send(far_a, far[0], right), k.send(far_b, far[1], left)]
    near = [k.send(right_b, halves(bufs.at[0])[1], right), k.send(left_a, halves(bufs.at[1])[0], left)]
    get = [k.local(right_a, halves(held)[0]), k.local(left_b, halves(held)[1])]
    yield
    for i, to in enumerate((right, left)):
        get[i].wait()
        first[i].wait_recv()
        here = halves(held)[i]
        add_blocks(here, [here, far[i]], 16)
        near.append(k.send(here, halves(bufs.at[i])[i], to))
    yield
    for copy in near:
        copy.wait_recv()


def staged_scratch(shapes, held=False):
    out = [pltpu.VMEM(shapes[0], BF16), pltpu.VMEM((3, *shapes[0]), BF16)]
    if held:
        out.append(pltpu.VMEM(shapes[0], BF16))
    for n, shape in enumerate(shapes[1:]):
        out.append(pltpu.VMEM((3, *shape), BF16))
        out.append(pltpu.VMEM(shape, BF16))
    return out


EVERY = slice(None)


def wg_stages(half):
    cols = pl.ds(half * FS, FS)
    if half == 0:
        return [
            ("y", lambda r, i: r.at[i // 2, :, i % 2, :, cols]),
            ("x", lambda r, i: r.at[i]),
        ]
    return [
        ("x", lambda r, i: r.at[:, i, :, :, cols]),
        ("y", lambda r, i: r.at[i // 2, i % 2]),
    ]


def wd_stages(p, half):
    cols = pl.ds(half * 512, 512)
    if half == 0:
        return [
            ("y", lambda r, i: r.at[i % 2, :, slab_place(p, y=i), :, cols]),
            ("x", lambda r, i: r.at[slab_place(p, x=i)]),
        ]
    return [
        ("x", lambda r, i: r.at[:, slab_place(p, x=i), :, :, cols]),
        ("y", lambda r, i: r.at[i % 2, slab_place(p, y=i)]),
    ]


def q_stages(half):
    cols = pl.ds(half * 128, 128)
    if half == 0:
        return [
            ("y", lambda r, i: r.at[i // 2, :, i % 2, :, cols]),
            ("x", lambda r, i: r.at[i]),
        ]
    return [
        ("x", lambda r, i: r.at[:, i, :, :, cols]),
        ("y", lambda r, i: r.at[i // 2, i % 2]),
    ]


def o_stages(part):
    cols = pl.ds(*O_PARTS[part])
    if part == 0:
        return [
            ("x", lambda r, i: r.at[:, i, :, :, :, cols]),
            ("z", lambda r, i: r.at[:, :, i]),
            ("y", lambda r, i: r.at[i // 2, i % 2]),
        ]
    if part == 1:
        return [
            ("y", lambda r, i: r.at[i // 2, :, i % 2, :, :, cols]),
            ("x", lambda r, i: r.at[i]),
            ("z", lambda r, i: r.at[i]),
        ]
    return [
        ("z", lambda r, i: r.at[:, :, :, i, :, cols]),
        ("y", lambda r, i: r.at[i // 2, :, i % 2]),
        ("x", lambda r, i: r.at[i]),
    ]


O_PARTS = ((0, 256), (256, 128), (384, 256))
PLANE_SHAPES = [
    [(4, 128, FS), (128, FS)],
    [(2, 2, 128, FS), (128, FS)],
    [(4, 80, 512), (80, 512)],
    [(2, 2, 80, 512), (80, 512)],
    [(4, 128, 128), (128, 128)],
    [(2, 2, 128, 128), (128, 128)],
]
O_SHAPES = [
    [(2, 2, 4, 32, 256), (2, 2, 32, 256), (32, 256)],
    [(4, 4, 32, 128), (4, 32, 128), (32, 128)],
    [(2, 4, 2, 32, 256), (4, 32, 256), (32, 256)],
]


def small_reduce(p, k, vec, recv):
    for n, axis in enumerate("zyxc"):
        steps = (1,) if axis == "c" else (1, 2, 3)
        here = recv.at[n, pl.ds(0, len(steps))]
        ring = k.together([(vec.at[n], recv.at[n, j - 1], p.step(axis, j)) for j in steps], here)
        yield
        ring.wait_recv()
        total = vec[n]
        for j in range(len(steps)):
            total = total + recv[n, j]
        vec[n + 1] = total


def swap(a, b):
    left = lax.broadcasted_iota(jnp.int32, a.shape, 1) < ROWS
    return jnp.where(left, a, pltpu.roll(b, ROWS, 1)), jnp.where(left, pltpu.roll(a, ROWS, 1), b)


def head_scale(v):
    return lax.rsqrt(jnp.mean(v * v, axis=-2, keepdims=True) + EPS)


def half_turn(v):
    half = HEAD // 2
    return jnp.concatenate([-v[..., half:, :], v[..., :half, :]], axis=-2)


def half_back(v):
    half = HEAD // 2
    return jnp.concatenate([v[..., half:, :], -v[..., :half, :]], axis=-2)


def low(v):
    return v.astype(BF16).astype(F32)


def query_units(packed_t, g, cos, sin, gain):
    raw = packed_t[pl.ds(pl.multiple_of(g * 256, 256), 256)].reshape(GROUP, HEAD, TOK)
    head = raw * head_scale(raw) * gain
    turned = low(head * cos + half_turn(head) * sin) * (HEAD ** -0.5)
    a0, a1 = swap(turned[0], turned[1])
    b0, b1 = swap(turned[2], turned[3])
    none = jnp.zeros((HEAD, 256), F32)
    return [
        jnp.concatenate([jnp.concatenate([a, b], axis=1), none], axis=0) for a, b in ((a0, b0), (a1, b1))
    ]


def fill_bias(bias, seg, s):
    lane = lax.broadcasted_iota(jnp.int32, (128, 128), 1)
    query = lane % ROWS + s * ROWS
    around = pl.ds(pl.multiple_of((s // 2) * 128, 128), 128)
    for m in range(MICRO):
        ids = jnp.broadcast_to(seg[m : m + 1, around].astype(F32), (128, 128))
        turned = pltpu.roll(ids, ROWS, 1)
        ids = jnp.where((lane < ROWS) == (s % 2 == 0), ids, turned)
        ids = jnp.where(ids >= 0, ids, -2.0)

        @pl.loop(0, SEQ, step=128)
        def _(t):
            at = pl.ds(pl.multiple_of(t, 128), 128)
            key = lax.broadcasted_iota(jnp.int32, (128, 128), 0) + t
            keys = jnp.broadcast_to(seg[m : m + 1, at].astype(F32), (128, 128)).T
            ok = ((key <= query) & (keys == ids)) | (key == query)
            bias[m, at] = jnp.where(ok, 3e38, -1e30)


def rope_parts():
    inverse = 10000.0 ** (-(np.arange(HEAD) % (HEAD // 2)) / (HEAD // 2))
    begin = inverse[:, None] * (np.arange(128)[None, :] % 16 * ROWS)
    inside = inverse[:, None] * (np.arange(128)[None, :] % ROWS)
    return np.stack([np.cos(begin), np.sin(begin), np.cos(inside), np.sin(inside)]).astype(np.float32)


def rope_tables(parts, s):
    here = lax.broadcasted_iota(jnp.int32, (HEAD, 128), 1) == s
    c0 = jnp.sum(jnp.where(here, parts[0], 0.0), axis=1, keepdims=True)
    s0 = jnp.sum(jnp.where(here, parts[1], 0.0), axis=1, keepdims=True)
    return c0 * parts[2] - s0 * parts[3], s0 * parts[2] + c0 * parts[3]


def column(row):
    n = row.shape[1]
    place = lax.broadcasted_iota(jnp.int32, (n, n), 0) == lax.broadcasted_iota(jnp.int32, (n, n), 1)
    return jnp.sum(jnp.where(place, jnp.broadcast_to(row, (n, n)), 0.0), axis=1, keepdims=True)


KV_PARTS = (pl.ds(0, 384), pl.ds(384, 256))


def unit_bias(bias, m):
    half = bias[m]
    return jnp.concatenate([half, half], axis=1)


def unit_kv(KV, m, g):
    cols = pl.ds(pl.multiple_of(g * 128, 128), 128)
    return KV[m, :, :, :, :, cols].reshape(SEQ, 128)


def front_body(*refs):
    (x_in, w_qkv, wo, wg, w_down, og, seg, g1, g2, g3, g4, parts) = refs[:12]
    (WO, WG, WD, OG, NA, KV, PT, PROBS, ATT, RESID, N2, WQIN, ROPE, GAINS, QKGAIN) = refs[12:27]
    (wq, wd, ogv, gains_out, rope, qkgain) = refs[27:33]
    (xs, na, wqm, wos, pks, pk, pt, kept, att, resid, n2, kvl, kvs, bias, qts, ots) = refs[33:49]
    ssem, rsem, lsem = refs[49:]
    p = Place()
    k = Links(ssem, rsem, lsem)
    yh, x, yl, z, c = p.yh, p.x, p.yl, p.z, p.c
    m = z * 2 + c
    sib = p.step("c", 1)
    yl_partner = p.at(y=p.yh * 2 + 1 - yl)
    partners = [p.step(a, j) for a in "xyz" for j in (1, 2, 3)]
    partners += [p.at(z=(z + j) % 4, c=1 - c) for j in range(4)]
    slab_to, slab_from = slab_target(p), slab_source(p)
    own_slab = same(p, slab_to)

    met = greet_plane(partners, slab_to, slab_from, own_slab)
    own_x = k.local(x_in, xs.at[z, c])
    get_og = k.local(og, ogv)
    spare = [column(row[...].astype(F32)) for row in (g1, g2)]
    wide = w_qkv[...].astype(F32)
    lane = lax.broadcasted_iota(jnp.int32, (16, 256), 1)
    rest = jnp.where(lane == 240, spare[0], jnp.where(lane == 241, spare[1], 0.0))
    for i in range(8):
        turned = pltpu.roll(wide, (QKV - 240 * i) % QKV, 1)[:, :256]
        wq[:, i * 256 : (i + 1) * 256] = jnp.where(lane < 240, turned, rest).astype(BF16)
    met()

    def spread(src_of, dst_of):
        far, near = [], None
        for dz in range(4):
            for dc in range(2):
                zz, cc = (z + dz) % 4, (c + dc) % 2
                src, dst = src_of(zz * 2 + cc), dst_of(m)
                if dz == 0 and dc == 0:
                    near = k.local(src, dst)
                else:
                    far.append(k.send(src, dst, p.at(z=zz, c=cc)))
        return near, far

    q0 = spread(
        lambda i: wq.at[:, pl.ds(pl.multiple_of(i * 256, 256), 256)], lambda i: wqm.at[yh, x, yl, i]
    )
    xcore = {0: k.send(x_in, xs.at[z, c], sib)}
    own_wo = k.local(wo, wos.at[yh, x, yl, z, c])

    def wo_at(part, *at):
        return wos.at[(*at, EVERY, pl.ds(part * 640, 640))]

    o1 = [k.send(wo, wos.at[yh, x, yl, z, c], p.step("z", j)) for j in (1, 2, 3)]
    g0 = [
        spread(
            lambda i: wg.at[:, pl.ds(pl.multiple_of(half * FF + i * FS, 128), FS)],
            lambda i: WG.at[yh, x, yl, i, :, pl.ds(half * FS, FS)],
        )
        for half in range(2)
    ]
    xring = RingGather(p, k, "z", lambda i: xs.at[i, c], x_in)

    def to_plane(blocks):
        return [k.send(b, b, p.step(axis, j)) for j in (1, 2, 3) for b, axis in blocks]

    ql, qh = pl.ds(0, 128), pl.ds(128, 128)
    lo, hi = pl.ds(0, FS), pl.ds(FS, FS)
    dlo, dhi = pl.ds(0, 384), pl.ds(384, 640)
    q0[0].wait()
    for copy in q0[1]:
        copy.wait_recv()
    q1 = to_plane(((wqm.at[yh, x, yl, :, :, ql], "x"), (wqm.at[yh, x, yl, :, :, qh], "y")))
    fill_bias(bias, seg, p.s)
    cos, sin = rope_tables(parts, p.s)
    rope[0], rope[1] = cos, sin
    qgain, kgain = column(g3[...].astype(F32)), column(g4[...].astype(F32))
    qkgain[...] = jnp.concatenate([jnp.broadcast_to(qgain, (HEAD, 128)), jnp.broadcast_to(kgain, (HEAD, 128))], axis=0)
    for copy in q1:
        copy.wait_recv()
    q2 = to_plane(((wqm.at[yh, :, yl, :, :, ql], "y"), (wqm.at[:, x, :, :, :, qh], "x")))
    for near, far in g0:
        near.wait()
        for copy in far:
            copy.wait_recv()
    plane = to_plane(((WG.at[yh, x, yl, :, :, lo], "x"), (WG.at[yh, x, yl, :, :, hi], "y")))
    slab_rows = w_down[...].astype(F32)
    wd[...] = jnp.concatenate([slab_rows[:, :1024], slab_rows[:, 1024:]], axis=0).astype(BF16)
    slab = Slab(k, wd, WD.at[yl, z, c], slab_to, own_slab)
    slab.start()
    xring.hand_on()
    for o in (1, 3):
        src = xs.at[(z + o) % 4, c]
        xcore[o] = k.send(src, src, sib)
    for copy in q2:
        copy.wait_recv()
    own_x.wait()
    own_wo.wait()
    pick = jnp.where(
        lax.broadcasted_iota(jnp.int32, (8, 128), 0) + 112 == lax.broadcasted_iota(jnp.int32, (8, 128), 1), 1.0, 0.0
    ).astype(BF16)
    gains_out[...] = dot_last(pick, wqm[:, :, :, :, :, pl.ds(128, 128)].reshape(D, 128))
    keep = [k.local(wq, WQIN), k.local(rope, ROPE), k.local(gains_out, GAINS), k.local(qkgain, QKGAIN)]
    k.settle(q0[1] + q1)
    packs = []
    for o in (0, 1, 3, 2):
        zz = (z + o) % 4
        if o == 2:
            xring.wait()
            xcore[o] = k.send(xs.at[zz, c], xs.at[zz, c], sib)
        xcore[o].wait_recv()
        rows = xs[zz].reshape(256, D).astype(F32)
        normed = (rows * rms_scale(rows) * gains_out[0:1, :]).astype(BF16)
        na[zz] = normed.reshape(2, TOK, D)
        pks[zz] = dot(normed, wqm[...].reshape(D, 256)).astype(BF16).reshape(2, TOK, 256)
        if o:
            packs.append(k.send(pks.at[zz, c], pk.at[m], p.at(z=zz)))
        else:
            own_pk = k.local(pks.at[z, c], pk.at[m])
        packs.append(k.send(pks.at[zz, 1 - c], pk.at[m], p.at(z=zz, c=1 - c)))
        if o == 1:
            for copy in o1:
                copy.wait_recv()
            o2 = to_plane(
                (
                    (wo_at(0, yh, x, yl, EVERY, c), "y"),
                    (wo_at(1, yh, x, yl, EVERY, c), "x"),
                ),
            )
        if o == 3:
            for copy in plane:
                copy.wait_recv()
            plane2 = [
                RingGather(p, k, "x", lambda i: WG.at[:, i, :, :, :, hi]),
                RingGather(p, k, "y", lambda i: WG.at[i // 2, :, i % 2, pl.ds(0, 4), :, lo]),
            ]
    slab.wait_recv()
    held = WD.at[yl, slab_place(p, x=x), slab_place(p, y=p.y)]
    plane_d = to_plane(((held.at[:, dlo], "x"), (held.at[:, dhi], "y")))
    for copy in o2:
        copy.wait_recv()
    o3 = [RingGather(p, k, "x", lambda i: wo_at(0, EVERY, i, EVERY, EVERY, c))]
    keep.append(k.local(na, NA))
    k.settle(q2 + o1 + [copy for _, far in g0 for copy in far])
    own_pk.wait()
    for copy in packs:
        copy.wait_recv()
    for i8 in range(8):
        pt[i8 * 240 : (i8 + 1) * 240] = pk[i8].astype(F32).T[:240]

    @pl.loop(0, KV_HEADS)
    def _(g):
        raw = pt[pl.ds(pl.multiple_of(QD + g * HEAD, HEAD), HEAD)]
        head = raw * head_scale(raw) * kgain
        key = head * cos + half_turn(head) * sin
        value = pt[pl.ds(pl.multiple_of(QD + KD + g * HEAD, HEAD), HEAD)]
        both = jnp.concatenate([key, value], axis=0).T.astype(BF16)
        cols = pl.ds(pl.multiple_of(g * 128, 128), 128)
        for mm in range(MICRO):
            kvl[mm, :, cols] = both[mm * ROWS : (mm + 1) * ROWS]

    own_kv = k.local(kvl, kvs.at[:, yl, z, c])
    across, ring = [], []
    for cols in KV_PARTS:
        across.append(k.send(kvl.at[:, :, cols], kvs.at[:, yl, z, c, :, cols], yl_partner))
        ring.append([k.send(kvl.at[:, :, cols], kvs.at[:, yl, z, c, :, cols], p.step("z", j)) for j in (1, 2, 3)])
    keep.append(k.local(pt, PT))

    @pl.loop(0, KV_HEADS)
    def _(g):
        for mm, unit in enumerate(query_units(pt, g, cos, sin, qgain)):
            qts[g, mm] = unit.astype(BF16)

    for copy, group, cols in zip(across, ring, KV_PARTS):
        copy.wait_recv()
        src = kvs.at[:, 1 - yl, z, c, :, cols]
        group += [k.send(src, src, p.step("z", j)) for j in (1, 2, 3)]
    get_og.wait()
    keep.append(k.local(ogv, OG.at[z, c]))
    rows = RingGather(p, k, "z", lambda i: OG.at[i, c], ogv)
    last = [k.send(ogv, OG.at[z, c], sib)]
    own_kv.wait()
    o3.append(RingGather(p, k, "y", lambda i: wo_at(1, i // 2, EVERY, i % 2, EVERY, c)))
    for ring4 in plane2:
        ring4.hand_on()
    oc = []
    for src in (
        wo_at(0, EVERY, x, EVERY, EVERY, c),
        wo_at(1, yh, EVERY, yl, EVERY, c),
    ):
        oc.append(k.send(src, src, sib))
    for copy in ring[0]:
        copy.wait_recv()
    src = kvs.at[:, :, :, c, :, KV_PARTS[0]]
    kvc = [k.send(src, src, sib)]
    o3[0].hand_on()
    o3[1].hand_on()
    for copy in plane_d:
        copy.wait_recv()
    plane2.append(RingGather(p, k, "x", lambda i: WD.at[:, slab_place(p, x=i), :, :, dhi]))
    plane2 += [
        RingGather(p, k, "y", lambda i: WD.at[i % 2, :, slab_place(p, y=i), :, dlo]),
        RingGather(p, k, "y", lambda i: WG.at[i // 2, :, i % 2, pl.ds(4, 4), :, lo]),
    ]
    for axis, ring4 in zip("xy", o3):
        for j in (1, 3):
            src = ring4.block(p.pos(axis, j))
            oc.append(k.send(src, src, sib))
    kvc[0].wait_recv()

    def unit(u):
        g, mm = u // 2, u % 2
        kv = unit_kv(kvs, mm, g)
        score = jnp.minimum(dot(kv, qts[g, mm]), unit_bias(bias, mm))
        peak = jnp.max(score, axis=0, keepdims=True)
        raised = jnp.exp(score - peak)
        total = jnp.sum(raised, axis=0, keepdims=True)
        probs = (raised * (1.0 / total)).astype(BF16)
        ots[g, mm] = dot_rows(kv, probs)[HEAD:]
        kept[u] = probs

    k.settle(packs + plane + plane_d)
    pl.loop(0, 6)(unit)
    for copy in ring[1]:
        copy.wait_recv()
    src = kvs.at[:, :, :, c, :, KV_PARTS[1]]
    kvc.append(k.send(src, src, sib))
    k.settle(o2 + xring.copies() + list(xcore.values()))
    kvc[1].wait_recv()
    keep.append(k.local(kvs, KV))
    for axis, ring4 in zip("xy", o3):
        ring4.wait()
        src = ring4.block(p.pos(axis, 2))
        oc.append(k.send(src, src, sib))
    pl.loop(6, 2 * KV_HEADS)(unit)
    for g in range(KV_HEADS):
        for t in range(2):
            cols = slice(t * 128, (t + 1) * 128)
            a, b = swap(ots[g, 0, :, cols], ots[g, 1, :, cols])
            at = (g * GROUP + 2 * t) * HEAD
            att[:, at : at + 128] = jnp.concatenate([a, b], axis=0).T.astype(BF16)
    keep += [k.local(kept, PROBS), k.local(att, ATT)]
    rows.hand_on()
    for j in (1, 3):
        src = OG.at[p.pos("z", j), c]
        last.append(k.send(src, src, sib))
    for copy in oc:
        copy.wait_recv()
    keep.append(k.local(wos, WO))

    @pl.loop(0, 8)
    def _(t):
        w = wos[t // 4, t % 4].reshape(256, QD)
        cols = pl.ds(pl.multiple_of(t * 256, 256), 256)
        resid[:, cols] = xs[z, c, :, cols].astype(F32) + dot_last(att[...], w)

    plane2[2].hand_on()
    plane2[3].hand_on()
    plane2[4].hand_on()
    value = resid[...]
    n2[...] = (value * rms_scale(value) * gains_out[1:2, :]).astype(BF16)
    keep += [k.local(resid, RESID), k.local(n2, N2)]
    rows.wait()
    src = OG.at[p.pos("z", 2), c]
    last.append(k.send(src, src, sib))
    for ring4 in plane2:
        ring4.wait()
    for copy in last:
        copy.wait_recv()
    for copy in keep:
        copy.wait()
    slab.wait_send()
    k.drain()


VMEM = pl.BlockSpec(memory_space=pltpu.VMEM)


def front(*args):
    hbm = [
        sds((2, 4, 2, 4, 2, 16, QD), BF16),
        sds((2, 4, 2, 8, 16, 2 * FS), BF16),
        sds((2, 4, 2, 80, 1024), BF16),
        sds((4, 2, TOK, D), BF16),
        sds((4, 2, TOK, D), BF16),
        sds((2, 2, 4, 2, ROWS, 2 * KD), BF16),
        sds((QKV, TOK), F32),
        sds((2 * KV_HEADS, SEQ, 256), BF16),
        sds((TOK, QD), BF16),
        sds((TOK, D), F32),
        sds((TOK, D), BF16),
        sds((16, 2048), BF16),
        sds((2, HEAD, TOK), F32),
        sds((8, D), F32),
        sds((2 * HEAD, 128), F32),
    ]
    scratch = [
        pltpu.VMEM((16, 2048), BF16),
        pltpu.VMEM((80, 1024), BF16),
        pltpu.VMEM((TOK, D), BF16),
        pltpu.VMEM((8, D), F32),
        pltpu.VMEM((2, HEAD, TOK), F32),
        pltpu.VMEM((2 * HEAD, 128), F32),
        pltpu.VMEM((4, 2, TOK, D), BF16),
        pltpu.VMEM((4, 2, TOK, D), BF16),
        pltpu.VMEM((2, 4, 2, 8, 16, 256), BF16),
        pltpu.VMEM((2, 4, 2, 4, 2, 16, QD), BF16),
        pltpu.VMEM((4, 2, TOK, 256), BF16),
        pltpu.VMEM((8, TOK, 256), BF16),
        pltpu.VMEM((QKV, TOK), F32),
        pltpu.VMEM((2 * KV_HEADS, SEQ, 256), BF16),
        pltpu.VMEM((TOK, QD), BF16),
        pltpu.VMEM((TOK, D), F32),
        pltpu.VMEM((TOK, D), BF16),
        pltpu.VMEM((2, ROWS, 2 * KD), BF16),
        pltpu.VMEM((2, 2, 4, 2, ROWS, 2 * KD), BF16),
        pltpu.VMEM((2, SEQ, 128), F32),
        pltpu.VMEM((KV_HEADS, 2, 128, 256), BF16),
        pltpu.VMEM((KV_HEADS, 2, HEAD, 256), F32),
        pltpu.SemaphoreType.DMA((80,)),
        pltpu.SemaphoreType.DMA((130,)),
        pltpu.SemaphoreType.DMA((14,)),
    ]
    return pl.pallas_call(
        front_body,
        out_shape=hbm,
        in_specs=[ANY, VMEM, VMEM, ANY, VMEM, ANY] + [VMEM] * 6,
        out_specs=[ANY] * len(hbm),
        scratch_shapes=scratch,
        name="front",
        compiler_params=pltpu.CompilerParams(
            collective_id=0, has_side_effects=True, vmem_limit_bytes=56 << 20
        ),
    )(*args)


def ffn_body(n2, OG, WG, WD, wq, d_out, mix_out, dwg_out, dwd_out, WQ, *scr):
    (rows, ogs, wgs, wd80, wds, dgu, inn, din, part, mixs, r0, s0, r1, m0, dwg, dwd32, dwd) = scr[:17]
    (dn, wqv, ssem, rsem, lsem, wsem, vsem, wlsem) = scr[17:]
    p = Place()
    k = Links(wsem, vsem, wlsem)
    yh, x, yl, z, c = p.yh, p.x, p.yl, p.z, p.c
    sib = p.step("c", 1)
    greet([p.step(a, j) for a in "xyz" for j in (1, 2, 3)] + [sib])

    def remote(src, dst, i, to):
        return pltpu.make_async_remote_copy(
            src_ref=src,
            dst_ref=dst,
            send_sem=ssem.at[i],
            recv_sem=rsem.at[i],
            device_id=to,
            device_id_type=MESH,
        )

    def local(src, dst, i):
        copy = pltpu.make_async_copy(src, dst, lsem.at[i])
        copy.start()
        return copy

    def half_of(half, *at):
        return WQ.at[(*at, EVERY, pl.ds(half * 1024, 1024))]

    whole = (EVERY, EVERY, EVERY, EVERY, c)
    get_wq = k.local(wq, wqv)
    q1 = [k.plan(wq, WQ.at[yh, x, yl, z, c], p.step("z", j)) for j in (1, 2, 3)]
    q2, q3 = [], []
    for j in (1, 2, 3):
        for half, axis in ((0, "y"), (1, "x")):
            src = half_of(half, yh, x, yl, EVERY, c)
            q2.append(k.plan(src, src, p.step(axis, j)))
    for j in (1, 2, 3):
        src = half_of(0, EVERY, x, EVERY, EVERY, c)
        q3.append(k.plan(src, src, p.step("x", j)))
        src = half_of(1, yh, EVERY, yl, EVERY, c)
        q3.append(k.plan(src, src, p.step("y", j)))
    q4 = k.plan(WQ.at[whole], WQ.at[whole], sib)

    sent = []
    for copy in q1:
        copy.start()
    for j in (1, 3):
        copy = remote(n2, rows.at[z, c], j, p.step("z", j))
        copy.start()
        sent.append(copy)
    half = halves(rows.at[p.pos("z", 1), c])[1], halves(rows.at[p.pos("z", 3), c])[0]
    on_left = remote(half[0], half[0], 0, p.step("z", 3))
    on_right = remote(half[1], half[1], 2, p.step("z", 1))
    sent += [on_left, on_right]
    remote(n2, rows.at[z, c], 4, sib).start()
    own = local(n2, rows.at[z, c], 0)
    get_wd = local(WD, wd80, 1)
    get_wg = local(WG, wgs, 2)
    get_og = local(OG, ogs, 3)
    get_wd.wait()

    @pl.loop(0, 8)
    def _(i):
        yl, x = i // 4, i % 4
        a, b = wd80[yl, x, 0].astype(F32), wd80[yl, x, 1].astype(F32)
        at = pl.ds(pl.multiple_of(i * 80, 80), 80)
        wds[at, :1024] = jnp.concatenate([a[:40], b[:40]], axis=0).astype(BF16)
        wds[at, 1024:] = jnp.concatenate([a[40:], b[40:]], axis=0).astype(BF16)

    own.wait()
    get_wg.wait()
    get_og.wait()
    get_wq.wait()
    own_wq = k.local(wqv, WQ.at[yh, x, yl, z, c])

    def ring_step(j):
        return jnp.where(j == 2, 3, jnp.where(j == 3, 2, j))

    def d_inner_of(zz):
        din[...] = dot_last(ogs[zz].reshape(256, D), wds[...])

    d_inner_of(z)
    own_wq.wait()
    for copy in q1:
        copy.wait_recv()
    for copy in q2:
        copy.start()

    top, end = pl.ds(0, D // 2), pl.ds(D // 2, D // 2)
    right, left = p.step("z", 1), p.step("z", 3)
    to_right, to_left, to_far = s0.at[p.pos("z", 1)], s0.at[p.pos("z", 3)], s0.at[p.pos("z", 2)]
    near_right = remote(to_right.at[end], r1.at[0, end], 12, right)
    near_left = remote(to_left.at[top], r1.at[1, top], 13, left)
    far_right = remote(to_far.at[top], r1.at[2, top], 14, right)
    far_left = remote(to_far.at[end], r1.at[2, end], 15, left)
    sum_right = remote(to_right.at[top], r1.at[0, top], 17, right)
    sum_left = remote(to_left.at[end], r1.at[1, end], 18, left)
    ring_sums = [near_right, near_left, far_right, far_left, sum_right, sum_left]

    @pl.loop(0, 4)
    def _(j):
        o = ring_step(j)
        zz = (z + o) % 4
        at = pl.ds(pl.multiple_of(zz * 256, 256), 256)

        @pl.when(j == 1)
        def _():
            remote(n2, rows.at[z, c], 3, sib).wait_recv()
            on_left.start()
            remote(n2, rows.at[z, c], 1, sib).wait_recv()
            on_right.start()
            for o_near in (1, 3):
                near = rows.at[(z + o_near) % 4, c]
                remote(near, near, 4 + o_near, sib).start()

        @pl.when(j == 2)
        def _():
            on_left.wait_recv()
            on_right.wait_recv()
            far = rows.at[(z + 2) % 4, c]
            remote(far, far, 4 + 2, sib).start()

        remote(rows.at[zz, c], rows.at[zz, 1 - c], 4 + o, sib).wait_recv()
        r = rows[zz].reshape(256, D)
        for t in range(5):
            lo, hi = slice(t * 128, (t + 1) * 128), slice(FS + t * 128, FS + (t + 1) * 128)
            w = jnp.concatenate(
                [wgs[:, :, :, :, :, lo].reshape(D, 128), wgs[:, :, :, :, :, hi].reshape(D, 128)], axis=1
            )
            both = dot(r, w)
            gate, upper = both[:, :128], both[:, 128:]
            sig = jax.nn.sigmoid(gate)
            active = gate * sig
            d_inner = din[:, lo]
            inn[at, lo] = (active * upper).astype(BF16)
            dgu[at, lo] = (d_inner * upper * sig * (1.0 + gate * (1.0 - sig))).astype(BF16)
            dgu[at, hi] = (d_inner * active).astype(BF16)

        for h in range(2):
            turned = dot_last(wgs[h].reshape(1024, 2 * FS), dgu[at]).astype(BF16)
            for cc in range(2):
                part[zz, cc, h * 1024 : (h + 1) * 1024] = turned[:, cc * TOK : (cc + 1) * TOK]

        remote(part.at[zz, 1 - c], r0.at[zz], 8 + o, sib).start()
        d_inner_of((z + ring_step((j + 1) % 4)) % 4)
        remote(part.at[zz, 1 - c], r0.at[zz], 8 + o, sib).wait_recv()

        @pl.loop(0, D, step=128)
        def _(t):
            here = pl.ds(pl.multiple_of(t, 128), 128)
            s0[zz, here] = (part[zz, c, here].astype(F32) + r0[zz, here].astype(F32)).astype(BF16)

        @pl.when(j == 1)
        def _():
            near_right.start()

        @pl.when(j == 2)
        def _():
            near_left.start()

        @pl.when(j == 3)
        def _():
            far_right.start()
            far_left.start()

        @pl.when(j == 0)
        def _():
            for t in range(8):
                left = rows[z, :, :, t * 256 : (t + 1) * 256].reshape(256, D // 8)
                dwg[t // 4, t % 4] = dot_rows(left, dgu[at]).astype(BF16).reshape(2, TOK, 2 * FS)
            for copy in q2:
                copy.wait_recv()
            for copy in q3:
                copy.start()

    @pl.loop(0, 4)
    def _(t):
        cols = pl.ds(pl.multiple_of(t * 512, 512), 512)
        mixs[:, :, :, cols] = dot(inn[...], wds[:, cols]).astype(BF16).reshape(4, 2, TOK, 512)

    mix_core = remote(mixs.at[:, 1 - c], m0, 16, sib)
    mix_core.start()
    others = [((z + o) % 4, pl.ds(pl.multiple_of((z + o) % 4 * 256, 256), 256)) for o in (1, 2, 3)]

    def gate_up_block(t):
        cols = pl.ds(pl.multiple_of(t * 256, 256), 256)
        total = dwg[t // 4, t % 4].reshape(256, 2 * FS).astype(F32)
        for zz, at in others:
            total = total + dot_rows(rows[zz, :, :, cols].reshape(256, 256), dgu[at])
        dwg[t // 4, t % 4] = total.astype(BF16).reshape(2, TOK, 2 * FS)

    pl.loop(0, 4)(gate_up_block)
    for first, over, add, at in ((far_right, sum_right, to_right, 0), (far_left, sum_left, to_left, D // 2)):
        first.wait_recv()

        @pl.loop(0, D // 2, step=128)
        def _(t, add=add, at=at):
            here = pl.ds(pl.multiple_of(t + at, 128), 128)
            add[here] = (add[here].astype(F32) + r1[2, here].astype(F32)).astype(BF16)

        over.start()
    pl.loop(4, 8)(gate_up_block)
    out_wg = local(dwg, dwg_out, 5)
    for copy in q3:
        copy.wait_recv()
    q4.start()

    @pl.loop(0, 5)
    def _(t):
        units = pl.ds(pl.multiple_of(t * 128, 128), 128)
        dwd32[units] = dot_rows(inn[:, units], ogs[...].reshape(8 * TOK, D))

    @pl.loop(0, 8)
    def _(i):
        yl, x = i // 4, i % 4
        at = pl.ds(pl.multiple_of(i * 80, 80), 80)
        lo, hi = dwd32[at, :1024], dwd32[at, 1024:]
        dwd[yl, x, 0] = jnp.concatenate([lo[:40], hi[:40]], axis=0).astype(BF16)
        dwd[yl, x, 1] = jnp.concatenate([lo[40:], hi[40:]], axis=0).astype(BF16)

    out_wd = local(dwd, dwd_out, 6)
    mix_core.wait_recv()

    @pl.loop(0, 4)
    def _(zz):
        @pl.loop(0, TOK, step=16)
        def _(t):
            here = pl.ds(pl.multiple_of(t, 16), 16)
            m0[zz, here] = (mixs[zz, c, here].astype(F32) + m0[zz, here].astype(F32)).astype(BF16)

    out_mix = local(m0, mix_out, 4)
    for copy in (near_right, near_left, sum_right, sum_left):
        copy.wait_recv()
    for t in range(0, D, 128):
        here = slice(t, t + 128)
        total = s0[z, here].astype(F32)
        for j in range(2):
            total = total + r1[j, here].astype(F32)
        dn[:, here] = total.T

    out_dn = local(dn, d_out, 7)
    q4.wait_recv()
    k.drain()
    for copy in sent:
        copy.wait_send()
    for o in range(4):
        remote(rows.at[0, 0], rows.at[0, 0], 4 + o, sib).wait_send()
        remote(part.at[0, 0], r0.at[0], 8 + o, sib).wait_send()
    for copy in ring_sums:
        copy.wait_send()
    mix_core.wait_send()
    for copy in (out_mix, out_wg, out_wd, out_dn):
        copy.wait()


def ffn(n2, OG, WG, WD, wq):
    outs = [
        sds((TOK, D), F32),
        sds((4, TOK, D), BF16),
        sds((2, 4, 2, TOK, 2 * FS), BF16),
        sds((2, 4, 2, 80, 1024), BF16),
        sds((2, 4, 2, 4, 2, 16, 2048), BF16),
    ]
    scratch = [
        pltpu.VMEM((4, 2, TOK, D), BF16),
        pltpu.VMEM((4, 2, TOK, D), BF16),
        pltpu.VMEM((2, 4, 2, 8, 16, 2 * FS), BF16),
        pltpu.VMEM((2, 4, 2, 80, 1024), BF16),
        pltpu.VMEM((FS, D), BF16),
        pltpu.VMEM((8 * TOK, 2 * FS), BF16),
        pltpu.VMEM((8 * TOK, FS), BF16),
        pltpu.VMEM((256, FS), F32),
        pltpu.VMEM((4, 2, D, TOK), BF16),
        pltpu.VMEM((4, 2, TOK, D), BF16),
        pltpu.VMEM((4, D, TOK), BF16),
        pltpu.VMEM((4, D, TOK), BF16),
        pltpu.VMEM((3, D, TOK), BF16),
        pltpu.VMEM((4, TOK, D), BF16),
        pltpu.VMEM((2, 4, 2, TOK, 2 * FS), BF16),
        pltpu.VMEM((FS, D), F32),
        pltpu.VMEM((2, 4, 2, 80, 1024), BF16),
        pltpu.VMEM((TOK, D), F32),
        pltpu.VMEM((16, 2048), BF16),
        pltpu.SemaphoreType.DMA((19,)),
        pltpu.SemaphoreType.DMA((19,)),
        pltpu.SemaphoreType.DMA((8,)),
        pltpu.SemaphoreType.DMA((16,)),
        pltpu.SemaphoreType.DMA((16,)),
        pltpu.SemaphoreType.DMA((1,)),
    ]
    return pl.pallas_call(
        ffn_body,
        out_shape=outs,
        in_specs=[ANY] * 5,
        out_specs=[ANY] * 5,
        scratch_shapes=scratch,
        name="ffn",
        compiler_params=pltpu.CompilerParams(
            collective_id=1, has_side_effects=True, vmem_limit_bytes=60 << 20
        ),
    )(n2, OG, WG, WD, wq)


def back_body(*refs):
    (DN, X_IN, OG_IN, RESID, ATT, PT, PROBS, WQ, WO, KV, mix_part, dwg, dwd, NA) = refs[:14]
    (ROPE, GAINS, QKGAIN) = refs[14:17]
    (IN_GRAD, MIXED, GWG, GWD, GQ, GO, SMALL) = refs[17:24]
    (dn, xv, ogv, resid, pt, kept, in_grad, mixed, kvs, qns, dts, dns, dqt, dpt, datt, dres) = refs[24:40]
    (kpart, k0, k1, ks1, k2, kres, w2, wo2, low2, att2, do, dp, dpm, na2, dqm, mix1) = refs[40:56]
    (rope, gains, qkgain, mix_held) = refs[56:60]
    scr = list(refs[60:])
    parts = []
    for i, shapes in enumerate(PLANE_SHAPES + O_SHAPES):
        n = 2 * len(shapes) + (i < 4)
        parts.append(scr[:n])
        scr = scr[n:]
    vec, vrecv, ssem, rsem, lsem = scr
    p = Place()
    k = Links(ssem, rsem, lsem)
    yl, z, c = p.yl, p.z, p.c
    m = z * 2 + c
    sib = p.step("c", 1)
    yl_partner = p.at(y=p.yh * 2 + 1 - yl)
    partners = [p.step(a, j) for a in "xyz" for j in (1, 2, 3)]
    partners += [p.at(z=(z + j) % 4, c=1 - c) for j in range(4)]
    slab_to, slab_from = slab_target(p), slab_source(p)
    own_slab = same(p, slab_to)
    met = greet_plane(partners, slab_to, slab_from, own_slab)
    get = {}

    def fetch(**pairs):
        for name, (src, dst) in pairs.items():
            get[name] = k.local(src, dst)

    fetch(dn=(DN, dn), og=(OG_IN, ogv), resid=(RESID, resid), gains=(GAINS, gains))
    get_w = [k.local(WO.at[t // 4, t % 4], wo2.at[t]) for t in range(8)]
    fetch(pt=(PT, pt), rope=(ROPE, rope), qkgain=(QKGAIN, qkgain), att=(ATT, att2.at[0]))
    met()
    plane = [
        ring_reduce(p, k, dwg, wg_stages(0), parts[0], 16),
        ring_reduce(p, k, dwg, wg_stages(1), parts[1], 16),
        ring_reduce(p, k, dwd, wd_stages(p, 0), parts[2], 16),
        ring_reduce(p, k, dwd, wd_stages(p, 1), parts[3], 16),
    ]
    for step in plane + plane:
        next(step)
    pair_att = k.send(ATT, att2.at[1], sib)

    mixing = mix_reduce(p, k, mix_part, mix1, mix_held)
    next(mixing)
    for name in ("dn", "og", "resid", "gains"):
        get[name].wait()
    value = resid[...]
    scale_two = rms_scale(value)
    norm_two = value * scale_two
    d_resid = ogv[...].astype(F32) + norm_back(dn[...], norm_two, scale_two, gains[1:2, :])
    dres[...] = d_resid
    low2[0] = d_resid.astype(BF16)
    pair_low = k.send(low2.at[0], low2.at[1], sib)
    fetch(kv=(KV, kvs), kept=(PROBS, kept))
    for name in ("pt", "rope", "qkgain"):
        get[name].wait()
    cos, sin = rope[0], rope[1]
    qgain, kgain = qkgain[:HEAD], qkgain[HEAD:]

    @pl.loop(0, KV_HEADS)
    def _(g):
        for mm, unit in enumerate(query_units(pt, g, cos, sin, qgain)):
            qns[g, mm] = unit.T.astype(BF16)

    for t in range(8):
        get_w[t].wait()
        term = dot(low2[0, :, t * 256 : (t + 1) * 256], wo2[t].reshape(256, QD))
        datt[...] = term if t == 0 else datt[...] + term
    for g in range(KV_HEADS):
        tiles = []
        for t in range(2):
            at = (g * GROUP + 2 * t) * HEAD
            both = low(datt[:, at : at + 128]).T
            tiles.append(swap(both[:HEAD], both[HEAD:]))
        for mm in range(MICRO):
            none = jnp.zeros((HEAD, 256), F32)
            unit = jnp.concatenate([none, jnp.concatenate([tiles[0][mm], tiles[1][mm]], axis=1)], axis=0)
            dts[g, mm] = unit.astype(BF16)
            dns[g, mm] = unit.T.astype(BF16)
    fetch(x=(X_IN, xv), mix=(mix_part.at[z], mix1.at[3]))
    get["kv"].wait()
    get["kept"].wait()

    def unit(u):
        g, mm = u // 2, u % 2
        kv = unit_kv(kvs, mm, g)
        low_again = kept[u]
        again = low_again.astype(F32)
        d_probs = dot(kv, dts[g, mm])
        inner = jnp.sum(again * d_probs, axis=0, keepdims=True)
        d_scores = (again * (d_probs - inner)).astype(BF16)
        d_kv = dot(d_scores, qns[g, mm]) + dot(low_again, dns[g, mm])
        cols = pl.ds(pl.multiple_of(g * 128, 128), 128)
        kpart[mm, :, :, :, :, cols] = d_kv.astype(BF16).reshape(2, 4, 2, ROWS, 128)
        dqt[g, mm] = dot_rows(kv, d_scores)[:HEAD] * (HEAD ** -0.5)

    def core_send(cols):
        return k.send(kpart.at[:, :, :, 1 - c, :, cols], k0.at[:, :, :, :, cols], sib)

    def ring_send(core, cols):
        core.wait_recv()

        @pl.loop(0, 4)
        def _(zz):
            for a in range(2):
                for b in range(2):
                    here = (a, b, zz, EVERY, cols)
                    both = kpart[a, b, zz, c, :, cols].astype(F32) + k0[here].astype(F32)
                    k0[here] = both.astype(BF16)

        return [
            k.send(k0.at[:, :, p.pos("z", j), :, cols], k1.at[j - 1, :, :, :, cols], p.step("z", j))
            for j in (1, 2, 3)
        ]

    pl.loop(0, 6)(unit)
    core = core_send(KV_PARTS[0])
    ring = ring_send(core, KV_PARTS[0])
    pl.loop(6, 2 * KV_HEADS)(unit)
    core = core_send(KV_PARTS[1])
    for step in plane:
        next(step)
    early = [copy for copy, _ in k.sent.values()]
    ring += ring_send(core, KV_PARTS[1])
    next(mixing)
    get["att"].wait()
    pair_att.wait_recv()
    pair_low.wait_recv()
    att_cols = pl.ds(pl.multiple_of(c * 640, 128), 640)

    @pl.loop(0, 8)
    def _(t):
        cols = pl.ds(pl.multiple_of(t * 256, 256), 256)
        left = low2[:, :, cols].reshape(2 * TOK, 256)
        right = att2[:, :, att_cols].reshape(2 * TOK, 640)
        do[t // 4, t % 4] = dot_rows(left, right).astype(BF16).reshape(2, 4, 32, 640)

    outward = [staged_reduce(p, k, do, o_stages(i), parts[6 + i], 16) for i in range(3)]
    next(outward[0])

    query_sum = jnp.zeros((HEAD, TOK), F32)
    for g in range(KV_HEADS):
        heads = []
        for t in range(2):
            cols = slice(t * 128, (t + 1) * 128)
            heads += list(swap(dqt[g, 0, :, cols], dqt[g, 1, :, cols]))
        for h in range(GROUP):
            at = (g * GROUP + h) * HEAD
            d_raw, term = head_back(pt[at : at + HEAD], heads[h], cos, sin, qgain)
            query_sum = query_sum + term
            dpt[at : at + HEAD] = d_raw

    for copy in ring:
        copy.wait_recv()
    for a in range(2):
        for b in range(2):
            total = k0[a, b, z].astype(F32)
            for j in range(3):
                total = total + k1[j, a, b].astype(F32)
            ks1[a, b] = total.astype(BF16)
    across = k.send(ks1.at[:, 1 - yl], k2, yl_partner)
    next(outward[1])
    next(plane[0])
    next(plane[2])
    across.wait_recv()
    for a in range(2):
        kres[pl.ds(a * ROWS, ROWS)] = ks1[a, yl].astype(F32) + k2[a].astype(F32)
    key_sum = jnp.zeros((HEAD, TOK), F32)
    for g in range(KV_HEADS):
        both = kres[:, g * 128 : (g + 1) * 128].T
        at = QD + g * HEAD
        d_raw, term = head_back(pt[at : at + HEAD], both[:HEAD], cos, sin, kgain)
        key_sum = key_sum + term
        dpt[at : at + HEAD] = d_raw
        dpt[at + KD : at + KD + HEAD] = both[HEAD:]
    get_q = [k.local(WQ.at[0, t], w2.at[t]) for t in range(2)]
    get_n = [k.local(NA.at[:, :, :, pl.ds(t * 256, 256)], na2.at[t]) for t in range(2)]
    for t in range(8):
        block = jnp.concatenate([dpt[t * 240 : (t + 1) * 240], jnp.zeros((16, TOK), F32)], axis=0)
        dp[t] = block.T.astype(BF16)
    sums = jnp.concatenate(
        [jnp.sum(query_sum.T, axis=0, keepdims=True), jnp.sum(key_sum.T, axis=0, keepdims=True)], axis=1
    )
    vec[0] = jnp.broadcast_to(sums, (8, 128))
    small = small_reduce(p, k, vec, vrecv)
    next(small)

    last, keep = [], []

    def to_owners(total, dst):
        far = []
        for dz in range(4):
            for dc in range(2):
                zz, cc = (z + dz) % 4, (c + dc) % 2
                src = total.at[pl.ds(pl.multiple_of((zz * 2 + cc) * 16, 16), 16)]
                if dz == 0 and dc == 0:
                    keep.append(k.local(src, dst))
                else:
                    far.append((src, dst, p.at(z=zz, c=cc)))
        last.append(k.together(far, total.at[pl.ds(0, 112)]))

    def slab_home(half):
        slab = Slab(k, parts[2 + half][-1], GWD.at[:, pl.ds(half * 512, 512)], slab_from, own_slab)
        slab.start()
        return slab

    members = []
    for dz in range(4):
        for dc in range(2):
            zz, cc = (z + dz) % 4, (c + dc) % 2
            src = dp.at[zz * 2 + cc]
            if dz == 0 and dc == 0:
                own_dp = k.local(src, dpm.at[z, c])
            else:
                members.append(k.send(src, dpm.at[z, c], p.at(z=zz, c=cc)))
    next(outward[2])
    next(plane[1])
    next(plane[3])
    k.settle(early)
    own_dp.wait()
    for copy in members:
        copy.wait_recv()
    next(small)
    for t in range(8):
        get_n[t].wait()
        total = dot_rows(na2[t % 2].reshape(8 * TOK, 256), dpm[...].reshape(8 * TOK, 256))
        dqm[t // 4, t % 4] = total.astype(BF16).reshape(2, TOK, 256)
        if t < 6:
            get_n.append(k.local(NA.at[:, :, :, pl.ds((t + 2) * 256, 256)], na2.at[t % 2]))
    inward = [staged_reduce(p, k, dqm, q_stages(i), parts[4 + i], 16) for i in range(2)]
    for step in inward:
        next(step)
    get["mix"].wait()
    next(mixing, None)

    @pl.loop(0, TOK, step=16)
    def _(t):
        at = pl.ds(pl.multiple_of(t, 16), 16)
        total = resid[at]
        for j in (3, 0, 1):
            total = total + mix1[j, at].astype(F32)
        mixed[at] = total.astype(BF16)

    keep.append(k.local(mixed, MIXED))
    next(outward[0])
    next(outward[1])
    for half in range(2):
        next(plane[half], None)
        to_owners(parts[half][-1], GWG.at[:, pl.ds(pl.multiple_of(half * FF + m * FS, 128), FS)])
    slabs = []
    for half in range(2):
        next(plane[2 + half], None)
        slabs.append(slab_home(half))
    left = jnp.concatenate([dp[i] for i in range(8)], axis=1)

    def d_normed_block(t):
        get_q[t].wait()
        w = w2[t % 2].reshape(256, 2048)
        in_grad[:, t * 256 : (t + 1) * 256] = dot_last(left, w)
        if t < 6:
            get_q.append(k.local(WQ.at[(t + 2) // 4, (t + 2) % 4], w2.at[t % 2]))

    for t in range(4):
        d_normed_block(t)
    next(small)
    for step in inward:
        next(step)
    next(outward[2])
    for t in range(4, 8):
        d_normed_block(t)
    next(small)
    for step in outward:
        next(step)
    for half, step in enumerate(inward):
        next(step, None)
        to_owners(parts[4 + half][-1], GQ.at[:, pl.ds(pl.multiple_of(m * 256 + half * 128, 128), 128)])
    get["x"].wait()
    hidden = xv[...].astype(F32)
    scale_one = rms_scale(hidden)
    in_grad[...] = dres[...] + norm_back(in_grad[...], hidden * scale_one, scale_one, gains[0:1, :])
    keep.append(k.local(in_grad, IN_GRAD))
    next(small, None)
    keep.append(k.local(vec.at[4], SMALL))
    for i, step in enumerate(outward):
        next(step, None)
        total = parts[6 + i][-1]
        dst = GO.at[c, :, pl.ds(*O_PARTS[i])]
        keep.append(k.local(total.at[pl.ds(pl.multiple_of(c * 16, 16), 16)], dst))
        last.append(k.send(total.at[pl.ds(pl.multiple_of((1 - c) * 16, 16), 16)], dst, sib))
    for copy in keep:
        copy.wait()
    for copy in last:
        copy.wait_recv()
    for slab in slabs:
        slab.wait_recv()
        slab.wait_send()
    k.drain()


def head_back(raw, grad, cos, sin, gain):
    scale = head_scale(raw)
    normed = raw * scale
    d_head = grad * cos + half_back(grad * sin)
    scaled = d_head * gain
    inner = jnp.mean(scaled * normed, axis=0, keepdims=True)
    return scale * (scaled - normed * inner), d_head * normed


def back(*args):
    w = 2 * KD
    outs = [
        sds((TOK, D), F32),
        sds((TOK, D), BF16),
        sds((16, 2 * FF), BF16),
        sds((80, 1024), BF16),
        sds((16, 2048), BF16),
        sds((2, 16, 640), BF16),
        sds((8, 128), F32),
    ]
    scratch = [
        pltpu.VMEM((TOK, D), F32),
        pltpu.VMEM((TOK, D), BF16),
        pltpu.VMEM((TOK, D), BF16),
        pltpu.VMEM((TOK, D), F32),
        pltpu.VMEM((QKV, TOK), F32),
        pltpu.VMEM((2 * KV_HEADS, SEQ, 256), BF16),
        pltpu.VMEM((TOK, D), F32),
        pltpu.VMEM((TOK, D), BF16),
        pltpu.VMEM((2, 2, 4, 2, ROWS, w), BF16),
        pltpu.VMEM((KV_HEADS, 2, 256, 128), BF16),
        pltpu.VMEM((KV_HEADS, 2, 128, 256), BF16),
        pltpu.VMEM((KV_HEADS, 2, 256, 128), BF16),
        pltpu.VMEM((KV_HEADS, 2, HEAD, 256), F32),
        pltpu.VMEM((QKV, TOK), F32),
        pltpu.VMEM((TOK, QD), F32),
        pltpu.VMEM((TOK, D), F32),
        pltpu.VMEM((2, 2, 4, 2, ROWS, w), BF16),
        pltpu.VMEM((2, 2, 4, ROWS, w), BF16),
        pltpu.VMEM((3, 2, 2, ROWS, w), BF16),
        pltpu.VMEM((2, 2, ROWS, w), BF16),
        pltpu.VMEM((2, ROWS, w), BF16),
        pltpu.VMEM((TOK, w), F32),
        pltpu.VMEM((2, 2, 4, 2, 16, 2048), BF16),
        pltpu.VMEM((8, 2, 4, 2, 16, QD), BF16),
        pltpu.VMEM((2, TOK, D), BF16),
        pltpu.VMEM((2, TOK, QD), BF16),
        pltpu.VMEM((2, 4, 2, 4, 32, 640), BF16),
        pltpu.VMEM((8, TOK, 256), BF16),
        pltpu.VMEM((4, 2, TOK, 256), BF16),
        pltpu.VMEM((2, 4, 2, TOK, 256), BF16),
        pltpu.VMEM((2, 4, 2, TOK, 256), BF16),
        pltpu.VMEM((4, TOK, D), BF16),
        pltpu.VMEM((2, HEAD, TOK), F32),
        pltpu.VMEM((8, D), F32),
        pltpu.VMEM((2 * HEAD, 128), F32),
        pltpu.VMEM((TOK, D), BF16),
    ]
    for i, shapes in enumerate(PLANE_SHAPES + O_SHAPES):
        scratch += staged_scratch(shapes, i < 4)
    scratch += [
        pltpu.VMEM((5, 8, 128), F32),
        pltpu.VMEM((4, 3, 8, 128), F32),
        pltpu.SemaphoreType.DMA((56,)),
        pltpu.SemaphoreType.DMA((78,)),
        pltpu.SemaphoreType.DMA((30,)),
    ]
    return pl.pallas_call(
        back_body,
        out_shape=outs,
        in_specs=[ANY] * 17,
        out_specs=[ANY] * 7,
        scratch_shapes=scratch,
        name="back",
        compiler_params=pltpu.CompilerParams(
            collective_id=2, has_side_effects=True, vmem_limit_bytes=60 << 20
        ),
    )(*args)


def finish_body(*refs):
    IN_GRAD, MIXED, GWG, GWD, GQ, GO, SUMS, WG, WQ, g1, g2 = refs[:11]
    in_out, mixed_out, Q, O, G, DOWN, ATTN, FFN, QG, KG = refs[11:21]
    (gwg, gwd, gq, go, sums, wg, wq, q, o, g, down, attn, ffn_, qg, kg, ing, mix, sem) = refs[21:]
    used = []

    def copy(src, dst):
        out = pltpu.make_async_copy(src, dst, sem.at[len(used)])
        out.start()
        used.append(out)
        return out

    rows = [copy(IN_GRAD, ing), copy(MIXED, mix)]
    through = []
    got = [copy(a, b) for a, b in ((GQ, gq), (WQ, wq), (GO, go), (SUMS, sums), (GWD, gwd), (GWG, gwg), (WG, wg))]
    for one in got[:5]:
        one.wait()
    for one, (src, dst) in zip(rows, ((ing, in_out), (mix, mixed_out))):
        one.wait()
        through.append(copy(src, dst))
    wide = gq[...].astype(F32)
    lane = lax.broadcasted_iota(jnp.int32, (16, QKV), 1)
    total = jnp.zeros((16, QKV), F32)
    for i in range(8):
        piece = jnp.concatenate([wide[:, i * 256 : (i + 1) * 256], jnp.zeros((16, QKV - 256), F32)], axis=1)
        here = (lane >= i * 240) & (lane < (i + 1) * 240)
        total = jnp.where(here, pltpu.roll(piece, 240 * i, 1) if i else piece, total)
    q[...] = total
    through.append(copy(q, Q))
    o[...] = jnp.concatenate([go[0].astype(F32), go[1].astype(F32)], axis=1)
    through.append(copy(o, O))
    slab = gwd[...].astype(F32)
    down[...] = jnp.concatenate([slab[:40], slab[40:]], axis=1)
    through.append(copy(down, DOWN))
    attn[...] = flat(jnp.sum(wq[...].astype(F32) * total, axis=1, keepdims=True)) / g1[...].astype(F32)
    through.append(copy(attn, ATTN))
    qg[...] = sums[0:1, :HEAD]
    kg[...] = pltpu.roll(sums[...], HEAD, 1)[0:1, :HEAD]
    through += [copy(qg, QG), copy(kg, KG)]
    for one in got[5:]:
        one.wait()
    grown = gwg[...].astype(F32)
    g[...] = grown
    through.append(copy(g, G))
    ffn_[...] = flat(jnp.sum(wg[...].astype(F32) * grown, axis=1, keepdims=True)) / g2[...].astype(F32)
    through.append(copy(ffn_, FFN))
    for one in through:
        one.wait()


def flat(col):
    n = col.shape[0]
    place = lax.broadcasted_iota(jnp.int32, (n, n), 0) == lax.broadcasted_iota(jnp.int32, (n, n), 1)
    return jnp.sum(jnp.where(place, jnp.broadcast_to(col, (n, n)), 0.0), axis=0, keepdims=True)


def finish(*args):
    outs = [
        sds((TOK, D), F32),
        sds((TOK, D), BF16),
        sds((16, QKV), F32),
        sds((16, QD), F32),
        sds((16, 2 * FF), F32),
        sds((40, D), F32),
        sds((1, 16), F32),
        sds((1, 16), F32),
        sds((1, HEAD), F32),
        sds((1, HEAD), F32),
    ]
    ins = [(16, 2 * FF), (80, 1024), (16, 2048), (2, 16, 640), (8, 128), (16, 2 * FF), (16, QKV)]
    scratch = [pltpu.VMEM(a, F32 if a == (8, 128) else BF16) for a in ins]
    scratch += [pltpu.VMEM(a.shape, a.dtype) for a in outs[2:] + outs[:2]]
    return pl.pallas_call(
        finish_body,
        out_shape=outs,
        in_specs=[ANY] * 9 + [VMEM] * 2,
        out_specs=[ANY] * 10,
        scratch_shapes=scratch + [pltpu.SemaphoreType.DMA((19,))],
        name="finish",
        compiler_params=pltpu.CompilerParams(vmem_limit_bytes=60 << 20),
    )(*args)


def per_device(
    tokens,
    segment_ids,
    w_qkv,
    w_out,
    w_gate_up,
    w_down,
    attn_gain,
    ffn_gain,
    query_gain,
    key_gain,
    out_grad,
):
    g1, g2, g3, g4 = [a.reshape(1, -1) for a in (attn_gain, ffn_gain, query_gain, key_gain)]
    og_in = out_grad.reshape(TOK, D)
    x_in = tokens.reshape(TOK, D)
    (WO, WG, WD, OG, NA, KV, pt, probs, attended, resid, n2, wq_in, rope, gain_rows, head_gains) = front(
        x_in, w_qkv, w_out.T, w_gate_up, w_down, og_in, segment_ids, g1, g2, g3, g4, rope_parts()
    )
    d_normed, mix_part, dwg, dwd, WQ = ffn(n2, OG, WG, WD, wq_in)
    in_grad, mixed, gwg, gwd, gq, go, sums = back(
        d_normed, x_in, og_in, resid, attended, pt, probs, WQ, WO, KV, mix_part, dwg, dwd, NA,
        rope, gain_rows, head_gains,
    )
    outs = finish(in_grad, mixed, gwg, gwd, gq, go, sums, w_gate_up, w_qkv, g1, g2)
    return (
        outs[1].reshape(MICRO, ROWS, D),
        outs[0].reshape(MICRO, ROWS, D),
        outs[2],
        outs[3].T,
        outs[4],
        outs[5],
        outs[6].reshape(16),
        outs[7].reshape(16),
        outs[8].reshape(HEAD),
        outs[9].reshape(HEAD),
    )


def solution(mesh):
    return jax.shard_map(
        per_device,
        mesh=mesh,
        in_specs=(
            P(None, ("grp", "seq"), None),
            P(None, "grp"),
            P(("grp", "seq"), None),
            P(None, ("grp", "seq")),
            P(("grp", "seq"), None),
            P(("grp", "seq"), None),
            P(("grp", "seq")),
            P(("grp", "seq")),
            P(),
            P(),
            P(None, ("grp", "seq"), None),
        ),
        out_specs=(
            P(None, ("grp", "seq"), None),
            P(None, ("grp", "seq"), None),
            P(("grp", "seq"), None),
            P(None, ("grp", "seq")),
            P(("grp", "seq"), None),
            P(("grp", "seq"), None),
            P(("grp", "seq")),
            P(("grp", "seq")),
            P(),
            P(),
        ),
        check_vma=False,
    )
```

```python
import jax
import jax.numpy as jnp
import numpy as np
from jax import lax
from jax.experimental import pallas as pl
from jax.experimental.pallas import tpu as pltpu
from jax.sharding import PartitionSpec as P

Q_HEADS = 20
KV_HEADS = 5
GROUP = 4
HEAD = 64
D = 2048
FF = 5120
QD = 1280
KD = 320
QKV = 1920
SEQ = 1024
MICRO = 2
ROWS = 64
TOK = 128
FS = 640
EPS = 1e-06
MESH = pl.DeviceIdType.MESH
F32 = jnp.float32
BF16 = jnp.bfloat16
ANY = pl.BlockSpec(memory_space=pl.ANY)


class Place:
    def __init__(self):
        g = lax.axis_index("grp")
        s = lax.axis_index("seq")
        self.g, self.s = g, s
        self.yh, self.x = g // 4, g % 4
        self.yl, self.z, self.c = s // 8, (s // 2) % 4, s % 2
        self.y = self.yh * 2 + self.yl

    def at(self, x=None, y=None, z=None, c=None):
        x = self.x if x is None else x
        y = self.y if y is None else y
        z = self.z if z is None else z
        c = self.c if c is None else c
        return ((y // 2) * 4 + x, (y % 2) * 8 + z * 2 + c)

    def step(self, axis, k):
        if axis == "x":
            return self.at(x=(self.x + k) % 4)
        if axis == "y":
            return self.at(y=(self.y + k) % 4)
        if axis == "z":
            return self.at(z=(self.z + k) % 4)
        return self.at(c=1 - self.c)

    def pos(self, axis, k):
        return (getattr(self, axis) + k) % 4


class Links:
    def __init__(self, send_sems, recv_sems, local_sems):
        self.send_sems, self.recv_sems, self.local_sems = send_sems, recv_sems, local_sems
        self.received = 0
        self.free = {"send": list(range(send_sems.shape[0]))[::-1], "local": list(range(local_sems.shape[0]))[::-1]}
        self.sent = {}

    def plan(self, src, dst, to):
        i = self.received
        self.received += 1
        assert i < self.recv_sems.shape[0], i
        slot = self.free["send"].pop()
        copy = pltpu.make_async_remote_copy(
            src_ref=src,
            dst_ref=dst,
            send_sem=self.send_sems.at[slot],
            recv_sem=self.recv_sems.at[i],
            device_id=to,
            device_id_type=MESH,
        )
        self.sent[id(copy)] = (copy, slot)
        return copy

    def send(self, src, dst, to):
        copy = self.plan(src, dst, to)
        copy.start()
        return copy

    def together(self, copies, region):
        i = self.received
        self.received += 1
        slot = self.free["send"].pop()
        for src, dst, to in copies:
            pltpu.make_async_remote_copy(
                src_ref=src,
                dst_ref=dst,
                send_sem=self.send_sems.at[slot],
                recv_sem=self.recv_sems.at[i],
                device_id=to,
                device_id_type=MESH,
            ).start()
        group = Group(self.send_sems.at[slot], self.recv_sems.at[i], region)
        self.sent[id(group)] = (group, slot)
        return group

    def local(self, src, dst):
        slot = self.free["local"].pop()
        copy = pltpu.make_async_copy(src, dst, self.local_sems.at[slot])
        copy.start()
        return Local(self, copy, slot)

    def settle(self, copies):
        for copy in copies:
            copy, slot = self.sent.pop(id(copy))
            copy.wait_send()
            self.free["send"].append(slot)

    def drain(self):
        self.settle([copy for copy, _ in list(self.sent.values())])


class Group:
    def __init__(self, send_sem, recv_sem, region):
        self.send_sem, self.recv_sem, self.region = send_sem, recv_sem, region

    def wait_recv(self):
        pltpu.make_async_copy(self.region, self.region, self.recv_sem).wait()

    def wait_send(self):
        pltpu.make_async_copy(self.region, self.region, self.send_sem).wait()


class Local:
    def __init__(self, links, copy, slot):
        self.links, self.copy, self.slot = links, copy, slot

    def wait(self):
        self.copy.wait()
        self.links.free["local"].append(self.slot)


def halves(ref):
    n = ref.shape[0] // 2
    return ref.at[pl.ds(0, n)], ref.at[pl.ds(n, n)]


class RingGather:
    def __init__(self, p, k, axis, block, src=None):
        self.p, self.k, self.axis, self.block = p, k, axis, block
        dst = block(p.pos(axis, 0))
        src = dst if src is None else src
        self.right = k.send(src, dst, p.step(axis, 1))
        self.left = k.send(src, dst, p.step(axis, 3))

    def from_before(self):
        self.right.wait_recv()
        half = halves(self.block(self.p.pos(self.axis, 3)))[0]
        self.far_right = self.k.send(half, half, self.p.step(self.axis, 1))

    def from_after(self):
        self.left.wait_recv()
        half = halves(self.block(self.p.pos(self.axis, 1)))[1]
        self.far_left = self.k.send(half, half, self.p.step(self.axis, 3))

    def hand_on(self):
        self.from_before()
        self.from_after()

    def wait(self):
        self.far_right.wait_recv()
        self.far_left.wait_recv()

    def copies(self):
        return [self.right, self.left, self.far_right, self.far_left]


def greet(partners):
    barrier = pltpu.get_barrier_semaphore()
    for to in partners:
        pl.semaphore_signal(barrier, inc=1, device_id=to, device_id_type=MESH)
    pl.semaphore_wait(barrier, len(partners))


def sds(shape, dtype):
    return jax.ShapeDtypeStruct(shape, dtype)


def rms_scale(values):
    return lax.rsqrt(jnp.mean(values * values, axis=-1, keepdims=True) + EPS)


def norm_back(upstream, normed, scale, gain):
    scaled = upstream * gain
    inner = jnp.mean(scaled * normed, axis=-1, keepdims=True)
    return scale * (scaled - normed * inner)


def dot(left, right):
    return jnp.dot(left, right, preferred_element_type=F32)


def dot_last(left, right):
    return lax.dot_general(left, right, (((1,), (1,)), ((), ())), preferred_element_type=F32)


def dot_rows(left, right):
    return lax.dot_general(left, right, (((0,), (0,)), ((), ())), preferred_element_type=F32)


def slab_target(p):
    return p.at(x=(p.z + p.x) % 4, y=(p.c + p.yh) % 2 * 2 + p.yl, z=p.g // 2, c=p.g % 2)


def slab_place(p, x=None, y=None):
    m = p.z * 2 + p.c
    if x is not None:
        return (x + 4 - m % 4) % 4
    return (y // 2 + 2 - m // 4) % 2


def slab_source(p):
    m = p.z * 2 + p.c
    return p.at(x=m % 4, y=(m // 4) * 2 + p.yl, z=slab_place(p, x=p.x), c=slab_place(p, y=p.y))


def same(p, to):
    return (to[0] == p.g) & (to[1] == p.s)


def greet_plane(partners, slab_to, slab_from, own_slab):
    barrier = pltpu.get_barrier_semaphore()
    for to in partners:
        pl.semaphore_signal(barrier, inc=1, device_id=to, device_id_type=MESH)

    @pl.when(jnp.logical_not(own_slab))
    def _():
        pl.semaphore_signal(barrier, inc=1, device_id=slab_to, device_id_type=MESH)
        pl.semaphore_signal(barrier, inc=1, device_id=slab_from, device_id_type=MESH)

    def wait():
        @pl.when(jnp.logical_not(own_slab))
        def _():
            pl.semaphore_wait(barrier, len(partners) + 2)

        @pl.when(own_slab)
        def _():
            pl.semaphore_wait(barrier, len(partners))

    return wait


class Slab:
    def __init__(self, k, src, dst, to, own):
        self.own, self.src, self.dst = own, src, dst
        self.far = k.plan(src, dst, to)
        k.sent.pop(id(self.far))
        self.near = pltpu.make_async_copy(src, dst, k.recv_sems.at[k.received - 1])

    def start(self):
        @pl.when(self.own)
        def _():
            self.near.start()

        @pl.when(jnp.logical_not(self.own))
        def _():
            self.far.start()

    def wait_recv(self):
        @pl.when(self.own)
        def _():
            self.near.wait()

        @pl.when(jnp.logical_not(self.own))
        def _():
            self.far.wait_recv()

    def wait_send(self):
        @pl.when(jnp.logical_not(self.own))
        def _():
            self.far.wait_send()


def add_blocks(dst, terms, chunk):
    lead, rows = dst.shape[:-2], dst.shape[-2]
    count = 1
    for n in lead:
        count *= n

    @pl.loop(0, count)
    def _(i):
        at = []
        rest = i
        for n in reversed(lead):
            at.insert(0, rest % n)
            rest = rest // n

        @pl.loop(0, rows, step=chunk)
        def _(t):
            here = (*at, pl.ds(pl.multiple_of(t, chunk), chunk))
            total = terms[0][here].astype(F32)
            for term in terms[1:]:
                total = total + term[here].astype(F32)
            dst[here] = total.astype(dst.dtype)


def staged_reduce(p, k, src, stages, scr, chunk):
    own = scr[0]
    cur = src
    for n, (axis, pick) in enumerate(stages):
        recv = scr[1] if n == 0 else scr[2 * n]
        if n == 0:
            mine = k.local(pick(src, p.pos(axis, 0)), own)
        ring = k.together(
            [(pick(cur, p.pos(axis, j)), recv.at[j - 1], p.step(axis, j)) for j in (1, 2, 3)], recv
        )
        yield
        if n == 0:
            mine.wait()
        ring.wait_recv()
        total = own if n == 0 else scr[2 * n + 1]
        add_blocks(total, [own if n == 0 else pick(cur, p.pos(axis, 0))] + [recv.at[j] for j in range(3)], chunk)
        cur = total


def ring_reduce(p, k, src, stages, scr, chunk):
    own, recv, held, recv2, total = scr
    axis, pick = stages[0]
    before, after, far = recv.at[0], recv.at[1], recv.at[2]
    far_a, far_b = halves(pick(src, p.pos(axis, 2)))
    right_a, right_b = halves(pick(src, p.pos(axis, 1)))
    left_a, left_b = halves(pick(src, p.pos(axis, 3)))
    right, left = p.step(axis, 1), p.step(axis, 3)
    on_right = k.send(far_a, halves(far)[0], right)
    on_left = k.send(far_b, halves(far)[1], left)
    get = [k.local(right_a, halves(held)[0]), k.local(left_b, halves(held)[1])]
    mine = k.local(pick(src, p.pos(axis, 0)), own)
    yield
    near = [k.send(right_b, halves(before)[1], right), k.send(left_a, halves(after)[0], left)]
    yield
    for i, (copy, to, dst) in enumerate(((on_right, right, before), (on_left, left, after))):
        get[i].wait()
        copy.wait_recv()
        here = halves(held)[i]
        add_blocks(here, [here, halves(far)[i]], chunk)
        near.append(k.send(here, halves(dst)[i], to))
    yield
    mine.wait()
    for copy in near:
        copy.wait_recv()
    add_blocks(own, [own, before, after], chunk)
    axis, pick = stages[1]
    ring = k.together([(pick(own, p.pos(axis, j)), recv2.at[j - 1], p.step(axis, j)) for j in (1, 2, 3)], recv2)
    yield
    ring.wait_recv()
    add_blocks(total, [pick(own, p.pos(axis, 0))] + [recv2.at[j] for j in range(3)], chunk)


def mix_reduce(p, k, part, bufs, held):
    right, left = p.step("z", 1), p.step("z", 3)
    far_a, far_b = halves(part.at[p.pos("z", 2)])
    right_a, right_b = halves(part.at[p.pos("z", 1)])
    left_a, left_b = halves(part.at[p.pos("z", 3)])
    far = halves(bufs.at[2])
    first = [k.send(far_a, far[0], right), k.send(far_b, far[1], left)]
    near = [k.send(right_b, halves(bufs.at[0])[1], right), k.send(left_a, halves(bufs.at[1])[0], left)]
    get = [k.local(right_a, halves(held)[0]), k.local(left_b, halves(held)[1])]
    yield
    for i, to in enumerate((right, left)):
        get[i].wait()
        first[i].wait_recv()
        here = halves(held)[i]
        add_blocks(here, [here, far[i]], 16)
        near.append(k.send(here, halves(bufs.at[i])[i], to))
    yield
    for copy in near:
        copy.wait_recv()


def staged_scratch(shapes, held=False):
    out = [pltpu.VMEM(shapes[0], BF16), pltpu.VMEM((3, *shapes[0]), BF16)]
    if held:
        out.append(pltpu.VMEM(shapes[0], BF16))
    for n, shape in enumerate(shapes[1:]):
        out.append(pltpu.VMEM((3, *shape), BF16))
        out.append(pltpu.VMEM(shape, BF16))
    return out


EVERY = slice(None)


def wg_stages(half):
    cols = pl.ds(half * FS, FS)
    if half == 0:
        return [
            ("y", lambda r, i: r.at[i // 2, :, i % 2, :, cols]),
            ("x", lambda r, i: r.at[i]),
        ]
    return [
        ("x", lambda r, i: r.at[:, i, :, :, cols]),
        ("y", lambda r, i: r.at[i // 2, i % 2]),
    ]


def wd_stages(p, half):
    cols = pl.ds(half * 512, 512)
    if half == 0:
        return [
            ("y", lambda r, i: r.at[i % 2, :, slab_place(p, y=i), :, cols]),
            ("x", lambda r, i: r.at[slab_place(p, x=i)]),
        ]
    return [
        ("x", lambda r, i: r.at[:, slab_place(p, x=i), :, :, cols]),
        ("y", lambda r, i: r.at[i % 2, slab_place(p, y=i)]),
    ]


def q_stages(half):
    cols = pl.ds(half * 128, 128)
    if half == 0:
        return [
            ("y", lambda r, i: r.at[i // 2, :, i % 2, :, cols]),
            ("x", lambda r, i: r.at[i]),
        ]
    return [
        ("x", lambda r, i: r.at[:, i, :, :, cols]),
        ("y", lambda r, i: r.at[i // 2, i % 2]),
    ]


def o_stages(part):
    cols = pl.ds(*O_PARTS[part])
    if part == 0:
        return [
            ("x", lambda r, i: r.at[:, i, :, :, :, cols]),
            ("z", lambda r, i: r.at[:, :, i]),
            ("y", lambda r, i: r.at[i // 2, i % 2]),
        ]
    if part == 1:
        return [
            ("y", lambda r, i: r.at[i // 2, :, i % 2, :, :, cols]),
            ("x", lambda r, i: r.at[i]),
            ("z", lambda r, i: r.at[i]),
        ]
    return [
        ("z", lambda r, i: r.at[:, :, :, i, :, cols]),
        ("y", lambda r, i: r.at[i // 2, :, i % 2]),
        ("x", lambda r, i: r.at[i]),
    ]


O_PARTS = ((0, 256), (256, 128), (384, 256))
PLANE_SHAPES = [
    [(4, 128, FS), (128, FS)],
    [(2, 2, 128, FS), (128, FS)],
    [(4, 80, 512), (80, 512)],
    [(2, 2, 80, 512), (80, 512)],
    [(4, 128, 128), (128, 128)],
    [(2, 2, 128, 128), (128, 128)],
]
O_SHAPES = [
    [(2, 2, 4, 32, 256), (2, 2, 32, 256), (32, 256)],
    [(4, 4, 32, 128), (4, 32, 128), (32, 128)],
    [(2, 4, 2, 32, 256), (4, 32, 256), (32, 256)],
]


def small_reduce(p, k, vec, recv):
    for n, axis in enumerate("zyxc"):
        steps = (1,) if axis == "c" else (1, 2, 3)
        here = recv.at[n, pl.ds(0, len(steps))]
        ring = k.together([(vec.at[n], recv.at[n, j - 1], p.step(axis, j)) for j in steps], here)
        yield
        ring.wait_recv()
        total = vec[n]
        for j in range(len(steps)):
            total = total + recv[n, j]
        vec[n + 1] = total


def swap(a, b):
    left = lax.broadcasted_iota(jnp.int32, a.shape, 1) < ROWS
    return jnp.where(left, a, pltpu.roll(b, ROWS, 1)), jnp.where(left, pltpu.roll(a, ROWS, 1), b)


def head_scale(v):
    return lax.rsqrt(jnp.mean(v * v, axis=-2, keepdims=True) + EPS)


def half_turn(v):
    half = HEAD // 2
    return jnp.concatenate([-v[..., half:, :], v[..., :half, :]], axis=-2)


def half_back(v):
    half = HEAD // 2
    return jnp.concatenate([v[..., half:, :], -v[..., :half, :]], axis=-2)


def low(v):
    return v.astype(BF16).astype(F32)


def query_units(packed_t, g, cos, sin, gain):
    raw = packed_t[pl.ds(pl.multiple_of(g * 256, 256), 256)].reshape(GROUP, HEAD, TOK)
    head = raw * head_scale(raw) * gain
    turned = low(head * cos + half_turn(head) * sin) * (HEAD ** -0.5)
    a0, a1 = swap(turned[0], turned[1])
    b0, b1 = swap(turned[2], turned[3])
    none = jnp.zeros((HEAD, 256), F32)
    return [
        jnp.concatenate([jnp.concatenate([a, b], axis=1), none], axis=0) for a, b in ((a0, b0), (a1, b1))
    ]


def fill_bias(bias, seg, s):
    lane = lax.broadcasted_iota(jnp.int32, (128, 128), 1)
    query = lane % ROWS + s * ROWS
    around = pl.ds(pl.multiple_of((s // 2) * 128, 128), 128)
    for m in range(MICRO):
        ids = jnp.broadcast_to(seg[m : m + 1, around].astype(F32), (128, 128))
        turned = pltpu.roll(ids, ROWS, 1)
        ids = jnp.where((lane < ROWS) == (s % 2 == 0), ids, turned)
        ids = jnp.where(ids >= 0, ids, -2.0)

        @pl.loop(0, SEQ, step=128)
        def _(t):
            at = pl.ds(pl.multiple_of(t, 128), 128)
            key = lax.broadcasted_iota(jnp.int32, (128, 128), 0) + t
            keys = jnp.broadcast_to(seg[m : m + 1, at].astype(F32), (128, 128)).T
            ok = ((key <= query) & (keys == ids)) | (key == query)
            bias[m, at] = jnp.where(ok, 3e38, -1e30)


def rope_parts():
    inverse = 10000.0 ** (-(np.arange(HEAD) % (HEAD // 2)) / (HEAD // 2))
    begin = inverse[:, None] * (np.arange(128)[None, :] % 16 * ROWS)
    inside = inverse[:, None] * (np.arange(128)[None, :] % ROWS)
    return np.stack([np.cos(begin), np.sin(begin), np.cos(inside), np.sin(inside)]).astype(np.float32)


def rope_tables(parts, s):
    here = lax.broadcasted_iota(jnp.int32, (HEAD, 128), 1) == s
    c0 = jnp.sum(jnp.where(here, parts[0], 0.0), axis=1, keepdims=True)
    s0 = jnp.sum(jnp.where(here, parts[1], 0.0), axis=1, keepdims=True)
    return c0 * parts[2] - s0 * parts[3], s0 * parts[2] + c0 * parts[3]


def column(row):
    n = row.shape[1]
    place = lax.broadcasted_iota(jnp.int32, (n, n), 0) == lax.broadcasted_iota(jnp.int32, (n, n), 1)
    return jnp.sum(jnp.where(place, jnp.broadcast_to(row, (n, n)), 0.0), axis=1, keepdims=True)


KV_PARTS = (pl.ds(0, 384), pl.ds(384, 256))


def unit_bias(bias, m):
    half = bias[m]
    return jnp.concatenate([half, half], axis=1)


def unit_kv(KV, m, g):
    cols = pl.ds(pl.multiple_of(g * 128, 128), 128)
    return KV[m, :, :, :, :, cols].reshape(SEQ, 128)


def front_body(*refs):
    (x_in, w_qkv, wo, wg, w_down, og, seg, g1, g2, g3, g4, parts) = refs[:12]
    (WO, WG, WD, OG, NA, KV, PT, PROBS, ATT, RESID, N2, WQIN, ROPE, GAINS, QKGAIN) = refs[12:27]
    (wq, wd, ogv, gains_out, rope, qkgain) = refs[27:33]
    (xs, na, wqm, wos, pks, pk, pt, kept, att, resid, n2, kvl, kvs, bias, qts, ots) = refs[33:49]
    ssem, rsem, lsem = refs[49:]
    p = Place()
    k = Links(ssem, rsem, lsem)
    yh, x, yl, z, c = p.yh, p.x, p.yl, p.z, p.c
    m = z * 2 + c
    sib = p.step("c", 1)
    yl_partner = p.at(y=p.yh * 2 + 1 - yl)
    partners = [p.step(a, j) for a in "xyz" for j in (1, 2, 3)]
    partners += [p.at(z=(z + j) % 4, c=1 - c) for j in range(4)]
    slab_to, slab_from = slab_target(p), slab_source(p)
    own_slab = same(p, slab_to)

    met = greet_plane(partners, slab_to, slab_from, own_slab)
    own_x = k.local(x_in, xs.at[z, c])
    get_og = k.local(og, ogv)
    spare = [column(row[...].astype(F32)) for row in (g1, g2)]
    wide = w_qkv[...].astype(F32)
    lane = lax.broadcasted_iota(jnp.int32, (16, 256), 1)
    rest = jnp.where(lane == 240, spare[0], jnp.where(lane == 241, spare[1], 0.0))
    for i in range(8):
        turned = pltpu.roll(wide, (QKV - 240 * i) % QKV, 1)[:, :256]
        wq[:, i * 256 : (i + 1) * 256] = jnp.where(lane < 240, turned, rest).astype(BF16)
    met()

    def spread(src_of, dst_of, region):
        far, near = [], None
        for dz in range(4):
            for dc in range(2):
                zz, cc = (z + dz) % 4, (c + dc) % 2
                src, dst = src_of(zz * 2 + cc), dst_of(m)
                if dz == 0 and dc == 0:
                    near = k.local(src, dst)
                else:
                    far.append((src, dst, p.at(z=zz, c=cc)))
        return near, [k.together(far, region)]

    q0 = spread(
        lambda i: wq.at[:, pl.ds(pl.multiple_of(i * 256, 256), 256)], lambda i: wqm.at[yh, x, yl, i],
        wqm.at[0, 0, 0, pl.ds(0, 7)],
    )
    xcore = {0: k.send(x_in, xs.at[z, c], sib)}
    own_wo = k.local(wo, wos.at[yh, x, yl, z, c])

    def wo_at(part, *at):
        return wos.at[(*at, EVERY, pl.ds(part * 640, 640))]

    o1 = [
        k.together(
            [(wo, wos.at[yh, x, yl, z, c], p.step("z", j)) for j in (1, 2, 3)], wos.at[0, 0, 0, pl.ds(0, 3), 0]
        )
    ]
    g0 = [
        spread(
            lambda i: wg.at[:, pl.ds(pl.multiple_of(half * FF + i * FS, 128), FS)],
            lambda i: WG.at[yh, x, yl, i, :, pl.ds(half * FS, FS)],
            WG.at[0, 0, 0, pl.ds(0, 7), :, pl.ds(0, FS)],
        )
        for half in range(2)
    ]
    xring = RingGather(p, k, "z", lambda i: xs.at[i, c], x_in)

    def to_plane(blocks):
        return [
            k.together([(b, b, p.step(axis, j)) for j in (1, 2, 3)], region) for b, axis, region in blocks
        ]

    ql, qh = pl.ds(0, 128), pl.ds(128, 128)
    lo, hi = pl.ds(0, FS), pl.ds(FS, FS)
    dlo, dhi = pl.ds(0, 384), pl.ds(384, 640)
    q0[0].wait()
    for copy in q0[1]:
        copy.wait_recv()
    one = wqm.at[0, pl.ds(0, 3), 0, :, :, ql]
    q1 = to_plane(((wqm.at[yh, x, yl, :, :, ql], "x", one), (wqm.at[yh, x, yl, :, :, qh], "y", one)))
    fill_bias(bias, seg, p.s)
    cos, sin = rope_tables(parts, p.s)
    rope[0], rope[1] = cos, sin
    qgain, kgain = column(g3[...].astype(F32)), column(g4[...].astype(F32))
    qkgain[...] = jnp.concatenate([jnp.broadcast_to(qgain, (HEAD, 128)), jnp.broadcast_to(kgain, (HEAD, 128))], axis=0)
    for copy in q1:
        copy.wait_recv()
    four = wqm.at[:, pl.ds(0, 3), :, :, :, ql]
    q2 = to_plane(((wqm.at[yh, :, yl, :, :, ql], "y", four), (wqm.at[:, x, :, :, :, qh], "x", four)))
    for near, far in g0:
        near.wait()
        for copy in far:
            copy.wait_recv()
    one = WG.at[0, pl.ds(0, 3), 0, :, :, lo]
    plane = to_plane(((WG.at[yh, x, yl, :, :, lo], "x", one), (WG.at[yh, x, yl, :, :, hi], "y", one)))
    slab_rows = w_down[...].astype(F32)
    wd[...] = jnp.concatenate([slab_rows[:, :1024], slab_rows[:, 1024:]], axis=0).astype(BF16)
    slab = Slab(k, wd, WD.at[yl, z, c], slab_to, own_slab)
    slab.start()
    xring.hand_on()
    for o in (1, 3):
        src = xs.at[(z + o) % 4, c]
        xcore[o] = k.send(src, src, sib)
    for copy in q2:
        copy.wait_recv()
    own_x.wait()
    own_wo.wait()
    pick = jnp.where(
        lax.broadcasted_iota(jnp.int32, (8, 128), 0) + 112 == lax.broadcasted_iota(jnp.int32, (8, 128), 1), 1.0, 0.0
    ).astype(BF16)
    gains_out[...] = dot_last(pick, wqm[:, :, :, :, :, pl.ds(128, 128)].reshape(D, 128))
    keep = [k.local(wq, WQIN), k.local(rope, ROPE), k.local(gains_out, GAINS), k.local(qkgain, QKGAIN)]
    k.settle(q0[1] + q1)
    packs = []
    for o in (0, 1, 3, 2):
        zz = (z + o) % 4
        if o == 2:
            xring.wait()
            xcore[o] = k.send(xs.at[zz, c], xs.at[zz, c], sib)
        xcore[o].wait_recv()
        rows = xs[zz].reshape(256, D).astype(F32)
        normed = (rows * rms_scale(rows) * gains_out[0:1, :]).astype(BF16)
        na[zz] = normed.reshape(2, TOK, D)
        pks[zz] = dot(normed, wqm[...].reshape(D, 256)).astype(BF16).reshape(2, TOK, 256)
        if o:
            packs.append(k.send(pks.at[zz, c], pk.at[m], p.at(z=zz)))
        else:
            own_pk = k.local(pks.at[z, c], pk.at[m])
        packs.append(k.send(pks.at[zz, 1 - c], pk.at[m], p.at(z=zz, c=1 - c)))
        if o == 1:
            for copy in o1:
                copy.wait_recv()
            four = wos.at[:, pl.ds(0, 3), :, 0, 0, :, pl.ds(0, 640)]
            o2 = to_plane(
                ((wo_at(0, yh, x, yl, EVERY, c), "y", four), (wo_at(1, yh, x, yl, EVERY, c), "x", four))
            )
        if o == 3:
            for copy in plane:
                copy.wait_recv()
            plane2 = [
                RingGather(p, k, "x", lambda i: WG.at[:, i, :, :, :, hi]),
                RingGather(p, k, "y", lambda i: WG.at[i // 2, :, i % 2, pl.ds(0, 4), :, lo]),
            ]
    slab.wait_recv()
    held = WD.at[yl, slab_place(p, x=x), slab_place(p, y=p.y)]
    few = WD.at[0, pl.ds(0, 3), 0]
    plane_d = to_plane(((held.at[:, dlo], "x", few.at[:, :, dlo]), (held.at[:, dhi], "y", few.at[:, :, dhi])))
    for copy in o2:
        copy.wait_recv()
    o3 = [RingGather(p, k, "x", lambda i: wo_at(0, EVERY, i, EVERY, EVERY, c))]
    keep.append(k.local(na, NA))
    k.settle(q2 + o1 + [copy for _, far in g0 for copy in far])
    own_pk.wait()
    for copy in packs:
        copy.wait_recv()
    for i8 in range(8):
        pt[i8 * 240 : (i8 + 1) * 240] = pk[i8].astype(F32).T[:240]

    @pl.loop(0, KV_HEADS)
    def _(g):
        raw = pt[pl.ds(pl.multiple_of(QD + g * HEAD, HEAD), HEAD)]
        head = raw * head_scale(raw) * kgain
        key = head * cos + half_turn(head) * sin
        value = pt[pl.ds(pl.multiple_of(QD + KD + g * HEAD, HEAD), HEAD)]
        both = jnp.concatenate([key, value], axis=0).T.astype(BF16)
        cols = pl.ds(pl.multiple_of(g * 128, 128), 128)
        for mm in range(MICRO):
            kvl[mm, :, cols] = both[mm * ROWS : (mm + 1) * ROWS]

    own_kv = k.local(kvl, kvs.at[:, yl, z, c])
    across, ring = [], []
    for cols in KV_PARTS:
        across.append(k.send(kvl.at[:, :, cols], kvs.at[:, yl, z, c, :, cols], yl_partner))
        three = kvs.at[:, 0, pl.ds(0, 3), 0, :, cols]
        sends = [(kvl.at[:, :, cols], kvs.at[:, yl, z, c, :, cols], p.step("z", j)) for j in (1, 2, 3)]
        ring.append([k.together(sends, three)])
    keep.append(k.local(pt, PT))

    @pl.loop(0, KV_HEADS)
    def _(g):
        for mm, unit in enumerate(query_units(pt, g, cos, sin, qgain)):
            qts[g, mm] = unit.astype(BF16)

    for copy, group, cols in zip(across, ring, KV_PARTS):
        copy.wait_recv()
        src = kvs.at[:, 1 - yl, z, c, :, cols]
        three = kvs.at[:, 0, pl.ds(0, 3), 0, :, cols]
        group.append(k.together([(src, src, p.step("z", j)) for j in (1, 2, 3)], three))
    get_og.wait()
    keep.append(k.local(ogv, OG.at[z, c]))
    rows = RingGather(p, k, "z", lambda i: OG.at[i, c], ogv)
    last = [k.send(ogv, OG.at[z, c], sib)]
    own_kv.wait()
    o3.append(RingGather(p, k, "y", lambda i: wo_at(1, i // 2, EVERY, i % 2, EVERY, c)))
    for ring4 in plane2:
        ring4.hand_on()
    oc = []
    for src in (
        wo_at(0, EVERY, x, EVERY, EVERY, c),
        wo_at(1, yh, EVERY, yl, EVERY, c),
    ):
        oc.append(k.send(src, src, sib))
    for copy in ring[0]:
        copy.wait_recv()
    src = kvs.at[:, :, :, c, :, KV_PARTS[0]]
    kvc = [k.send(src, src, sib)]
    o3[0].hand_on()
    o3[1].hand_on()
    for copy in plane_d:
        copy.wait_recv()
    plane2.append(RingGather(p, k, "x", lambda i: WD.at[:, slab_place(p, x=i), :, :, dhi]))
    plane2 += [
        RingGather(p, k, "y", lambda i: WD.at[i % 2, :, slab_place(p, y=i), :, dlo]),
        RingGather(p, k, "y", lambda i: WG.at[i // 2, :, i % 2, pl.ds(4, 4), :, lo]),
    ]
    for axis, ring4 in zip("xy", o3):
        for j in (1, 3):
            src = ring4.block(p.pos(axis, j))
            oc.append(k.send(src, src, sib))
    kvc[0].wait_recv()

    def unit(u):
        g, mm = u // 2, u % 2
        kv = unit_kv(kvs, mm, g)
        score = jnp.minimum(dot(kv, qts[g, mm]), unit_bias(bias, mm))
        peak = jnp.max(score, axis=0, keepdims=True)
        raised = jnp.exp(score - peak)
        total = jnp.sum(raised, axis=0, keepdims=True)
        probs = (raised * (1.0 / total)).astype(BF16)
        ots[g, mm] = dot_rows(kv, probs)[HEAD:]
        kept[u] = probs

    k.settle(packs + plane + plane_d)
    pl.loop(0, 6)(unit)
    for copy in ring[1]:
        copy.wait_recv()
    src = kvs.at[:, :, :, c, :, KV_PARTS[1]]
    kvc.append(k.send(src, src, sib))
    k.settle(o2 + xring.copies() + list(xcore.values()))
    kvc[1].wait_recv()
    keep.append(k.local(kvs, KV))
    for axis, ring4 in zip("xy", o3):
        ring4.wait()
        src = ring4.block(p.pos(axis, 2))
        oc.append(k.send(src, src, sib))
    pl.loop(6, 2 * KV_HEADS)(unit)
    for g in range(KV_HEADS):
        for t in range(2):
            cols = slice(t * 128, (t + 1) * 128)
            a, b = swap(ots[g, 0, :, cols], ots[g, 1, :, cols])
            at = (g * GROUP + 2 * t) * HEAD
            att[:, at : at + 128] = jnp.concatenate([a, b], axis=0).T.astype(BF16)
    keep += [k.local(kept, PROBS), k.local(att, ATT)]
    rows.hand_on()
    for j in (1, 3):
        src = OG.at[p.pos("z", j), c]
        last.append(k.send(src, src, sib))
    for copy in oc:
        copy.wait_recv()
    keep.append(k.local(wos, WO))

    @pl.loop(0, 8)
    def _(t):
        w = wos[t // 4, t % 4].reshape(256, QD)
        cols = pl.ds(pl.multiple_of(t * 256, 256), 256)
        resid[:, cols] = xs[z, c, :, cols].astype(F32) + dot_last(att[...], w)

    plane2[2].hand_on()
    plane2[3].hand_on()
    plane2[4].hand_on()
    value = resid[...]
    n2[...] = (value * rms_scale(value) * gains_out[1:2, :]).astype(BF16)
    keep += [k.local(resid, RESID), k.local(n2, N2)]
    rows.wait()
    src = OG.at[p.pos("z", 2), c]
    last.append(k.send(src, src, sib))
    for ring4 in plane2:
        ring4.wait()
    for copy in last:
        copy.wait_recv()
    for copy in keep:
        copy.wait()
    slab.wait_send()
    k.drain()


VMEM = pl.BlockSpec(memory_space=pltpu.VMEM)


def front(*args):
    hbm = [
        sds((2, 4, 2, 4, 2, 16, QD), BF16),
        sds((2, 4, 2, 8, 16, 2 * FS), BF16),
        sds((2, 4, 2, 80, 1024), BF16),
        sds((4, 2, TOK, D), BF16),
        sds((4, 2, TOK, D), BF16),
        sds((2, 2, 4, 2, ROWS, 2 * KD), BF16),
        sds((QKV, TOK), F32),
        sds((2 * KV_HEADS, SEQ, 256), BF16),
        sds((TOK, QD), BF16),
        sds((TOK, D), F32),
        sds((TOK, D), BF16),
        sds((16, 2048), BF16),
        sds((2, HEAD, TOK), F32),
        sds((8, D), F32),
        sds((2 * HEAD, 128), F32),
    ]
    scratch = [
        pltpu.VMEM((16, 2048), BF16),
        pltpu.VMEM((80, 1024), BF16),
        pltpu.VMEM((TOK, D), BF16),
        pltpu.VMEM((8, D), F32),
        pltpu.VMEM((2, HEAD, TOK), F32),
        pltpu.VMEM((2 * HEAD, 128), F32),
        pltpu.VMEM((4, 2, TOK, D), BF16),
        pltpu.VMEM((4, 2, TOK, D), BF16),
        pltpu.VMEM((2, 4, 2, 8, 16, 256), BF16),
        pltpu.VMEM((2, 4, 2, 4, 2, 16, QD), BF16),
        pltpu.VMEM((4, 2, TOK, 256), BF16),
        pltpu.VMEM((8, TOK, 256), BF16),
        pltpu.VMEM((QKV, TOK), F32),
        pltpu.VMEM((2 * KV_HEADS, SEQ, 256), BF16),
        pltpu.VMEM((TOK, QD), BF16),
        pltpu.VMEM((TOK, D), F32),
        pltpu.VMEM((TOK, D), BF16),
        pltpu.VMEM((2, ROWS, 2 * KD), BF16),
        pltpu.VMEM((2, 2, 4, 2, ROWS, 2 * KD), BF16),
        pltpu.VMEM((2, SEQ, 128), F32),
        pltpu.VMEM((KV_HEADS, 2, 128, 256), BF16),
        pltpu.VMEM((KV_HEADS, 2, HEAD, 256), F32),
        pltpu.SemaphoreType.DMA((60,)),
        pltpu.SemaphoreType.DMA((82,)),
        pltpu.SemaphoreType.DMA((14,)),
    ]
    return pl.pallas_call(
        front_body,
        out_shape=hbm,
        in_specs=[ANY, VMEM, VMEM, ANY, VMEM, ANY] + [VMEM] * 6,
        out_specs=[ANY] * len(hbm),
        scratch_shapes=scratch,
        name="front",
        compiler_params=pltpu.CompilerParams(
            collective_id=0, has_side_effects=True, vmem_limit_bytes=56 << 20
        ),
    )(*args)


def ffn_body(n2, OG, WG, WD, wq, d_out, mix_out, dwg_out, dwd_out, WQ, *scr):
    (rows, ogs, wgs, wd80, wds, dgu, inn, din, part, mixs, r0, s0, r1, m0, dwg, dwd32, dwd) = scr[:17]
    (dn, wqv, ssem, rsem, lsem, wsem, vsem, wlsem) = scr[17:]
    p = Place()
    k = Links(wsem, vsem, wlsem)
    yh, x, yl, z, c = p.yh, p.x, p.yl, p.z, p.c
    sib = p.step("c", 1)
    greet([p.step(a, j) for a in "xyz" for j in (1, 2, 3)] + [sib])

    def remote(src, dst, i, to):
        return pltpu.make_async_remote_copy(
            src_ref=src,
            dst_ref=dst,
            send_sem=ssem.at[i],
            recv_sem=rsem.at[i],
            device_id=to,
            device_id_type=MESH,
        )

    def local(src, dst, i):
        copy = pltpu.make_async_copy(src, dst, lsem.at[i])
        copy.start()
        return copy

    def half_of(half, *at):
        return WQ.at[(*at, EVERY, pl.ds(half * 1024, 1024))]

    whole = (EVERY, EVERY, EVERY, EVERY, c)
    get_wq = k.local(wq, wqv)
    q1 = [k.plan(wq, WQ.at[yh, x, yl, z, c], p.step("z", j)) for j in (1, 2, 3)]
    q2, q3 = [], []
    for j in (1, 2, 3):
        for half, axis in ((0, "y"), (1, "x")):
            src = half_of(half, yh, x, yl, EVERY, c)
            q2.append(k.plan(src, src, p.step(axis, j)))
    for j in (1, 2, 3):
        src = half_of(0, EVERY, x, EVERY, EVERY, c)
        q3.append(k.plan(src, src, p.step("x", j)))
        src = half_of(1, yh, EVERY, yl, EVERY, c)
        q3.append(k.plan(src, src, p.step("y", j)))
    q4 = k.plan(WQ.at[whole], WQ.at[whole], sib)

    sent = []
    for copy in q1:
        copy.start()
    for j in (1, 3):
        copy = remote(n2, rows.at[z, c], j, p.step("z", j))
        copy.start()
        sent.append(copy)
    half = halves(rows.at[p.pos("z", 1), c])[1], halves(rows.at[p.pos("z", 3), c])[0]
    on_left = remote(half[0], half[0], 0, p.step("z", 3))
    on_right = remote(half[1], half[1], 2, p.step("z", 1))
    sent += [on_left, on_right]
    remote(n2, rows.at[z, c], 4, sib).start()
    own = local(n2, rows.at[z, c], 0)
    get_wd = local(WD, wd80, 1)
    get_wg = local(WG, wgs, 2)
    get_og = local(OG, ogs, 3)
    get_wd.wait()

    @pl.loop(0, 8)
    def _(i):
        yl, x = i // 4, i % 4
        a, b = wd80[yl, x, 0].astype(F32), wd80[yl, x, 1].astype(F32)
        at = pl.ds(pl.multiple_of(i * 80, 80), 80)
        wds[at, :1024] = jnp.concatenate([a[:40], b[:40]], axis=0).astype(BF16)
        wds[at, 1024:] = jnp.concatenate([a[40:], b[40:]], axis=0).astype(BF16)

    own.wait()
    get_wg.wait()
    get_og.wait()
    get_wq.wait()
    own_wq = k.local(wqv, WQ.at[yh, x, yl, z, c])

    def ring_step(j):
        return jnp.where(j == 2, 3, jnp.where(j == 3, 2, j))

    def d_inner_of(zz):
        din[...] = dot_last(ogs[zz].reshape(256, D), wds[...])

    d_inner_of(z)
    own_wq.wait()
    for copy in q1:
        copy.wait_recv()
    for copy in q2:
        copy.start()

    top, end = pl.ds(0, D // 2), pl.ds(D // 2, D // 2)
    right, left = p.step("z", 1), p.step("z", 3)
    to_right, to_left, to_far = s0.at[p.pos("z", 1)], s0.at[p.pos("z", 3)], s0.at[p.pos("z", 2)]
    near_right = remote(to_right.at[end], r1.at[0, end], 12, right)
    near_left = remote(to_left.at[top], r1.at[1, top], 13, left)
    far_right = remote(to_far.at[top], r1.at[2, top], 14, right)
    far_left = remote(to_far.at[end], r1.at[2, end], 15, left)
    sum_right = remote(to_right.at[top], r1.at[0, top], 17, right)
    sum_left = remote(to_left.at[end], r1.at[1, end], 18, left)
    ring_sums = [near_right, near_left, far_right, far_left, sum_right, sum_left]

    @pl.loop(0, 4)
    def _(j):
        o = ring_step(j)
        zz = (z + o) % 4
        at = pl.ds(pl.multiple_of(zz * 256, 256), 256)

        @pl.when(j == 1)
        def _():
            remote(n2, rows.at[z, c], 3, sib).wait_recv()
            on_left.start()
            remote(n2, rows.at[z, c], 1, sib).wait_recv()
            on_right.start()
            for o_near in (1, 3):
                near = rows.at[(z + o_near) % 4, c]
                remote(near, near, 4 + o_near, sib).start()

        @pl.when(j == 2)
        def _():
            on_left.wait_recv()
            on_right.wait_recv()
            far = rows.at[(z + 2) % 4, c]
            remote(far, far, 4 + 2, sib).start()

        remote(rows.at[zz, c], rows.at[zz, 1 - c], 4 + o, sib).wait_recv()
        r = rows[zz].reshape(256, D)
        for t in range(5):
            lo, hi = slice(t * 128, (t + 1) * 128), slice(FS + t * 128, FS + (t + 1) * 128)
            w = jnp.concatenate(
                [wgs[:, :, :, :, :, lo].reshape(D, 128), wgs[:, :, :, :, :, hi].reshape(D, 128)], axis=1
            )
            both = dot(r, w)
            gate, upper = both[:, :128], both[:, 128:]
            sig = jax.nn.sigmoid(gate)
            active = gate * sig
            d_inner = din[:, lo]
            inn[at, lo] = (active * upper).astype(BF16)
            dgu[at, lo] = (d_inner * upper * sig * (1.0 + gate * (1.0 - sig))).astype(BF16)
            dgu[at, hi] = (d_inner * active).astype(BF16)

        for h in range(2):
            turned = dot_last(wgs[h].reshape(1024, 2 * FS), dgu[at]).astype(BF16)
            for cc in range(2):
                part[zz, cc, h * 1024 : (h + 1) * 1024] = turned[:, cc * TOK : (cc + 1) * TOK]

        remote(part.at[zz, 1 - c], r0.at[zz], 8 + o, sib).start()
        d_inner_of((z + ring_step((j + 1) % 4)) % 4)
        remote(part.at[zz, 1 - c], r0.at[zz], 8 + o, sib).wait_recv()

        @pl.loop(0, D, step=128)
        def _(t):
            here = pl.ds(pl.multiple_of(t, 128), 128)
            s0[zz, here] = (part[zz, c, here].astype(F32) + r0[zz, here].astype(F32)).astype(BF16)

        @pl.when(j == 1)
        def _():
            near_right.start()

        @pl.when(j == 2)
        def _():
            near_left.start()

        @pl.when(j == 3)
        def _():
            far_right.start()
            far_left.start()

        @pl.when(j == 0)
        def _():
            for t in range(8):
                left = rows[z, :, :, t * 256 : (t + 1) * 256].reshape(256, D // 8)
                dwg[t // 4, t % 4] = dot_rows(left, dgu[at]).astype(BF16).reshape(2, TOK, 2 * FS)
            for copy in q2:
                copy.wait_recv()
            for copy in q3:
                copy.start()

    @pl.loop(0, 4)
    def _(t):
        cols = pl.ds(pl.multiple_of(t * 512, 512), 512)
        mixs[:, :, :, cols] = dot(inn[...], wds[:, cols]).astype(BF16).reshape(4, 2, TOK, 512)

    mix_core = remote(mixs.at[:, 1 - c], m0, 16, sib)
    mix_core.start()
    others = [((z + o) % 4, pl.ds(pl.multiple_of((z + o) % 4 * 256, 256), 256)) for o in (1, 2, 3)]

    def gate_up_block(t):
        cols = pl.ds(pl.multiple_of(t * 256, 256), 256)
        total = dwg[t // 4, t % 4].reshape(256, 2 * FS).astype(F32)
        for zz, at in others:
            total = total + dot_rows(rows[zz, :, :, cols].reshape(256, 256), dgu[at])
        dwg[t // 4, t % 4] = total.astype(BF16).reshape(2, TOK, 2 * FS)

    pl.loop(0, 4)(gate_up_block)
    for first, over, add, at in ((far_right, sum_right, to_right, 0), (far_left, sum_left, to_left, D // 2)):
        first.wait_recv()

        @pl.loop(0, D // 2, step=128)
        def _(t, add=add, at=at):
            here = pl.ds(pl.multiple_of(t + at, 128), 128)
            add[here] = (add[here].astype(F32) + r1[2, here].astype(F32)).astype(BF16)

        over.start()
    pl.loop(4, 8)(gate_up_block)
    out_wg = local(dwg, dwg_out, 5)
    for copy in q3:
        copy.wait_recv()
    q4.start()

    @pl.loop(0, 5)
    def _(t):
        units = pl.ds(pl.multiple_of(t * 128, 128), 128)
        dwd32[units] = dot_rows(inn[:, units], ogs[...].reshape(8 * TOK, D))

    @pl.loop(0, 8)
    def _(i):
        yl, x = i // 4, i % 4
        at = pl.ds(pl.multiple_of(i * 80, 80), 80)
        lo, hi = dwd32[at, :1024], dwd32[at, 1024:]
        dwd[yl, x, 0] = jnp.concatenate([lo[:40], hi[:40]], axis=0).astype(BF16)
        dwd[yl, x, 1] = jnp.concatenate([lo[40:], hi[40:]], axis=0).astype(BF16)

    out_wd = local(dwd, dwd_out, 6)
    mix_core.wait_recv()

    @pl.loop(0, 4)
    def _(zz):
        @pl.loop(0, TOK, step=16)
        def _(t):
            here = pl.ds(pl.multiple_of(t, 16), 16)
            m0[zz, here] = (mixs[zz, c, here].astype(F32) + m0[zz, here].astype(F32)).astype(BF16)

    out_mix = local(m0, mix_out, 4)
    for copy in (near_right, near_left, sum_right, sum_left):
        copy.wait_recv()
    for t in range(0, D, 128):
        here = slice(t, t + 128)
        total = s0[z, here].astype(F32)
        for j in range(2):
            total = total + r1[j, here].astype(F32)
        dn[:, here] = total.T

    out_dn = local(dn, d_out, 7)
    q4.wait_recv()
    k.drain()
    for copy in sent:
        copy.wait_send()
    for o in range(4):
        remote(rows.at[0, 0], rows.at[0, 0], 4 + o, sib).wait_send()
        remote(part.at[0, 0], r0.at[0], 8 + o, sib).wait_send()
    for copy in ring_sums:
        copy.wait_send()
    mix_core.wait_send()
    for copy in (out_mix, out_wg, out_wd, out_dn):
        copy.wait()


def ffn(n2, OG, WG, WD, wq):
    outs = [
        sds((TOK, D), F32),
        sds((4, TOK, D), BF16),
        sds((2, 4, 2, TOK, 2 * FS), BF16),
        sds((2, 4, 2, 80, 1024), BF16),
        sds((2, 4, 2, 4, 2, 16, 2048), BF16),
    ]
    scratch = [
        pltpu.VMEM((4, 2, TOK, D), BF16),
        pltpu.VMEM((4, 2, TOK, D), BF16),
        pltpu.VMEM((2, 4, 2, 8, 16, 2 * FS), BF16),
        pltpu.VMEM((2, 4, 2, 80, 1024), BF16),
        pltpu.VMEM((FS, D), BF16),
        pltpu.VMEM((8 * TOK, 2 * FS), BF16),
        pltpu.VMEM((8 * TOK, FS), BF16),
        pltpu.VMEM((256, FS), F32),
        pltpu.VMEM((4, 2, D, TOK), BF16),
        pltpu.VMEM((4, 2, TOK, D), BF16),
        pltpu.VMEM((4, D, TOK), BF16),
        pltpu.VMEM((4, D, TOK), BF16),
        pltpu.VMEM((3, D, TOK), BF16),
        pltpu.VMEM((4, TOK, D), BF16),
        pltpu.VMEM((2, 4, 2, TOK, 2 * FS), BF16),
        pltpu.VMEM((FS, D), F32),
        pltpu.VMEM((2, 4, 2, 80, 1024), BF16),
        pltpu.VMEM((TOK, D), F32),
        pltpu.VMEM((16, 2048), BF16),
        pltpu.SemaphoreType.DMA((19,)),
        pltpu.SemaphoreType.DMA((19,)),
        pltpu.SemaphoreType.DMA((8,)),
        pltpu.SemaphoreType.DMA((16,)),
        pltpu.SemaphoreType.DMA((16,)),
        pltpu.SemaphoreType.DMA((1,)),
    ]
    return pl.pallas_call(
        ffn_body,
        out_shape=outs,
        in_specs=[ANY] * 5,
        out_specs=[ANY] * 5,
        scratch_shapes=scratch,
        name="ffn",
        compiler_params=pltpu.CompilerParams(
            collective_id=1, has_side_effects=True, vmem_limit_bytes=60 << 20
        ),
    )(n2, OG, WG, WD, wq)


def back_body(*refs):
    (DN, X_IN, OG_IN, RESID, ATT, PT, PROBS, WQ, WO, KV, mix_part, dwg, dwd, NA) = refs[:14]
    (ROPE, GAINS, QKGAIN) = refs[14:17]
    (IN_GRAD, MIXED, GWG, GWD, GQ, GO, SMALL) = refs[17:24]
    (dn, xv, ogv, resid, pt, kept, in_grad, mixed, kvs, qns, dts, dns, dqt, dpt, datt, dres) = refs[24:40]
    (kpart, k0, k1, ks1, k2, kres, w2, wo2, low2, att2, do, dp, dpm, na2, dqm, mix1) = refs[40:56]
    (rope, gains, qkgain, mix_held) = refs[56:60]
    scr = list(refs[60:])
    parts = []
    for i, shapes in enumerate(PLANE_SHAPES + O_SHAPES):
        n = 2 * len(shapes) + (i < 4)
        parts.append(scr[:n])
        scr = scr[n:]
    vec, vrecv, ssem, rsem, lsem = scr
    p = Place()
    k = Links(ssem, rsem, lsem)
    yl, z, c = p.yl, p.z, p.c
    m = z * 2 + c
    sib = p.step("c", 1)
    yl_partner = p.at(y=p.yh * 2 + 1 - yl)
    partners = [p.step(a, j) for a in "xyz" for j in (1, 2, 3)]
    partners += [p.at(z=(z + j) % 4, c=1 - c) for j in range(4)]
    slab_to, slab_from = slab_target(p), slab_source(p)
    own_slab = same(p, slab_to)
    met = greet_plane(partners, slab_to, slab_from, own_slab)
    get = {}

    def fetch(**pairs):
        for name, (src, dst) in pairs.items():
            get[name] = k.local(src, dst)

    fetch(dn=(DN, dn), og=(OG_IN, ogv), resid=(RESID, resid), gains=(GAINS, gains))
    get_w = [k.local(WO.at[t // 4, t % 4], wo2.at[t]) for t in range(8)]
    fetch(pt=(PT, pt), rope=(ROPE, rope), qkgain=(QKGAIN, qkgain), att=(ATT, att2.at[0]))
    met()
    plane = [
        ring_reduce(p, k, dwg, wg_stages(0), parts[0], 16),
        ring_reduce(p, k, dwg, wg_stages(1), parts[1], 16),
        ring_reduce(p, k, dwd, wd_stages(p, 0), parts[2], 16),
        ring_reduce(p, k, dwd, wd_stages(p, 1), parts[3], 16),
    ]
    for step in plane + plane:
        next(step)
    pair_att = k.send(ATT, att2.at[1], sib)

    mixing = mix_reduce(p, k, mix_part, mix1, mix_held)
    next(mixing)
    for name in ("dn", "og", "resid", "gains"):
        get[name].wait()
    value = resid[...]
    scale_two = rms_scale(value)
    norm_two = value * scale_two
    d_resid = ogv[...].astype(F32) + norm_back(dn[...], norm_two, scale_two, gains[1:2, :])
    dres[...] = d_resid
    low2[0] = d_resid.astype(BF16)
    pair_low = k.send(low2.at[0], low2.at[1], sib)
    fetch(kv=(KV, kvs), kept=(PROBS, kept))
    for name in ("pt", "rope", "qkgain"):
        get[name].wait()
    cos, sin = rope[0], rope[1]
    qgain, kgain = qkgain[:HEAD], qkgain[HEAD:]

    @pl.loop(0, KV_HEADS)
    def _(g):
        for mm, unit in enumerate(query_units(pt, g, cos, sin, qgain)):
            qns[g, mm] = unit.T.astype(BF16)

    for t in range(8):
        get_w[t].wait()
        term = dot(low2[0, :, t * 256 : (t + 1) * 256], wo2[t].reshape(256, QD))
        datt[...] = term if t == 0 else datt[...] + term
    for g in range(KV_HEADS):
        tiles = []
        for t in range(2):
            at = (g * GROUP + 2 * t) * HEAD
            both = low(datt[:, at : at + 128]).T
            tiles.append(swap(both[:HEAD], both[HEAD:]))
        for mm in range(MICRO):
            none = jnp.zeros((HEAD, 256), F32)
            unit = jnp.concatenate([none, jnp.concatenate([tiles[0][mm], tiles[1][mm]], axis=1)], axis=0)
            dts[g, mm] = unit.astype(BF16)
            dns[g, mm] = unit.T.astype(BF16)
    fetch(x=(X_IN, xv), mix=(mix_part.at[z], mix1.at[3]))
    get["kv"].wait()
    get["kept"].wait()

    def unit(u):
        g, mm = u // 2, u % 2
        kv = unit_kv(kvs, mm, g)
        low_again = kept[u]
        again = low_again.astype(F32)
        d_probs = dot(kv, dts[g, mm])
        inner = jnp.sum(again * d_probs, axis=0, keepdims=True)
        d_scores = (again * (d_probs - inner)).astype(BF16)
        d_kv = dot(d_scores, qns[g, mm]) + dot(low_again, dns[g, mm])
        cols = pl.ds(pl.multiple_of(g * 128, 128), 128)
        kpart[mm, :, :, :, :, cols] = d_kv.astype(BF16).reshape(2, 4, 2, ROWS, 128)
        dqt[g, mm] = dot_rows(kv, d_scores)[:HEAD] * (HEAD ** -0.5)

    def core_send(cols):
        return k.send(kpart.at[:, :, :, 1 - c, :, cols], k0.at[:, :, :, :, cols], sib)

    def ring_send(core, cols):
        core.wait_recv()

        @pl.loop(0, 4)
        def _(zz):
            for a in range(2):
                for b in range(2):
                    here = (a, b, zz, EVERY, cols)
                    both = kpart[a, b, zz, c, :, cols].astype(F32) + k0[here].astype(F32)
                    k0[here] = both.astype(BF16)

        return [
            k.send(k0.at[:, :, p.pos("z", j), :, cols], k1.at[j - 1, :, :, :, cols], p.step("z", j))
            for j in (1, 2, 3)
        ]

    pl.loop(0, 6)(unit)
    core = core_send(KV_PARTS[0])
    ring = ring_send(core, KV_PARTS[0])
    pl.loop(6, 2 * KV_HEADS)(unit)
    core = core_send(KV_PARTS[1])
    for step in plane:
        next(step)
    early = [copy for copy, _ in k.sent.values()]
    ring += ring_send(core, KV_PARTS[1])
    next(mixing)
    get["att"].wait()
    pair_att.wait_recv()
    pair_low.wait_recv()
    att_cols = pl.ds(pl.multiple_of(c * 640, 128), 640)

    @pl.loop(0, 8)
    def _(t):
        cols = pl.ds(pl.multiple_of(t * 256, 256), 256)
        left = low2[:, :, cols].reshape(2 * TOK, 256)
        right = att2[:, :, att_cols].reshape(2 * TOK, 640)
        do[t // 4, t % 4] = dot_rows(left, right).astype(BF16).reshape(2, 4, 32, 640)

    outward = [staged_reduce(p, k, do, o_stages(i), parts[6 + i], 16) for i in range(3)]
    next(outward[0])

    query_sum = jnp.zeros((HEAD, TOK), F32)
    for g in range(KV_HEADS):
        heads = []
        for t in range(2):
            cols = slice(t * 128, (t + 1) * 128)
            heads += list(swap(dqt[g, 0, :, cols], dqt[g, 1, :, cols]))
        for h in range(GROUP):
            at = (g * GROUP + h) * HEAD
            d_raw, term = head_back(pt[at : at + HEAD], heads[h], cos, sin, qgain)
            query_sum = query_sum + term
            dpt[at : at + HEAD] = d_raw

    for copy in ring:
        copy.wait_recv()
    for a in range(2):
        for b in range(2):
            total = k0[a, b, z].astype(F32)
            for j in range(3):
                total = total + k1[j, a, b].astype(F32)
            ks1[a, b] = total.astype(BF16)
    across = k.send(ks1.at[:, 1 - yl], k2, yl_partner)
    next(outward[1])
    next(plane[0])
    next(plane[2])
    across.wait_recv()
    for a in range(2):
        kres[pl.ds(a * ROWS, ROWS)] = ks1[a, yl].astype(F32) + k2[a].astype(F32)
    key_sum = jnp.zeros((HEAD, TOK), F32)
    for g in range(KV_HEADS):
        both = kres[:, g * 128 : (g + 1) * 128].T
        at = QD + g * HEAD
        d_raw, term = head_back(pt[at : at + HEAD], both[:HEAD], cos, sin, kgain)
        key_sum = key_sum + term
        dpt[at : at + HEAD] = d_raw
        dpt[at + KD : at + KD + HEAD] = both[HEAD:]
    get_q = [k.local(WQ.at[0, t], w2.at[t]) for t in range(2)]
    get_n = [k.local(NA.at[:, :, :, pl.ds(t * 256, 256)], na2.at[t]) for t in range(2)]
    for t in range(8):
        block = jnp.concatenate([dpt[t * 240 : (t + 1) * 240], jnp.zeros((16, TOK), F32)], axis=0)
        dp[t] = block.T.astype(BF16)
    sums = jnp.concatenate(
        [jnp.sum(query_sum.T, axis=0, keepdims=True), jnp.sum(key_sum.T, axis=0, keepdims=True)], axis=1
    )
    vec[0] = jnp.broadcast_to(sums, (8, 128))
    small = small_reduce(p, k, vec, vrecv)
    next(small)

    last, keep = [], []

    def to_owners(total, dst):
        far = []
        for dz in range(4):
            for dc in range(2):
                zz, cc = (z + dz) % 4, (c + dc) % 2
                src = total.at[pl.ds(pl.multiple_of((zz * 2 + cc) * 16, 16), 16)]
                if dz == 0 and dc == 0:
                    keep.append(k.local(src, dst))
                else:
                    far.append((src, dst, p.at(z=zz, c=cc)))
        last.append(k.together(far, total.at[pl.ds(0, 112)]))

    def slab_home(half):
        slab = Slab(k, parts[2 + half][-1], GWD.at[:, pl.ds(half * 512, 512)], slab_from, own_slab)
        slab.start()
        return slab

    members = []
    for dz in range(4):
        for dc in range(2):
            zz, cc = (z + dz) % 4, (c + dc) % 2
            src = dp.at[zz * 2 + cc]
            if dz == 0 and dc == 0:
                own_dp = k.local(src, dpm.at[z, c])
            else:
                members.append(k.send(src, dpm.at[z, c], p.at(z=zz, c=cc)))
    next(outward[2])
    next(plane[1])
    next(plane[3])
    k.settle(early)
    own_dp.wait()
    for copy in members:
        copy.wait_recv()
    next(small)
    for t in range(8):
        get_n[t].wait()
        total = dot_rows(na2[t % 2].reshape(8 * TOK, 256), dpm[...].reshape(8 * TOK, 256))
        dqm[t // 4, t % 4] = total.astype(BF16).reshape(2, TOK, 256)
        if t < 6:
            get_n.append(k.local(NA.at[:, :, :, pl.ds((t + 2) * 256, 256)], na2.at[t % 2]))
    inward = [staged_reduce(p, k, dqm, q_stages(i), parts[4 + i], 16) for i in range(2)]
    for step in inward:
        next(step)
    get["mix"].wait()
    next(mixing, None)

    @pl.loop(0, TOK, step=16)
    def _(t):
        at = pl.ds(pl.multiple_of(t, 16), 16)
        total = resid[at]
        for j in (3, 0, 1):
            total = total + mix1[j, at].astype(F32)
        mixed[at] = total.astype(BF16)

    keep.append(k.local(mixed, MIXED))
    next(outward[0])
    next(outward[1])
    for half in range(2):
        next(plane[half], None)
        to_owners(parts[half][-1], GWG.at[:, pl.ds(pl.multiple_of(half * FF + m * FS, 128), FS)])
    slabs = []
    for half in range(2):
        next(plane[2 + half], None)
        slabs.append(slab_home(half))
    left = jnp.concatenate([dp[i] for i in range(8)], axis=1)

    def d_normed_block(t):
        get_q[t].wait()
        w = w2[t % 2].reshape(256, 2048)
        in_grad[:, t * 256 : (t + 1) * 256] = dot_last(left, w)
        if t < 6:
            get_q.append(k.local(WQ.at[(t + 2) // 4, (t + 2) % 4], w2.at[t % 2]))

    for t in range(4):
        d_normed_block(t)
    next(small)
    for step in inward:
        next(step)
    next(outward[2])
    for t in range(4, 8):
        d_normed_block(t)
    next(small)
    for step in outward:
        next(step)
    for half, step in enumerate(inward):
        next(step, None)
        to_owners(parts[4 + half][-1], GQ.at[:, pl.ds(pl.multiple_of(m * 256 + half * 128, 128), 128)])
    get["x"].wait()
    hidden = xv[...].astype(F32)
    scale_one = rms_scale(hidden)
    in_grad[...] = dres[...] + norm_back(in_grad[...], hidden * scale_one, scale_one, gains[0:1, :])
    keep.append(k.local(in_grad, IN_GRAD))
    next(small, None)
    keep.append(k.local(vec.at[4], SMALL))
    for i, step in enumerate(outward):
        next(step, None)
        total = parts[6 + i][-1]
        dst = GO.at[c, :, pl.ds(*O_PARTS[i])]
        keep.append(k.local(total.at[pl.ds(pl.multiple_of(c * 16, 16), 16)], dst))
        last.append(k.send(total.at[pl.ds(pl.multiple_of((1 - c) * 16, 16), 16)], dst, sib))
    for copy in keep:
        copy.wait()
    for copy in last:
        copy.wait_recv()
    for slab in slabs:
        slab.wait_recv()
        slab.wait_send()
    k.drain()


def head_back(raw, grad, cos, sin, gain):
    scale = head_scale(raw)
    normed = raw * scale
    d_head = grad * cos + half_back(grad * sin)
    scaled = d_head * gain
    inner = jnp.mean(scaled * normed, axis=0, keepdims=True)
    return scale * (scaled - normed * inner), d_head * normed


def back(*args):
    w = 2 * KD
    outs = [
        sds((TOK, D), F32),
        sds((TOK, D), BF16),
        sds((16, 2 * FF), BF16),
        sds((80, 1024), BF16),
        sds((16, 2048), BF16),
        sds((2, 16, 640), BF16),
        sds((8, 128), F32),
    ]
    scratch = [
        pltpu.VMEM((TOK, D), F32),
        pltpu.VMEM((TOK, D), BF16),
        pltpu.VMEM((TOK, D), BF16),
        pltpu.VMEM((TOK, D), F32),
        pltpu.VMEM((QKV, TOK), F32),
        pltpu.VMEM((2 * KV_HEADS, SEQ, 256), BF16),
        pltpu.VMEM((TOK, D), F32),
        pltpu.VMEM((TOK, D), BF16),
        pltpu.VMEM((2, 2, 4, 2, ROWS, w), BF16),
        pltpu.VMEM((KV_HEADS, 2, 256, 128), BF16),
        pltpu.VMEM((KV_HEADS, 2, 128, 256), BF16),
        pltpu.VMEM((KV_HEADS, 2, 256, 128), BF16),
        pltpu.VMEM((KV_HEADS, 2, HEAD, 256), F32),
        pltpu.VMEM((QKV, TOK), F32),
        pltpu.VMEM((TOK, QD), F32),
        pltpu.VMEM((TOK, D), F32),
        pltpu.VMEM((2, 2, 4, 2, ROWS, w), BF16),
        pltpu.VMEM((2, 2, 4, ROWS, w), BF16),
        pltpu.VMEM((3, 2, 2, ROWS, w), BF16),
        pltpu.VMEM((2, 2, ROWS, w), BF16),
        pltpu.VMEM((2, ROWS, w), BF16),
        pltpu.VMEM((TOK, w), F32),
        pltpu.VMEM((2, 2, 4, 2, 16, 2048), BF16),
        pltpu.VMEM((8, 2, 4, 2, 16, QD), BF16),
        pltpu.VMEM((2, TOK, D), BF16),
        pltpu.VMEM((2, TOK, QD), BF16),
        pltpu.VMEM((2, 4, 2, 4, 32, 640), BF16),
        pltpu.VMEM((8, TOK, 256), BF16),
        pltpu.VMEM((4, 2, TOK, 256), BF16),
        pltpu.VMEM((2, 4, 2, TOK, 256), BF16),
        pltpu.VMEM((2, 4, 2, TOK, 256), BF16),
        pltpu.VMEM((4, TOK, D), BF16),
        pltpu.VMEM((2, HEAD, TOK), F32),
        pltpu.VMEM((8, D), F32),
        pltpu.VMEM((2 * HEAD, 128), F32),
        pltpu.VMEM((TOK, D), BF16),
    ]
    for i, shapes in enumerate(PLANE_SHAPES + O_SHAPES):
        scratch += staged_scratch(shapes, i < 4)
    scratch += [
        pltpu.VMEM((5, 8, 128), F32),
        pltpu.VMEM((4, 3, 8, 128), F32),
        pltpu.SemaphoreType.DMA((56,)),
        pltpu.SemaphoreType.DMA((78,)),
        pltpu.SemaphoreType.DMA((30,)),
    ]
    return pl.pallas_call(
        back_body,
        out_shape=outs,
        in_specs=[ANY] * 17,
        out_specs=[ANY] * 7,
        scratch_shapes=scratch,
        name="back",
        compiler_params=pltpu.CompilerParams(
            collective_id=2, has_side_effects=True, vmem_limit_bytes=60 << 20
        ),
    )(*args)


def finish_body(*refs):
    IN_GRAD, MIXED, GWG, GWD, GQ, GO, SUMS, WG, WQ, g1, g2 = refs[:11]
    in_out, mixed_out, Q, O, G, DOWN, ATTN, FFN, QG, KG = refs[11:21]
    (gwg, gwd, gq, go, sums, wg, wq, q, o, g, down, attn, ffn_, qg, kg, ing, mix, sem) = refs[21:]
    used = []

    def copy(src, dst):
        out = pltpu.make_async_copy(src, dst, sem.at[len(used)])
        out.start()
        used.append(out)
        return out

    rows = [copy(IN_GRAD, ing), copy(MIXED, mix)]
    through = []
    got = [copy(a, b) for a, b in ((GQ, gq), (WQ, wq), (GO, go), (SUMS, sums), (GWD, gwd), (GWG, gwg), (WG, wg))]
    for one in got[:5]:
        one.wait()
    for one, (src, dst) in zip(rows, ((ing, in_out), (mix, mixed_out))):
        one.wait()
        through.append(copy(src, dst))
    wide = gq[...].astype(F32)
    lane = lax.broadcasted_iota(jnp.int32, (16, QKV), 1)
    total = jnp.zeros((16, QKV), F32)
    for i in range(8):
        piece = jnp.concatenate([wide[:, i * 256 : (i + 1) * 256], jnp.zeros((16, QKV - 256), F32)], axis=1)
        here = (lane >= i * 240) & (lane < (i + 1) * 240)
        total = jnp.where(here, pltpu.roll(piece, 240 * i, 1) if i else piece, total)
    q[...] = total
    through.append(copy(q, Q))
    o[...] = jnp.concatenate([go[0].astype(F32), go[1].astype(F32)], axis=1)
    through.append(copy(o, O))
    slab = gwd[...].astype(F32)
    down[...] = jnp.concatenate([slab[:40], slab[40:]], axis=1)
    through.append(copy(down, DOWN))
    attn[...] = flat(jnp.sum(wq[...].astype(F32) * total, axis=1, keepdims=True)) / g1[...].astype(F32)
    through.append(copy(attn, ATTN))
    qg[...] = sums[0:1, :HEAD]
    kg[...] = pltpu.roll(sums[...], HEAD, 1)[0:1, :HEAD]
    through += [copy(qg, QG), copy(kg, KG)]
    for one in got[5:]:
        one.wait()
    grown = gwg[...].astype(F32)
    g[...] = grown
    through.append(copy(g, G))
    ffn_[...] = flat(jnp.sum(wg[...].astype(F32) * grown, axis=1, keepdims=True)) / g2[...].astype(F32)
    through.append(copy(ffn_, FFN))
    for one in through:
        one.wait()


def flat(col):
    n = col.shape[0]
    place = lax.broadcasted_iota(jnp.int32, (n, n), 0) == lax.broadcasted_iota(jnp.int32, (n, n), 1)
    return jnp.sum(jnp.where(place, jnp.broadcast_to(col, (n, n)), 0.0), axis=0, keepdims=True)


def finish(*args):
    outs = [
        sds((TOK, D), F32),
        sds((TOK, D), BF16),
        sds((16, QKV), F32),
        sds((16, QD), F32),
        sds((16, 2 * FF), F32),
        sds((40, D), F32),
        sds((1, 16), F32),
        sds((1, 16), F32),
        sds((1, HEAD), F32),
        sds((1, HEAD), F32),
    ]
    ins = [(16, 2 * FF), (80, 1024), (16, 2048), (2, 16, 640), (8, 128), (16, 2 * FF), (16, QKV)]
    scratch = [pltpu.VMEM(a, F32 if a == (8, 128) else BF16) for a in ins]
    scratch += [pltpu.VMEM(a.shape, a.dtype) for a in outs[2:] + outs[:2]]
    return pl.pallas_call(
        finish_body,
        out_shape=outs,
        in_specs=[ANY] * 9 + [VMEM] * 2,
        out_specs=[ANY] * 10,
        scratch_shapes=scratch + [pltpu.SemaphoreType.DMA((19,))],
        name="finish",
        compiler_params=pltpu.CompilerParams(vmem_limit_bytes=60 << 20),
    )(*args)


def per_device(
    tokens,
    segment_ids,
    w_qkv,
    w_out,
    w_gate_up,
    w_down,
    attn_gain,
    ffn_gain,
    query_gain,
    key_gain,
    out_grad,
):
    g1, g2, g3, g4 = [a.reshape(1, -1) for a in (attn_gain, ffn_gain, query_gain, key_gain)]
    og_in = out_grad.reshape(TOK, D)
    x_in = tokens.reshape(TOK, D)
    (WO, WG, WD, OG, NA, KV, pt, probs, attended, resid, n2, wq_in, rope, gain_rows, head_gains) = front(
        x_in, w_qkv, w_out.T, w_gate_up, w_down, og_in, segment_ids, g1, g2, g3, g4, rope_parts()
    )
    d_normed, mix_part, dwg, dwd, WQ = ffn(n2, OG, WG, WD, wq_in)
    in_grad, mixed, gwg, gwd, gq, go, sums = back(
        d_normed, x_in, og_in, resid, attended, pt, probs, WQ, WO, KV, mix_part, dwg, dwd, NA,
        rope, gain_rows, head_gains,
    )
    outs = finish(in_grad, mixed, gwg, gwd, gq, go, sums, w_gate_up, w_qkv, g1, g2)
    return (
        outs[1].reshape(MICRO, ROWS, D),
        outs[0].reshape(MICRO, ROWS, D),
        outs[2],
        outs[3].T,
        outs[4],
        outs[5],
        outs[6].reshape(16),
        outs[7].reshape(16),
        outs[8].reshape(HEAD),
        outs[9].reshape(HEAD),
    )


def solution(mesh):
    return jax.shard_map(
        per_device,
        mesh=mesh,
        in_specs=(
            P(None, ("grp", "seq"), None),
            P(None, "grp"),
            P(("grp", "seq"), None),
            P(None, ("grp", "seq")),
            P(("grp", "seq"), None),
            P(("grp", "seq"), None),
            P(("grp", "seq")),
            P(("grp", "seq")),
            P(),
            P(),
            P(None, ("grp", "seq"), None),
        ),
        out_specs=(
            P(None, ("grp", "seq"), None),
            P(None, ("grp", "seq"), None),
            P(("grp", "seq"), None),
            P(None, ("grp", "seq")),
            P(("grp", "seq"), None),
            P(("grp", "seq"), None),
            P(("grp", "seq")),
            P(("grp", "seq")),
            P(),
            P(),
        ),
        check_vma=False,
    )
```
